32 devices in a mesh: sec: 2 (over y), gx: 4 (over z), gy: 4 (over x, core).
Axes of the slice: x: 2, y: 2, z: 4, core: 2. Of those that a mesh axis runs over, the one named last changes fastest.
Arguments:
- atm_flux: bfloat16 [5120, 8, 128], P(('sec', 'gx', 'gy')), may hold values from -6 to 6
- remap_weights: bfloat16 [20480, 128, 128], P(('sec', 'gx', 'gy')), may hold values from -0.25 to 0.25
- remap_src: int32 [20480], P(('sec', 'gx', 'gy')), may hold values from 0 to 159
- remap_dst: int32 [20480], P(('sec', 'gx', 'gy')), may hold values from 0 to 127
- remap_owner: int32 [20480, 1], P(('sec', 'gx', 'gy')), may hold values from 0 to 31; in each aligned block of 640 rows (0 to 639, 640 to 1279, ...) at most 40 rows name the same one
- tracers: float32 [2, 16, 1024, 512], P(None, None, ('sec', 'gx'), 'gy'), may hold values from -6 to 6
- currents: float32 [2, 16, 1024, 512], P(None, None, ('sec', 'gx'), 'gy'), may hold values from -4 to 4
- land_sea: int32 [1024, 512], P(('sec', 'gx'), 'gy'), may hold values 0 or 1
Outputs:
- tracers_out: float32 [2, 16, 1024, 512], P(None, None, ('sec', 'gx'), 'gy')
- atmosphere_surface_temp: float32 [5120, 128], P(('sec', 'gx', 'gy'))
The draws below stay inside these ranges and needn't reach their ends.
Inputs may be any that keep to these rules, and one draw needn't show every extreme that they name: `remap_owner`: among the 640 nonzero blocks of each device, no ocean device is named more than 40 times; some ocean device is named exactly 40 times.
All inputs are finite; a program needn't handle non-finite values. No bound on the sum of `land_sea` on one device may be relied on, other than what follows from the above.
Results may differ from the reference program's by a relative error of at most 0.0031.
Values may be sent and summed in bfloat16 or wider, within the bound.
No kernel may reach another device: no remote copies, remote signals or barrier semaphores. Data moves between devices by JAX's collectives and lax.ppermute only.
A program may use at most 128 MiB of HBM per device.

```python
import math
import jax
import jax.numpy as jnp
import numpy as np
from jax import lax

REMAP_CELLS = 128
NF = 8
NL = 16
FANOUT = 4
ATMOS_BLOCKS = 160
CX = 128
NNZ_DEV = 640
CAP = 40
A_BLOCKS = 5120
NNZ = 20480
OCEAN_ROW_COUNT = 1024
NY = 512
N_SEC = 2
N_GX = 4
N_GY = 4
DEVICES = 32


def place_ends(result, key, smallest, largest):
    index_at = [jax.random.randint(jax.random.fold_in(key, axis), (), 0, length) for axis, length in enumerate(result.shape)]
    widest = result.shape.index(max(result.shape))
    next_to = index_at[:widest] + [(index_at[widest] + 1) % result.shape[widest]] + index_at[widest + 1:]
    return result.at[tuple(index_at)].set(smallest).at[tuple(next_to)].set(largest)


def shard_levels(stream_key, shape, split, low, high):
    loudness = 1.0
    for axis_at, shards_of in split:
        steps = jax.random.uniform(jax.random.fold_in(jax.random.fold_in(stream_key, 6), axis_at), (shards_of,), jnp.float32, low / len(split), high / len(split))
        loudness = loudness * jnp.repeat(jnp.exp(steps), shape[axis_at] // shards_of).reshape((-1,) + (1,) * (len(shape) - 1 - axis_at))
    return loudness


def shared_out(stream_key, own, number, rows, count, top, reach, slope):
    order = jax.random.permutation(stream_key, count)
    heavy_load, usual = shares(count, rows * top, reach, slope, True), shares(count, rows * top, reach, slope, False)
    places = jnp.arange(count)

    def named(sizes, offset_by):
        used = int((sizes > 0).sum())
        fixed = max(1, used // 4)
        shifted = fixed + (places - fixed + offset_by * (used - fixed)) % max(1, count - fixed)
        return jnp.zeros((count,), jnp.int32).at[order[jnp.where(places < fixed, places, shifted)]].set(jnp.asarray(sizes, jnp.int32))

    sizes = jnp.where(number % 4 == 0, named(heavy_load, number // 4), named(usual, number - number // 4 - 1))
    mixed = jax.random.permutation(jax.random.fold_in(own, 3), count)
    donor, receiver = mixed[0:count // 2 * 2:2], mixed[1:count // 2 * 2:2]
    margin = jnp.minimum(sizes[donor] - 1, reach - sizes[receiver]) // 2
    margin = jnp.where((donor == order[0]) | (receiver == order[0]) | (sizes[receiver] == 0), 0, jnp.maximum(margin, 0))
    shifted = jax.random.randint(jax.random.fold_in(own, 4), (count // 2,), 0, 1 << 20) % (margin + 1)
    sizes = sizes.at[donor].add(-shifted).at[receiver].add(shifted)
    members = jnp.searchsorted(jnp.cumsum(sizes), jnp.arange(rows * top), side="right").astype(jnp.int32)
    table = members.reshape(top, rows).T
    table = table[jax.random.permutation(jax.random.fold_in(own, 1), rows)]
    offset_by = jax.random.randint(jax.random.fold_in(own, 2), (rows, 1), 0, top)
    return jnp.take_along_axis(table, (jnp.arange(top)[None, :] + offset_by) % top, axis=1)


def shares(amount, total, reach, slope, full):
    weights = [(1 << 20) // math.isqrt(rank ** slope) + 1 for rank in range(1, amount + 1)]
    largest = reach if full else min(reach, max(-(-total // amount), total * weights[0] // sum(weights)))
    least = 1 if total - largest >= amount - 1 else 0
    given, surplus = [largest] + [least] * (amount - 1), total - largest - least * (amount - 1)
    while surplus > 0:
        candidates = [i for i in range(1, amount) if given[i] < largest] or [i for i in range(1, amount) if given[i] < reach]
        mass, remaining = sum([weights[i] for i in candidates]), surplus
        for i in candidates:
            more = min(reach - given[i], max(1, remaining * weights[i] // mass), surplus)
            given[i] = given[i] + more
            surplus = surplus - more
    return np.array(given)


def noise(stream_key, shape, width, reach, split=(), kind=jnp.bfloat16):
    gain = shard_levels(stream_key, shape, split, -0.22, 0.18) if split else 1.0
    values = jax.random.normal(stream_key, shape, jnp.float32) * width * gain
    return jnp.minimum(jnp.maximum(values, -reach), reach).astype(kind)


def setup_inputs(seed: int = 0) -> dict:
    arg_keys = jax.random.split(jax.random.key(seed), 9)
    atm_flux = noise(arg_keys[0], (A_BLOCKS, NF, REMAP_CELLS), 1.0, 6.0, ((0, 32),))
    remap_weights = noise(arg_keys[1], (NNZ, REMAP_CELLS, REMAP_CELLS), (REMAP_CELLS * FANOUT * ATMOS_BLOCKS // CX) ** -0.5, 0.25, ((0, 32),))
    remap_src = place_ends(jax.random.randint(arg_keys[2], (NNZ,), 0, ATMOS_BLOCKS), jax.random.fold_in(arg_keys[2], 1), 0, ATMOS_BLOCKS - 1).astype(jnp.int32)
    remap_dst = place_ends(jax.random.randint(arg_keys[3], (NNZ,), 0, CX), jax.random.fold_in(arg_keys[3], 1), 0, CX - 1).astype(jnp.int32)
    remap_owner_keys = jax.random.split(jax.random.fold_in(arg_keys[4], 1), NNZ // NNZ_DEV)
    remap_owner_turns = jax.random.permutation(jax.random.fold_in(arg_keys[4], 3), NNZ // NNZ_DEV)
    remap_owner = jax.vmap(lambda own, number: shared_out(jax.random.fold_in(arg_keys[4], 2), own, number, NNZ_DEV, DEVICES, 1, CAP, 1))(remap_owner_keys, remap_owner_turns).reshape((NNZ, 1))
    tracers = noise(arg_keys[5], (2, NL, OCEAN_ROW_COUNT, NY), 1.0, 6.0, ((2, 8), (3, 4)), jnp.float32)
    currents = noise(arg_keys[6], (2, NL, OCEAN_ROW_COUNT, NY), 0.3, 4.0, ((2, 8), (3, 4)), jnp.float32)
    land_sea = place_ends((jax.random.randint(arg_keys[7], (OCEAN_ROW_COUNT, NY), 0, 10) < 7).astype(jnp.int32), jax.random.fold_in(arg_keys[7], 1), 0, 1)
    return {"atm_flux": atm_flux, "remap_weights": remap_weights, "remap_src": remap_src, "remap_dst": remap_dst, "remap_owner": remap_owner, "tracers": tracers, "currents": currents, "land_sea": land_sea}


KH = 0.1
KV = 0.1


def substep(tracer_field, velocity, wetness, heat, salt, shortwave):
    levels = tracer_field.shape[1]
    centre = tracer_field[..., 1:-1, 1:-1]
    east = tracer_field[..., 1:-1, 2:]
    west = tracer_field[..., 1:-1, :-2]
    north = tracer_field[..., 2:, 1:-1]
    south = tracer_field[..., :-2, 1:-1]
    wet_centre = wetness[1:-1, 1:-1]
    open_east = wet_centre * wetness[1:-1, 2:]
    open_west = wet_centre * wetness[1:-1, :-2]
    open_north = wet_centre * wetness[2:, 1:-1]
    open_south = wet_centre * wetness[:-2, 1:-1]
    u_along = velocity[0]
    v_along = velocity[1]
    flow_east = 0.5 * (u_along[:, 1:-1, 1:-1] + u_along[:, 1:-1, 2:]) * open_east
    flow_west = 0.5 * (u_along[:, 1:-1, :-2] + u_along[:, 1:-1, 1:-1]) * open_west
    flow_north = 0.5 * (v_along[:, 1:-1, 1:-1] + v_along[:, 2:, 1:-1]) * open_north
    flow_south = 0.5 * (v_along[:, :-2, 1:-1] + v_along[:, 1:-1, 1:-1]) * open_south
    advect = -(flow_east * 0.5 * (centre + east) - flow_west * 0.5 * (west + centre)
               + flow_north * 0.5 * (centre + north) - flow_south * 0.5 * (south + centre))
    spread = KH * (open_east * (east - centre) + open_west * (west - centre)
                   + open_north * (north - centre) + open_south * (south - centre))
    mixing = KV * (centre[:, 1:] - centre[:, :-1])
    blank = jnp.zeros_like(centre[:, :1])
    vertical = jnp.concatenate([mixing, blank], axis=1) - jnp.concatenate([blank, mixing], axis=1)
    depth = jnp.arange(levels, dtype=jnp.float32)
    profile = jnp.exp(-depth / 4.0) * (1.0 - jnp.exp(jnp.float32(-0.25)))
    surface = (depth == 0.0).astype(jnp.float32)
    warm = 0.3 * profile[:, None, None] * shortwave[None] + surface[:, None, None] * heat[None]
    fresh = surface[:, None, None] * salt[None] + jnp.zeros_like(warm)
    forcing = jnp.stack([warm, fresh])
    return centre + wet_centre * (advect + spread + vertical + forcing)


def forcing_fields(ocean_flux, currents, levels):
    surface = (jnp.arange(levels) == 0).astype(jnp.float32)[:, None, None]
    u_eff = currents[0] + 0.1 * surface * ocean_flux[6][None]
    v_eff = currents[1] + 0.1 * surface * ocean_flux[7][None]
    heat = 0.2 * (ocean_flux[1] + ocean_flux[2] + ocean_flux[3]) - 0.15 * ocean_flux[5]
    salt = 0.2 * ocean_flux[4] - 0.1 * ocean_flux[5]
    return u_eff, v_eff, heat, salt, ocean_flux[0]


def reference(atm_flux, remap_weights, remap_src, remap_dst, remap_owner, tracers, currents, land_sea):
    device_list = N_SEC * N_GX * N_GY
    total = remap_src.shape[0]
    device_share = total // device_list
    device_of = (jnp.arange(total, dtype=jnp.int32) // device_share).astype(jnp.int32)
    worldwide_source = (device_of * ATMOS_BLOCKS + remap_src).astype(jnp.int32)
    owners = remap_owner[:, 0]
    ocean_row = ((owners // N_GY) * CX + remap_dst).astype(jnp.int32)
    marine_block = (ocean_row * N_GY + owners % N_GY).astype(jnp.int32)
    weight_groups = remap_weights.reshape(device_list, device_share, REMAP_CELLS, REMAP_CELLS)
    source_groups = worldwide_source.reshape(device_list, device_share)

    def forward(pair):
        weights, sources = pair
        rows = jnp.take(atm_flux, sources, axis=0).astype(jnp.float32)
        return jnp.einsum("kij,kfj->kfi", weights.astype(jnp.float32), rows).astype(jnp.bfloat16)

    partial_flux = lax.map(forward, (weight_groups, source_groups)).reshape(total, NF, REMAP_CELLS)
    blocks = jnp.zeros((OCEAN_ROW_COUNT * N_GY, NF, REMAP_CELLS), jnp.float32).at[marine_block].add(partial_flux.astype(jnp.float32))
    ocean_flux = blocks.reshape(OCEAN_ROW_COUNT, N_GY, NF, REMAP_CELLS).transpose(2, 0, 1, 3).reshape(NF, OCEAN_ROW_COUNT, N_GY * REMAP_CELLS)
    u_eff, v_eff, heat, salt, shortwave = forcing_fields(ocean_flux, currents, NL)
    wetness = jnp.pad(land_sea.astype(jnp.float32), 1)
    velocity = jnp.pad(jnp.stack([u_eff, v_eff]), ((0, 0), (0, 0), (1, 1), (1, 1)))
    tracer_field = tracers
    for repeat in range(2):
        padded = jnp.pad(tracer_field, ((0, 0), (0, 0), (1, 1), (1, 1)))
        tracer_field = substep(padded, velocity, wetness, heat, salt, shortwave)
    surface_temp_blocks = tracer_field[0, 0].astype(jnp.bfloat16).reshape(OCEAN_ROW_COUNT * N_GY, REMAP_CELLS)
    selected_cells = jnp.take(surface_temp_blocks, marine_block, axis=0).reshape(device_list, device_share, REMAP_CELLS)

    def backward(pair):
        weights, values = pair
        return jnp.einsum("kij,ki->kj", weights.astype(jnp.float32), values.astype(jnp.float32))

    returning_terms = lax.map(backward, (weight_groups, selected_cells)).reshape(total, REMAP_CELLS)
    atmosphere_surface_temp = jnp.zeros((device_list * ATMOS_BLOCKS, REMAP_CELLS), jnp.float32).at[worldwide_source].add(returning_terms)
    return tracer_field, atmosphere_surface_temp
```

```python
import functools

import jax
import jax.numpy as jnp
from jax import lax
from jax.experimental import pallas as pl
from jax.experimental.pallas import tpu as pltpu
from jax.sharding import PartitionSpec as P

F32 = jnp.float32
BF16 = jnp.bfloat16
NT = (((1,), (1,)), ((), ()))
NN = (((1,), (0,)), ((), ()))
TN = (((0,), (0,)), ((), ()))
EVERY = ("sec", "gx", "gy")
NORTH = ("sec", "gx")
SENT = 5
KH = 0.1
KV = 0.1


def dot(left, right, dims):
    return lax.dot_general(left, right, dims, preferred_element_type=F32)


def iota(shape, dim):
    return lax.broadcasted_iota(jnp.int32, shape, dim)


def up(number, step):
    return -(-number // step) * step


def kernel_params(mebibytes):
    return pltpu.CompilerParams(vmem_limit_bytes=mebibytes << 20)


VMEM = pl.BlockSpec(memory_space=pltpu.VMEM)
SMEM = pl.BlockSpec(memory_space=pltpu.SMEM)
ANY = pl.BlockSpec(memory_space=pl.ANY)


def forward_kernel(parts, cap, gy, src, own, dst, flux, w, send, slots, held, mixed, acc, rows, xs, counts, sems):
    devices, chunk, wide = send.shape
    total, width, _ = held.shape
    batch = total // parts
    fields = flux.shape[1]
    first = chunk - 8
    last = width - 1

    def copy(c):
        return pltpu.make_async_copy(w.at[pl.ds(c * batch, batch)], held.at[pl.ds(c * batch, batch)], sems.at[c])

    for c in range(parts):
        copy(c).start()

    def clear(o, _):
        counts[o] = 0
        return 0

    lax.fori_loop(0, devices, clear, 0)
    rows[...] = jnp.full_like(rows, 255.0)
    acc[...] = jnp.zeros_like(acc)
    xs[...] = jnp.zeros_like(xs)
    full = flux[...].astype(F32)
    one = [full[:, f : f + 1] for f in range(fields)]
    heat = 0.2 * (one[1] + one[2] + one[3]) - 0.15 * one[5]
    salt = 0.2 * one[4] - 0.1 * one[5]
    heat_high = heat.astype(BF16).astype(F32)
    salt_high = salt.astype(BF16).astype(F32)
    mixed[...] = jnp.concatenate(
        [one[0], heat_high, salt_high, one[6], one[7], heat - heat_high, salt - salt_high, jnp.zeros_like(heat)], axis=1
    ).astype(BF16)

    def place(k, _):
        owner = own[k]
        at = counts[owner]
        counts[owner] = at + 1
        slot = owner * cap + jnp.minimum(at, cap - 1)
        slots[k] = slot
        rows[pl.ds(slot, 1), :] = jnp.full((1, width), dst[k].astype(F32), F32)
        return 0

    lax.fori_loop(0, total, place, 0, unroll=8)
    low_rows = iota((fields, width), 0)
    low_rows = (low_rows == 1) | (low_rows == 2)

    def work(c, _):
        copy(c).wait()
        for b in range(0, batch, 2):
            k = c * batch + b
            left = jnp.concatenate([mixed[src[k]], mixed[src[k + 1]]], axis=0)
            both = dot(left, held[pl.ds(k, 2)].reshape(2 * width, width), NT)
            for z, part in enumerate((both[:fields, :width], both[fields:, width:])):
                part = part + jnp.where(low_rows, pltpu.roll(part, fields - 4, 0), 0.0)
                acc[pl.ds(pl.multiple_of(slots[k + z] * fields, fields), fields), :] = part
        return 0

    lax.fori_loop(0, parts, work, 0)

    lane = iota((cap, width), 1).astype(F32)
    sub = iota((cap, width), 0).astype(F32)
    row = iota((24, wide), 0)
    picks = {
        4: (0, 0), 5: (1, 0), 6: (3, 0), 7: (4, 0), 12: (0, last), 13: (1, last), 14: (3, last), 15: (4, last),
        20: (2, 0), 21: (3, 1), 22: (2, last), 23: (3, last - 1),
    }
    pick = jnp.full((24, wide), -1, jnp.int32)
    for at, (field, column) in picks.items():
        pick = jnp.where(row == at, field * width + column, pick)
    select = (iota((24, wide), 1) == pick).astype(F32).astype(BF16)
    row = iota((8, cap), 0)
    wanted = jnp.zeros((8, cap), F32)
    for at, x in enumerate((0, 1, last, last - 1, 0, 0, last, last)):
        wanted = jnp.where(row == at, float(x), wanted)
    group = 8

    def owners(g, _):
        ds = [g * group + j for j in range(group)]
        five = []
        for d in ds:
            x = [acc[pl.ds(d * cap * fields + f, cap, stride=fields), :] for f in range(SENT)]
            x = jnp.concatenate(x, axis=1)
            xs[d, 0:cap, :] = x
            five.append(x.astype(BF16))
        where = [rows[pl.ds(pl.multiple_of(d * cap, 8), cap), :] for d in ds]
        hot = [(lane == r).astype(F32).astype(BF16) for r in where]
        flat = [jnp.sum(jnp.where(lane == sub, r, 0.0), axis=0, keepdims=True) for r in where]
        flat = [jnp.where(lane[:1] < cap, f, 255.0) for f in flat]
        edge = [dot(select, x, NT).astype(BF16) for x in five]
        sides = [dot(e, h, NN) for e, h in zip(edge, hot)]
        ends = [dot((f[:, :cap] == wanted).astype(F32).astype(BF16), x, NN) for f, x in zip(flat, five)]
        for d, f, side, end in zip(ds, flat, sides, ends):

            def at(offset):
                return lax.rem(d + offset + 2 * devices, devices)

            xs[at(-gy), first : first + 1, :] = end[0:1]
            xs[at(-gy), first + 1 : first + 2, 4 * width :] = end[1:2, 4 * width :]
            xs[at(gy), first + 2 : first + 3, :] = end[2:3]
            xs[at(gy), first + 3 : first + 4, 4 * width :] = end[3:4, 4 * width :]
            xs[at(-gy - 1), first + 4 : first + 5, 3 * width :] = end[4:5, 3 * width :]
            xs[at(-gy + 1), first + 5 : first + 6, 3 * width :] = end[5:6, 3 * width :]
            xs[at(gy - 1), first + 6 : first + 7, 3 * width :] = end[6:7, 3 * width :]
            xs[at(gy + 1), first + 7 : first + 8, 3 * width :] = end[7:8, 3 * width :]
            xs[at(-1), first + 4 : first + 8, 0:width] = side[4:8]
            xs[at(1), first + 4 : first + 8, width : 2 * width] = side[12:16]
            xs[at(-1), first + 4 : first + 6, 2 * width : 3 * width] = side[20:22]
            xs[at(1), first + 6 : first + 8, 2 * width : 3 * width] = side[22:24]
            xs[d, first + 1 : first + 2, 0:width] = f
        return 0

    lax.fori_loop(0, devices // group, owners, 0)

    def out(d, _):
        send[d] = xs[d].astype(BF16)
        return 0

    lax.fori_loop(0, devices, out, 0, unroll=8)


def forward(flux, w, src, own, dst, devices, cap, gy, parts=20):
    total, width, _ = w.shape
    chunk = up(cap + 8, 16)
    fields = flux.shape[1]
    wide = SENT * width
    return pl.pallas_call(
        functools.partial(forward_kernel, parts, cap, gy),
        in_specs=[SMEM, SMEM, SMEM, VMEM, ANY],
        out_specs=[VMEM, SMEM],
        scratch_shapes=[
            pltpu.VMEM(w.shape, BF16),
            pltpu.VMEM(flux.shape, BF16),
            pltpu.VMEM((devices * cap * fields, width), F32),
            pltpu.VMEM((devices * cap, width), F32),
            pltpu.VMEM((devices, chunk, wide), F32),
            pltpu.SMEM((devices,), jnp.int32),
            pltpu.SemaphoreType.DMA((parts,)),
        ],
        out_shape=[jax.ShapeDtypeStruct((devices, chunk, wide), BF16), jax.ShapeDtypeStruct((total,), jnp.int32)],
        compiler_params=kernel_params(58),
        cost_estimate=pl.CostEstimate(flops=2 * total * 8 * width * width, bytes_accessed=total * width * width * 2, transcendentals=0),
        name="forward_remap",
    )(src, own, dst, flux, w)


def columns_kernel(tracers, currents, land, west, east):
    levels = tracers.shape[1]
    width = tracers.shape[3]
    last = width - 1
    lane = iota((width, width), 1)

    def put(held, plane, row, column):
        return jnp.where(lane == row, pltpu.roll(plane, lax.rem(row - column + width, width), 1), held)

    def level(l, held):
        w, e = held
        for t in range(2):
            q = tracers[t, l]
            w = put(put(w, q, t * levels + l, 0), q, (2 + t) * levels + l, 1)
            e = put(put(e, q, t * levels + l, last), q, (2 + t) * levels + l, last - 1)
        u = currents[0, l]
        w = put(put(w, u, 4 * levels + l, 0), u, 6 * levels + l, 1)
        e = put(put(e, u, 4 * levels + l, last), u, 6 * levels + l, last - 1)
        v = currents[1, l]
        return put(w, v, 5 * levels + l, 0), put(e, v, 5 * levels + l, last)

    zero = jnp.zeros((width, width), F32)
    w, e = lax.fori_loop(0, levels, level, (zero, zero))
    wet = land[...].astype(F32)
    w = put(put(w, wet, 7 * levels, 0), wet, 7 * levels + 1, 1)
    e = put(put(e, wet, 7 * levels, last), wet, 7 * levels + 1, last - 1)
    west[...] = w.T
    east[...] = e.T


def rows_kernel(tracers, currents, land, from_west, from_east, south, north):
    levels = tracers.shape[0] // 2 // land.shape[0]
    height, width = land.shape
    lane = iota((1, width), 1)
    for out, edge, second in ((south, 0, 1), (north, height - 1, height - 2)):
        out[0 : 2 * levels] = tracers[pl.ds(edge, 2 * levels, stride=height), :]
        out[2 * levels : 4 * levels] = tracers[pl.ds(second, 2 * levels, stride=height), :]
        out[4 * levels : 6 * levels] = currents[pl.ds(edge, 2 * levels, stride=height), :]
        out[6 * levels : 7 * levels] = currents[pl.ds(levels * height + second, levels, stride=height), :]
        wet = [land[x : x + 1, :].astype(F32) for x in (edge, second)]
        out[7 * levels : 7 * levels + 8] = jnp.concatenate(wet + [jnp.zeros((6, width), F32)], axis=0)
    base = 7 * levels + 8
    for start, stop, at in ((0, 2 * levels, 0), (4 * levels, 6 * levels, 2 * levels), (7 * levels, 7 * levels + 8, 4 * levels)):
        w, e = from_west[start:stop], from_east[start:stop]
        there = slice(base + at, base + at + stop - start)
        south[there] = jnp.where(lane == 0, w, pltpu.roll(e, width - 1, 1))
        north[there] = jnp.where(lane == width - 1, e, pltpu.roll(w, 1, 1))


def plus_side(q, other, speed, speed_other, passable):
    return KH * passable * (other - q) - 0.25 * (speed + speed_other) * passable * (q + other)


def minus_side(q, other, speed, speed_other, passable):
    return KH * passable * (other - q) + 0.25 * (speed_other + speed) * passable * (other + q)


def level_profile(levels, width):
    depth = iota((levels, width), 0).astype(F32)
    return jnp.exp(-depth / 4.0) * (1.0 - jnp.exp(jnp.full((levels, width), -0.25, F32)))


def strip_step(q, q_plus, q_minus, across, across_plus, across_minus, along, corner_q, corner_along, wet, wet_plus, wet_minus, corner_wet, forcing):
    levels, width = q.shape
    lane = iota((1, width), 1)
    row = iota((levels, 1), 0)

    def ahead(x, corner):
        return jnp.where(lane == width - 1, corner, pltpu.roll(x, width - 1, 1))

    def behind(x, corner):
        return jnp.where(lane == 0, corner, pltpu.roll(x, 1, 1))

    total = plus_side(q, q_plus, across, across_plus, wet * wet_plus)
    total += minus_side(q, q_minus, across, across_minus, wet * wet_minus)
    total += plus_side(q, ahead(q, corner_q), along, ahead(along, corner_along), wet * ahead(wet, corner_wet))
    total += minus_side(q, behind(q, corner_q), along, behind(along, corner_along), wet * behind(wet, corner_wet))
    below = jnp.where(row < levels - 1, pltpu.roll(q, levels - 1, 0) - q, 0.0)
    above = jnp.where(row > 0, q - pltpu.roll(q, 1, 0), 0.0)
    return q + total + wet * (KV * (below - above) + forcing)


def strips(tracer, levels, inner, outer, flux):
    width = outer[0].shape[1]
    lane = iota((1, width), 1)
    base = 7 * levels + 8
    north, south, east, west = outer

    def part(x, at, count=levels):
        return x[at : at + count]

    def corners(at, count):
        n, s = part(north, base + at, count), part(south, base + at, count)
        e = jnp.where(lane == width - 1, n, pltpu.roll(s, 1, 1))
        w = jnp.where(lane == width - 1, pltpu.roll(n, width - 1, 1), s)
        return n, s, e, w

    corner_q = corners(tracer * levels, levels)
    corner_u = corners(2 * levels, levels)
    corner_v = corners(3 * levels, levels)
    corner_wet = corners(4 * levels, 1)
    top = (iota((levels, 1), 0) == 0).astype(F32)
    profile = level_profile(levels, width)
    results = []
    for side in range(4):
        near, far = inner[side], outer[side]
        beside, out = part(near, tracer * levels), part(far, (2 + tracer) * levels)
        mid = part(far, tracer * levels)
        speed = 5 if side < 2 else 4
        along = part(far, (9 - speed) * levels)
        corner_along = (corner_u if side < 2 else corner_v)[side]
        across, across_in, across_out = part(far, speed * levels), part(near, speed * levels), part(far, 6 * levels)
        wet, wet_in, wet_out = part(far, 7 * levels, 1), part(near, 7 * levels, 1), part(far, 7 * levels + 1, 1)
        shortwave, heat, salt = flux[side]
        forcing = 0.3 * profile * shortwave + top * heat if tracer == 0 else top * salt
        if side % 2 == 0:
            pairs = (out, beside, across, across_out, across_in)
            wets = (wet, wet_out, wet_in)
        else:
            pairs = (beside, out, across, across_in, across_out)
            wets = (wet, wet_in, wet_out)
        results.append(strip_step(mid, *pairs, along, corner_q[side], corner_along, *wets, corner_wet[side], forcing))
    return results


def shifts(plane, north, south, east, west):
    height, width = plane.shape
    lane, row = iota(plane.shape, 1), iota(plane.shape, 0)
    return (
        jnp.where(lane == width - 1, east, pltpu.roll(plane, width - 1, 1)),
        jnp.where(lane == 0, west, pltpu.roll(plane, 1, 1)),
        jnp.where(row == height - 1, north, pltpu.roll(plane, height - 1, 0)),
        jnp.where(row == 0, south, pltpu.roll(plane, 1, 0)),
    )


def wet_products(wet, north, south, east, west):
    return [wet * other for other in shifts(wet, north, south, east, west)]


def coefficients(u, v, u_east, u_west, v_north, v_south, passable):
    east, west, north, south = passable
    height, width = u.shape
    lane, row = iota(u.shape, 1), iota(u.shape, 0)
    e = jnp.where(lane == width - 1, u_east, pltpu.roll(u, width - 1, 1))
    w = jnp.where(lane == 0, u_west, pltpu.roll(u, 1, 1))
    n = jnp.where(row == height - 1, v_north, pltpu.roll(v, height - 1, 0))
    s = jnp.where(row == 0, v_south, pltpu.roll(v, 1, 0))
    flow_e, flow_w = 0.25 * (u + e) * east, 0.25 * (w + u) * west
    flow_n, flow_s = 0.25 * (v + n) * north, 0.25 * (s + v) * south
    own = 1.0 + (flow_w - flow_e) + (flow_s - flow_n) - KH * (east + west + north + south)
    return own, KH * east - flow_e, KH * west + flow_w, KH * north - flow_n, KH * south + flow_s


def column(turned, index, lane):
    return pltpu.roll(turned, lax.rem(lane - index + 2 * turned.shape[1], turned.shape[1]), 1)


def corrected(edge, x_rows):
    row = iota((edge.shape[0], 1), 0)
    for at, x in x_rows:
        edge = edge + jnp.where(row == at, 0.1 * x, 0.0)
    return edge


def surface_kernel(
    cap, levels, got, tracers, currents, land, own_n, own_s, own_e, own_w, from_n, from_s, from_e, from_w,
    back, flux, rim, in_n, in_s, in_e, in_w, out_n, out_s, out_e, out_w,
):
    devices, chunk, wide = got.shape
    height, width = land.shape
    first = chunk - 8
    last = width - 1
    lane = iota((1, width), 1)
    ext = got[0, first:chunk, :].astype(F32)
    lines = [ext[1:2, :chunk]]
    for d in range(1, devices):
        piece = got[d, first:chunk, :].astype(F32)
        lines.append(piece[1:2, :chunk])
        ext = ext + piece
    where = jnp.concatenate(lines, axis=1)
    hot = (iota((height, devices * chunk), 0).astype(F32) == where).astype(F32)
    sums = dot(hot.astype(BF16), got[...].reshape(devices * chunk, wide), NN)
    shortwave, heat, salt, stress_u, stress_v = [sums[:, f * width : (f + 1) * width] for f in range(SENT)]
    wet = land[...].astype(F32)
    u0 = currents[0, 0] + 0.1 * stress_u
    v0 = currents[1, 0] + 0.1 * stress_v
    flux[0], flux[1], flux[2], flux[3], flux[4] = shortwave, heat, salt, u0, v0
    rim[...] = ext

    def block(r, b):
        return ext[r : r + 1, b * width : (b + 1) * width]

    n_flux, s_flux = [[block(r, b) for b in range(SENT)] for r in (0, 2)]
    ne, nw, se, sw = [[block(r, b) for b in (3, 4)] for r in (4, 5, 6, 7)]
    level0_u, level0_v, second = 4 * levels, 5 * levels, 6 * levels
    base = 7 * levels + 8
    corner_n = jnp.where(lane == last, pltpu.roll(ne[0], last, 1), pltpu.roll(nw[0], 1, 1))
    corner_s = jnp.where(lane == last, pltpu.roll(se[0], last, 1), pltpu.roll(sw[0], 1, 1))
    corner_n_v = jnp.where(lane == last, pltpu.roll(ne[1], last, 1), pltpu.roll(nw[1], 1, 1))
    corner_s_v = jnp.where(lane == last, pltpu.roll(se[1], last, 1), pltpu.roll(sw[1], 1, 1))
    far_n = corrected(
        from_n[...],
        [(level0_u, n_flux[3]), (level0_v, n_flux[4]), (second, block(1, 4)), (base + 2 * levels, corner_n), (base + 3 * levels, corner_n_v)],
    )
    far_s = corrected(
        from_s[...],
        [(level0_u, s_flux[3]), (level0_v, s_flux[4]), (second, block(3, 4)), (base + 2 * levels, corner_s), (base + 3 * levels, corner_s_v)],
    )
    far_e = corrected(from_e[...], [(level0_u, block(6, 0)), (level0_v, block(7, 0)), (second, block(5, 2))])
    far_w = corrected(from_w[...], [(level0_u, block(6, 1)), (level0_v, block(7, 1)), (second, block(7, 2))])
    turned = stress_u.T
    near_n = corrected(own_n[...], [(level0_v, stress_v[height - 1 : height])])
    near_s = corrected(own_s[...], [(level0_v, stress_v[0:1])])
    near_e = corrected(own_e[...], [(level0_u, turned[last : last + 1])])
    near_w = corrected(own_w[...], [(level0_u, turned[0:1])])
    in_n[...], in_s[...], in_e[...], in_w[...] = near_n, near_s, near_e, near_w
    out_n[...], out_s[...], out_e[...], out_w[...] = far_n, far_s, far_e, far_w

    e_turned, w_turned = far_e.T, far_w.T
    east = lambda index: column(e_turned, index, last)
    west = lambda index: column(w_turned, index, 0)
    passable = wet_products(
        wet, far_n[7 * levels : 7 * levels + 1], far_s[7 * levels : 7 * levels + 1], east(7 * levels), west(7 * levels)
    )
    lines = strips(0, levels, (near_n, near_s, near_e, near_w), (far_n, far_s, far_e, far_w), rim_flux(ext, width))
    profile = level_profile(levels, width)
    mix = KV * wet
    warm = 0.3 * wet * shortwave

    def weights(l, u, v):
        v_n, v_s = [x[5 * levels + l : 5 * levels + l + 1] for x in (far_n, far_s)]
        return coefficients(u, v, east(4 * levels + l), west(4 * levels + l), v_n, v_s, passable)

    def horizontal(c, q, halo):
        e, w, n, s = shifts(q, *halo)
        return c[0] * q + c[1] * e + c[2] * w + c[3] * n + c[4] * s

    def start(l):
        return far_n[l : l + 1], far_s[l : l + 1], east(l), west(l)

    q0, q1, q2 = tracers[0, 0], tracers[0, 1], tracers[0, 2]
    c0 = weights(0, u0, v0)
    c1 = weights(1, currents[0, 1], currents[1, 1])
    t0 = horizontal(c0, q0, start(0)) + mix * (q1 - q0) + warm * profile[0:1] + wet * heat
    t1 = horizontal(c1, q1, start(1)) + mix * ((q2 - q1) - (q1 - q0)) + warm * profile[1:2]
    sides = jnp.concatenate([lines[2][0:8], lines[3][0:8], jnp.zeros((width - 16, width), F32)], axis=0).T
    halo = lines[0][0:1], lines[1][0:1], column(sides, 0, last), column(sides, 8, 0)
    t0 = horizontal(c0, t0, halo) + mix * (t1 - t0) + warm * profile[0:1] + wet * heat
    sst = t0.astype(BF16)
    picked = dot(hot.T.astype(BF16), sst, NN).reshape(devices, chunk, width)
    back[...] = picked[:, :cap].astype(BF16)


def rim_flux(ext, width):
    def block(r, b):
        return ext[r : r + 1, b * width : (b + 1) * width]

    return (
        (block(0, 0), block(0, 1), block(0, 2)),
        (block(2, 0), block(2, 1), block(2, 2)),
        (block(4, 0), block(5, 0), block(4, 2)),
        (block(4, 1), block(5, 1), block(6, 2)),
    )


def stencil_kernel(
    tracers, currents, land, flux, rim, in_n, in_s, in_e, in_w, out_n, out_s, out_e, out_w,
    out, held, weights, line_n, line_s, depth, forced, passing,
):
    levels = tracers.shape[1]
    height, width = land.shape
    last = width - 1
    wet = land[...].astype(F32)
    far_n, far_s, far_e, far_w = out_n[...], out_s[...], out_e[...], out_w[...]
    e_turned, w_turned = far_e.T, far_w.T
    at = 7 * levels
    for i, x in enumerate(
        wet_products(wet, far_n[at : at + 1], far_s[at : at + 1], column(e_turned, at, last), column(w_turned, at, 0))
    ):
        passing[i] = x
    forced[0], forced[1], forced[2] = 0.3 * wet * flux[0], wet * flux[1], wet * flux[2]
    depth[...] = level_profile(levels, width)
    columns = []
    for tracer in range(2):
        lines = strips(
            tracer, levels, (in_n[...], in_s[...], in_e[...], in_w[...]), (far_n, far_s, far_e, far_w), rim_flux(rim[...], width)
        )
        line_n[tracer * levels : (tracer + 1) * levels] = lines[0]
        line_s[tracer * levels : (tracer + 1) * levels] = lines[1]
        columns.append(lines[2:])
    blank = jnp.zeros((width - 2 * levels, width), F32)
    e_later, w_later = [jnp.concatenate([columns[0][i], columns[1][i], blank], axis=0).T for i in range(2)]

    def update(c, q, halo, under, over, forcing):
        e, w, n, s = shifts(q, *halo)
        mixed = KV * land[...].astype(F32) * ((under - q) - (q - over))
        return c[0] * q + c[1] * e + c[2] * w + c[3] * n + c[4] * s + mixed + forcing

    def forcing(tracer, l):
        top = jnp.where(l == 0, 1.0, 0.0)
        if tracer == 0:
            return forced[0] * depth[pl.ds(l, 1), :] + top * forced[1]
        return top * forced[2]

    def first_step(l, _):
        surface = l == 0
        u = jnp.where(surface, flux[3], currents[0, l])
        v = jnp.where(surface, flux[4], currents[1, l])
        row = 5 * levels + l
        c = coefficients(
            u, v, column(e_turned, 4 * levels + l, last), column(w_turned, 4 * levels + l, 0),
            out_n[pl.ds(row, 1), :], out_s[pl.ds(row, 1), :], [passing[i] for i in range(4)],
        )
        for i, x in enumerate(c):
            weights[i, l] = x
        for tracer in range(2):
            row = tracer * levels + l
            halo = out_n[pl.ds(row, 1), :], out_s[pl.ds(row, 1), :], column(e_turned, row, last), column(w_turned, row, 0)
            under, over = tracers[tracer, jnp.minimum(l + 1, levels - 1)], tracers[tracer, jnp.maximum(l - 1, 0)]
            held[tracer, l] = update(c, tracers[tracer, l], halo, under, over, forcing(tracer, l))
        return 0

    lax.fori_loop(0, levels, first_step, 0)

    def second_step(l, _):
        c = [weights[i, l] for i in range(5)]
        for tracer in range(2):
            row = tracer * levels + l
            halo = line_n[pl.ds(row, 1), :], line_s[pl.ds(row, 1), :], column(e_later, row, last), column(w_later, row, 0)
            under, over = held[tracer, jnp.minimum(l + 1, levels - 1)], held[tracer, jnp.maximum(l - 1, 0)]
            out[tracer, l] = update(c, held[tracer, l], halo, under, over, forcing(tracer, l))
        return 0

    lax.fori_loop(0, levels, second_step, 0)


def backward_kernel(batch, slots, src, back, w, out, wide, picked, terms):
    step = pl.program_id(0)
    total, width = terms.shape
    blocks = out.shape[0]

    @pl.when(step == 0)
    def _():
        wide[...] = back[...].astype(F32).reshape(wide.shape)

        def pick(i, _):
            for j in range(8):
                picked[pl.ds(i * 8 + j, 1), :] = wide[pl.ds(slots[i * 8 + j], 1), :]
            return 0

        lax.fori_loop(0, total // 8, pick, 0, unroll=2)

    row = iota((16, width), 0)
    for g in range(batch // 16):
        at = pl.multiple_of(step * batch + g * 16, 16)
        rows = picked[pl.ds(at, 16), :]
        left = [jnp.where((row == r) | (row == 8 + r), rows, 0.0).astype(BF16) for r in range(8)]
        block = w[g * 16 : (g + 1) * 16].reshape(2, 8 * width, width)
        both = dot(jnp.concatenate(left, axis=1), jnp.concatenate([block[0], block[1]], axis=1), NN)
        terms[pl.ds(at, 8), :] = both[:8, :width]
        terms[pl.ds(at + 8, 8), :] = both[8:, width:]

    @pl.when(step == pl.num_programs(0) - 1)
    def _():
        hot = (iota((blocks, total), 0) == src[...]).astype(F32).astype(BF16)
        value = terms[...]
        high = value.astype(BF16)
        low = (value - high.astype(F32)).astype(BF16)
        both = dot(hot, jnp.concatenate([high, low], axis=1), NN)
        out[...] = both[:, :width] + both[:, width:]


def backward(back, w, src, slots, blocks, batch=64):
    total, width, _ = w.shape
    devices, cap, _ = back.shape
    return pl.pallas_call(
        functools.partial(backward_kernel, batch),
        grid_spec=pltpu.PrefetchScalarGridSpec(
            num_scalar_prefetch=1,
            grid=(total // batch,),
            in_specs=[
                pl.BlockSpec((1, total), lambda i, *_: (0, 0)),
                pl.BlockSpec(back.shape, lambda i, *_: (0, 0, 0)),
                pl.BlockSpec((batch, width, width), lambda i, *_: (i, 0, 0)),
            ],
            out_specs=pl.BlockSpec((blocks, width), lambda i, *_: (0, 0)),
            scratch_shapes=[
                pltpu.VMEM((devices * cap, width), F32),
                pltpu.VMEM((total, width), F32),
                pltpu.VMEM((total, width), F32),
            ],
        ),
        out_shape=jax.ShapeDtypeStruct((blocks, width), F32),
        compiler_params=kernel_params(24),
        cost_estimate=pl.CostEstimate(flops=2 * total * 8 * width * width, bytes_accessed=total * width * width * 2, transcendentals=0),
        name="backward_remap",
    )(slots, src.reshape(1, total), back, w)


def kernel(body, outs, name, mebibytes, bytes_accessed, scratch=()):
    return pl.pallas_call(
        body,
        out_shape=[jax.ShapeDtypeStruct(shape, dtype) for shape, dtype in outs],
        scratch_shapes=list(scratch),
        compiler_params=kernel_params(mebibytes),
        cost_estimate=pl.CostEstimate(flops=bytes_accessed, bytes_accessed=bytes_accessed, transcendentals=0),
        name=name,
    )


def neighbours(axis):
    count = lax.axis_size(axis)
    forward_pairs = [(i, i + 1) for i in range(count - 1)]
    return forward_pairs, [(b, a) for a, b in forward_pairs]


def on_device(atm_flux, remap_weights, remap_src, remap_dst, remap_owner, tracers, currents, land_sea):
    devices = lax.axis_size(EVERY)
    gy = lax.axis_size("gy")
    total, width, _ = remap_weights.shape
    _, levels, height, _ = tracers.shape
    cap = up(2 * total // devices, 8)

    send, slots = forward(atm_flux, remap_weights, remap_src, remap_owner[:, 0], remap_dst, devices, cap, gy)
    got = lax.all_to_all(send, EVERY, split_axis=0, concat_axis=0, tiled=True)

    side = (width, width)
    end = (7 * levels + 80, width)
    own_w, own_e = kernel(columns_kernel, [(side, F32)] * 2, "edge_columns", 16, 1 << 22)(tracers, currents, land_sea)
    to_north, to_south = neighbours(NORTH)
    to_east, to_west = neighbours("gy")
    from_e = lax.ppermute(own_w, "gy", to_west)
    from_w = lax.ppermute(own_e, "gy", to_east)
    own_s, own_n = kernel(rows_kernel, [(end, F32)] * 2, "edge_rows", 16, 1 << 20)(
        tracers.reshape(-1, width), currents.reshape(-1, width), land_sea, from_w, from_e
    )
    from_n = lax.ppermute(own_s, NORTH, to_south)
    from_s = lax.ppermute(own_n, NORTH, to_north)

    back, flux, rim, *edges = kernel(
        functools.partial(surface_kernel, cap, levels),
        [((devices, cap, width), BF16), ((5, height, width), F32), ((8, SENT * width), F32)] + ([(end, F32)] * 2 + [(side, F32)] * 2) * 2,
        "surface",
        32,
        1 << 22,
    )(got, tracers[0:1, 0:3], currents[:, 0:2], land_sea, own_n, own_s, own_e, own_w, from_n, from_s, from_e, from_w)
    returned = lax.all_to_all(back, EVERY, split_axis=0, concat_axis=0, tiled=True)

    plane = (height, width)
    (tracers_out,) = kernel(
        stencil_kernel,
        [(tracers.shape, F32)],
        "substeps",
        32,
        1 << 24,
        [
            pltpu.VMEM(tracers.shape, F32),
            pltpu.VMEM((5, levels) + plane, F32),
            pltpu.VMEM((2 * levels, width), F32),
            pltpu.VMEM((2 * levels, width), F32),
            pltpu.VMEM((levels, width), F32),
            pltpu.VMEM((3,) + plane, F32),
            pltpu.VMEM((4,) + plane, F32),
        ],
    )(tracers, currents, land_sea, flux, rim, *edges)
    return tracers_out, backward(returned, remap_weights, remap_src, slots, atm_flux.shape[0])


def solution(mesh):
    return jax.shard_map(
        on_device,
        mesh=mesh,
        in_specs=(
            P(EVERY, None, None),
            P(EVERY, None, None),
            P(EVERY),
            P(EVERY),
            P(EVERY, None),
            P(None, None, NORTH, "gy"),
            P(None, None, NORTH, "gy"),
            P(NORTH, "gy"),
        ),
        out_specs=(P(None, None, NORTH, "gy"), P(EVERY, None)),
        check_vma=False,
    )
```

```python
import functools

import jax
import jax.numpy as jnp
from jax import lax
from jax.experimental import pallas as pl
from jax.experimental.pallas import tpu as pltpu
from jax.sharding import PartitionSpec as P

F32 = jnp.float32
BF16 = jnp.bfloat16
NT = (((1,), (1,)), ((), ()))
NN = (((1,), (0,)), ((), ()))
TN = (((0,), (0,)), ((), ()))
EVERY = ("sec", "gx", "gy")
NORTH = ("sec", "gx")
SENT = 5
KH = 0.1
KV = 0.1


def dot(left, right, dims):
    return lax.dot_general(left, right, dims, preferred_element_type=F32)


def iota(shape, dim):
    return lax.broadcasted_iota(jnp.int32, shape, dim)


def up(number, step):
    return -(-number // step) * step


def kernel_params(mebibytes):
    return pltpu.CompilerParams(vmem_limit_bytes=mebibytes << 20)


VMEM = pl.BlockSpec(memory_space=pltpu.VMEM)
SMEM = pl.BlockSpec(memory_space=pltpu.SMEM)
ANY = pl.BlockSpec(memory_space=pl.ANY)


def forward_kernel(parts, cap, grid, src, own, dst, flux, w, *refs):
    sends, (slots, held, mixed, acc, rows, xs, counts, sems) = refs[:-8], refs[-8:]
    n_sec, n_gx, n_gy = grid
    devices, chunk, wide = xs.shape
    total, width, _ = held.shape
    batch = total // parts
    fields = flux.shape[1]
    first = chunk - 8
    last = width - 1

    def copy(c):
        return pltpu.make_async_copy(w.at[pl.ds(c * batch, batch)], held.at[pl.ds(c * batch, batch)], sems.at[c])

    for c in range(parts):
        copy(c).start()

    def clear(o, _):
        counts[o] = 0
        return 0

    lax.fori_loop(0, devices, clear, 0)
    rows[...] = jnp.full_like(rows, 255.0)
    acc[...] = jnp.zeros_like(acc)
    xs[...] = jnp.zeros_like(xs)
    full = flux[...].astype(F32)
    one = [full[:, f : f + 1] for f in range(fields)]
    heat = 0.2 * (one[1] + one[2] + one[3]) - 0.15 * one[5]
    salt = 0.2 * one[4] - 0.1 * one[5]
    heat_high = heat.astype(BF16).astype(F32)
    salt_high = salt.astype(BF16).astype(F32)
    mixed[...] = jnp.concatenate(
        [one[0], heat_high, salt_high, one[6], one[7], heat - heat_high, salt - salt_high, jnp.zeros_like(heat)], axis=1
    ).astype(BF16)

    def place(k, _):
        owner = own[k]
        at = counts[owner]
        counts[owner] = at + 1
        slot = owner * cap + jnp.minimum(at, cap - 1)
        slots[k] = slot
        rows[pl.ds(slot, 1), :] = jnp.full((1, width), dst[k].astype(F32), F32)
        return 0

    lax.fori_loop(0, total, place, 0, unroll=8)
    low_rows = iota((fields, width), 0)
    low_rows = (low_rows == 1) | (low_rows == 2)

    def work(c, _):
        copy(c).wait()
        for b in range(0, batch, 2):
            k = c * batch + b
            left = jnp.concatenate([mixed[src[k]], mixed[src[k + 1]]], axis=0)
            both = dot(left, held[pl.ds(k, 2)].reshape(2 * width, width), NT)
            for z, part in enumerate((both[:fields, :width], both[fields:, width:])):
                part = part + jnp.where(low_rows, pltpu.roll(part, fields - 4, 0), 0.0)
                acc[pl.ds(pl.multiple_of(slots[k + z] * fields, fields), fields), :] = part
        return 0

    lax.fori_loop(0, parts, work, 0)

    lane = iota((cap, width), 1).astype(F32)
    sub = iota((cap, width), 0).astype(F32)
    row = iota((24, wide), 0)
    picks = {
        4: (0, 0), 5: (1, 0), 6: (3, 0), 7: (4, 0), 12: (0, last), 13: (1, last), 14: (3, last), 15: (4, last),
        20: (2, 0), 21: (3, 1), 22: (2, last), 23: (3, last - 1),
    }
    pick = jnp.full((24, wide), -1, jnp.int32)
    for at, (field, column) in picks.items():
        pick = jnp.where(row == at, field * width + column, pick)
    select = (iota((24, wide), 1) == pick).astype(F32).astype(BF16)
    row = iota((8, cap), 0)
    wanted = jnp.zeros((8, cap), F32)
    for at, x in enumerate((0, 1, last, last - 1, 0, 0, last, last)):
        wanted = jnp.where(row == at, float(x), wanted)
    group = 8
    plane = lax.axis_index("sec") * n_gy + lax.axis_index("gy")
    line = lax.axis_index("gx")

    def owners(g, _):
        ds = [g * group + j for j in range(group)]
        five = []
        for d in ds:
            x = [acc[pl.ds(d * cap * fields + f, cap, stride=fields), :] for f in range(SENT)]
            x = jnp.concatenate(x, axis=1)
            xs[d, 0:cap, :] = x
            five.append(x.astype(BF16))
        where = [rows[pl.ds(pl.multiple_of(d * cap, 8), cap), :] for d in ds]
        hot = [(lane == r).astype(F32).astype(BF16) for r in where]
        flat = [jnp.sum(jnp.where(lane == sub, r, 0.0), axis=0, keepdims=True) for r in where]
        flat = [jnp.where(lane[:1] < cap, f, 255.0) for f in flat]
        edge = [dot(select, x, NT).astype(BF16) for x in five]
        sides = [dot(e, h, NN) for e, h in zip(edge, hot)]
        ends = [dot((f[:, :cap] == wanted).astype(F32).astype(BF16), x, NN) for f, x in zip(flat, five)]
        for d, f, side, end in zip(ds, flat, sides, ends):
            here = lax.div(d, n_gx) ^ plane
            here = (lax.div(here, n_gy) * n_gx + (lax.rem(d, n_gx) ^ line)) * n_gy + lax.rem(here, n_gy)

            def at(offset):
                there = lax.rem(here + offset + 2 * devices, devices)
                x = lax.div(there, n_gy)
                there = lax.div(x, n_gx) * n_gy + lax.rem(there, n_gy)
                return (there ^ plane) * n_gx + (lax.rem(x, n_gx) ^ line)

            south_of, north_of, west_of, east_of = at(-n_gy), at(n_gy), at(-1), at(1)

            xs[south_of, first : first + 1, :] = end[0:1]
            xs[south_of, first + 1 : first + 2, 4 * width :] = end[1:2, 4 * width :]
            xs[north_of, first + 2 : first + 3, :] = end[2:3]
            xs[north_of, first + 3 : first + 4, 4 * width :] = end[3:4, 4 * width :]
            xs[at(-n_gy - 1), first + 4 : first + 5, 3 * width :] = end[4:5, 3 * width :]
            xs[at(-n_gy + 1), first + 5 : first + 6, 3 * width :] = end[5:6, 3 * width :]
            xs[at(n_gy - 1), first + 6 : first + 7, 3 * width :] = end[6:7, 3 * width :]
            xs[at(n_gy + 1), first + 7 : first + 8, 3 * width :] = end[7:8, 3 * width :]
            xs[west_of, first + 4 : first + 8, 0:width] = side[4:8]
            xs[east_of, first + 4 : first + 8, width : 2 * width] = side[12:16]
            xs[west_of, first + 4 : first + 6, 2 * width : 3 * width] = side[20:22]
            xs[east_of, first + 6 : first + 8, 2 * width : 3 * width] = side[22:24]
            xs[d, first + 1 : first + 2, 0:width] = f
        return 0

    lax.fori_loop(0, devices // group, owners, 0)

    for m, send in enumerate(sends):
        send[...] = xs[m * n_gx : (m + 1) * n_gx].astype(BF16)


def forward(flux, w, src, own, dst, grid, cap, parts=20):
    n_sec, n_gx, n_gy = grid
    devices = n_sec * n_gx * n_gy
    total, width, _ = w.shape
    chunk = up(cap + 8, 16)
    fields = flux.shape[1]
    wide = SENT * width
    return pl.pallas_call(
        functools.partial(forward_kernel, parts, cap, grid),
        in_specs=[SMEM, SMEM, SMEM, VMEM, ANY],
        out_specs=[VMEM] * (n_sec * n_gy) + [SMEM],
        scratch_shapes=[
            pltpu.VMEM(w.shape, BF16),
            pltpu.VMEM(flux.shape, BF16),
            pltpu.VMEM((devices * cap * fields, width), F32),
            pltpu.VMEM((devices * cap, width), F32),
            pltpu.VMEM((devices, chunk, wide), F32),
            pltpu.SMEM((devices,), jnp.int32),
            pltpu.SemaphoreType.DMA((parts,)),
        ],
        out_shape=[jax.ShapeDtypeStruct((n_gx, chunk, wide), BF16)] * (n_sec * n_gy) + [jax.ShapeDtypeStruct((total,), jnp.int32)],
        compiler_params=kernel_params(58),
        cost_estimate=pl.CostEstimate(flops=2 * total * 8 * width * width, bytes_accessed=total * width * width * 2, transcendentals=0),
        name="forward_remap",
    )(src, own, dst, flux, w)


def merge_kernel(n_sources, *refs):
    sources, lines_out, outs = refs[:n_sources], refs[n_sources], refs[n_sources + 1 :]
    n_gx, chunk, wide = sources[0].shape
    height = outs[0].shape[0] - 8
    first = chunk - 8
    count = len(sources) * chunk
    for z in range(n_gx):
        ext = None
        where = []
        for source in sources:
            piece = source[z, first:chunk, :].astype(F32)
            where.append(piece[1:2, :chunk])
            ext = piece if ext is None else ext + piece
        where = jnp.concatenate(where, axis=1)
        lines_out[z] = where
        hot = (iota((height, count), 0).astype(F32) == where).astype(F32).astype(BF16)
        sums = dot(hot, jnp.concatenate([source[z] for source in sources], axis=0), NN)
        outs[z][...] = jnp.concatenate([sums, ext], axis=0).astype(outs[z].dtype)


def spread_kernel(cap, *refs):
    n_gx, _, count = refs[0].shape
    lines, tiles, backs = refs[0], refs[1 : 1 + n_gx], refs[1 + n_gx :]
    chunk = count // len(backs)
    height, width = tiles[0].shape
    for z in range(n_gx):
        hot = (iota((height, count), 0).astype(F32) == lines[z]).astype(F32)
        picked = dot(hot.T.astype(BF16), tiles[z][...], NN).reshape(len(backs), chunk, width)
        for m, back in enumerate(backs):
            back[z] = picked[m, :cap].astype(BF16)


def columns_kernel(tracers, currents, land, west, east):
    levels = tracers.shape[1]
    width = tracers.shape[3]
    last = width - 1
    lane = iota((width, width), 1)

    def put(held, plane, row, column):
        return jnp.where(lane == row, pltpu.roll(plane, lax.rem(row - column + width, width), 1), held)

    def level(l, held):
        w, e = held
        for t in range(2):
            q = tracers[t, l]
            w = put(put(w, q, t * levels + l, 0), q, (2 + t) * levels + l, 1)
            e = put(put(e, q, t * levels + l, last), q, (2 + t) * levels + l, last - 1)
        u = currents[0, l]
        w = put(put(w, u, 4 * levels + l, 0), u, 6 * levels + l, 1)
        e = put(put(e, u, 4 * levels + l, last), u, 6 * levels + l, last - 1)
        v = currents[1, l]
        return put(w, v, 5 * levels + l, 0), put(e, v, 5 * levels + l, last)

    zero = jnp.zeros((width, width), F32)
    w, e = lax.fori_loop(0, levels, level, (zero, zero))
    wet = land[...].astype(F32)
    w = put(put(w, wet, 7 * levels, 0), wet, 7 * levels + 1, 1)
    e = put(put(e, wet, 7 * levels, last), wet, 7 * levels + 1, last - 1)
    west[...] = w.T
    east[...] = e.T


def rows_kernel(tracers, currents, land, from_west, from_east, south, north):
    levels = tracers.shape[0] // 2 // land.shape[0]
    height, width = land.shape
    lane = iota((1, width), 1)
    for out, edge, second in ((south, 0, 1), (north, height - 1, height - 2)):
        out[0 : 2 * levels] = tracers[pl.ds(edge, 2 * levels, stride=height), :]
        out[2 * levels : 4 * levels] = tracers[pl.ds(second, 2 * levels, stride=height), :]
        out[4 * levels : 6 * levels] = currents[pl.ds(edge, 2 * levels, stride=height), :]
        out[6 * levels : 7 * levels] = currents[pl.ds(levels * height + second, levels, stride=height), :]
        wet = [land[x : x + 1, :].astype(F32) for x in (edge, second)]
        out[7 * levels : 7 * levels + 8] = jnp.concatenate(wet + [jnp.zeros((6, width), F32)], axis=0)
    base = 7 * levels + 8
    for start, stop, at in ((0, 2 * levels, 0), (4 * levels, 6 * levels, 2 * levels), (7 * levels, 7 * levels + 8, 4 * levels)):
        w, e = from_west[start:stop], from_east[start:stop]
        there = slice(base + at, base + at + stop - start)
        south[there] = jnp.where(lane == 0, w, pltpu.roll(e, width - 1, 1))
        north[there] = jnp.where(lane == width - 1, e, pltpu.roll(w, 1, 1))


def plus_side(q, other, speed, speed_other, passable):
    return KH * passable * (other - q) - 0.25 * (speed + speed_other) * passable * (q + other)


def minus_side(q, other, speed, speed_other, passable):
    return KH * passable * (other - q) + 0.25 * (speed_other + speed) * passable * (other + q)


def level_profile(levels, width):
    depth = iota((levels, width), 0).astype(F32)
    return jnp.exp(-depth / 4.0) * (1.0 - jnp.exp(jnp.full((levels, width), -0.25, F32)))


def strip_step(q, q_plus, q_minus, across, across_plus, across_minus, along, corner_q, corner_along, wet, wet_plus, wet_minus, corner_wet, forcing):
    levels, width = q.shape
    lane = iota((1, width), 1)
    row = iota((levels, 1), 0)

    def ahead(x, corner):
        return jnp.where(lane == width - 1, corner, pltpu.roll(x, width - 1, 1))

    def behind(x, corner):
        return jnp.where(lane == 0, corner, pltpu.roll(x, 1, 1))

    total = plus_side(q, q_plus, across, across_plus, wet * wet_plus)
    total += minus_side(q, q_minus, across, across_minus, wet * wet_minus)
    total += plus_side(q, ahead(q, corner_q), along, ahead(along, corner_along), wet * ahead(wet, corner_wet))
    total += minus_side(q, behind(q, corner_q), along, behind(along, corner_along), wet * behind(wet, corner_wet))
    below = jnp.where(row < levels - 1, pltpu.roll(q, levels - 1, 0) - q, 0.0)
    above = jnp.where(row > 0, q - pltpu.roll(q, 1, 0), 0.0)
    return q + total + wet * (KV * (below - above) + forcing)


def strips(tracer, levels, inner, outer, flux):
    width = outer[0].shape[1]
    lane = iota((1, width), 1)
    base = 7 * levels + 8
    north, south, east, west = outer

    def part(x, at, count=levels):
        return x[at : at + count]

    def corners(at, count):
        n, s = part(north, base + at, count), part(south, base + at, count)
        e = jnp.where(lane == width - 1, n, pltpu.roll(s, 1, 1))
        w = jnp.where(lane == width - 1, pltpu.roll(n, width - 1, 1), s)
        return n, s, e, w

    corner_q = corners(tracer * levels, levels)
    corner_u = corners(2 * levels, levels)
    corner_v = corners(3 * levels, levels)
    corner_wet = corners(4 * levels, 1)
    top = (iota((levels, 1), 0) == 0).astype(F32)
    profile = level_profile(levels, width)
    results = []
    for side in range(4):
        near, far = inner[side], outer[side]
        beside, out = part(near, tracer * levels), part(far, (2 + tracer) * levels)
        mid = part(far, tracer * levels)
        speed = 5 if side < 2 else 4
        along = part(far, (9 - speed) * levels)
        corner_along = (corner_u if side < 2 else corner_v)[side]
        across, across_in, across_out = part(far, speed * levels), part(near, speed * levels), part(far, 6 * levels)
        wet, wet_in, wet_out = part(far, 7 * levels, 1), part(near, 7 * levels, 1), part(far, 7 * levels + 1, 1)
        shortwave, heat, salt = flux[side]
        forcing = 0.3 * profile * shortwave + top * heat if tracer == 0 else top * salt
        if side % 2 == 0:
            pairs = (out, beside, across, across_out, across_in)
            wets = (wet, wet_out, wet_in)
        else:
            pairs = (beside, out, across, across_in, across_out)
            wets = (wet, wet_in, wet_out)
        results.append(strip_step(mid, *pairs, along, corner_q[side], corner_along, *wets, corner_wet[side], forcing))
    return results


def shifts(plane, north, south, east, west):
    height, width = plane.shape
    lane, row = iota(plane.shape, 1), iota(plane.shape, 0)
    return (
        jnp.where(lane == width - 1, east, pltpu.roll(plane, width - 1, 1)),
        jnp.where(lane == 0, west, pltpu.roll(plane, 1, 1)),
        jnp.where(row == height - 1, north, pltpu.roll(plane, height - 1, 0)),
        jnp.where(row == 0, south, pltpu.roll(plane, 1, 0)),
    )


def wet_products(wet, north, south, east, west):
    return [wet * other for other in shifts(wet, north, south, east, west)]


def coefficients(u, v, u_east, u_west, v_north, v_south, passable):
    east, west, north, south = passable
    height, width = u.shape
    lane, row = iota(u.shape, 1), iota(u.shape, 0)
    e = jnp.where(lane == width - 1, u_east, pltpu.roll(u, width - 1, 1))
    w = jnp.where(lane == 0, u_west, pltpu.roll(u, 1, 1))
    n = jnp.where(row == height - 1, v_north, pltpu.roll(v, height - 1, 0))
    s = jnp.where(row == 0, v_south, pltpu.roll(v, 1, 0))
    flow_e, flow_w = 0.25 * (u + e) * east, 0.25 * (w + u) * west
    flow_n, flow_s = 0.25 * (v + n) * north, 0.25 * (s + v) * south
    own = 1.0 + (flow_w - flow_e) + (flow_s - flow_n) - KH * (east + west + north + south)
    return own, KH * east - flow_e, KH * west + flow_w, KH * north - flow_n, KH * south + flow_s


def column(turned, index, lane):
    return pltpu.roll(turned, lax.rem(lane - index + 2 * turned.shape[1], turned.shape[1]), 1)


def corrected(edge, x_rows):
    row = iota((edge.shape[0], 1), 0)
    for at, x in x_rows:
        edge = edge + jnp.where(row == at, 0.1 * x, 0.0)
    return edge


def surface_kernel(n_gx, levels, *refs):
    parts, refs = refs[:n_gx], refs[n_gx:]
    tracers, currents, land, own_n, own_s, own_e, own_w, from_n, from_s, from_e, from_w, *refs = refs
    surface, flux, rim, in_n, in_s, in_e, in_w, out_n, out_s, out_e, out_w = refs
    height, width = land.shape
    last = width - 1
    lane = iota((1, width), 1)
    sums = parts[0][...]
    for part in parts[1:]:
        sums = sums + part[...].astype(F32)
    sums, ext = sums[:height], sums[height:]
    shortwave, heat, salt, stress_u, stress_v = [sums[:, f * width : (f + 1) * width] for f in range(SENT)]
    wet = land[...].astype(F32)
    u0 = currents[0, 0] + 0.1 * stress_u
    v0 = currents[1, 0] + 0.1 * stress_v
    flux[0], flux[1], flux[2], flux[3], flux[4] = shortwave, heat, salt, u0, v0
    rim[...] = ext

    def block(r, b):
        return ext[r : r + 1, b * width : (b + 1) * width]

    n_flux, s_flux = [[block(r, b) for b in range(SENT)] for r in (0, 2)]
    ne, nw, se, sw = [[block(r, b) for b in (3, 4)] for r in (4, 5, 6, 7)]
    level0_u, level0_v, second = 4 * levels, 5 * levels, 6 * levels
    base = 7 * levels + 8
    corner_n = jnp.where(lane == last, pltpu.roll(ne[0], last, 1), pltpu.roll(nw[0], 1, 1))
    corner_s = jnp.where(lane == last, pltpu.roll(se[0], last, 1), pltpu.roll(sw[0], 1, 1))
    corner_n_v = jnp.where(lane == last, pltpu.roll(ne[1], last, 1), pltpu.roll(nw[1], 1, 1))
    corner_s_v = jnp.where(lane == last, pltpu.roll(se[1], last, 1), pltpu.roll(sw[1], 1, 1))
    far_n = corrected(
        from_n[...],
        [(level0_u, n_flux[3]), (level0_v, n_flux[4]), (second, block(1, 4)), (base + 2 * levels, corner_n), (base + 3 * levels, corner_n_v)],
    )
    far_s = corrected(
        from_s[...],
        [(level0_u, s_flux[3]), (level0_v, s_flux[4]), (second, block(3, 4)), (base + 2 * levels, corner_s), (base + 3 * levels, corner_s_v)],
    )
    far_e = corrected(from_e[...], [(level0_u, block(6, 0)), (level0_v, block(7, 0)), (second, block(5, 2))])
    far_w = corrected(from_w[...], [(level0_u, block(6, 1)), (level0_v, block(7, 1)), (second, block(7, 2))])
    turned = stress_u.T
    near_n = corrected(own_n[...], [(level0_v, stress_v[height - 1 : height])])
    near_s = corrected(own_s[...], [(level0_v, stress_v[0:1])])
    near_e = corrected(own_e[...], [(level0_u, turned[last : last + 1])])
    near_w = corrected(own_w[...], [(level0_u, turned[0:1])])
    in_n[...], in_s[...], in_e[...], in_w[...] = near_n, near_s, near_e, near_w
    out_n[...], out_s[...], out_e[...], out_w[...] = far_n, far_s, far_e, far_w

    e_turned, w_turned = far_e.T, far_w.T
    east = lambda index: column(e_turned, index, last)
    west = lambda index: column(w_turned, index, 0)
    passable = wet_products(
        wet, far_n[7 * levels : 7 * levels + 1], far_s[7 * levels : 7 * levels + 1], east(7 * levels), west(7 * levels)
    )
    lines = strips(0, levels, (near_n, near_s, near_e, near_w), (far_n, far_s, far_e, far_w), rim_flux(ext, width))
    profile = level_profile(levels, width)
    mix = KV * wet
    warm = 0.3 * wet * shortwave

    def weights(l, u, v):
        v_n, v_s = [x[5 * levels + l : 5 * levels + l + 1] for x in (far_n, far_s)]
        return coefficients(u, v, east(4 * levels + l), west(4 * levels + l), v_n, v_s, passable)

    def horizontal(c, q, halo):
        e, w, n, s = shifts(q, *halo)
        return c[0] * q + c[1] * e + c[2] * w + c[3] * n + c[4] * s

    def start(l):
        return far_n[l : l + 1], far_s[l : l + 1], east(l), west(l)

    q0, q1, q2 = tracers[0, 0], tracers[0, 1], tracers[0, 2]
    c0 = weights(0, u0, v0)
    c1 = weights(1, currents[0, 1], currents[1, 1])
    t0 = horizontal(c0, q0, start(0)) + mix * (q1 - q0) + warm * profile[0:1] + wet * heat
    t1 = horizontal(c1, q1, start(1)) + mix * ((q2 - q1) - (q1 - q0)) + warm * profile[1:2]
    sides = jnp.concatenate([lines[2][0:8], lines[3][0:8], jnp.zeros((width - 16, width), F32)], axis=0).T
    halo = lines[0][0:1], lines[1][0:1], column(sides, 0, last), column(sides, 8, 0)
    t0 = horizontal(c0, t0, halo) + mix * (t1 - t0) + warm * profile[0:1] + wet * heat
    surface[...] = t0.astype(BF16)


def rim_flux(ext, width):
    def block(r, b):
        return ext[r : r + 1, b * width : (b + 1) * width]

    return (
        (block(0, 0), block(0, 1), block(0, 2)),
        (block(2, 0), block(2, 1), block(2, 2)),
        (block(4, 0), block(5, 0), block(4, 2)),
        (block(4, 1), block(5, 1), block(6, 2)),
    )


def stencil_kernel(
    tracers, currents, land, flux, rim, in_n, in_s, in_e, in_w, out_n, out_s, out_e, out_w,
    out, held, weights, line_n, line_s, depth, forced, passing,
):
    levels = tracers.shape[1]
    height, width = land.shape
    last = width - 1
    wet = land[...].astype(F32)
    far_n, far_s, far_e, far_w = out_n[...], out_s[...], out_e[...], out_w[...]
    e_turned, w_turned = far_e.T, far_w.T
    at = 7 * levels
    for i, x in enumerate(
        wet_products(wet, far_n[at : at + 1], far_s[at : at + 1], column(e_turned, at, last), column(w_turned, at, 0))
    ):
        passing[i] = x
    forced[0], forced[1], forced[2] = 0.3 * wet * flux[0], wet * flux[1], wet * flux[2]
    depth[...] = level_profile(levels, width)
    columns = []
    for tracer in range(2):
        lines = strips(
            tracer, levels, (in_n[...], in_s[...], in_e[...], in_w[...]), (far_n, far_s, far_e, far_w), rim_flux(rim[...], width)
        )
        line_n[tracer * levels : (tracer + 1) * levels] = lines[0]
        line_s[tracer * levels : (tracer + 1) * levels] = lines[1]
        columns.append(lines[2:])
    blank = jnp.zeros((width - 2 * levels, width), F32)
    e_later, w_later = [jnp.concatenate([columns[0][i], columns[1][i], blank], axis=0).T for i in range(2)]

    def update(c, q, halo, under, over, forcing):
        e, w, n, s = shifts(q, *halo)
        mixed = KV * land[...].astype(F32) * ((under - q) - (q - over))
        return c[0] * q + c[1] * e + c[2] * w + c[3] * n + c[4] * s + mixed + forcing

    def forcing(tracer, l):
        top = jnp.where(l == 0, 1.0, 0.0)
        if tracer == 0:
            return forced[0] * depth[pl.ds(l, 1), :] + top * forced[1]
        return top * forced[2]

    def first_step(l, _):
        surface = l == 0
        u = jnp.where(surface, flux[3], currents[0, l])
        v = jnp.where(surface, flux[4], currents[1, l])
        row = 5 * levels + l
        c = coefficients(
            u, v, column(e_turned, 4 * levels + l, last), column(w_turned, 4 * levels + l, 0),
            out_n[pl.ds(row, 1), :], out_s[pl.ds(row, 1), :], [passing[i] for i in range(4)],
        )
        for i, x in enumerate(c):
            weights[i, l] = x
        for tracer in range(2):
            row = tracer * levels + l
            halo = out_n[pl.ds(row, 1), :], out_s[pl.ds(row, 1), :], column(e_turned, row, last), column(w_turned, row, 0)
            under, over = tracers[tracer, jnp.minimum(l + 1, levels - 1)], tracers[tracer, jnp.maximum(l - 1, 0)]
            held[tracer, l] = update(c, tracers[tracer, l], halo, under, over, forcing(tracer, l))
        return 0

    lax.fori_loop(0, levels, first_step, 0)

    def second_step(l, _):
        c = [weights[i, l] for i in range(5)]
        for tracer in range(2):
            row = tracer * levels + l
            halo = line_n[pl.ds(row, 1), :], line_s[pl.ds(row, 1), :], column(e_later, row, last), column(w_later, row, 0)
            under, over = held[tracer, jnp.minimum(l + 1, levels - 1)], held[tracer, jnp.maximum(l - 1, 0)]
            out[tracer, l] = update(c, held[tracer, l], halo, under, over, forcing(tracer, l))
        return 0

    lax.fori_loop(0, levels, second_step, 0)


def backward_kernel(batch, n_backs, slots, src, *refs):
    backs, (w, out, wide, picked, terms) = refs[:n_backs], refs[n_backs:]
    step = pl.program_id(0)
    total, width = terms.shape
    blocks = out.shape[0]

    @pl.when(step == 0)
    def _():
        rows = wide.shape[0] // n_backs
        for m, back in enumerate(backs):
            wide[m * rows : (m + 1) * rows] = back[...].astype(F32).reshape(rows, width)

        def pick(i, _):
            for j in range(8):
                picked[pl.ds(i * 8 + j, 1), :] = wide[pl.ds(slots[i * 8 + j], 1), :]
            return 0

        lax.fori_loop(0, total // 8, pick, 0, unroll=2)

    row = iota((16, width), 0)
    for g in range(batch // 16):
        at = pl.multiple_of(step * batch + g * 16, 16)
        rows = picked[pl.ds(at, 16), :]
        left = [jnp.where((row == r) | (row == 8 + r), rows, 0.0).astype(BF16) for r in range(8)]
        block = w[g * 16 : (g + 1) * 16].reshape(2, 8 * width, width)
        both = dot(jnp.concatenate(left, axis=1), jnp.concatenate([block[0], block[1]], axis=1), NN)
        terms[pl.ds(at, 8), :] = both[:8, :width]
        terms[pl.ds(at + 8, 8), :] = both[8:, width:]

    @pl.when(step == pl.num_programs(0) - 1)
    def _():
        hot = (iota((blocks, total), 0) == src[...]).astype(F32).astype(BF16)
        value = terms[...]
        high = value.astype(BF16)
        low = (value - high.astype(F32)).astype(BF16)
        both = dot(hot, jnp.concatenate([high, low], axis=1), NN)
        out[...] = both[:, :width] + both[:, width:]


def backward(backs, w, src, slots, blocks, batch=64):
    total, width, _ = w.shape
    n_gx, cap, _ = backs[0].shape
    return pl.pallas_call(
        functools.partial(backward_kernel, batch, len(backs)),
        grid_spec=pltpu.PrefetchScalarGridSpec(
            num_scalar_prefetch=1,
            grid=(total // batch,),
            in_specs=[
                pl.BlockSpec((1, total), lambda i, *_: (0, 0)),
                *[pl.BlockSpec((n_gx, cap, width), lambda i, *_: (0, 0, 0))] * len(backs),
                pl.BlockSpec((batch, width, width), lambda i, *_: (i, 0, 0)),
            ],
            out_specs=pl.BlockSpec((blocks, width), lambda i, *_: (0, 0)),
            scratch_shapes=[
                pltpu.VMEM((len(backs) * n_gx * cap, width), F32),
                pltpu.VMEM((total, width), F32),
                pltpu.VMEM((total, width), F32),
            ],
        ),
        out_shape=jax.ShapeDtypeStruct((blocks, width), F32),
        compiler_params=kernel_params(24),
        cost_estimate=pl.CostEstimate(flops=2 * total * 8 * width * width, bytes_accessed=total * width * width * 2, transcendentals=0),
        name="backward_remap",
    )(slots, src.reshape(1, total), *backs, w)


def kernel(body, outs, name, mebibytes, bytes_accessed, scratch=()):
    return pl.pallas_call(
        body,
        out_shape=[jax.ShapeDtypeStruct(shape, dtype) for shape, dtype in outs],
        scratch_shapes=list(scratch),
        compiler_params=kernel_params(mebibytes),
        cost_estimate=pl.CostEstimate(flops=bytes_accessed, bytes_accessed=bytes_accessed, transcendentals=0),
        name=name,
    )


def neighbours(axis):
    count = lax.axis_size(axis)
    forward_pairs = [(i, i + 1) for i in range(count - 1)]
    return forward_pairs, [(b, a) for a, b in forward_pairs]


def swapped(array, axes, count, step):
    return lax.ppermute(array, axes, [(i, i ^ step) for i in range(count)])


def on_device(atm_flux, remap_weights, remap_src, remap_dst, remap_owner, tracers, currents, land_sea):
    grid = n_sec, n_gx, n_gy = [lax.axis_size(axis) for axis in EVERY]
    planes = n_sec * n_gy
    total, width, _ = remap_weights.shape
    _, levels, height, _ = tracers.shape
    cap = up(2 * total // (planes * n_gx), 8)
    wide = SENT * width

    plane = lax.axis_index("sec") * n_gy + lax.axis_index("gy")
    owner = remap_owner[:, 0]
    x, y = owner // n_gy, owner % n_gy
    owner = (((x // n_gx) * n_gy + y) ^ plane) * n_gx + ((x % n_gx) ^ lax.axis_index("gx"))
    *sends, slots = forward(atm_flux, remap_weights, remap_src, owner, remap_dst, grid, cap)
    got = [sends[0]] + [swapped(sends[m], ("sec", "gy"), planes, m) for m in range(1, planes)]
    chunk = sends[0].shape[1]
    lines, *merged = kernel(
        functools.partial(merge_kernel, planes),
        [((n_gx, 1, planes * chunk), F32), ((height + 8, wide), F32)] + [((height + 8, wide), BF16)] * (n_gx - 1),
        "merge",
        32,
        1 << 22,
    )(*got)
    parts = [merged[0]] + [swapped(merged[m], "gx", n_gx, m) for m in range(1, n_gx)]

    side = (width, width)
    end = (7 * levels + 80, width)
    own_w, own_e = kernel(columns_kernel, [(side, F32)] * 2, "edge_columns", 16, 1 << 22)(tracers, currents, land_sea)
    to_north, to_south = neighbours(NORTH)
    to_east, to_west = neighbours("gy")
    from_e = lax.ppermute(own_w, "gy", to_west)
    from_w = lax.ppermute(own_e, "gy", to_east)
    own_s, own_n = kernel(rows_kernel, [(end, F32)] * 2, "edge_rows", 16, 1 << 20)(
        tracers.reshape(-1, width), currents.reshape(-1, width), land_sea, from_w, from_e
    )
    from_n = lax.ppermute(own_s, NORTH, to_south)
    from_s = lax.ppermute(own_n, NORTH, to_north)

    surface, flux, rim, *edges = kernel(
        functools.partial(surface_kernel, n_gx, levels),
        [((height, width), BF16), ((5, height, width), F32), ((8, wide), F32)] + ([(end, F32)] * 2 + [(side, F32)] * 2) * 2,
        "surface",
        32,
        1 << 22,
    )(*parts, tracers[0:1, 0:3], currents[:, 0:2], land_sea, own_n, own_s, own_e, own_w, from_n, from_s, from_e, from_w)
    tiles = [surface] + [swapped(surface, "gx", n_gx, m) for m in range(1, n_gx)]
    backs = kernel(
        functools.partial(spread_kernel, cap), [((n_gx, cap, width), BF16)] * planes, "spread", 32, 1 << 22
    )(lines, *tiles)
    returned = [backs[0]] + [swapped(backs[m], ("sec", "gy"), planes, m) for m in range(1, planes)]

    plane = (height, width)
    (tracers_out,) = kernel(
        stencil_kernel,
        [(tracers.shape, F32)],
        "substeps",
        32,
        1 << 24,
        [
            pltpu.VMEM(tracers.shape, F32),
            pltpu.VMEM((5, levels) + plane, F32),
            pltpu.VMEM((2 * levels, width), F32),
            pltpu.VMEM((2 * levels, width), F32),
            pltpu.VMEM((levels, width), F32),
            pltpu.VMEM((3,) + plane, F32),
            pltpu.VMEM((4,) + plane, F32),
        ],
    )(tracers, currents, land_sea, flux, rim, *edges)
    return tracers_out, backward(returned, remap_weights, remap_src, slots, atm_flux.shape[0])


def solution(mesh):
    return jax.shard_map(
        on_device,
        mesh=mesh,
        in_specs=(
            P(EVERY, None, None),
            P(EVERY, None, None),
            P(EVERY),
            P(EVERY),
            P(EVERY, None),
            P(None, None, NORTH, "gy"),
            P(None, None, NORTH, "gy"),
            P(NORTH, "gy"),
        ),
        out_specs=(P(None, None, NORTH, "gy"), P(EVERY, None)),
        check_vma=False,
    )
```

```python
import functools

import jax
import jax.numpy as jnp
from jax import lax
from jax.experimental import pallas as pl
from jax.experimental.pallas import tpu as pltpu
from jax.sharding import PartitionSpec as P

F32 = jnp.float32
BF16 = jnp.bfloat16
NT = (((1,), (1,)), ((), ()))
NN = (((1,), (0,)), ((), ()))
TN = (((0,), (0,)), ((), ()))
EVERY = ("sec", "gx", "gy")
NORTH = ("sec", "gx")
SENT = 5
KH = 0.1
KV = 0.1


def dot(left, right, dims):
    return lax.dot_general(left, right, dims, preferred_element_type=F32)


def iota(shape, dim):
    return lax.broadcasted_iota(jnp.int32, shape, dim)


def up(number, step):
    return -(-number // step) * step


def kernel_params(mebibytes):
    return pltpu.CompilerParams(vmem_limit_bytes=mebibytes << 20)


VMEM = pl.BlockSpec(memory_space=pltpu.VMEM)
SMEM = pl.BlockSpec(memory_space=pltpu.SMEM)
ANY = pl.BlockSpec(memory_space=pl.ANY)


def forward_kernel(parts, cap, grid, src, own, dst, flux, w, *refs):
    sends, (slots, held, mixed, acc, rows, xs, counts, renumbered, sems) = refs[:-9], refs[-9:]
    n_sec, n_gx, n_gy = grid
    devices, chunk, wide = xs.shape
    total, width, _ = held.shape
    batch = total // parts
    fields = flux.shape[1]
    first = chunk - 8
    last = width - 1

    def copy(c):
        return pltpu.make_async_copy(w.at[pl.ds(c * batch, batch)], held.at[pl.ds(c * batch, batch)], sems.at[c])

    for c in range(parts):
        copy(c).start()

    plane = lax.axis_index("sec") * n_gy + lax.axis_index("gy")
    line = lax.axis_index("gx")

    def renumber(owner):
        x = lax.div(owner, n_gy)
        there = lax.div(x, n_gx) * n_gy + lax.rem(owner, n_gy)
        return (there ^ plane) * n_gx + (lax.rem(x, n_gx) ^ line)

    def clear(o, _):
        counts[o] = 0
        renumbered[o] = renumber(o)
        return 0

    lax.fori_loop(0, devices, clear, 0)
    rows[...] = jnp.full_like(rows, 255.0)
    acc[...] = jnp.zeros_like(acc)
    xs[...] = jnp.zeros_like(xs)
    full = flux[...].astype(F32)
    one = [full[:, f : f + 1] for f in range(fields)]
    heat = 0.2 * (one[1] + one[2] + one[3]) - 0.15 * one[5]
    salt = 0.2 * one[4] - 0.1 * one[5]
    heat_high = heat.astype(BF16).astype(F32)
    salt_high = salt.astype(BF16).astype(F32)
    mixed[...] = jnp.concatenate(
        [one[0], heat_high, salt_high, one[6], one[7], heat - heat_high, salt - salt_high, jnp.zeros_like(heat)], axis=1
    ).astype(BF16)

    low_rows = iota((fields, width), 0)
    low_rows = (low_rows == 1) | (low_rows == 2)

    def work(c, _):
        copy(c).wait()
        for b in range(0, batch, 2):
            k = c * batch + b
            left = jnp.concatenate([mixed[src[k]], mixed[src[k + 1]]], axis=0)
            both = dot(left, held[pl.ds(k, 2)].reshape(2 * width, width), NT)
            for z, part in enumerate((both[:fields, :width], both[fields:, width:])):
                part = part + jnp.where(low_rows, pltpu.roll(part, fields - 4, 0), 0.0)
                owner = own[k + z]
                at = counts[owner]
                counts[owner] = at + 1
                at = jnp.minimum(at, cap - 1)
                slots[k + z] = owner * cap + at
                slot = renumbered[owner] * cap + at
                acc[pl.ds(pl.multiple_of(slot * fields, fields), fields), :] = part
                rows[pl.ds(slot, 1), :] = jnp.full((1, width), dst[k + z].astype(F32), F32)
        return 0

    lax.fori_loop(0, parts, work, 0)

    lane = iota((cap, width), 1).astype(F32)
    sub = iota((cap, width), 0).astype(F32)
    row = iota((24, wide), 0)
    picks = {
        4: (0, 0), 5: (1, 0), 6: (3, 0), 7: (4, 0), 12: (0, last), 13: (1, last), 14: (3, last), 15: (4, last),
        20: (2, 0), 21: (3, 1), 22: (2, last), 23: (3, last - 1),
    }
    pick = jnp.full((24, wide), -1, jnp.int32)
    for at, (field, column) in picks.items():
        pick = jnp.where(row == at, field * width + column, pick)
    select = (iota((24, wide), 1) == pick).astype(F32).astype(BF16)
    row = iota((8, cap), 0)
    wanted = jnp.zeros((8, cap), F32)
    for at, x in enumerate((0, 1, last, last - 1, 0, 0, last, last)):
        wanted = jnp.where(row == at, float(x), wanted)
    group = 8

    def owners(g, _):
        ds = [g * group + j for j in range(group)]
        five = []
        for d in ds:
            x = [acc[pl.ds(d * cap * fields + f, cap, stride=fields), :] for f in range(SENT)]
            x = jnp.concatenate(x, axis=1)
            xs[d, 0:cap, :] = x
            five.append(x.astype(BF16))
        where = [rows[pl.ds(pl.multiple_of(d * cap, 8), cap), :] for d in ds]
        hot = [(lane == r).astype(F32).astype(BF16) for r in where]
        flat = [jnp.sum(jnp.where(lane == sub, r, 0.0), axis=0, keepdims=True) for r in where]
        flat = [jnp.where(lane[:1] < cap, f, 255.0) for f in flat]
        edge = [dot(select, x, NT).astype(BF16) for x in five]
        sides = [dot(e, h, NN) for e, h in zip(edge, hot)]
        ends = [dot((f[:, :cap] == wanted).astype(F32).astype(BF16), x, NN) for f, x in zip(flat, five)]
        for d, f, side, end in zip(ds, flat, sides, ends):
            here = lax.div(d, n_gx) ^ plane
            here = (lax.div(here, n_gy) * n_gx + (lax.rem(d, n_gx) ^ line)) * n_gy + lax.rem(here, n_gy)

            def at(offset):
                return renumbered[lax.rem(here + offset + 2 * devices, devices)]

            south_of, north_of, west_of, east_of = at(-n_gy), at(n_gy), at(-1), at(1)

            xs[south_of, first : first + 1, :] = end[0:1]
            xs[south_of, first + 1 : first + 2, 4 * width :] = end[1:2, 4 * width :]
            xs[north_of, first + 2 : first + 3, :] = end[2:3]
            xs[north_of, first + 3 : first + 4, 4 * width :] = end[3:4, 4 * width :]
            xs[at(-n_gy - 1), first + 4 : first + 5, 3 * width :] = end[4:5, 3 * width :]
            xs[at(-n_gy + 1), first + 5 : first + 6, 3 * width :] = end[5:6, 3 * width :]
            xs[at(n_gy - 1), first + 6 : first + 7, 3 * width :] = end[6:7, 3 * width :]
            xs[at(n_gy + 1), first + 7 : first + 8, 3 * width :] = end[7:8, 3 * width :]
            xs[west_of, first + 4 : first + 8, 0:width] = side[4:8]
            xs[east_of, first + 4 : first + 8, width : 2 * width] = side[12:16]
            xs[west_of, first + 4 : first + 6, 2 * width : 3 * width] = side[20:22]
            xs[east_of, first + 6 : first + 8, 2 * width : 3 * width] = side[22:24]
            xs[d, first + 1 : first + 2, 0:width] = f
        return 0

    lax.fori_loop(0, devices // group, owners, 0)

    half = n_gx // 2
    planes = n_sec * n_gy
    for m in range(planes):
        sends[m][...] = xs[m * n_gx + half : (m + 1) * n_gx].astype(BF16)
        sends[planes + m][...] = xs[m * n_gx : m * n_gx + half].astype(BF16)


def forward(flux, w, src, own, dst, grid, cap, parts=20):
    n_sec, n_gx, n_gy = grid
    devices = n_sec * n_gx * n_gy
    total, width, _ = w.shape
    chunk = up(cap + 8, 16)
    fields = flux.shape[1]
    wide = SENT * width
    return pl.pallas_call(
        functools.partial(forward_kernel, parts, cap, grid),
        in_specs=[SMEM, SMEM, SMEM, VMEM, ANY],
        out_specs=[VMEM] * (2 * n_sec * n_gy) + [SMEM],
        scratch_shapes=[
            pltpu.VMEM(w.shape, BF16),
            pltpu.VMEM(flux.shape, BF16),
            pltpu.VMEM((devices * cap * fields, width), F32),
            pltpu.VMEM((devices * cap, width), F32),
            pltpu.VMEM((devices, chunk, wide), F32),
            pltpu.SMEM((devices,), jnp.int32),
            pltpu.SMEM((devices,), jnp.int32),
            pltpu.SemaphoreType.DMA((parts,)),
        ],
        out_shape=[jax.ShapeDtypeStruct((n_gx // 2, chunk, wide), BF16)] * (2 * n_sec * n_gy) + [jax.ShapeDtypeStruct((total,), jnp.int32)],
        compiler_params=kernel_params(42),
        cost_estimate=pl.CostEstimate(flops=2 * total * 8 * width * width, bytes_accessed=total * width * width * 2, transcendentals=0),
        name="forward_remap",
    )(src, own, dst, flux, w)


def merge_kernel(n_sources, *refs):
    sources, outs = refs[:n_sources], refs[n_sources:]
    chunk = sources[0].shape[1]
    height = outs[0].shape[0] - 8
    first = chunk - 8
    count = n_sources * chunk
    for z, out in enumerate(outs):
        ext = None
        where = []
        for source in sources:
            piece = source[z, first:chunk, :].astype(F32)
            where.append(piece[1:2, :chunk])
            ext = piece if ext is None else ext + piece
        where = jnp.concatenate(where, axis=1)
        hot = (iota((height, count), 0).astype(F32) == where).astype(F32).astype(BF16)
        sums = dot(hot, jnp.concatenate([source[z] for source in sources], axis=0), NN)
        row3 = jnp.concatenate([where, ext[3:4, count:]], axis=1)
        ext = jnp.where(iota((8, 1), 0) == 3, row3, ext)
        out[...] = jnp.concatenate([sums, ext], axis=0).astype(out.dtype)


def columns_kernel(tracers, currents, land, west, east):
    levels = tracers.shape[1]
    width = tracers.shape[3]
    last = width - 1
    west[...] = jnp.zeros_like(west)
    east[...] = jnp.zeros_like(east)

    def put(plane, near, far):
        turned = plane.T
        for out, edge, second in ((west, 0, 1), (east, last, last - 1)):
            out[pl.ds(near, 1), :] = turned[edge : edge + 1]
            if far is not None:
                out[pl.ds(far, 1), :] = turned[second : second + 1]

    def level(l, _):
        for t in range(2):
            put(tracers[t, l], t * levels + l, (2 + t) * levels + l)
        put(currents[0, l], 4 * levels + l, 6 * levels + l)
        put(currents[1, l], 5 * levels + l, None)
        return 0

    lax.fori_loop(0, levels, level, 0, unroll=2)
    put(land[...].astype(F32), 7 * levels, 7 * levels + 1)


def rows_kernel(tracers, currents, land, from_west, from_east, south, north):
    levels = tracers.shape[0] // 2 // land.shape[0]
    height, width = land.shape
    lane = iota((1, width), 1)
    for out, edge, second in ((south, 0, 1), (north, height - 1, height - 2)):
        out[0 : 2 * levels] = tracers[pl.ds(edge, 2 * levels, stride=height), :]
        out[2 * levels : 4 * levels] = tracers[pl.ds(second, 2 * levels, stride=height), :]
        out[4 * levels : 6 * levels] = currents[pl.ds(edge, 2 * levels, stride=height), :]
        out[6 * levels : 7 * levels] = currents[pl.ds(levels * height + second, levels, stride=height), :]
        wet = [land[x : x + 1, :].astype(F32) for x in (edge, second)]
        out[7 * levels : 7 * levels + 8] = jnp.concatenate(wet + [jnp.zeros((6, width), F32)], axis=0)
    base = 7 * levels + 8
    for start, stop, at in ((0, 2 * levels, 0), (4 * levels, 6 * levels, 2 * levels), (7 * levels, 7 * levels + 8, 4 * levels)):
        w, e = from_west[start:stop], from_east[start:stop]
        there = slice(base + at, base + at + stop - start)
        south[there] = jnp.where(lane == 0, w, pltpu.roll(e, width - 1, 1))
        north[there] = jnp.where(lane == width - 1, e, pltpu.roll(w, 1, 1))


def plus_side(q, other, speed, speed_other, passable):
    return KH * passable * (other - q) - 0.25 * (speed + speed_other) * passable * (q + other)


def minus_side(q, other, speed, speed_other, passable):
    return KH * passable * (other - q) + 0.25 * (speed_other + speed) * passable * (other + q)


def level_profile(levels, width):
    depth = iota((levels, width), 0).astype(F32)
    return jnp.exp(-depth / 4.0) * (1.0 - jnp.exp(jnp.full((levels, width), -0.25, F32)))


def strip_step(q, q_plus, q_minus, across, across_plus, across_minus, along, corner_q, corner_along, wet, wet_plus, wet_minus, corner_wet, forcing):
    levels, width = q.shape
    lane = iota((1, width), 1)
    row = iota((levels, 1), 0)

    def ahead(x, corner):
        return jnp.where(lane == width - 1, corner, pltpu.roll(x, width - 1, 1))

    def behind(x, corner):
        return jnp.where(lane == 0, corner, pltpu.roll(x, 1, 1))

    total = plus_side(q, q_plus, across, across_plus, wet * wet_plus)
    total += minus_side(q, q_minus, across, across_minus, wet * wet_minus)
    total += plus_side(q, ahead(q, corner_q), along, ahead(along, corner_along), wet * ahead(wet, corner_wet))
    total += minus_side(q, behind(q, corner_q), along, behind(along, corner_along), wet * behind(wet, corner_wet))
    below = jnp.where(row < levels - 1, pltpu.roll(q, levels - 1, 0) - q, 0.0)
    above = jnp.where(row > 0, q - pltpu.roll(q, 1, 0), 0.0)
    return q + total + wet * (KV * (below - above) + forcing)


def strips(tracer, levels, inner, outer, flux):
    width = outer[0].shape[1]
    lane = iota((1, width), 1)
    base = 7 * levels + 8
    north, south, east, west = outer

    def part(x, at, count=levels):
        return x[at : at + count]

    def corners(at, count):
        n, s = part(north, base + at, count), part(south, base + at, count)
        e = jnp.where(lane == width - 1, n, pltpu.roll(s, 1, 1))
        w = jnp.where(lane == width - 1, pltpu.roll(n, width - 1, 1), s)
        return n, s, e, w

    corner_q = corners(tracer * levels, levels)
    corner_u = corners(2 * levels, levels)
    corner_v = corners(3 * levels, levels)
    corner_wet = corners(4 * levels, 1)
    top = (iota((levels, 1), 0) == 0).astype(F32)
    profile = level_profile(levels, width)
    results = []
    for side in range(4):
        near, far = inner[side], outer[side]
        beside, out = part(near, tracer * levels), part(far, (2 + tracer) * levels)
        mid = part(far, tracer * levels)
        speed = 5 if side < 2 else 4
        along = part(far, (9 - speed) * levels)
        corner_along = (corner_u if side < 2 else corner_v)[side]
        across, across_in, across_out = part(far, speed * levels), part(near, speed * levels), part(far, 6 * levels)
        wet, wet_in, wet_out = part(far, 7 * levels, 1), part(near, 7 * levels, 1), part(far, 7 * levels + 1, 1)
        shortwave, heat, salt = flux[side]
        forcing = 0.3 * profile * shortwave + top * heat if tracer == 0 else top * salt
        if side % 2 == 0:
            pairs = (out, beside, across, across_out, across_in)
            wets = (wet, wet_out, wet_in)
        else:
            pairs = (beside, out, across, across_in, across_out)
            wets = (wet, wet_in, wet_out)
        results.append(strip_step(mid, *pairs, along, corner_q[side], corner_along, *wets, corner_wet[side], forcing))
    return results


def shifts(plane, north, south, east, west):
    height, width = plane.shape
    lane, row = iota(plane.shape, 1), iota(plane.shape, 0)
    return (
        jnp.where(lane == width - 1, east, pltpu.roll(plane, width - 1, 1)),
        jnp.where(lane == 0, west, pltpu.roll(plane, 1, 1)),
        jnp.where(row == height - 1, north, pltpu.roll(plane, height - 1, 0)),
        jnp.where(row == 0, south, pltpu.roll(plane, 1, 0)),
    )


def wet_products(wet, north, south, east, west):
    return [wet * other for other in shifts(wet, north, south, east, west)]


def coefficients(u, v, u_east, u_west, v_north, v_south, passable):
    east, west, north, south = passable
    height, width = u.shape
    lane, row = iota(u.shape, 1), iota(u.shape, 0)
    e = jnp.where(lane == width - 1, u_east, pltpu.roll(u, width - 1, 1))
    w = jnp.where(lane == 0, u_west, pltpu.roll(u, 1, 1))
    n = jnp.where(row == height - 1, v_north, pltpu.roll(v, height - 1, 0))
    s = jnp.where(row == 0, v_south, pltpu.roll(v, 1, 0))
    flow_e, flow_w = 0.25 * (u + e) * east, 0.25 * (w + u) * west
    flow_n, flow_s = 0.25 * (v + n) * north, 0.25 * (s + v) * south
    own = 1.0 + (flow_w - flow_e) + (flow_s - flow_n) - KH * (east + west + north + south)
    return own, KH * east - flow_e, KH * west + flow_w, KH * north - flow_n, KH * south + flow_s


def column(turned, index, lane):
    return pltpu.roll(turned, lax.rem(lane - index + 2 * turned.shape[1], turned.shape[1]), 1)


def corrected(edge, x_rows):
    row = iota((edge.shape[0], 1), 0)
    for at, x in x_rows:
        edge = edge + jnp.where(row == at, 0.1 * x, 0.0)
    return edge


def surface_kernel(grid, chunk, levels, *refs):
    n_sec, n_gx, n_gy = grid
    planes = n_sec * n_gy
    parts, refs = refs[:n_gx], refs[n_gx:]
    tracers, currents, land, own_n, own_s, own_e, own_w, from_n, from_s, from_e, from_w, *refs = refs
    back, flux, rim, in_n, in_s, in_e, in_w, out_n, out_s, out_e, out_w = refs
    height, width = land.shape
    last = width - 1
    lane = iota((1, width), 1)
    sums = parts[0][...]
    for part in parts[1:]:
        sums = sums + part[...].astype(F32)
    sums, ext = sums[:height], sums[height : height + 8]
    shortwave, heat, salt, stress_u, stress_v = [sums[:, f * width : (f + 1) * width] for f in range(SENT)]
    wet = land[...].astype(F32)
    u0 = currents[0, 0] + 0.1 * stress_u
    v0 = currents[1, 0] + 0.1 * stress_v
    flux[0], flux[1], flux[2], flux[3], flux[4] = shortwave, heat, salt, u0, v0
    rim[...] = ext

    def block(r, b):
        return ext[r : r + 1, b * width : (b + 1) * width]

    n_flux, s_flux = [[block(r, b) for b in range(SENT)] for r in (0, 2)]
    ne, nw, se, sw = [[block(r, b) for b in (3, 4)] for r in (4, 5, 6, 7)]
    level0_u, level0_v, second = 4 * levels, 5 * levels, 6 * levels
    base = 7 * levels + 8
    corner_n = jnp.where(lane == last, pltpu.roll(ne[0], last, 1), pltpu.roll(nw[0], 1, 1))
    corner_s = jnp.where(lane == last, pltpu.roll(se[0], last, 1), pltpu.roll(sw[0], 1, 1))
    corner_n_v = jnp.where(lane == last, pltpu.roll(ne[1], last, 1), pltpu.roll(nw[1], 1, 1))
    corner_s_v = jnp.where(lane == last, pltpu.roll(se[1], last, 1), pltpu.roll(sw[1], 1, 1))
    far_n = corrected(
        from_n[...],
        [(level0_u, n_flux[3]), (level0_v, n_flux[4]), (second, block(1, 4)), (base + 2 * levels, corner_n), (base + 3 * levels, corner_n_v)],
    )
    far_s = corrected(
        from_s[...],
        [(level0_u, s_flux[3]), (level0_v, s_flux[4]), (second, block(3, 4)), (base + 2 * levels, corner_s), (base + 3 * levels, corner_s_v)],
    )
    far_e = corrected(from_e[...], [(level0_u, block(6, 0)), (level0_v, block(7, 0)), (second, block(5, 2))])
    far_w = corrected(from_w[...], [(level0_u, block(6, 1)), (level0_v, block(7, 1)), (second, block(7, 2))])
    turned = stress_u.T
    near_n = corrected(own_n[...], [(level0_v, stress_v[height - 1 : height])])
    near_s = corrected(own_s[...], [(level0_v, stress_v[0:1])])
    near_e = corrected(own_e[...], [(level0_u, turned[last : last + 1])])
    near_w = corrected(own_w[...], [(level0_u, turned[0:1])])
    in_n[...], in_s[...], in_e[...], in_w[...] = near_n, near_s, near_e, near_w
    out_n[...], out_s[...], out_e[...], out_w[...] = far_n, far_s, far_e, far_w

    e_turned, w_turned = far_e.T, far_w.T
    east = lambda index: column(e_turned, index, last)
    west = lambda index: column(w_turned, index, 0)
    passable = wet_products(
        wet, far_n[7 * levels : 7 * levels + 1], far_s[7 * levels : 7 * levels + 1], east(7 * levels), west(7 * levels)
    )
    lines = strips(0, levels, (near_n, near_s, near_e, near_w), (far_n, far_s, far_e, far_w), rim_flux(ext, width))
    profile = level_profile(levels, width)
    mix = KV * wet
    warm = 0.3 * wet * shortwave

    def weights(l, u, v):
        v_n, v_s = [x[5 * levels + l : 5 * levels + l + 1] for x in (far_n, far_s)]
        return coefficients(u, v, east(4 * levels + l), west(4 * levels + l), v_n, v_s, passable)

    def horizontal(c, q, halo):
        e, w, n, s = shifts(q, *halo)
        return c[0] * q + c[1] * e + c[2] * w + c[3] * n + c[4] * s

    def start(l):
        return far_n[l : l + 1], far_s[l : l + 1], east(l), west(l)

    q0, q1, q2 = tracers[0, 0], tracers[0, 1], tracers[0, 2]
    c0 = weights(0, u0, v0)
    c1 = weights(1, currents[0, 1], currents[1, 1])
    t0 = horizontal(c0, q0, start(0)) + mix * (q1 - q0) + warm * profile[0:1] + wet * heat
    t1 = horizontal(c1, q1, start(1)) + mix * ((q2 - q1) - (q1 - q0)) + warm * profile[1:2]
    sides = jnp.concatenate([lines[2][0:8], lines[3][0:8], jnp.zeros((width - 16, width), F32)], axis=0).T
    halo = lines[0][0:1], lines[1][0:1], column(sides, 0, last), column(sides, 8, 0)
    t0 = horizontal(c0, t0, halo) + mix * (t1 - t0) + warm * profile[0:1] + wet * heat
    sst = t0.astype(BF16)
    plane = lax.axis_index("sec") * n_gy + lax.axis_index("gy")
    line = lax.axis_index("gx")
    for z, part in enumerate(parts):
        where = part[height + 3 : height + 4, : planes * chunk].astype(F32)
        hot = (iota((height, planes * chunk), 0).astype(F32) == where).astype(F32)
        picked = dot(hot.T.astype(BF16), sst, NN).reshape(planes, chunk, width)
        for m in range(planes):
            there = plane ^ m
            device = (lax.div(there, n_gy) * n_gx + (line ^ z)) * n_gy + lax.rem(there, n_gy)
            back[device] = picked[m, : back.shape[1]].astype(BF16)


def rim_flux(ext, width):
    def block(r, b):
        return ext[r : r + 1, b * width : (b + 1) * width]

    return (
        (block(0, 0), block(0, 1), block(0, 2)),
        (block(2, 0), block(2, 1), block(2, 2)),
        (block(4, 0), block(5, 0), block(4, 2)),
        (block(4, 1), block(5, 1), block(6, 2)),
    )


def stencil_kernel(
    tracers, currents, land, flux, rim, in_n, in_s, in_e, in_w, out_n, out_s, out_e, out_w,
    out, held, weights, line_n, line_s, depth, forced, passing,
):
    levels = tracers.shape[1]
    height, width = land.shape
    last = width - 1
    wet = land[...].astype(F32)
    far_n, far_s, far_e, far_w = out_n[...], out_s[...], out_e[...], out_w[...]
    e_turned, w_turned = far_e.T, far_w.T
    at = 7 * levels
    for i, x in enumerate(
        wet_products(wet, far_n[at : at + 1], far_s[at : at + 1], column(e_turned, at, last), column(w_turned, at, 0))
    ):
        passing[i] = x
    forced[0], forced[1], forced[2] = 0.3 * wet * flux[0], wet * flux[1], wet * flux[2]
    depth[...] = level_profile(levels, width)
    columns = []
    for tracer in range(2):
        lines = strips(
            tracer, levels, (in_n[...], in_s[...], in_e[...], in_w[...]), (far_n, far_s, far_e, far_w), rim_flux(rim[...], width)
        )
        line_n[tracer * levels : (tracer + 1) * levels] = lines[0]
        line_s[tracer * levels : (tracer + 1) * levels] = lines[1]
        columns.append(lines[2:])
    blank = jnp.zeros((width - 2 * levels, width), F32)
    e_later, w_later = [jnp.concatenate([columns[0][i], columns[1][i], blank], axis=0).T for i in range(2)]

    def update(c, q, halo, under, over, forcing):
        e, w, n, s = shifts(q, *halo)
        mixed = KV * land[...].astype(F32) * ((under - q) - (q - over))
        return c[0] * q + c[1] * e + c[2] * w + c[3] * n + c[4] * s + mixed + forcing

    def forcing(tracer, l):
        top = jnp.where(l == 0, 1.0, 0.0)
        if tracer == 0:
            return forced[0] * depth[pl.ds(l, 1), :] + top * forced[1]
        return top * forced[2]

    def first_step(l, _):
        surface = l == 0
        u = jnp.where(surface, flux[3], currents[0, l])
        v = jnp.where(surface, flux[4], currents[1, l])
        row = 5 * levels + l
        c = coefficients(
            u, v, column(e_turned, 4 * levels + l, last), column(w_turned, 4 * levels + l, 0),
            out_n[pl.ds(row, 1), :], out_s[pl.ds(row, 1), :], [passing[i] for i in range(4)],
        )
        for i, x in enumerate(c):
            weights[i, l] = x
        for tracer in range(2):
            row = tracer * levels + l
            halo = out_n[pl.ds(row, 1), :], out_s[pl.ds(row, 1), :], column(e_turned, row, last), column(w_turned, row, 0)
            under, over = tracers[tracer, jnp.minimum(l + 1, levels - 1)], tracers[tracer, jnp.maximum(l - 1, 0)]
            held[tracer, l] = update(c, tracers[tracer, l], halo, under, over, forcing(tracer, l))
        return 0

    lax.fori_loop(0, levels, first_step, 0)

    def second_step(l, _):
        c = [weights[i, l] for i in range(5)]
        for tracer in range(2):
            row = tracer * levels + l
            halo = line_n[pl.ds(row, 1), :], line_s[pl.ds(row, 1), :], column(e_later, row, last), column(w_later, row, 0)
            under, over = held[tracer, jnp.minimum(l + 1, levels - 1)], held[tracer, jnp.maximum(l - 1, 0)]
            out[tracer, l] = update(c, held[tracer, l], halo, under, over, forcing(tracer, l))
        return 0

    lax.fori_loop(0, levels, second_step, 0)


def backward_kernel(parts, slots, src, back, w, out, held, wide, picked, terms, sems):
    total, width = terms.shape
    blocks = out.shape[0]
    batch = total // parts

    def copy(c):
        return pltpu.make_async_copy(w.at[pl.ds(c * batch, batch)], held.at[pl.ds(c * batch, batch)], sems.at[c])

    for c in range(parts):
        copy(c).start()
    wide[...] = back[...].astype(F32).reshape(wide.shape)

    def pick(i, _):
        for j in range(16):
            picked[pl.ds(i * 16 + j, 1), :] = wide[pl.ds(slots[i * 16 + j], 1), :]
        return 0

    lax.fori_loop(0, total // 16, pick, 0, unroll=2)
    row = iota((16, width), 0)

    def work(c, _):
        copy(c).wait()
        for g in range(batch // 16):
            at = pl.multiple_of(c * batch + g * 16, 16)
            rows = picked[pl.ds(at, 16), :]
            left = [jnp.where((row == r) | (row == 8 + r), rows, 0.0).astype(BF16) for r in range(8)]
            block = held[pl.ds(at, 16)].reshape(2, 8 * width, width)
            both = dot(jnp.concatenate(left, axis=1), jnp.concatenate([block[0], block[1]], axis=1), NN)
            terms[pl.ds(at, 8), :] = both[:8, :width]
            terms[pl.ds(at + 8, 8), :] = both[8:, width:]
        return 0

    lax.fori_loop(0, parts, work, 0)
    hot = (iota((blocks, total), 0) == src[...]).astype(F32).astype(BF16)
    value = terms[...]
    high = value.astype(BF16)
    low = (value - high.astype(F32)).astype(BF16)
    both = dot(hot, jnp.concatenate([high, low], axis=1), NN)
    out[...] = both[:, :width] + both[:, width:]


def backward(back, w, src, slots, blocks, parts=20):
    total, width, _ = w.shape
    devices, cap, _ = back.shape
    return pl.pallas_call(
        functools.partial(backward_kernel, parts),
        in_specs=[SMEM, VMEM, VMEM, ANY],
        out_specs=VMEM,
        scratch_shapes=[
            pltpu.VMEM(w.shape, BF16),
            pltpu.VMEM((devices * cap, width), F32),
            pltpu.VMEM((total, width), F32),
            pltpu.VMEM((total, width), F32),
            pltpu.SemaphoreType.DMA((parts,)),
        ],
        out_shape=jax.ShapeDtypeStruct((blocks, width), F32),
        compiler_params=kernel_params(58),
        cost_estimate=pl.CostEstimate(flops=2 * total * 8 * width * width, bytes_accessed=total * width * width * 2, transcendentals=0),
        name="backward_remap",
    )(slots, src.reshape(1, total), back, w)


def kernel(body, outs, name, mebibytes, bytes_accessed, scratch=()):
    return pl.pallas_call(
        body,
        out_shape=[jax.ShapeDtypeStruct(shape, dtype) for shape, dtype in outs],
        scratch_shapes=list(scratch),
        compiler_params=kernel_params(mebibytes),
        cost_estimate=pl.CostEstimate(flops=bytes_accessed, bytes_accessed=bytes_accessed, transcendentals=0),
        name=name,
    )


def neighbours(axis):
    count = lax.axis_size(axis)
    forward_pairs = [(i, i + 1) for i in range(count - 1)]
    return forward_pairs, [(b, a) for a, b in forward_pairs]


def swapped(array, axes, count, step):
    return lax.ppermute(array, axes, [(i, i ^ step) for i in range(count)])


def on_device(atm_flux, remap_weights, remap_src, remap_dst, remap_owner, tracers, currents, land_sea):
    grid = n_sec, n_gx, n_gy = [lax.axis_size(axis) for axis in EVERY]
    planes = n_sec * n_gy
    total, width, _ = remap_weights.shape
    _, levels, height, _ = tracers.shape
    cap = up(2 * total // (planes * n_gx), 8)
    wide = SENT * width

    *sends, slots = forward(atm_flux, remap_weights, remap_src, remap_owner.reshape(total), remap_dst, grid, cap)
    chunk = sends[0].shape[1]
    sends = sends[:planes], sends[planes:]
    got = [[send[0]] + [swapped(send[m], ("sec", "gy"), planes, m) for m in range(1, planes)] for send in sends]

    side = (width, width)
    end = (7 * levels + 80, width)
    own_w, own_e = kernel(columns_kernel, [(side, F32)] * 2, "edge_columns", 16, 1 << 22)(tracers, currents, land_sea)
    to_north, to_south = neighbours(NORTH)
    to_east, to_west = neighbours("gy")
    from_e = lax.ppermute(own_w, "gy", to_west)
    from_w = lax.ppermute(own_e, "gy", to_east)
    own_s, own_n = kernel(rows_kernel, [(end, F32)] * 2, "edge_rows", 16, 1 << 20)(
        tracers.reshape(-1, width), currents.reshape(-1, width), land_sea, from_w, from_e
    )
    from_n = lax.ppermute(own_s, NORTH, to_south)
    from_s = lax.ppermute(own_n, NORTH, to_north)

    merged = []
    for far, chunks in zip((1, 0), got):
        if far:
            chunks, from_n, from_s = lax.optimization_barrier((chunks, from_n, from_s))
        here = [((height + 8, wide), BF16)] * (n_gx // 2)
        if not far:
            here = [((height + 8, wide), F32)] + here[1:]
        merged.append(kernel(functools.partial(merge_kernel, planes), here, "merge", 24, 1 << 22)(*chunks))
    merged = list(merged[1]) + list(merged[0])
    parts = [merged[0]] + [swapped(merged[m], "gx", n_gx, m) for m in range(1, n_gx)]

    back, flux, rim, *edges = kernel(
        functools.partial(surface_kernel, grid, chunk, levels),
        [((planes * n_gx, cap, width), BF16), ((5, height, width), F32), ((8, wide), F32)] + ([(end, F32)] * 2 + [(side, F32)] * 2) * 2,
        "surface",
        58,
        1 << 22,
    )(*parts, tracers[0:1, 0:3], currents[:, 0:2], land_sea, own_n, own_s, own_e, own_w, from_n, from_s, from_e, from_w)
    returned = lax.all_to_all(back, EVERY, split_axis=0, concat_axis=0, tiled=True)

    plane = (height, width)
    (tracers_out,) = kernel(
        stencil_kernel,
        [(tracers.shape, F32)],
        "substeps",
        32,
        1 << 24,
        [
            pltpu.VMEM(tracers.shape, F32),
            pltpu.VMEM((5, levels) + plane, F32),
            pltpu.VMEM((2 * levels, width), F32),
            pltpu.VMEM((2 * levels, width), F32),
            pltpu.VMEM((levels, width), F32),
            pltpu.VMEM((3,) + plane, F32),
            pltpu.VMEM((4,) + plane, F32),
        ],
    )(tracers, currents, land_sea, flux, rim, *edges)
    return tracers_out, backward(returned, remap_weights, remap_src, slots, atm_flux.shape[0])


def solution(mesh):
    return jax.shard_map(
        on_device,
        mesh=mesh,
        in_specs=(
            P(EVERY, None, None),
            P(EVERY, None, None),
            P(EVERY),
            P(EVERY),
            P(EVERY, None),
            P(None, None, NORTH, "gy"),
            P(None, None, NORTH, "gy"),
            P(NORTH, "gy"),
        ),
        out_specs=(P(None, None, NORTH, "gy"), P(EVERY, None)),
        check_vma=False,
    )
```

```python
import functools

import jax
import jax.numpy as jnp
from jax import lax
from jax.experimental import pallas as pl
from jax.experimental.pallas import tpu as pltpu
from jax.sharding import PartitionSpec as P

F32 = jnp.float32
BF16 = jnp.bfloat16
NT = (((1,), (1,)), ((), ()))
NN = (((1,), (0,)), ((), ()))
TN = (((0,), (0,)), ((), ()))
EVERY = ("sec", "gx", "gy")
NORTH = ("sec", "gx")
SENT = 5
KH = 0.1
KV = 0.1


def dot(left, right, dims):
    return lax.dot_general(left, right, dims, preferred_element_type=F32)


def iota(shape, dim):
    return lax.broadcasted_iota(jnp.int32, shape, dim)


def up(number, step):
    return -(-number // step) * step


def kernel_params(mebibytes):
    return pltpu.CompilerParams(vmem_limit_bytes=mebibytes << 20)


VMEM = pl.BlockSpec(memory_space=pltpu.VMEM)
SMEM = pl.BlockSpec(memory_space=pltpu.SMEM)
ANY = pl.BlockSpec(memory_space=pl.ANY)


def forward_kernel(parts, cap, grid, src, own, dst, flux, w, *refs):
    sends, (slots, held, mixed, acc, rows, xs, counts, renumbered, sems) = refs[:-9], refs[-9:]
    n_sec, n_gx, n_gy = grid
    devices, chunk, wide = xs.shape
    total, width, _ = held.shape
    batch = total // parts
    fields = flux.shape[1]
    first = chunk - 8
    last = width - 1

    def copy(c):
        return pltpu.make_async_copy(w.at[pl.ds(c * batch, batch)], held.at[pl.ds(c * batch, batch)], sems.at[c])

    for c in range(parts):
        copy(c).start()

    plane = lax.axis_index("sec") * n_gy + lax.axis_index("gy")
    line = lax.axis_index("gx")

    def renumber(owner):
        x = lax.div(owner, n_gy)
        there = lax.div(x, n_gx) * n_gy + lax.rem(owner, n_gy)
        return (there ^ plane) * n_gx + (lax.rem(x, n_gx) ^ line)

    def clear(o, _):
        counts[o] = 0
        renumbered[o] = renumber(o)
        return 0

    lax.fori_loop(0, devices, clear, 0)
    rows[...] = jnp.full_like(rows, 255.0)
    acc[...] = jnp.zeros_like(acc)
    xs[...] = jnp.zeros_like(xs)
    full = flux[...].astype(F32)
    one = [full[:, f : f + 1] for f in range(fields)]
    heat = 0.2 * (one[1] + one[2] + one[3]) - 0.15 * one[5]
    salt = 0.2 * one[4] - 0.1 * one[5]
    heat_high = heat.astype(BF16).astype(F32)
    salt_high = salt.astype(BF16).astype(F32)
    mixed[...] = jnp.concatenate(
        [one[0], heat_high, salt_high, one[6], one[7], heat - heat_high, salt - salt_high, jnp.zeros_like(heat)], axis=1
    ).astype(BF16)

    low_rows = iota((fields, width), 0)
    low_rows = (low_rows == 1) | (low_rows == 2)

    def work(c, _):
        copy(c).wait()
        for b in range(0, batch, 2):
            k = c * batch + b
            left = jnp.concatenate([mixed[src[k]], mixed[src[k + 1]]], axis=0)
            both = dot(left, held[pl.ds(k, 2)].reshape(2 * width, width), NT)
            for z, part in enumerate((both[:fields, :width], both[fields:, width:])):
                part = part + jnp.where(low_rows, pltpu.roll(part, fields - 4, 0), 0.0)
                owner = own[k + z]
                at = counts[owner]
                counts[owner] = at + 1
                at = jnp.minimum(at, cap - 1)
                slots[k + z] = owner * cap + at
                slot = renumbered[owner] * cap + at
                acc[pl.ds(pl.multiple_of(slot * fields, fields), fields), :] = part
                rows[pl.ds(slot, 1), :] = jnp.full((1, width), dst[k + z].astype(F32), F32)
        return 0

    lax.fori_loop(0, parts, work, 0)

    lane = iota((cap, width), 1).astype(F32)
    sub = iota((cap, width), 0).astype(F32)
    row = iota((24, wide), 0)
    picks = {
        4: (0, 0), 5: (1, 0), 6: (3, 0), 7: (4, 0), 12: (0, last), 13: (1, last), 14: (3, last), 15: (4, last),
        20: (2, 0), 21: (3, 1), 22: (2, last), 23: (3, last - 1),
    }
    pick = jnp.full((24, wide), -1, jnp.int32)
    for at, (field, column) in picks.items():
        pick = jnp.where(row == at, field * width + column, pick)
    select = (iota((24, wide), 1) == pick).astype(F32).astype(BF16)
    row = iota((8, cap), 0)
    wanted = jnp.zeros((8, cap), F32)
    for at, x in enumerate((0, 1, last, last - 1, 0, 0, last, last)):
        wanted = jnp.where(row == at, float(x), wanted)
    group = 8

    def owners(g, _):
        ds = [g * group + j for j in range(group)]
        five = []
        for d in ds:
            x = [acc[pl.ds(d * cap * fields + f, cap, stride=fields), :] for f in range(SENT)]
            x = jnp.concatenate(x, axis=1)
            xs[d, 0:cap, :] = x
            five.append(x.astype(BF16))
        where = [rows[pl.ds(pl.multiple_of(d * cap, 8), cap), :] for d in ds]
        hot = [(lane == r).astype(F32).astype(BF16) for r in where]
        flat = [jnp.sum(jnp.where(lane == sub, r, 0.0), axis=0, keepdims=True) for r in where]
        flat = [jnp.where(lane[:1] < cap, f, 255.0) for f in flat]
        edge = [dot(select, x, NT).astype(BF16) for x in five]
        sides = [dot(e, h, NN) for e, h in zip(edge, hot)]
        ends = [dot((f[:, :cap] == wanted).astype(F32).astype(BF16), x, NN) for f, x in zip(flat, five)]
        for d, f, side, end in zip(ds, flat, sides, ends):
            here = lax.div(d, n_gx) ^ plane
            here = (lax.div(here, n_gy) * n_gx + (lax.rem(d, n_gx) ^ line)) * n_gy + lax.rem(here, n_gy)

            def at(offset):
                return renumbered[lax.rem(here + offset + 2 * devices, devices)]

            south_of, north_of, west_of, east_of = at(-n_gy), at(n_gy), at(-1), at(1)

            xs[south_of, first : first + 1, :] = end[0:1]
            xs[south_of, first + 1 : first + 2, 4 * width :] = end[1:2, 4 * width :]
            xs[north_of, first + 2 : first + 3, :] = end[2:3]
            xs[north_of, first + 3 : first + 4, 4 * width :] = end[3:4, 4 * width :]
            xs[at(-n_gy - 1), first + 4 : first + 5, 3 * width :] = end[4:5, 3 * width :]
            xs[at(-n_gy + 1), first + 5 : first + 6, 3 * width :] = end[5:6, 3 * width :]
            xs[at(n_gy - 1), first + 6 : first + 7, 3 * width :] = end[6:7, 3 * width :]
            xs[at(n_gy + 1), first + 7 : first + 8, 3 * width :] = end[7:8, 3 * width :]
            xs[west_of, first + 4 : first + 8, 0:width] = side[4:8]
            xs[east_of, first + 4 : first + 8, width : 2 * width] = side[12:16]
            xs[west_of, first + 4 : first + 6, 2 * width : 3 * width] = side[20:22]
            xs[east_of, first + 6 : first + 8, 2 * width : 3 * width] = side[22:24]
            xs[d, first + 1 : first + 2, 0:width] = f
        return 0

    lax.fori_loop(0, devices // group, owners, 0)

    half = n_gx // 2
    planes = n_sec * n_gy
    for m in range(planes):
        sends[m][...] = xs[m * n_gx + half : (m + 1) * n_gx].astype(BF16)
        sends[planes + m][...] = xs[m * n_gx : m * n_gx + half].astype(BF16)


def forward(flux, w, src, own, dst, grid, cap, parts=20):
    n_sec, n_gx, n_gy = grid
    devices = n_sec * n_gx * n_gy
    total, width, _ = w.shape
    chunk = up(cap + 8, 16)
    fields = flux.shape[1]
    wide = SENT * width
    return pl.pallas_call(
        functools.partial(forward_kernel, parts, cap, grid),
        in_specs=[SMEM, SMEM, SMEM, VMEM, ANY],
        out_specs=[VMEM] * (2 * n_sec * n_gy) + [SMEM],
        scratch_shapes=[
            pltpu.VMEM(w.shape, BF16),
            pltpu.VMEM(flux.shape, BF16),
            pltpu.VMEM((devices * cap * fields, width), F32),
            pltpu.VMEM((devices * cap, width), F32),
            pltpu.VMEM((devices, chunk, wide), F32),
            pltpu.SMEM((devices,), jnp.int32),
            pltpu.SMEM((devices,), jnp.int32),
            pltpu.SemaphoreType.DMA((parts,)),
        ],
        out_shape=[jax.ShapeDtypeStruct((n_gx // 2, chunk, wide), BF16)] * (2 * n_sec * n_gy) + [jax.ShapeDtypeStruct((total,), jnp.int32)],
        compiler_params=kernel_params(58),
        cost_estimate=pl.CostEstimate(flops=2 * total * 8 * width * width, bytes_accessed=total * width * width * 2, transcendentals=0),
        name="forward_remap",
    )(src, own, dst, flux, w)


def merge_kernel(n_sources, *refs):
    sources, outs = refs[:n_sources], refs[n_sources:]
    chunk = sources[0].shape[1]
    height = outs[0].shape[0] - 8
    first = chunk - 8
    count = n_sources * chunk
    for z, out in enumerate(outs):
        ext = None
        where = []
        for source in sources:
            piece = source[z, first:chunk, :].astype(F32)
            where.append(piece[1:2, :chunk])
            ext = piece if ext is None else ext + piece
        where = jnp.concatenate(where, axis=1)
        hot = (iota((height, count), 0).astype(F32) == where).astype(F32).astype(BF16)
        sums = dot(hot, jnp.concatenate([source[z] for source in sources], axis=0), NN)
        row3 = jnp.concatenate([where, ext[3:4, count:]], axis=1)
        ext = jnp.where(iota((8, 1), 0) == 3, row3, ext)
        out[...] = jnp.concatenate([sums, ext], axis=0).astype(out.dtype)


def columns_kernel(tracers, currents, land, west, east):
    levels = tracers.shape[1]
    width = tracers.shape[3]
    last = width - 1
    west[...] = jnp.zeros_like(west)
    east[...] = jnp.zeros_like(east)

    def put(plane, near, far):
        turned = plane.T
        for out, edge, second in ((west, 0, 1), (east, last, last - 1)):
            out[pl.ds(near, 1), :] = turned[edge : edge + 1]
            if far is not None:
                out[pl.ds(far, 1), :] = turned[second : second + 1]

    def level(l, _):
        for t in range(2):
            put(tracers[t, l], t * levels + l, (2 + t) * levels + l)
        put(currents[0, l], 4 * levels + l, 6 * levels + l)
        put(currents[1, l], 5 * levels + l, None)
        return 0

    lax.fori_loop(0, levels, level, 0, unroll=2)
    put(land[...].astype(F32), 7 * levels, 7 * levels + 1)


def rows_kernel(tracers, currents, land, from_west, from_east, south, north):
    levels = tracers.shape[0] // 2 // land.shape[0]
    height, width = land.shape
    lane = iota((1, width), 1)
    for out, edge, second in ((south, 0, 1), (north, height - 1, height - 2)):
        out[0 : 2 * levels] = tracers[pl.ds(edge, 2 * levels, stride=height), :]
        out[2 * levels : 4 * levels] = tracers[pl.ds(second, 2 * levels, stride=height), :]
        out[4 * levels : 6 * levels] = currents[pl.ds(edge, 2 * levels, stride=height), :]
        out[6 * levels : 7 * levels] = currents[pl.ds(levels * height + second, levels, stride=height), :]
        wet = [land[x : x + 1, :].astype(F32) for x in (edge, second)]
        out[7 * levels : 7 * levels + 8] = jnp.concatenate(wet + [jnp.zeros((6, width), F32)], axis=0)
    base = 7 * levels + 8
    for start, stop, at in ((0, 2 * levels, 0), (4 * levels, 6 * levels, 2 * levels), (7 * levels, 7 * levels + 8, 4 * levels)):
        w, e = from_west[start:stop], from_east[start:stop]
        there = slice(base + at, base + at + stop - start)
        south[there] = jnp.where(lane == 0, w, pltpu.roll(e, width - 1, 1))
        north[there] = jnp.where(lane == width - 1, e, pltpu.roll(w, 1, 1))


def plus_side(q, other, speed, speed_other, passable):
    return KH * passable * (other - q) - 0.25 * (speed + speed_other) * passable * (q + other)


def minus_side(q, other, speed, speed_other, passable):
    return KH * passable * (other - q) + 0.25 * (speed_other + speed) * passable * (other + q)


def level_profile(levels, width):
    depth = iota((levels, width), 0).astype(F32)
    return jnp.exp(-depth / 4.0) * (1.0 - jnp.exp(jnp.full((levels, width), -0.25, F32)))


def strip_step(q, q_plus, q_minus, across, across_plus, across_minus, along, corner_q, corner_along, wet, wet_plus, wet_minus, corner_wet, forcing):
    levels, width = q.shape
    lane = iota((1, width), 1)
    row = iota((levels, 1), 0)

    def ahead(x, corner):
        return jnp.where(lane == width - 1, corner, pltpu.roll(x, width - 1, 1))

    def behind(x, corner):
        return jnp.where(lane == 0, corner, pltpu.roll(x, 1, 1))

    total = plus_side(q, q_plus, across, across_plus, wet * wet_plus)
    total += minus_side(q, q_minus, across, across_minus, wet * wet_minus)
    total += plus_side(q, ahead(q, corner_q), along, ahead(along, corner_along), wet * ahead(wet, corner_wet))
    total += minus_side(q, behind(q, corner_q), along, behind(along, corner_along), wet * behind(wet, corner_wet))
    below = jnp.where(row < levels - 1, pltpu.roll(q, levels - 1, 0) - q, 0.0)
    above = jnp.where(row > 0, q - pltpu.roll(q, 1, 0), 0.0)
    return q + total + wet * (KV * (below - above) + forcing)


def strips(tracer, levels, inner, outer, flux):
    width = outer[0].shape[1]
    lane = iota((1, width), 1)
    base = 7 * levels + 8
    north, south, east, west = outer

    def part(x, at, count=levels):
        return x[at : at + count]

    def corners(at, count):
        n, s = part(north, base + at, count), part(south, base + at, count)
        e = jnp.where(lane == width - 1, n, pltpu.roll(s, 1, 1))
        w = jnp.where(lane == width - 1, pltpu.roll(n, width - 1, 1), s)
        return n, s, e, w

    corner_q = corners(tracer * levels, levels)
    corner_u = corners(2 * levels, levels)
    corner_v = corners(3 * levels, levels)
    corner_wet = corners(4 * levels, 1)
    top = (iota((levels, 1), 0) == 0).astype(F32)
    profile = level_profile(levels, width)
    results = []
    for side in range(4):
        near, far = inner[side], outer[side]
        beside, out = part(near, tracer * levels), part(far, (2 + tracer) * levels)
        mid = part(far, tracer * levels)
        speed = 5 if side < 2 else 4
        along = part(far, (9 - speed) * levels)
        corner_along = (corner_u if side < 2 else corner_v)[side]
        across, across_in, across_out = part(far, speed * levels), part(near, speed * levels), part(far, 6 * levels)
        wet, wet_in, wet_out = part(far, 7 * levels, 1), part(near, 7 * levels, 1), part(far, 7 * levels + 1, 1)
        shortwave, heat, salt = flux[side]
        forcing = 0.3 * profile * shortwave + top * heat if tracer == 0 else top * salt
        if side % 2 == 0:
            pairs = (out, beside, across, across_out, across_in)
            wets = (wet, wet_out, wet_in)
        else:
            pairs = (beside, out, across, across_in, across_out)
            wets = (wet, wet_in, wet_out)
        results.append(strip_step(mid, *pairs, along, corner_q[side], corner_along, *wets, corner_wet[side], forcing))
    return results


def shifts(plane, north, south, east, west):
    height, width = plane.shape
    lane, row = iota(plane.shape, 1), iota(plane.shape, 0)
    return (
        jnp.where(lane == width - 1, east, pltpu.roll(plane, width - 1, 1)),
        jnp.where(lane == 0, west, pltpu.roll(plane, 1, 1)),
        jnp.where(row == height - 1, north, pltpu.roll(plane, height - 1, 0)),
        jnp.where(row == 0, south, pltpu.roll(plane, 1, 0)),
    )


def wet_products(wet, north, south, east, west):
    return [wet * other for other in shifts(wet, north, south, east, west)]


def coefficients(u, v, u_east, u_west, v_north, v_south, passable):
    east, west, north, south = passable
    height, width = u.shape
    lane, row = iota(u.shape, 1), iota(u.shape, 0)
    e = jnp.where(lane == width - 1, u_east, pltpu.roll(u, width - 1, 1))
    w = jnp.where(lane == 0, u_west, pltpu.roll(u, 1, 1))
    n = jnp.where(row == height - 1, v_north, pltpu.roll(v, height - 1, 0))
    s = jnp.where(row == 0, v_south, pltpu.roll(v, 1, 0))
    flow_e, flow_w = 0.25 * (u + e) * east, 0.25 * (w + u) * west
    flow_n, flow_s = 0.25 * (v + n) * north, 0.25 * (s + v) * south
    own = 1.0 + (flow_w - flow_e) + (flow_s - flow_n) - KH * (east + west + north + south)
    return own, KH * east - flow_e, KH * west + flow_w, KH * north - flow_n, KH * south + flow_s


def column(turned, index, lane):
    return pltpu.roll(turned, lax.rem(lane - index + 2 * turned.shape[1], turned.shape[1]), 1)


def corrected(edge, x_rows):
    row = iota((edge.shape[0], 1), 0)
    for at, x in x_rows:
        edge = edge + jnp.where(row == at, 0.1 * x, 0.0)
    return edge


def surface_kernel(grid, chunk, levels, *refs):
    n_sec, n_gx, n_gy = grid
    planes = n_sec * n_gy
    parts, refs = refs[:n_gx], refs[n_gx:]
    tracers, currents, land, own_n, own_s, own_e, own_w, from_n, from_s, from_e, from_w, *refs = refs
    back, flux, rim, in_n, in_s, in_e, in_w, out_n, out_s, out_e, out_w = refs
    height, width = land.shape
    last = width - 1
    lane = iota((1, width), 1)
    sums = parts[0][...]
    for part in parts[1:]:
        sums = sums + part[...].astype(F32)
    sums, ext = sums[:height], sums[height : height + 8]
    shortwave, heat, salt, stress_u, stress_v = [sums[:, f * width : (f + 1) * width] for f in range(SENT)]
    wet = land[...].astype(F32)
    u0 = currents[0, 0] + 0.1 * stress_u
    v0 = currents[1, 0] + 0.1 * stress_v
    flux[0], flux[1], flux[2], flux[3], flux[4] = shortwave, heat, salt, u0, v0
    rim[...] = ext

    def block(r, b):
        return ext[r : r + 1, b * width : (b + 1) * width]

    n_flux, s_flux = [[block(r, b) for b in range(SENT)] for r in (0, 2)]
    ne, nw, se, sw = [[block(r, b) for b in (3, 4)] for r in (4, 5, 6, 7)]
    level0_u, level0_v, second = 4 * levels, 5 * levels, 6 * levels
    base = 7 * levels + 8
    corner_n = jnp.where(lane == last, pltpu.roll(ne[0], last, 1), pltpu.roll(nw[0], 1, 1))
    corner_s = jnp.where(lane == last, pltpu.roll(se[0], last, 1), pltpu.roll(sw[0], 1, 1))
    corner_n_v = jnp.where(lane == last, pltpu.roll(ne[1], last, 1), pltpu.roll(nw[1], 1, 1))
    corner_s_v = jnp.where(lane == last, pltpu.roll(se[1], last, 1), pltpu.roll(sw[1], 1, 1))
    far_n = corrected(
        from_n[...],
        [(level0_u, n_flux[3]), (level0_v, n_flux[4]), (second, block(1, 4)), (base + 2 * levels, corner_n), (base + 3 * levels, corner_n_v)],
    )
    far_s = corrected(
        from_s[...],
        [(level0_u, s_flux[3]), (level0_v, s_flux[4]), (second, block(3, 4)), (base + 2 * levels, corner_s), (base + 3 * levels, corner_s_v)],
    )
    far_e = corrected(from_e[...], [(level0_u, block(6, 0)), (level0_v, block(7, 0)), (second, block(5, 2))])
    far_w = corrected(from_w[...], [(level0_u, block(6, 1)), (level0_v, block(7, 1)), (second, block(7, 2))])
    turned = stress_u.T
    near_n = corrected(own_n[...], [(level0_v, stress_v[height - 1 : height])])
    near_s = corrected(own_s[...], [(level0_v, stress_v[0:1])])
    near_e = corrected(own_e[...], [(level0_u, turned[last : last + 1])])
    near_w = corrected(own_w[...], [(level0_u, turned[0:1])])
    in_n[...], in_s[...], in_e[...], in_w[...] = near_n, near_s, near_e, near_w
    out_n[...], out_s[...], out_e[...], out_w[...] = far_n, far_s, far_e, far_w

    e_turned, w_turned = far_e.T, far_w.T
    east = lambda index: column(e_turned, index, last)
    west = lambda index: column(w_turned, index, 0)
    passable = wet_products(
        wet, far_n[7 * levels : 7 * levels + 1], far_s[7 * levels : 7 * levels + 1], east(7 * levels), west(7 * levels)
    )
    lines = strips(0, levels, (near_n, near_s, near_e, near_w), (far_n, far_s, far_e, far_w), rim_flux(ext, width))
    profile = level_profile(levels, width)
    mix = KV * wet
    warm = 0.3 * wet * shortwave

    def weights(l, u, v):
        v_n, v_s = [x[5 * levels + l : 5 * levels + l + 1] for x in (far_n, far_s)]
        return coefficients(u, v, east(4 * levels + l), west(4 * levels + l), v_n, v_s, passable)

    def horizontal(c, q, halo):
        e, w, n, s = shifts(q, *halo)
        return c[0] * q + c[1] * e + c[2] * w + c[3] * n + c[4] * s

    def start(l):
        return far_n[l : l + 1], far_s[l : l + 1], east(l), west(l)

    q0, q1, q2 = tracers[0, 0], tracers[0, 1], tracers[0, 2]
    c0 = weights(0, u0, v0)
    c1 = weights(1, currents[0, 1], currents[1, 1])
    t0 = horizontal(c0, q0, start(0)) + mix * (q1 - q0) + warm * profile[0:1] + wet * heat
    t1 = horizontal(c1, q1, start(1)) + mix * ((q2 - q1) - (q1 - q0)) + warm * profile[1:2]
    sides = jnp.concatenate([lines[2][0:8], lines[3][0:8], jnp.zeros((width - 16, width), F32)], axis=0).T
    halo = lines[0][0:1], lines[1][0:1], column(sides, 0, last), column(sides, 8, 0)
    t0 = horizontal(c0, t0, halo) + mix * (t1 - t0) + warm * profile[0:1] + wet * heat
    sst = t0.astype(BF16)
    plane = lax.axis_index("sec") * n_gy + lax.axis_index("gy")
    line = lax.axis_index("gx")
    for z, part in enumerate(parts):
        where = part[height + 3 : height + 4, : planes * chunk].astype(F32)
        hot = (iota((height, planes * chunk), 0).astype(F32) == where).astype(F32)
        picked = dot(hot.T.astype(BF16), sst, NN).reshape(planes, chunk, width)
        for m in range(planes):
            there = plane ^ m
            device = (lax.div(there, n_gy) * n_gx + (line ^ z)) * n_gy + lax.rem(there, n_gy)
            back[device] = picked[m, : back.shape[1]].astype(BF16)


def rim_flux(ext, width):
    def block(r, b):
        return ext[r : r + 1, b * width : (b + 1) * width]

    return (
        (block(0, 0), block(0, 1), block(0, 2)),
        (block(2, 0), block(2, 1), block(2, 2)),
        (block(4, 0), block(5, 0), block(4, 2)),
        (block(4, 1), block(5, 1), block(6, 2)),
    )


def stencil_kernel(
    tracers, currents, land, flux, rim, in_n, in_s, in_e, in_w, out_n, out_s, out_e, out_w,
    out, held, weights, line_n, line_s, depth, forced, passing,
):
    levels = tracers.shape[1]
    height, width = land.shape
    last = width - 1
    wet = land[...].astype(F32)
    far_n, far_s, far_e, far_w = out_n[...], out_s[...], out_e[...], out_w[...]
    e_turned, w_turned = far_e.T, far_w.T
    at = 7 * levels
    for i, x in enumerate(
        wet_products(wet, far_n[at : at + 1], far_s[at : at + 1], column(e_turned, at, last), column(w_turned, at, 0))
    ):
        passing[i] = x
    forced[0], forced[1], forced[2] = 0.3 * wet * flux[0], wet * flux[1], wet * flux[2]
    depth[...] = level_profile(levels, width)
    columns = []
    for tracer in range(2):
        lines = strips(
            tracer, levels, (in_n[...], in_s[...], in_e[...], in_w[...]), (far_n, far_s, far_e, far_w), rim_flux(rim[...], width)
        )
        line_n[tracer * levels : (tracer + 1) * levels] = lines[0]
        line_s[tracer * levels : (tracer + 1) * levels] = lines[1]
        columns.append(lines[2:])
    blank = jnp.zeros((width - 2 * levels, width), F32)
    e_later, w_later = [jnp.concatenate([columns[0][i], columns[1][i], blank], axis=0).T for i in range(2)]

    def update(c, q, halo, under, over, forcing):
        e, w, n, s = shifts(q, *halo)
        mixed = KV * land[...].astype(F32) * ((under - q) - (q - over))
        return c[0] * q + c[1] * e + c[2] * w + c[3] * n + c[4] * s + mixed + forcing

    def forcing(tracer, l):
        top = jnp.where(l == 0, 1.0, 0.0)
        if tracer == 0:
            return forced[0] * depth[pl.ds(l, 1), :] + top * forced[1]
        return top * forced[2]

    def first_step(l, _):
        surface = l == 0
        u = jnp.where(surface, flux[3], currents[0, l])
        v = jnp.where(surface, flux[4], currents[1, l])
        row = 5 * levels + l
        c = coefficients(
            u, v, column(e_turned, 4 * levels + l, last), column(w_turned, 4 * levels + l, 0),
            out_n[pl.ds(row, 1), :], out_s[pl.ds(row, 1), :], [passing[i] for i in range(4)],
        )
        for i, x in enumerate(c):
            weights[i, l] = x
        for tracer in range(2):
            row = tracer * levels + l
            halo = out_n[pl.ds(row, 1), :], out_s[pl.ds(row, 1), :], column(e_turned, row, last), column(w_turned, row, 0)
            under, over = tracers[tracer, jnp.minimum(l + 1, levels - 1)], tracers[tracer, jnp.maximum(l - 1, 0)]
            held[tracer, l] = update(c, tracers[tracer, l], halo, under, over, forcing(tracer, l))
        return 0

    lax.fori_loop(0, levels, first_step, 0)

    def second_step(l, _):
        c = [weights[i, l] for i in range(5)]
        for tracer in range(2):
            row = tracer * levels + l
            halo = line_n[pl.ds(row, 1), :], line_s[pl.ds(row, 1), :], column(e_later, row, last), column(w_later, row, 0)
            under, over = held[tracer, jnp.minimum(l + 1, levels - 1)], held[tracer, jnp.maximum(l - 1, 0)]
            out[tracer, l] = update(c, held[tracer, l], halo, under, over, forcing(tracer, l))
        return 0

    lax.fori_loop(0, levels, second_step, 0)


def backward_kernel(parts, slots, src, back, w, out, held, wide, picked, terms, sems):
    total, width = terms.shape
    blocks = out.shape[0]
    batch = total // parts

    def copy(c):
        return pltpu.make_async_copy(w.at[pl.ds(c * batch, batch)], held.at[pl.ds(c * batch, batch)], sems.at[c])

    for c in range(parts):
        copy(c).start()
    wide[...] = back[...].astype(F32).reshape(wide.shape)

    def pick(i, _):
        for j in range(16):
            picked[pl.ds(i * 16 + j, 1), :] = wide[pl.ds(slots[i * 16 + j], 1), :]
        return 0

    lax.fori_loop(0, total // 16, pick, 0, unroll=2)
    row = iota((16, width), 0)

    def work(c, _):
        copy(c).wait()
        for g in range(batch // 16):
            at = pl.multiple_of(c * batch + g * 16, 16)
            rows = picked[pl.ds(at, 16), :]
            left = [jnp.where((row == r) | (row == 8 + r), rows, 0.0).astype(BF16) for r in range(8)]
            block = held[pl.ds(at, 16)].reshape(2, 8 * width, width)
            both = dot(jnp.concatenate(left, axis=1), jnp.concatenate([block[0], block[1]], axis=1), NN)
            terms[pl.ds(at, 8), :] = both[:8, :width]
            terms[pl.ds(at + 8, 8), :] = both[8:, width:]
        return 0

    lax.fori_loop(0, parts, work, 0)
    hot = (iota((blocks, total), 0) == src[...]).astype(F32).astype(BF16)
    value = terms[...]
    high = value.astype(BF16)
    low = (value - high.astype(F32)).astype(BF16)
    both = dot(hot, jnp.concatenate([high, low], axis=1), NN)
    out[...] = both[:, :width] + both[:, width:]


def backward(back, w, src, slots, blocks, parts=20):
    total, width, _ = w.shape
    devices, cap, _ = back.shape
    return pl.pallas_call(
        functools.partial(backward_kernel, parts),
        in_specs=[SMEM, VMEM, VMEM, ANY],
        out_specs=VMEM,
        scratch_shapes=[
            pltpu.VMEM(w.shape, BF16),
            pltpu.VMEM((devices * cap, width), F32),
            pltpu.VMEM((total, width), F32),
            pltpu.VMEM((total, width), F32),
            pltpu.SemaphoreType.DMA((parts,)),
        ],
        out_shape=jax.ShapeDtypeStruct((blocks, width), F32),
        compiler_params=kernel_params(58),
        cost_estimate=pl.CostEstimate(flops=2 * total * 8 * width * width, bytes_accessed=total * width * width * 2, transcendentals=0),
        name="backward_remap",
    )(slots, src.reshape(1, total), back, w)


def kernel(body, outs, name, mebibytes, bytes_accessed, scratch=()):
    return pl.pallas_call(
        body,
        out_shape=[jax.ShapeDtypeStruct(shape, dtype) for shape, dtype in outs],
        scratch_shapes=list(scratch),
        compiler_params=kernel_params(mebibytes),
        cost_estimate=pl.CostEstimate(flops=bytes_accessed, bytes_accessed=bytes_accessed, transcendentals=0),
        name=name,
    )


def neighbours(axis):
    count = lax.axis_size(axis)
    forward_pairs = [(i, i + 1) for i in range(count - 1)]
    return forward_pairs, [(b, a) for a, b in forward_pairs]


def swapped(array, axes, count, step):
    return lax.ppermute(array, axes, [(i, i ^ step) for i in range(count)])


def on_device(atm_flux, remap_weights, remap_src, remap_dst, remap_owner, tracers, currents, land_sea):
    grid = n_sec, n_gx, n_gy = [lax.axis_size(axis) for axis in EVERY]
    planes = n_sec * n_gy
    total, width, _ = remap_weights.shape
    _, levels, height, _ = tracers.shape
    cap = up(2 * total // (planes * n_gx), 8)
    wide = SENT * width

    *sends, slots = forward(atm_flux, remap_weights, remap_src, remap_owner.reshape(total), remap_dst, grid, cap)
    chunk = sends[0].shape[1]
    far_sends, near_sends = sends[:planes], sends[planes:]

    def in_plane(chunks):
        return [chunks[0]] + [swapped(chunks[m], ("sec", "gy"), planes, m) for m in range(1, planes)]

    def merge(chunks, dtypes):
        outs = [((height + 8, wide), dtype) for dtype in dtypes]
        return kernel(functools.partial(merge_kernel, planes), outs, "merge", 24, 1 << 22)(*chunks)

    side = (width, width)
    end = (7 * levels + 80, width)
    own_w, own_e = kernel(columns_kernel, [(side, F32)] * 2, "edge_columns", 16, 1 << 22)(tracers, currents, land_sea)
    to_north, to_south = neighbours(NORTH)
    to_east, to_west = neighbours("gy")
    from_e = lax.ppermute(own_w, "gy", to_west)
    from_w = lax.ppermute(own_e, "gy", to_east)

    far = merge(in_plane(far_sends), [BF16] * (n_gx // 2))
    far, near_sends, from_e, from_w = lax.optimization_barrier((far, near_sends, from_e, from_w))
    far = [swapped(part, "gx", n_gx, n_gx // 2 + m) for m, part in enumerate(far)]
    own_s, own_n = kernel(rows_kernel, [(end, F32)] * 2, "edge_rows", 16, 1 << 20)(
        tracers.reshape(-1, width), currents.reshape(-1, width), land_sea, from_w, from_e
    )
    from_n = lax.ppermute(own_s, NORTH, to_south)
    from_s = lax.ppermute(own_n, NORTH, to_north)
    near, from_n, from_s = lax.optimization_barrier((in_plane(near_sends), from_n, from_s))
    near = merge(near, [F32] + [BF16] * (n_gx // 2 - 1))
    parts = [near[0]] + [swapped(near[m], "gx", n_gx, m) for m in range(1, n_gx // 2)] + far

    back, flux, rim, *edges = kernel(
        functools.partial(surface_kernel, grid, chunk, levels),
        [((planes * n_gx, cap, width), BF16), ((5, height, width), F32), ((8, wide), F32)] + ([(end, F32)] * 2 + [(side, F32)] * 2) * 2,
        "surface",
        58,
        1 << 22,
    )(*parts, tracers[0:1, 0:3], currents[:, 0:2], land_sea, own_n, own_s, own_e, own_w, from_n, from_s, from_e, from_w)
    returned = lax.all_to_all(back, EVERY, split_axis=0, concat_axis=0, tiled=True)

    plane = (height, width)
    (tracers_out,) = kernel(
        stencil_kernel,
        [(tracers.shape, F32)],
        "substeps",
        58,
        1 << 24,
        [
            pltpu.VMEM(tracers.shape, F32),
            pltpu.VMEM((5, levels) + plane, F32),
            pltpu.VMEM((2 * levels, width), F32),
            pltpu.VMEM((2 * levels, width), F32),
            pltpu.VMEM((levels, width), F32),
            pltpu.VMEM((3,) + plane, F32),
            pltpu.VMEM((4,) + plane, F32),
        ],
    )(tracers, currents, land_sea, flux, rim, *edges)
    return tracers_out, backward(returned, remap_weights, remap_src, slots, atm_flux.shape[0])


def solution(mesh):
    return jax.shard_map(
        on_device,
        mesh=mesh,
        in_specs=(
            P(EVERY, None, None),
            P(EVERY, None, None),
            P(EVERY),
            P(EVERY),
            P(EVERY, None),
            P(None, None, NORTH, "gy"),
            P(None, None, NORTH, "gy"),
            P(NORTH, "gy"),
        ),
        out_specs=(P(None, None, NORTH, "gy"), P(EVERY, None)),
        check_vma=False,
    )
```

```python
import functools

import jax
import jax.numpy as jnp
from jax import lax
from jax.experimental import pallas as pl
from jax.experimental.pallas import tpu as pltpu
from jax.sharding import PartitionSpec as P

F32 = jnp.float32
BF16 = jnp.bfloat16
NT = (((1,), (1,)), ((), ()))
NN = (((1,), (0,)), ((), ()))
TN = (((0,), (0,)), ((), ()))
EVERY = ("sec", "gx", "gy")
NORTH = ("sec", "gx")
SENT = 5
KH = 0.1
KV = 0.1


def dot(left, right, dims):
    return lax.dot_general(left, right, dims, preferred_element_type=F32)


def iota(shape, dim):
    return lax.broadcasted_iota(jnp.int32, shape, dim)


def up(number, step):
    return -(-number // step) * step


def kernel_params(mebibytes):
    return pltpu.CompilerParams(vmem_limit_bytes=mebibytes << 20)


VMEM = pl.BlockSpec(memory_space=pltpu.VMEM)
SMEM = pl.BlockSpec(memory_space=pltpu.SMEM)
ANY = pl.BlockSpec(memory_space=pl.ANY)


def forward_kernel(parts, cap, grid, src, own, dst, flux, w, *refs):
    sends, (slots, held, mixed, acc, rows, xs, counts, renumbered, sems) = refs[:-9], refs[-9:]
    n_sec, n_gx, n_gy = grid
    devices, chunk, wide = xs.shape
    total, width, _ = held.shape
    batch = total // parts
    fields = flux.shape[1]
    first = chunk - 8
    last = width - 1

    def copy(c):
        return pltpu.make_async_copy(w.at[pl.ds(c * batch, batch)], held.at[pl.ds(c * batch, batch)], sems.at[c])

    for c in range(parts):
        copy(c).start()

    plane = lax.axis_index("sec") * n_gy + lax.axis_index("gy")
    line = lax.axis_index("gx")

    def renumber(owner):
        x = lax.div(owner, n_gy)
        there = lax.div(x, n_gx) * n_gy + lax.rem(owner, n_gy)
        return (there ^ plane) * n_gx + (lax.rem(x, n_gx) ^ line)

    def clear(o, _):
        counts[o] = 0
        renumbered[o] = renumber(o)
        return 0

    lax.fori_loop(0, devices, clear, 0)
    rows[...] = jnp.full_like(rows, 255.0)
    acc[...] = jnp.zeros_like(acc)
    xs[...] = jnp.zeros_like(xs)
    full = flux[...].astype(F32)
    one = [full[:, f : f + 1] for f in range(fields)]
    heat = 0.2 * (one[1] + one[2] + one[3]) - 0.15 * one[5]
    salt = 0.2 * one[4] - 0.1 * one[5]
    heat_high = heat.astype(BF16).astype(F32)
    salt_high = salt.astype(BF16).astype(F32)
    mixed[...] = jnp.concatenate(
        [one[0], heat_high, salt_high, one[6], one[7], heat - heat_high, salt - salt_high, jnp.zeros_like(heat)], axis=1
    ).astype(BF16)

    low_rows = iota((fields, width), 0)
    low_rows = (low_rows == 1) | (low_rows == 2)

    def work(c, _):
        copy(c).wait()
        for b in range(0, batch, 2):
            k = c * batch + b
            left = jnp.concatenate([mixed[src[k]], mixed[src[k + 1]]], axis=0)
            both = dot(left, held[pl.ds(k, 2)].reshape(2 * width, width), NT)
            for z, part in enumerate((both[:fields, :width], both[fields:, width:])):
                part = part + jnp.where(low_rows, pltpu.roll(part, fields - 4, 0), 0.0)
                owner = own[k + z]
                at = counts[owner]
                counts[owner] = at + 1
                at = jnp.minimum(at, cap - 1)
                slots[k + z] = owner * cap + at
                slot = renumbered[owner] * cap + at
                acc[pl.ds(pl.multiple_of(slot * fields, fields), fields), :] = part
                rows[pl.ds(slot, 1), :] = jnp.full((1, width), dst[k + z].astype(F32), F32)
        return 0

    lax.fori_loop(0, parts, work, 0)

    lane = iota((cap, width), 1).astype(F32)
    sub = iota((cap, width), 0).astype(F32)
    row = iota((24, wide), 0)
    picks = {
        4: (0, 0), 5: (1, 0), 6: (3, 0), 7: (4, 0), 12: (0, last), 13: (1, last), 14: (3, last), 15: (4, last),
        20: (2, 0), 21: (3, 1), 22: (2, last), 23: (3, last - 1),
    }
    pick = jnp.full((24, wide), -1, jnp.int32)
    for at, (field, column) in picks.items():
        pick = jnp.where(row == at, field * width + column, pick)
    select = (iota((24, wide), 1) == pick).astype(F32).astype(BF16)
    row = iota((8, cap), 0)
    wanted = jnp.zeros((8, cap), F32)
    for at, x in enumerate((0, 1, last, last - 1, 0, 0, last, last)):
        wanted = jnp.where(row == at, float(x), wanted)
    group = 8

    def owners(g, _):
        ds = [g * group + j for j in range(group)]
        five = []
        for d in ds:
            x = [acc[pl.ds(d * cap * fields + f, cap, stride=fields), :] for f in range(SENT)]
            x = jnp.concatenate(x, axis=1)
            xs[d, 0:cap, :] = x
            five.append(x.astype(BF16))
        where = [rows[pl.ds(pl.multiple_of(d * cap, 8), cap), :] for d in ds]
        hot = [(lane == r).astype(F32).astype(BF16) for r in where]
        flat = [jnp.sum(jnp.where(lane == sub, r, 0.0), axis=0, keepdims=True) for r in where]
        flat = [jnp.where(lane[:1] < cap, f, 255.0) for f in flat]
        edge = [dot(select, x, NT).astype(BF16) for x in five]
        sides = [dot(e, h, NN) for e, h in zip(edge, hot)]
        ends = [dot((f[:, :cap] == wanted).astype(F32).astype(BF16), x, NN) for f, x in zip(flat, five)]
        for d, f, side, end in zip(ds, flat, sides, ends):
            here = lax.div(d, n_gx) ^ plane
            here = (lax.div(here, n_gy) * n_gx + (lax.rem(d, n_gx) ^ line)) * n_gy + lax.rem(here, n_gy)

            def at(offset):
                return renumbered[lax.rem(here + offset + 2 * devices, devices)]

            south_of, north_of, west_of, east_of = at(-n_gy), at(n_gy), at(-1), at(1)

            xs[south_of, first : first + 1, :] = end[0:1]
            xs[south_of, first + 1 : first + 2, 4 * width :] = end[1:2, 4 * width :]
            xs[north_of, first + 2 : first + 3, :] = end[2:3]
            xs[north_of, first + 3 : first + 4, 4 * width :] = end[3:4, 4 * width :]
            xs[at(-n_gy - 1), first + 4 : first + 5, 3 * width :] = end[4:5, 3 * width :]
            xs[at(-n_gy + 1), first + 5 : first + 6, 3 * width :] = end[5:6, 3 * width :]
            xs[at(n_gy - 1), first + 6 : first + 7, 3 * width :] = end[6:7, 3 * width :]
            xs[at(n_gy + 1), first + 7 : first + 8, 3 * width :] = end[7:8, 3 * width :]
            xs[west_of, first + 4 : first + 8, 0:width] = side[4:8]
            xs[east_of, first + 4 : first + 8, width : 2 * width] = side[12:16]
            xs[west_of, first + 4 : first + 6, 2 * width : 3 * width] = side[20:22]
            xs[east_of, first + 6 : first + 8, 2 * width : 3 * width] = side[22:24]
            xs[d, first + 1 : first + 2, 0:width] = f
        return 0

    lax.fori_loop(0, devices // group, owners, 0)

    for m, send in enumerate(sends):
        send[...] = xs[m * n_gx : (m + 1) * n_gx].astype(BF16)


def forward(flux, w, src, own, dst, grid, cap, parts=20):
    n_sec, n_gx, n_gy = grid
    devices = n_sec * n_gx * n_gy
    total, width, _ = w.shape
    chunk = up(cap + 8, 16)
    fields = flux.shape[1]
    wide = SENT * width
    return pl.pallas_call(
        functools.partial(forward_kernel, parts, cap, grid),
        in_specs=[SMEM, SMEM, SMEM, VMEM, ANY],
        out_specs=[VMEM] * (n_sec * n_gy) + [SMEM],
        scratch_shapes=[
            pltpu.VMEM(w.shape, BF16),
            pltpu.VMEM(flux.shape, BF16),
            pltpu.VMEM((devices * cap * fields, width), F32),
            pltpu.VMEM((devices * cap, width), F32),
            pltpu.VMEM((devices, chunk, wide), F32),
            pltpu.SMEM((devices,), jnp.int32),
            pltpu.SMEM((devices,), jnp.int32),
            pltpu.SemaphoreType.DMA((parts,)),
        ],
        out_shape=[jax.ShapeDtypeStruct((n_gx, chunk, wide), BF16)] * (n_sec * n_gy) + [jax.ShapeDtypeStruct((total,), jnp.int32)],
        compiler_params=kernel_params(58),
        cost_estimate=pl.CostEstimate(flops=2 * total * 8 * width * width, bytes_accessed=total * width * width * 2, transcendentals=0),
        name="forward_remap",
    )(src, own, dst, flux, w)


def merge_kernel(n_sources, *refs):
    sources, outs = refs[:n_sources], refs[n_sources:]
    chunk = sources[0].shape[1]
    height = outs[0].shape[0] - 8
    first = chunk - 8
    count = n_sources * chunk
    for z, out in enumerate(outs):
        ext = None
        where = []
        for source in sources:
            piece = source[z, first:chunk, :].astype(F32)
            where.append(piece[1:2, :chunk])
            ext = piece if ext is None else ext + piece
        where = jnp.concatenate(where, axis=1)
        hot = (iota((height, count), 0).astype(F32) == where).astype(F32).astype(BF16)
        sums = dot(hot, jnp.concatenate([source[z] for source in sources], axis=0), NN)
        row3 = jnp.concatenate([where, ext[3:4, count:]], axis=1)
        ext = jnp.where(iota((8, 1), 0) == 3, row3, ext)
        out[...] = jnp.concatenate([sums, ext], axis=0).astype(out.dtype)


def columns_kernel(tracers, currents, land, west, east):
    levels = tracers.shape[1]
    width = tracers.shape[3]
    last = width - 1
    west[...] = jnp.zeros_like(west)
    east[...] = jnp.zeros_like(east)

    def put(plane, near, far):
        turned = plane.T
        for out, edge, second in ((west, 0, 1), (east, last, last - 1)):
            out[pl.ds(near, 1), :] = turned[edge : edge + 1]
            if far is not None:
                out[pl.ds(far, 1), :] = turned[second : second + 1]

    def level(l, _):
        for t in range(2):
            put(tracers[t, l], t * levels + l, (2 + t) * levels + l)
        put(currents[0, l], 4 * levels + l, 6 * levels + l)
        put(currents[1, l], 5 * levels + l, None)
        return 0

    lax.fori_loop(0, levels, level, 0, unroll=2)
    put(land[...].astype(F32), 7 * levels, 7 * levels + 1)


def rows_kernel(tracers, currents, land, from_west, from_east, south, north):
    levels = tracers.shape[0] // 2 // land.shape[0]
    height, width = land.shape
    lane = iota((1, width), 1)
    for out, edge, second in ((south, 0, 1), (north, height - 1, height - 2)):
        out[0 : 2 * levels] = tracers[pl.ds(edge, 2 * levels, stride=height), :]
        out[2 * levels : 4 * levels] = tracers[pl.ds(second, 2 * levels, stride=height), :]
        out[4 * levels : 6 * levels] = currents[pl.ds(edge, 2 * levels, stride=height), :]
        out[6 * levels : 7 * levels] = currents[pl.ds(levels * height + second, levels, stride=height), :]
        wet = [land[x : x + 1, :].astype(F32) for x in (edge, second)]
        out[7 * levels : 7 * levels + 8] = jnp.concatenate(wet + [jnp.zeros((6, width), F32)], axis=0)
    base = 7 * levels + 8
    for start, stop, at in ((0, 2 * levels, 0), (4 * levels, 6 * levels, 2 * levels), (7 * levels, 7 * levels + 8, 4 * levels)):
        w, e = from_west[start:stop], from_east[start:stop]
        there = slice(base + at, base + at + stop - start)
        south[there] = jnp.where(lane == 0, w, pltpu.roll(e, width - 1, 1))
        north[there] = jnp.where(lane == width - 1, e, pltpu.roll(w, 1, 1))


def plus_side(q, other, speed, speed_other, passable):
    return KH * passable * (other - q) - 0.25 * (speed + speed_other) * passable * (q + other)


def minus_side(q, other, speed, speed_other, passable):
    return KH * passable * (other - q) + 0.25 * (speed_other + speed) * passable * (other + q)


def level_profile(levels, width):
    depth = iota((levels, width), 0).astype(F32)
    return jnp.exp(-depth / 4.0) * (1.0 - jnp.exp(jnp.full((levels, width), -0.25, F32)))


def strip_step(q, q_plus, q_minus, across, across_plus, across_minus, along, corner_q, corner_along, wet, wet_plus, wet_minus, corner_wet, forcing):
    levels, width = q.shape
    lane = iota((1, width), 1)
    row = iota((levels, 1), 0)

    def ahead(x, corner):
        return jnp.where(lane == width - 1, corner, pltpu.roll(x, width - 1, 1))

    def behind(x, corner):
        return jnp.where(lane == 0, corner, pltpu.roll(x, 1, 1))

    total = plus_side(q, q_plus, across, across_plus, wet * wet_plus)
    total += minus_side(q, q_minus, across, across_minus, wet * wet_minus)
    total += plus_side(q, ahead(q, corner_q), along, ahead(along, corner_along), wet * ahead(wet, corner_wet))
    total += minus_side(q, behind(q, corner_q), along, behind(along, corner_along), wet * behind(wet, corner_wet))
    below = jnp.where(row < levels - 1, pltpu.roll(q, levels - 1, 0) - q, 0.0)
    above = jnp.where(row > 0, q - pltpu.roll(q, 1, 0), 0.0)
    return q + total + wet * (KV * (below - above) + forcing)


def strips(tracer, levels, inner, outer, flux):
    width = outer[0].shape[1]
    lane = iota((1, width), 1)
    base = 7 * levels + 8
    north, south, east, west = outer

    def part(x, at, count=levels):
        return x[at : at + count]

    def corners(at, count):
        n, s = part(north, base + at, count), part(south, base + at, count)
        e = jnp.where(lane == width - 1, n, pltpu.roll(s, 1, 1))
        w = jnp.where(lane == width - 1, pltpu.roll(n, width - 1, 1), s)
        return n, s, e, w

    corner_q = corners(tracer * levels, levels)
    corner_u = corners(2 * levels, levels)
    corner_v = corners(3 * levels, levels)
    corner_wet = corners(4 * levels, 1)
    top = (iota((levels, 1), 0) == 0).astype(F32)
    profile = level_profile(levels, width)
    results = []
    for side in range(4):
        near, far = inner[side], outer[side]
        beside, out = part(near, tracer * levels), part(far, (2 + tracer) * levels)
        mid = part(far, tracer * levels)
        speed = 5 if side < 2 else 4
        along = part(far, (9 - speed) * levels)
        corner_along = (corner_u if side < 2 else corner_v)[side]
        across, across_in, across_out = part(far, speed * levels), part(near, speed * levels), part(far, 6 * levels)
        wet, wet_in, wet_out = part(far, 7 * levels, 1), part(near, 7 * levels, 1), part(far, 7 * levels + 1, 1)
        shortwave, heat, salt = flux[side]
        forcing = 0.3 * profile * shortwave + top * heat if tracer == 0 else top * salt
        if side % 2 == 0:
            pairs = (out, beside, across, across_out, across_in)
            wets = (wet, wet_out, wet_in)
        else:
            pairs = (beside, out, across, across_in, across_out)
            wets = (wet, wet_in, wet_out)
        results.append(strip_step(mid, *pairs, along, corner_q[side], corner_along, *wets, corner_wet[side], forcing))
    return results


def shifts(plane, north, south, east, west):
    height, width = plane.shape
    lane, row = iota(plane.shape, 1), iota(plane.shape, 0)
    return (
        jnp.where(lane == width - 1, east, pltpu.roll(plane, width - 1, 1)),
        jnp.where(lane == 0, west, pltpu.roll(plane, 1, 1)),
        jnp.where(row == height - 1, north, pltpu.roll(plane, height - 1, 0)),
        jnp.where(row == 0, south, pltpu.roll(plane, 1, 0)),
    )


def wet_products(wet, north, south, east, west):
    return [wet * other for other in shifts(wet, north, south, east, west)]


def coefficients(u, v, u_east, u_west, v_north, v_south, passable):
    east, west, north, south = passable
    height, width = u.shape
    lane, row = iota(u.shape, 1), iota(u.shape, 0)
    e = jnp.where(lane == width - 1, u_east, pltpu.roll(u, width - 1, 1))
    w = jnp.where(lane == 0, u_west, pltpu.roll(u, 1, 1))
    n = jnp.where(row == height - 1, v_north, pltpu.roll(v, height - 1, 0))
    s = jnp.where(row == 0, v_south, pltpu.roll(v, 1, 0))
    flow_e, flow_w = 0.25 * (u + e) * east, 0.25 * (w + u) * west
    flow_n, flow_s = 0.25 * (v + n) * north, 0.25 * (s + v) * south
    own = 1.0 + (flow_w - flow_e) + (flow_s - flow_n) - KH * (east + west + north + south)
    return own, KH * east - flow_e, KH * west + flow_w, KH * north - flow_n, KH * south + flow_s


def column(turned, index, lane):
    return pltpu.roll(turned, lax.rem(lane - index + 2 * turned.shape[1], turned.shape[1]), 1)


def corrected(edge, x_rows):
    row = iota((edge.shape[0], 1), 0)
    for at, x in x_rows:
        edge = edge + jnp.where(row == at, 0.1 * x, 0.0)
    return edge


def surface_kernel(grid, chunk, levels, *refs):
    n_sec, n_gx, n_gy = grid
    planes = n_sec * n_gy
    parts, refs = refs[:n_gx], refs[n_gx:]
    tracers, currents, land, own_n, own_s, own_e, own_w, from_n, from_s, from_e, from_w, *refs = refs
    back, flux, rim, in_n, in_s, in_e, in_w, out_n, out_s, out_e, out_w = refs
    height, width = land.shape
    last = width - 1
    lane = iota((1, width), 1)
    sums = parts[0][...]
    for part in parts[1:]:
        sums = sums + part[...].astype(F32)
    sums, ext = sums[:height], sums[height : height + 8]
    shortwave, heat, salt, stress_u, stress_v = [sums[:, f * width : (f + 1) * width] for f in range(SENT)]
    wet = land[...].astype(F32)
    u0 = currents[0, 0] + 0.1 * stress_u
    v0 = currents[1, 0] + 0.1 * stress_v
    flux[0], flux[1], flux[2], flux[3], flux[4] = shortwave, heat, salt, u0, v0
    rim[...] = ext

    def block(r, b):
        return ext[r : r + 1, b * width : (b + 1) * width]

    n_flux, s_flux = [[block(r, b) for b in range(SENT)] for r in (0, 2)]
    ne, nw, se, sw = [[block(r, b) for b in (3, 4)] for r in (4, 5, 6, 7)]
    level0_u, level0_v, second = 4 * levels, 5 * levels, 6 * levels
    base = 7 * levels + 8
    corner_n = jnp.where(lane == last, pltpu.roll(ne[0], last, 1), pltpu.roll(nw[0], 1, 1))
    corner_s = jnp.where(lane == last, pltpu.roll(se[0], last, 1), pltpu.roll(sw[0], 1, 1))
    corner_n_v = jnp.where(lane == last, pltpu.roll(ne[1], last, 1), pltpu.roll(nw[1], 1, 1))
    corner_s_v = jnp.where(lane == last, pltpu.roll(se[1], last, 1), pltpu.roll(sw[1], 1, 1))
    far_n = corrected(
        from_n[...],
        [(level0_u, n_flux[3]), (level0_v, n_flux[4]), (second, block(1, 4)), (base + 2 * levels, corner_n), (base + 3 * levels, corner_n_v)],
    )
    far_s = corrected(
        from_s[...],
        [(level0_u, s_flux[3]), (level0_v, s_flux[4]), (second, block(3, 4)), (base + 2 * levels, corner_s), (base + 3 * levels, corner_s_v)],
    )
    far_e = corrected(from_e[...], [(level0_u, block(6, 0)), (level0_v, block(7, 0)), (second, block(5, 2))])
    far_w = corrected(from_w[...], [(level0_u, block(6, 1)), (level0_v, block(7, 1)), (second, block(7, 2))])
    turned = stress_u.T
    near_n = corrected(own_n[...], [(level0_v, stress_v[height - 1 : height])])
    near_s = corrected(own_s[...], [(level0_v, stress_v[0:1])])
    near_e = corrected(own_e[...], [(level0_u, turned[last : last + 1])])
    near_w = corrected(own_w[...], [(level0_u, turned[0:1])])
    in_n[...], in_s[...], in_e[...], in_w[...] = near_n, near_s, near_e, near_w
    out_n[...], out_s[...], out_e[...], out_w[...] = far_n, far_s, far_e, far_w

    e_turned, w_turned = far_e.T, far_w.T
    east = lambda index: column(e_turned, index, last)
    west = lambda index: column(w_turned, index, 0)
    passable = wet_products(
        wet, far_n[7 * levels : 7 * levels + 1], far_s[7 * levels : 7 * levels + 1], east(7 * levels), west(7 * levels)
    )
    lines = strips(0, levels, (near_n, near_s, near_e, near_w), (far_n, far_s, far_e, far_w), rim_flux(ext, width))
    profile = level_profile(levels, width)
    mix = KV * wet
    warm = 0.3 * wet * shortwave

    def weights(l, u, v):
        v_n, v_s = [x[5 * levels + l : 5 * levels + l + 1] for x in (far_n, far_s)]
        return coefficients(u, v, east(4 * levels + l), west(4 * levels + l), v_n, v_s, passable)

    def horizontal(c, q, halo):
        e, w, n, s = shifts(q, *halo)
        return c[0] * q + c[1] * e + c[2] * w + c[3] * n + c[4] * s

    def start(l):
        return far_n[l : l + 1], far_s[l : l + 1], east(l), west(l)

    q0, q1, q2 = tracers[0, 0], tracers[0, 1], tracers[0, 2]
    c0 = weights(0, u0, v0)
    c1 = weights(1, currents[0, 1], currents[1, 1])
    t0 = horizontal(c0, q0, start(0)) + mix * (q1 - q0) + warm * profile[0:1] + wet * heat
    t1 = horizontal(c1, q1, start(1)) + mix * ((q2 - q1) - (q1 - q0)) + warm * profile[1:2]
    sides = jnp.concatenate([lines[2][0:8], lines[3][0:8], jnp.zeros((width - 16, width), F32)], axis=0).T
    halo = lines[0][0:1], lines[1][0:1], column(sides, 0, last), column(sides, 8, 0)
    t0 = horizontal(c0, t0, halo) + mix * (t1 - t0) + warm * profile[0:1] + wet * heat
    sst = t0.astype(BF16)
    plane = lax.axis_index("sec") * n_gy + lax.axis_index("gy")
    line = lax.axis_index("gx")
    for z, part in enumerate(parts):
        where = part[height + 3 : height + 4, : planes * chunk].astype(F32)
        hot = (iota((height, planes * chunk), 0).astype(F32) == where).astype(F32)
        picked = dot(hot.T.astype(BF16), sst, NN).reshape(planes, chunk, width)
        for m in range(planes):
            there = plane ^ m
            device = (lax.div(there, n_gy) * n_gx + (line ^ z)) * n_gy + lax.rem(there, n_gy)
            back[device] = picked[m, : back.shape[1]].astype(BF16)


def rim_flux(ext, width):
    def block(r, b):
        return ext[r : r + 1, b * width : (b + 1) * width]

    return (
        (block(0, 0), block(0, 1), block(0, 2)),
        (block(2, 0), block(2, 1), block(2, 2)),
        (block(4, 0), block(5, 0), block(4, 2)),
        (block(4, 1), block(5, 1), block(6, 2)),
    )


def stencil_kernel(
    tracers, currents, land, flux, rim, in_n, in_s, in_e, in_w, out_n, out_s, out_e, out_w,
    out, held, weights, line_n, line_s, depth, forced, passing,
):
    levels = tracers.shape[1]
    height, width = land.shape
    last = width - 1
    wet = land[...].astype(F32)
    far_n, far_s, far_e, far_w = out_n[...], out_s[...], out_e[...], out_w[...]
    e_turned, w_turned = far_e.T, far_w.T
    at = 7 * levels
    for i, x in enumerate(
        wet_products(wet, far_n[at : at + 1], far_s[at : at + 1], column(e_turned, at, last), column(w_turned, at, 0))
    ):
        passing[i] = x
    forced[0], forced[1], forced[2] = 0.3 * wet * flux[0], wet * flux[1], wet * flux[2]
    depth[...] = level_profile(levels, width)
    columns = []
    for tracer in range(2):
        lines = strips(
            tracer, levels, (in_n[...], in_s[...], in_e[...], in_w[...]), (far_n, far_s, far_e, far_w), rim_flux(rim[...], width)
        )
        line_n[tracer * levels : (tracer + 1) * levels] = lines[0]
        line_s[tracer * levels : (tracer + 1) * levels] = lines[1]
        columns.append(lines[2:])
    blank = jnp.zeros((width - 2 * levels, width), F32)
    e_later, w_later = [jnp.concatenate([columns[0][i], columns[1][i], blank], axis=0).T for i in range(2)]

    def update(c, q, halo, under, over, forcing):
        e, w, n, s = shifts(q, *halo)
        mixed = KV * land[...].astype(F32) * ((under - q) - (q - over))
        return c[0] * q + c[1] * e + c[2] * w + c[3] * n + c[4] * s + mixed + forcing

    def forcing(tracer, l):
        top = jnp.where(l == 0, 1.0, 0.0)
        if tracer == 0:
            return forced[0] * depth[pl.ds(l, 1), :] + top * forced[1]
        return top * forced[2]

    def first_step(l, _):
        surface = l == 0
        u = jnp.where(surface, flux[3], currents[0, l])
        v = jnp.where(surface, flux[4], currents[1, l])
        row = 5 * levels + l
        c = coefficients(
            u, v, column(e_turned, 4 * levels + l, last), column(w_turned, 4 * levels + l, 0),
            out_n[pl.ds(row, 1), :], out_s[pl.ds(row, 1), :], [passing[i] for i in range(4)],
        )
        for i, x in enumerate(c):
            weights[i, l] = x
        for tracer in range(2):
            row = tracer * levels + l
            halo = out_n[pl.ds(row, 1), :], out_s[pl.ds(row, 1), :], column(e_turned, row, last), column(w_turned, row, 0)
            under, over = tracers[tracer, jnp.minimum(l + 1, levels - 1)], tracers[tracer, jnp.maximum(l - 1, 0)]
            held[tracer, l] = update(c, tracers[tracer, l], halo, under, over, forcing(tracer, l))
        return 0

    lax.fori_loop(0, levels, first_step, 0)

    def second_step(l, _):
        c = [weights[i, l] for i in range(5)]
        for tracer in range(2):
            row = tracer * levels + l
            halo = line_n[pl.ds(row, 1), :], line_s[pl.ds(row, 1), :], column(e_later, row, last), column(w_later, row, 0)
            under, over = held[tracer, jnp.minimum(l + 1, levels - 1)], held[tracer, jnp.maximum(l - 1, 0)]
            out[tracer, l] = update(c, held[tracer, l], halo, under, over, forcing(tracer, l))
        return 0

    lax.fori_loop(0, levels, second_step, 0)


def backward_kernel(parts, slots, src, back, w, out, held, wide, picked, terms, sems):
    total, width = terms.shape
    blocks = out.shape[0]
    batch = total // parts

    def copy(c):
        return pltpu.make_async_copy(w.at[pl.ds(c * batch, batch)], held.at[pl.ds(c * batch, batch)], sems.at[c])

    for c in range(parts):
        copy(c).start()
    wide[...] = back[...].astype(F32).reshape(wide.shape)

    def pick(i, _):
        for j in range(16):
            picked[pl.ds(i * 16 + j, 1), :] = wide[pl.ds(slots[i * 16 + j], 1), :]
        return 0

    lax.fori_loop(0, total // 16, pick, 0, unroll=2)
    row = iota((16, width), 0)

    def work(c, _):
        copy(c).wait()
        for g in range(batch // 16):
            at = pl.multiple_of(c * batch + g * 16, 16)
            rows = picked[pl.ds(at, 16), :]
            left = [jnp.where((row == r) | (row == 8 + r), rows, 0.0).astype(BF16) for r in range(8)]
            block = held[pl.ds(at, 16)].reshape(2, 8 * width, width)
            both = dot(jnp.concatenate(left, axis=1), jnp.concatenate([block[0], block[1]], axis=1), NN)
            terms[pl.ds(at, 8), :] = both[:8, :width]
            terms[pl.ds(at + 8, 8), :] = both[8:, width:]
        return 0

    lax.fori_loop(0, parts, work, 0)
    hot = (iota((blocks, total), 0) == src[...]).astype(F32).astype(BF16)
    value = terms[...]
    high = value.astype(BF16)
    low = (value - high.astype(F32)).astype(BF16)
    both = dot(hot, jnp.concatenate([high, low], axis=1), NN)
    out[...] = both[:, :width] + both[:, width:]


def backward(back, w, src, slots, blocks, parts=20):
    total, width, _ = w.shape
    devices, cap, _ = back.shape
    return pl.pallas_call(
        functools.partial(backward_kernel, parts),
        in_specs=[SMEM, VMEM, VMEM, ANY],
        out_specs=VMEM,
        scratch_shapes=[
            pltpu.VMEM(w.shape, BF16),
            pltpu.VMEM((devices * cap, width), F32),
            pltpu.VMEM((total, width), F32),
            pltpu.VMEM((total, width), F32),
            pltpu.SemaphoreType.DMA((parts,)),
        ],
        out_shape=jax.ShapeDtypeStruct((blocks, width), F32),
        compiler_params=kernel_params(58),
        cost_estimate=pl.CostEstimate(flops=2 * total * 8 * width * width, bytes_accessed=total * width * width * 2, transcendentals=0),
        name="backward_remap",
    )(slots, src.reshape(1, total), back, w)


def kernel(body, outs, name, mebibytes, bytes_accessed, scratch=()):
    return pl.pallas_call(
        body,
        out_shape=[jax.ShapeDtypeStruct(shape, dtype) for shape, dtype in outs],
        scratch_shapes=list(scratch),
        compiler_params=kernel_params(mebibytes),
        cost_estimate=pl.CostEstimate(flops=bytes_accessed, bytes_accessed=bytes_accessed, transcendentals=0),
        name=name,
    )


def neighbours(axis):
    count = lax.axis_size(axis)
    forward_pairs = [(i, i + 1) for i in range(count - 1)]
    return forward_pairs, [(b, a) for a, b in forward_pairs]


def swapped(array, axes, count, step):
    return lax.ppermute(array, axes, [(i, i ^ step) for i in range(count)])


def on_device(atm_flux, remap_weights, remap_src, remap_dst, remap_owner, tracers, currents, land_sea):
    grid = n_sec, n_gx, n_gy = [lax.axis_size(axis) for axis in EVERY]
    planes = n_sec * n_gy
    total, width, _ = remap_weights.shape
    _, levels, height, _ = tracers.shape
    cap = up(2 * total // (planes * n_gx), 8)
    wide = SENT * width

    *sends, slots = forward(atm_flux, remap_weights, remap_src, remap_owner.reshape(total), remap_dst, grid, cap)
    chunk = sends[0].shape[1]
    got = [sends[0]] + [swapped(sends[m], ("sec", "gy"), planes, m) for m in range(1, planes)]

    side = (width, width)
    end = (7 * levels + 80, width)
    own_w, own_e = kernel(columns_kernel, [(side, F32)] * 2, "edge_columns", 16, 1 << 22)(tracers, currents, land_sea)
    to_north, to_south = neighbours(NORTH)
    to_east, to_west = neighbours("gy")
    from_e = lax.ppermute(own_w, "gy", to_west)
    from_w = lax.ppermute(own_e, "gy", to_east)

    own_s, own_n = kernel(rows_kernel, [(end, F32)] * 2, "edge_rows", 16, 1 << 20)(
        tracers.reshape(-1, width), currents.reshape(-1, width), land_sea, from_w, from_e
    )
    from_n = lax.ppermute(own_s, NORTH, to_south)
    from_s = lax.ppermute(own_n, NORTH, to_north)
    got, from_n, from_s = lax.optimization_barrier((got, from_n, from_s))
    part = (height + 8, wide)
    merged = kernel(functools.partial(merge_kernel, planes), [(part, F32)] + [(part, BF16)] * (n_gx - 1), "merge", 24, 1 << 22)(*got)
    parts = [merged[0]] + [swapped(merged[m], "gx", n_gx, m) for m in range(1, n_gx)]

    back, flux, rim, *edges = kernel(
        functools.partial(surface_kernel, grid, chunk, levels),
        [((planes * n_gx, cap, width), BF16), ((5, height, width), F32), ((8, wide), F32)] + ([(end, F32)] * 2 + [(side, F32)] * 2) * 2,
        "surface",
        58,
        1 << 22,
    )(*parts, tracers[0:1, 0:3], currents[:, 0:2], land_sea, own_n, own_s, own_e, own_w, from_n, from_s, from_e, from_w)
    returned = lax.all_to_all(back, EVERY, split_axis=0, concat_axis=0, tiled=True)

    plane = (height, width)
    (tracers_out,) = kernel(
        stencil_kernel,
        [(tracers.shape, F32)],
        "substeps",
        58,
        1 << 24,
        [
            pltpu.VMEM(tracers.shape, F32),
            pltpu.VMEM((5, levels) + plane, F32),
            pltpu.VMEM((2 * levels, width), F32),
            pltpu.VMEM((2 * levels, width), F32),
            pltpu.VMEM((levels, width), F32),
            pltpu.VMEM((3,) + plane, F32),
            pltpu.VMEM((4,) + plane, F32),
        ],
    )(tracers, currents, land_sea, flux, rim, *edges)
    return tracers_out, backward(returned, remap_weights, remap_src, slots, atm_flux.shape[0])


def solution(mesh):
    return jax.shard_map(
        on_device,
        mesh=mesh,
        in_specs=(
            P(EVERY, None, None),
            P(EVERY, None, None),
            P(EVERY),
            P(EVERY),
            P(EVERY, None),
            P(None, None, NORTH, "gy"),
            P(None, None, NORTH, "gy"),
            P(NORTH, "gy"),
        ),
        out_specs=(P(None, None, NORTH, "gy"), P(EVERY, None)),
        check_vma=False,
    )
```

```python
import functools

import jax
import jax.numpy as jnp
from jax import lax
from jax.experimental import pallas as pl
from jax.experimental.pallas import tpu as pltpu
from jax.sharding import PartitionSpec as P

F32 = jnp.float32
BF16 = jnp.bfloat16
NT = (((1,), (1,)), ((), ()))
NN = (((1,), (0,)), ((), ()))
TN = (((0,), (0,)), ((), ()))
EVERY = ("sec", "gx", "gy")
NORTH = ("sec", "gx")
SENT = 5
KH = 0.1
KV = 0.1


def dot(left, right, dims):
    return lax.dot_general(left, right, dims, preferred_element_type=F32)


def iota(shape, dim):
    return lax.broadcasted_iota(jnp.int32, shape, dim)


def up(number, step):
    return -(-number // step) * step


def kernel_params(mebibytes):
    return pltpu.CompilerParams(vmem_limit_bytes=mebibytes << 20)


VMEM = pl.BlockSpec(memory_space=pltpu.VMEM)
SMEM = pl.BlockSpec(memory_space=pltpu.SMEM)
ANY = pl.BlockSpec(memory_space=pl.ANY)


def forward_kernel(parts, cap, grid, src, own, dst, flux, w, *refs):
    sends, (slots, held, mixed, acc, rows, xs, counts, renumbered, sems) = refs[:-9], refs[-9:]
    n_sec, n_gx, n_gy = grid
    devices, chunk, wide = xs.shape
    total, width, _ = held.shape
    batch = total // parts
    fields = flux.shape[1]
    first = chunk - 8
    last = width - 1

    def copy(c):
        return pltpu.make_async_copy(w.at[pl.ds(c * batch, batch)], held.at[pl.ds(c * batch, batch)], sems.at[c])

    for c in range(parts):
        copy(c).start()

    plane = lax.axis_index("sec") * n_gy + lax.axis_index("gy")
    line = lax.axis_index("gx")

    def renumber(owner):
        x = lax.div(owner, n_gy)
        there = lax.div(x, n_gx) * n_gy + lax.rem(owner, n_gy)
        return (there ^ plane) * n_gx + (lax.rem(x, n_gx) ^ line)

    def clear(o, _):
        counts[o] = 0
        renumbered[o] = renumber(o)
        return 0

    lax.fori_loop(0, devices, clear, 0)
    rows[...] = jnp.full_like(rows, 255.0)
    acc[...] = jnp.zeros_like(acc)
    xs[...] = jnp.zeros_like(xs)
    full = flux[...].astype(F32)
    one = [full[:, f : f + 1] for f in range(fields)]
    heat = 0.2 * (one[1] + one[2] + one[3]) - 0.15 * one[5]
    salt = 0.2 * one[4] - 0.1 * one[5]
    heat_high = heat.astype(BF16).astype(F32)
    salt_high = salt.astype(BF16).astype(F32)
    mixed[...] = jnp.concatenate(
        [one[0], heat_high, salt_high, one[6], one[7], heat - heat_high, salt - salt_high, jnp.zeros_like(heat)], axis=1
    ).astype(BF16)

    low_rows = iota((fields, width), 0)
    low_rows = (low_rows == 1) | (low_rows == 2)

    def work(c, _):
        copy(c).wait()
        for b in range(0, batch, 2):
            k = c * batch + b
            left = jnp.concatenate([mixed[src[k]], mixed[src[k + 1]]], axis=0)
            both = dot(left, held[pl.ds(k, 2)].reshape(2 * width, width), NT)
            for z, part in enumerate((both[:fields, :width], both[fields:, width:])):
                part = part + jnp.where(low_rows, pltpu.roll(part, fields - 4, 0), 0.0)
                owner = own[k + z]
                at = counts[owner]
                counts[owner] = at + 1
                at = jnp.minimum(at, cap - 1)
                slots[k + z] = owner * cap + at
                slot = renumbered[owner] * cap + at
                acc[pl.ds(pl.multiple_of(slot * fields, fields), fields), :] = part
                rows[pl.ds(slot, 1), :] = jnp.full((1, width), dst[k + z].astype(F32), F32)
        return 0

    lax.fori_loop(0, parts, work, 0)

    lane = iota((cap, width), 1).astype(F32)
    sub = iota((cap, width), 0).astype(F32)
    row = iota((24, wide), 0)
    picks = {
        4: (0, 0), 5: (1, 0), 6: (3, 0), 7: (4, 0), 12: (0, last), 13: (1, last), 14: (3, last), 15: (4, last),
        20: (2, 0), 21: (3, 1), 22: (2, last), 23: (3, last - 1),
    }
    pick = jnp.full((24, wide), -1, jnp.int32)
    for at, (field, column) in picks.items():
        pick = jnp.where(row == at, field * width + column, pick)
    select = (iota((24, wide), 1) == pick).astype(F32).astype(BF16)
    row = iota((8, cap), 0)
    wanted = jnp.zeros((8, cap), F32)
    for at, x in enumerate((0, 1, last, last - 1, 0, 0, last, last)):
        wanted = jnp.where(row == at, float(x), wanted)
    group = 8

    def owners(g, _):
        ds = [g * group + j for j in range(group)]
        five = []
        for d in ds:
            x = [acc[pl.ds(d * cap * fields + f, cap, stride=fields), :] for f in range(SENT)]
            x = jnp.concatenate(x, axis=1)
            xs[d, 0:cap, :] = x
            five.append(x.astype(BF16))
        where = [rows[pl.ds(pl.multiple_of(d * cap, 8), cap), :] for d in ds]
        hot = [(lane == r).astype(F32).astype(BF16) for r in where]
        flat = [jnp.sum(jnp.where(lane == sub, r, 0.0), axis=0, keepdims=True) for r in where]
        flat = [jnp.where(lane[:1] < cap, f, 255.0) for f in flat]
        edge = [dot(select, x, NT).astype(BF16) for x in five]
        sides = [dot(e, h, NN) for e, h in zip(edge, hot)]
        ends = [dot((f[:, :cap] == wanted).astype(F32).astype(BF16), x, NN) for f, x in zip(flat, five)]
        for d, f, side, end in zip(ds, flat, sides, ends):
            here = lax.div(d, n_gx) ^ plane
            here = (lax.div(here, n_gy) * n_gx + (lax.rem(d, n_gx) ^ line)) * n_gy + lax.rem(here, n_gy)

            def at(offset):
                return renumbered[lax.rem(here + offset + 2 * devices, devices)]

            south_of, north_of, west_of, east_of = at(-n_gy), at(n_gy), at(-1), at(1)

            xs[south_of, first : first + 1, :] = end[0:1]
            xs[south_of, first + 1 : first + 2, 4 * width :] = end[1:2, 4 * width :]
            xs[north_of, first + 2 : first + 3, :] = end[2:3]
            xs[north_of, first + 3 : first + 4, 4 * width :] = end[3:4, 4 * width :]
            xs[at(-n_gy - 1), first + 4 : first + 5, 3 * width :] = end[4:5, 3 * width :]
            xs[at(-n_gy + 1), first + 5 : first + 6, 3 * width :] = end[5:6, 3 * width :]
            xs[at(n_gy - 1), first + 6 : first + 7, 3 * width :] = end[6:7, 3 * width :]
            xs[at(n_gy + 1), first + 7 : first + 8, 3 * width :] = end[7:8, 3 * width :]
            xs[west_of, first + 4 : first + 8, 0:width] = side[4:8]
            xs[east_of, first + 4 : first + 8, width : 2 * width] = side[12:16]
            xs[west_of, first + 4 : first + 6, 2 * width : 3 * width] = side[20:22]
            xs[east_of, first + 6 : first + 8, 2 * width : 3 * width] = side[22:24]
            xs[d, first + 1 : first + 2, 0:width] = f
        return 0

    lax.fori_loop(0, devices // group, owners, 0)

    for m, send in enumerate(sends):
        send[...] = xs[m * n_gx : (m + 1) * n_gx].astype(BF16)


def forward(flux, w, src, own, dst, grid, cap, parts=20):
    n_sec, n_gx, n_gy = grid
    devices = n_sec * n_gx * n_gy
    total, width, _ = w.shape
    chunk = up(cap + 8, 16)
    fields = flux.shape[1]
    wide = SENT * width
    return pl.pallas_call(
        functools.partial(forward_kernel, parts, cap, grid),
        in_specs=[SMEM, SMEM, SMEM, VMEM, ANY],
        out_specs=[VMEM] * (n_sec * n_gy) + [SMEM],
        scratch_shapes=[
            pltpu.VMEM(w.shape, BF16),
            pltpu.VMEM(flux.shape, BF16),
            pltpu.VMEM((devices * cap * fields, width), F32),
            pltpu.VMEM((devices * cap, width), F32),
            pltpu.VMEM((devices, chunk, wide), F32),
            pltpu.SMEM((devices,), jnp.int32),
            pltpu.SMEM((devices,), jnp.int32),
            pltpu.SemaphoreType.DMA((parts,)),
        ],
        out_shape=[jax.ShapeDtypeStruct((n_gx, chunk, wide), BF16)] * (n_sec * n_gy) + [jax.ShapeDtypeStruct((total,), jnp.int32)],
        compiler_params=kernel_params(58),
        cost_estimate=pl.CostEstimate(flops=2 * total * 8 * width * width, bytes_accessed=total * width * width * 2, transcendentals=0),
        name="forward_remap",
    )(src, own, dst, flux, w)


def merge_kernel(n_sources, *refs):
    sources, outs = refs[:n_sources], refs[n_sources:]
    chunk = sources[0].shape[1]
    height = outs[0].shape[0] - 8
    first = chunk - 8
    count = n_sources * chunk
    for z, out in enumerate(outs):
        ext = None
        where = []
        for source in sources:
            piece = source[z, first:chunk, :].astype(F32)
            where.append(piece[1:2, :chunk])
            ext = piece if ext is None else ext + piece
        where = jnp.concatenate(where, axis=1)
        hot = (iota((height, count), 0).astype(F32) == where).astype(F32).astype(BF16)
        sums = dot(hot, jnp.concatenate([source[z] for source in sources], axis=0), NN)
        row3 = jnp.concatenate([where, ext[3:4, count:]], axis=1)
        ext = jnp.where(iota((8, 1), 0) == 3, row3, ext)
        out[...] = jnp.concatenate([sums, ext], axis=0).astype(out.dtype)


def columns_kernel(tracers, currents, land, west, east):
    levels = tracers.shape[1]
    width = tracers.shape[3]
    last = width - 1
    west[...] = jnp.zeros_like(west)
    east[...] = jnp.zeros_like(east)

    def put(plane, near, far):
        turned = plane.T
        for out, edge, second in ((west, 0, 1), (east, last, last - 1)):
            out[pl.ds(near, 1), :] = turned[edge : edge + 1]
            if far is not None:
                out[pl.ds(far, 1), :] = turned[second : second + 1]

    def level(l, _):
        for t in range(2):
            put(tracers[t, l], t * levels + l, (2 + t) * levels + l)
        put(currents[0, l], 4 * levels + l, 6 * levels + l)
        put(currents[1, l], 5 * levels + l, None)
        return 0

    lax.fori_loop(0, levels, level, 0, unroll=2)
    put(land[...].astype(F32), 7 * levels, 7 * levels + 1)


def rows_kernel(tracers, currents, land, from_west, from_east, south, north):
    levels = tracers.shape[0] // 2 // land.shape[0]
    height, width = land.shape
    lane = iota((1, width), 1)
    for out, edge, second in ((south, 0, 1), (north, height - 1, height - 2)):
        out[0 : 2 * levels] = tracers[pl.ds(edge, 2 * levels, stride=height), :]
        out[2 * levels : 4 * levels] = tracers[pl.ds(second, 2 * levels, stride=height), :]
        out[4 * levels : 6 * levels] = currents[pl.ds(edge, 2 * levels, stride=height), :]
        out[6 * levels : 7 * levels] = currents[pl.ds(levels * height + second, levels, stride=height), :]
        wet = [land[x : x + 1, :].astype(F32) for x in (edge, second)]
        out[7 * levels : 7 * levels + 8] = jnp.concatenate(wet + [jnp.zeros((6, width), F32)], axis=0)
    base = 7 * levels + 8
    for start, stop, at in ((0, 2 * levels, 0), (4 * levels, 6 * levels, 2 * levels), (7 * levels, 7 * levels + 8, 4 * levels)):
        w, e = from_west[start:stop], from_east[start:stop]
        there = slice(base + at, base + at + stop - start)
        south[there] = jnp.where(lane == 0, w, pltpu.roll(e, width - 1, 1))
        north[there] = jnp.where(lane == width - 1, e, pltpu.roll(w, 1, 1))


def plus_side(q, other, speed, speed_other, passable):
    return KH * passable * (other - q) - 0.25 * (speed + speed_other) * passable * (q + other)


def minus_side(q, other, speed, speed_other, passable):
    return KH * passable * (other - q) + 0.25 * (speed_other + speed) * passable * (other + q)


def level_profile(levels, width):
    depth = iota((levels, width), 0).astype(F32)
    return jnp.exp(-depth / 4.0) * (1.0 - jnp.exp(jnp.full((levels, width), -0.25, F32)))


def strip_step(q, q_plus, q_minus, across, across_plus, across_minus, along, corner_q, corner_along, wet, wet_plus, wet_minus, corner_wet, forcing):
    levels, width = q.shape
    lane = iota((1, width), 1)
    row = iota((levels, 1), 0)

    def ahead(x, corner):
        return jnp.where(lane == width - 1, corner, pltpu.roll(x, width - 1, 1))

    def behind(x, corner):
        return jnp.where(lane == 0, corner, pltpu.roll(x, 1, 1))

    total = plus_side(q, q_plus, across, across_plus, wet * wet_plus)
    total += minus_side(q, q_minus, across, across_minus, wet * wet_minus)
    total += plus_side(q, ahead(q, corner_q), along, ahead(along, corner_along), wet * ahead(wet, corner_wet))
    total += minus_side(q, behind(q, corner_q), along, behind(along, corner_along), wet * behind(wet, corner_wet))
    below = jnp.where(row < levels - 1, pltpu.roll(q, levels - 1, 0) - q, 0.0)
    above = jnp.where(row > 0, q - pltpu.roll(q, 1, 0), 0.0)
    return q + total + wet * (KV * (below - above) + forcing)


def strips(tracer, levels, inner, outer, flux):
    width = outer[0].shape[1]
    lane = iota((1, width), 1)
    base = 7 * levels + 8
    north, south, east, west = outer

    def part(x, at, count=levels):
        return x[at : at + count]

    def corners(at, count):
        n, s = part(north, base + at, count), part(south, base + at, count)
        e = jnp.where(lane == width - 1, n, pltpu.roll(s, 1, 1))
        w = jnp.where(lane == width - 1, pltpu.roll(n, width - 1, 1), s)
        return n, s, e, w

    corner_q = corners(tracer * levels, levels)
    corner_u = corners(2 * levels, levels)
    corner_v = corners(3 * levels, levels)
    corner_wet = corners(4 * levels, 1)
    top = (iota((levels, 1), 0) == 0).astype(F32)
    profile = level_profile(levels, width)
    results = []
    for side in range(4):
        near, far = inner[side], outer[side]
        beside, out = part(near, tracer * levels), part(far, (2 + tracer) * levels)
        mid = part(far, tracer * levels)
        speed = 5 if side < 2 else 4
        along = part(far, (9 - speed) * levels)
        corner_along = (corner_u if side < 2 else corner_v)[side]
        across, across_in, across_out = part(far, speed * levels), part(near, speed * levels), part(far, 6 * levels)
        wet, wet_in, wet_out = part(far, 7 * levels, 1), part(near, 7 * levels, 1), part(far, 7 * levels + 1, 1)
        shortwave, heat, salt = flux[side]
        forcing = 0.3 * profile * shortwave + top * heat if tracer == 0 else top * salt
        if side % 2 == 0:
            pairs = (out, beside, across, across_out, across_in)
            wets = (wet, wet_out, wet_in)
        else:
            pairs = (beside, out, across, across_in, across_out)
            wets = (wet, wet_in, wet_out)
        results.append(strip_step(mid, *pairs, along, corner_q[side], corner_along, *wets, corner_wet[side], forcing))
    return results


def shifts(plane, north, south, east, west):
    height, width = plane.shape
    lane, row = iota(plane.shape, 1), iota(plane.shape, 0)
    return (
        jnp.where(lane == width - 1, east, pltpu.roll(plane, width - 1, 1)),
        jnp.where(lane == 0, west, pltpu.roll(plane, 1, 1)),
        jnp.where(row == height - 1, north, pltpu.roll(plane, height - 1, 0)),
        jnp.where(row == 0, south, pltpu.roll(plane, 1, 0)),
    )


def wet_products(wet, north, south, east, west):
    return [wet * other for other in shifts(wet, north, south, east, west)]


def coefficients(u, v, u_east, u_west, v_north, v_south, passable):
    east, west, north, south = passable
    height, width = u.shape
    lane, row = iota(u.shape, 1), iota(u.shape, 0)
    e = jnp.where(lane == width - 1, u_east, pltpu.roll(u, width - 1, 1))
    w = jnp.where(lane == 0, u_west, pltpu.roll(u, 1, 1))
    n = jnp.where(row == height - 1, v_north, pltpu.roll(v, height - 1, 0))
    s = jnp.where(row == 0, v_south, pltpu.roll(v, 1, 0))
    flow_e, flow_w = 0.25 * (u + e) * east, 0.25 * (w + u) * west
    flow_n, flow_s = 0.25 * (v + n) * north, 0.25 * (s + v) * south
    own = 1.0 + (flow_w - flow_e) + (flow_s - flow_n) - KH * (east + west + north + south)
    return own, KH * east - flow_e, KH * west + flow_w, KH * north - flow_n, KH * south + flow_s


def column(turned, index, lane):
    return pltpu.roll(turned, lax.rem(lane - index + 2 * turned.shape[1], turned.shape[1]), 1)


def corrected(edge, x_rows):
    row = iota((edge.shape[0], 1), 0)
    for at, x in x_rows:
        edge = edge + jnp.where(row == at, 0.1 * x, 0.0)
    return edge


def surface_kernel(grid, chunk, levels, *refs):
    n_sec, n_gx, n_gy = grid
    planes = n_sec * n_gy
    parts, refs = refs[:n_gx], refs[n_gx:]
    tracers, currents, land, own_n, own_s, own_e, own_w, from_n, from_s, from_e, from_w, *refs = refs
    back, flux, rim, in_n, in_s, in_e, in_w, out_n, out_s, out_e, out_w = refs
    height, width = land.shape
    last = width - 1
    lane = iota((1, width), 1)
    sums = parts[0][...]
    for part in parts[1:]:
        sums = sums + part[...].astype(F32)
    sums, ext = sums[:height], sums[height : height + 8]
    shortwave, heat, salt, stress_u, stress_v = [sums[:, f * width : (f + 1) * width] for f in range(SENT)]
    wet = land[...].astype(F32)
    u0 = currents[0, 0] + 0.1 * stress_u
    v0 = currents[1, 0] + 0.1 * stress_v
    flux[0], flux[1], flux[2], flux[3], flux[4] = shortwave, heat, salt, u0, v0
    rim[...] = ext

    def block(r, b):
        return ext[r : r + 1, b * width : (b + 1) * width]

    n_flux, s_flux = [[block(r, b) for b in range(SENT)] for r in (0, 2)]
    ne, nw, se, sw = [[block(r, b) for b in (3, 4)] for r in (4, 5, 6, 7)]
    level0_u, level0_v, second = 4 * levels, 5 * levels, 6 * levels
    base = 7 * levels + 8
    corner_n = jnp.where(lane == last, pltpu.roll(ne[0], last, 1), pltpu.roll(nw[0], 1, 1))
    corner_s = jnp.where(lane == last, pltpu.roll(se[0], last, 1), pltpu.roll(sw[0], 1, 1))
    corner_n_v = jnp.where(lane == last, pltpu.roll(ne[1], last, 1), pltpu.roll(nw[1], 1, 1))
    corner_s_v = jnp.where(lane == last, pltpu.roll(se[1], last, 1), pltpu.roll(sw[1], 1, 1))
    far_n = corrected(
        from_n[...],
        [(level0_u, n_flux[3]), (level0_v, n_flux[4]), (second, block(1, 4)), (base + 2 * levels, corner_n), (base + 3 * levels, corner_n_v)],
    )
    far_s = corrected(
        from_s[...],
        [(level0_u, s_flux[3]), (level0_v, s_flux[4]), (second, block(3, 4)), (base + 2 * levels, corner_s), (base + 3 * levels, corner_s_v)],
    )
    far_e = corrected(from_e[...], [(level0_u, block(6, 0)), (level0_v, block(7, 0)), (second, block(5, 2))])
    far_w = corrected(from_w[...], [(level0_u, block(6, 1)), (level0_v, block(7, 1)), (second, block(7, 2))])
    turned = stress_u.T
    near_n = corrected(own_n[...], [(level0_v, stress_v[height - 1 : height])])
    near_s = corrected(own_s[...], [(level0_v, stress_v[0:1])])
    near_e = corrected(own_e[...], [(level0_u, turned[last : last + 1])])
    near_w = corrected(own_w[...], [(level0_u, turned[0:1])])
    in_n[...], in_s[...], in_e[...], in_w[...] = near_n, near_s, near_e, near_w
    out_n[...], out_s[...], out_e[...], out_w[...] = far_n, far_s, far_e, far_w

    e_turned, w_turned = far_e.T, far_w.T
    east = lambda index: column(e_turned, index, last)
    west = lambda index: column(w_turned, index, 0)
    passable = wet_products(
        wet, far_n[7 * levels : 7 * levels + 1], far_s[7 * levels : 7 * levels + 1], east(7 * levels), west(7 * levels)
    )
    lines = strips(0, levels, (near_n, near_s, near_e, near_w), (far_n, far_s, far_e, far_w), rim_flux(ext, width))
    profile = level_profile(levels, width)
    mix = KV * wet
    warm = 0.3 * wet * shortwave

    def weights(l, u, v):
        v_n, v_s = [x[5 * levels + l : 5 * levels + l + 1] for x in (far_n, far_s)]
        return coefficients(u, v, east(4 * levels + l), west(4 * levels + l), v_n, v_s, passable)

    def horizontal(c, q, halo):
        e, w, n, s = shifts(q, *halo)
        return c[0] * q + c[1] * e + c[2] * w + c[3] * n + c[4] * s

    def start(l):
        return far_n[l : l + 1], far_s[l : l + 1], east(l), west(l)

    q0, q1, q2 = tracers[0, 0], tracers[0, 1], tracers[0, 2]
    c0 = weights(0, u0, v0)
    c1 = weights(1, currents[0, 1], currents[1, 1])
    t0 = horizontal(c0, q0, start(0)) + mix * (q1 - q0) + warm * profile[0:1] + wet * heat
    t1 = horizontal(c1, q1, start(1)) + mix * ((q2 - q1) - (q1 - q0)) + warm * profile[1:2]
    sides = jnp.concatenate([lines[2][0:8], lines[3][0:8], jnp.zeros((width - 16, width), F32)], axis=0).T
    halo = lines[0][0:1], lines[1][0:1], column(sides, 0, last), column(sides, 8, 0)
    t0 = horizontal(c0, t0, halo) + mix * (t1 - t0) + warm * profile[0:1] + wet * heat
    sst = t0.astype(BF16)
    plane = lax.axis_index("sec") * n_gy + lax.axis_index("gy")
    line = lax.axis_index("gx")
    for z, part in enumerate(parts):
        where = part[height + 3 : height + 4, : planes * chunk].astype(F32)
        hot = (iota((height, planes * chunk), 0).astype(F32) == where).astype(F32)
        picked = dot(hot.T.astype(BF16), sst, NN).reshape(planes, chunk, width)
        for m in range(planes):
            there = plane ^ m
            device = (lax.div(there, n_gy) * n_gx + (line ^ z)) * n_gy + lax.rem(there, n_gy)
            back[device] = picked[m, : back.shape[1]].astype(BF16)


def rim_flux(ext, width):
    def block(r, b):
        return ext[r : r + 1, b * width : (b + 1) * width]

    return (
        (block(0, 0), block(0, 1), block(0, 2)),
        (block(2, 0), block(2, 1), block(2, 2)),
        (block(4, 0), block(5, 0), block(4, 2)),
        (block(4, 1), block(5, 1), block(6, 2)),
    )


def stencil_kernel(
    tracers, currents, land, flux, rim, in_n, in_s, in_e, in_w, out_n, out_s, out_e, out_w,
    out, held, weights, line_n, line_s, depth, forced, passing,
):
    levels = tracers.shape[1]
    height, width = land.shape
    last = width - 1
    wet = land[...].astype(F32)
    far_n, far_s, far_e, far_w = out_n[...], out_s[...], out_e[...], out_w[...]
    e_turned, w_turned = far_e.T, far_w.T
    at = 7 * levels
    for i, x in enumerate(
        wet_products(wet, far_n[at : at + 1], far_s[at : at + 1], column(e_turned, at, last), column(w_turned, at, 0))
    ):
        passing[i] = x
    forced[0], forced[1], forced[2] = 0.3 * wet * flux[0], wet * flux[1], wet * flux[2]
    depth[...] = level_profile(levels, width)
    columns = []
    for tracer in range(2):
        lines = strips(
            tracer, levels, (in_n[...], in_s[...], in_e[...], in_w[...]), (far_n, far_s, far_e, far_w), rim_flux(rim[...], width)
        )
        line_n[tracer * levels : (tracer + 1) * levels] = lines[0]
        line_s[tracer * levels : (tracer + 1) * levels] = lines[1]
        columns.append(lines[2:])
    blank = jnp.zeros((width - 2 * levels, width), F32)
    e_later, w_later = [jnp.concatenate([columns[0][i], columns[1][i], blank], axis=0).T for i in range(2)]

    def update(c, q, halo, under, over, forcing):
        e, w, n, s = shifts(q, *halo)
        mixed = KV * land[...].astype(F32) * ((under - q) - (q - over))
        return c[0] * q + c[1] * e + c[2] * w + c[3] * n + c[4] * s + mixed + forcing

    def forcing(tracer, l):
        top = jnp.where(l == 0, 1.0, 0.0)
        if tracer == 0:
            return forced[0] * depth[pl.ds(l, 1), :] + top * forced[1]
        return top * forced[2]

    def first_step(l, _):
        surface = l == 0
        u = jnp.where(surface, flux[3], currents[0, l])
        v = jnp.where(surface, flux[4], currents[1, l])
        row = 5 * levels + l
        c = coefficients(
            u, v, column(e_turned, 4 * levels + l, last), column(w_turned, 4 * levels + l, 0),
            out_n[pl.ds(row, 1), :], out_s[pl.ds(row, 1), :], [passing[i] for i in range(4)],
        )
        for i, x in enumerate(c):
            weights[i, l] = x
        for tracer in range(2):
            row = tracer * levels + l
            halo = out_n[pl.ds(row, 1), :], out_s[pl.ds(row, 1), :], column(e_turned, row, last), column(w_turned, row, 0)
            under, over = tracers[tracer, jnp.minimum(l + 1, levels - 1)], tracers[tracer, jnp.maximum(l - 1, 0)]
            held[tracer, l] = update(c, tracers[tracer, l], halo, under, over, forcing(tracer, l))
        return 0

    lax.fori_loop(0, levels, first_step, 0)

    def second_step(l, _):
        c = [weights[i, l] for i in range(5)]
        for tracer in range(2):
            row = tracer * levels + l
            halo = line_n[pl.ds(row, 1), :], line_s[pl.ds(row, 1), :], column(e_later, row, last), column(w_later, row, 0)
            under, over = held[tracer, jnp.minimum(l + 1, levels - 1)], held[tracer, jnp.maximum(l - 1, 0)]
            out[tracer, l] = update(c, held[tracer, l], halo, under, over, forcing(tracer, l))
        return 0

    lax.fori_loop(0, levels, second_step, 0)


def backward_kernel(parts, slots, src, back, w, out, held, wide, picked, terms, sems):
    total, width = terms.shape
    blocks = out.shape[0]
    batch = total // parts

    def copy(c):
        return pltpu.make_async_copy(w.at[pl.ds(c * batch, batch)], held.at[pl.ds(c * batch, batch)], sems.at[c])

    for c in range(parts):
        copy(c).start()
    wide[...] = back[...].astype(F32).reshape(wide.shape)

    def pick(i, _):
        for j in range(16):
            picked[pl.ds(i * 16 + j, 1), :] = wide[pl.ds(slots[i * 16 + j], 1), :]
        return 0

    lax.fori_loop(0, total // 16, pick, 0, unroll=2)
    row = iota((16, width), 0)

    def work(c, _):
        copy(c).wait()
        for g in range(batch // 16):
            at = pl.multiple_of(c * batch + g * 16, 16)
            rows = picked[pl.ds(at, 16), :]
            left = [jnp.where((row == r) | (row == 8 + r), rows, 0.0).astype(BF16) for r in range(8)]
            block = held[pl.ds(at, 16)].reshape(2, 8 * width, width)
            both = dot(jnp.concatenate(left, axis=1), jnp.concatenate([block[0], block[1]], axis=1), NN)
            terms[pl.ds(at, 8), :] = both[:8, :width]
            terms[pl.ds(at + 8, 8), :] = both[8:, width:]
        return 0

    lax.fori_loop(0, parts, work, 0)
    hot = (iota((blocks, total), 0) == src[...]).astype(F32).astype(BF16)
    value = terms[...]
    high = value.astype(BF16)
    low = (value - high.astype(F32)).astype(BF16)
    both = dot(hot, jnp.concatenate([high, low], axis=1), NN)
    out[...] = both[:, :width] + both[:, width:]


def backward(back, w, src, slots, blocks, parts=20):
    total, width, _ = w.shape
    devices, cap, _ = back.shape
    return pl.pallas_call(
        functools.partial(backward_kernel, parts),
        in_specs=[SMEM, VMEM, VMEM, ANY],
        out_specs=VMEM,
        scratch_shapes=[
            pltpu.VMEM(w.shape, BF16),
            pltpu.VMEM((devices * cap, width), F32),
            pltpu.VMEM((total, width), F32),
            pltpu.VMEM((total, width), F32),
            pltpu.SemaphoreType.DMA((parts,)),
        ],
        out_shape=jax.ShapeDtypeStruct((blocks, width), F32),
        compiler_params=kernel_params(58),
        cost_estimate=pl.CostEstimate(flops=2 * total * 8 * width * width, bytes_accessed=total * width * width * 2, transcendentals=0),
        name="backward_remap",
    )(slots, src.reshape(1, total), back, w)


def kernel(body, outs, name, mebibytes, bytes_accessed, scratch=()):
    return pl.pallas_call(
        body,
        out_shape=[jax.ShapeDtypeStruct(shape, dtype) for shape, dtype in outs],
        scratch_shapes=list(scratch),
        compiler_params=kernel_params(mebibytes),
        cost_estimate=pl.CostEstimate(flops=bytes_accessed, bytes_accessed=bytes_accessed, transcendentals=0),
        name=name,
    )


def neighbours(axis):
    count = lax.axis_size(axis)
    forward_pairs = [(i, i + 1) for i in range(count - 1)]
    return forward_pairs, [(b, a) for a, b in forward_pairs]


def swapped(array, axes, count, step):
    return lax.ppermute(array, axes, [(i, i ^ step) for i in range(count)])


def on_device(atm_flux, remap_weights, remap_src, remap_dst, remap_owner, tracers, currents, land_sea):
    grid = n_sec, n_gx, n_gy = [lax.axis_size(axis) for axis in EVERY]
    planes = n_sec * n_gy
    total, width, _ = remap_weights.shape
    _, levels, height, _ = tracers.shape
    cap = up(2 * total // (planes * n_gx), 8)
    wide = SENT * width

    *sends, slots = forward(atm_flux, remap_weights, remap_src, remap_owner.reshape(total), remap_dst, grid, cap)
    chunk = sends[0].shape[1]
    got = [sends[0]] + [swapped(sends[m], ("sec", "gy"), planes, m) for m in range(1, planes)]

    side = (width, width)
    end = (7 * levels + 80, width)
    got[1], planes_in, currents_in = lax.optimization_barrier((got[1], tracers, currents))
    own_w, own_e = kernel(columns_kernel, [(side, F32)] * 2, "edge_columns", 16, 1 << 22)(planes_in, currents_in, land_sea)
    to_north, to_south = neighbours(NORTH)
    to_east, to_west = neighbours("gy")
    from_e = lax.ppermute(own_w, "gy", to_west)
    from_w = lax.ppermute(own_e, "gy", to_east)

    got, from_e, from_w = lax.optimization_barrier((got, from_e, from_w))
    own_s, own_n = kernel(rows_kernel, [(end, F32)] * 2, "edge_rows", 16, 1 << 20)(
        tracers.reshape(-1, width), currents.reshape(-1, width), land_sea, from_w, from_e
    )
    from_n = lax.ppermute(own_s, NORTH, to_south)
    from_s = lax.ppermute(own_n, NORTH, to_north)
    part = (height + 8, wide)
    merged = kernel(functools.partial(merge_kernel, planes), [(part, F32)] + [(part, BF16)] * (n_gx - 1), "merge", 24, 1 << 22)(*got)
    parts = [merged[0]] + [swapped(merged[m], "gx", n_gx, m) for m in range(1, n_gx)]

    back, flux, rim, *edges = kernel(
        functools.partial(surface_kernel, grid, chunk, levels),
        [((planes * n_gx, cap, width), BF16), ((5, height, width), F32), ((8, wide), F32)] + ([(end, F32)] * 2 + [(side, F32)] * 2) * 2,
        "surface",
        58,
        1 << 22,
    )(*parts, tracers[0:1, 0:3], currents[:, 0:2], land_sea, own_n, own_s, own_e, own_w, from_n, from_s, from_e, from_w)
    returned = lax.all_to_all(back, EVERY, split_axis=0, concat_axis=0, tiled=True)

    plane = (height, width)
    (tracers_out,) = kernel(
        stencil_kernel,
        [(tracers.shape, F32)],
        "substeps",
        58,
        1 << 24,
        [
            pltpu.VMEM(tracers.shape, F32),
            pltpu.VMEM((5, levels) + plane, F32),
            pltpu.VMEM((2 * levels, width), F32),
            pltpu.VMEM((2 * levels, width), F32),
            pltpu.VMEM((levels, width), F32),
            pltpu.VMEM((3,) + plane, F32),
            pltpu.VMEM((4,) + plane, F32),
        ],
    )(tracers, currents, land_sea, flux, rim, *edges)
    return tracers_out, backward(returned, remap_weights, remap_src, slots, atm_flux.shape[0])


def solution(mesh):
    return jax.shard_map(
        on_device,
        mesh=mesh,
        in_specs=(
            P(EVERY, None, None),
            P(EVERY, None, None),
            P(EVERY),
            P(EVERY),
            P(EVERY, None),
            P(None, None, NORTH, "gy"),
            P(None, None, NORTH, "gy"),
            P(NORTH, "gy"),
        ),
        out_specs=(P(None, None, NORTH, "gy"), P(EVERY, None)),
        check_vma=False,
    )
```

```python
import functools

import jax
import jax.numpy as jnp
from jax import lax
from jax.experimental import pallas as pl
from jax.experimental.pallas import tpu as pltpu
from jax.sharding import PartitionSpec as P

F32 = jnp.float32
BF16 = jnp.bfloat16
NT = (((1,), (1,)), ((), ()))
NN = (((1,), (0,)), ((), ()))
TN = (((0,), (0,)), ((), ()))
EVERY = ("sec", "gx", "gy")
NORTH = ("sec", "gx")
SENT = 5
KH = 0.1
KV = 0.1


def dot(left, right, dims):
    return lax.dot_general(left, right, dims, preferred_element_type=F32)


def iota(shape, dim):
    return lax.broadcasted_iota(jnp.int32, shape, dim)


def up(number, step):
    return -(-number // step) * step


def kernel_params(mebibytes):
    return pltpu.CompilerParams(vmem_limit_bytes=mebibytes << 20)


VMEM = pl.BlockSpec(memory_space=pltpu.VMEM)
SMEM = pl.BlockSpec(memory_space=pltpu.SMEM)
ANY = pl.BlockSpec(memory_space=pl.ANY)


def forward_kernel(parts, cap, grid, src, own, dst, flux, w, *refs):
    sends, (slots, held, mixed, acc, rows, xs, counts, renumbered, sems) = refs[:-9], refs[-9:]
    n_sec, n_gx, n_gy = grid
    devices, chunk, wide = xs.shape
    total, width, _ = held.shape
    batch = total // parts
    fields = flux.shape[1]
    first = chunk - 8
    last = width - 1

    def copy(c):
        return pltpu.make_async_copy(w.at[pl.ds(c * batch, batch)], held.at[pl.ds(c * batch, batch)], sems.at[c])

    for c in range(parts):
        copy(c).start()

    plane = lax.axis_index("sec") * n_gy + lax.axis_index("gy")
    line = lax.axis_index("gx")

    def renumber(owner):
        x = lax.div(owner, n_gy)
        there = lax.div(x, n_gx) * n_gy + lax.rem(owner, n_gy)
        return (there ^ plane) * n_gx + (lax.rem(x, n_gx) ^ line)

    def clear(o, _):
        counts[o] = 0
        renumbered[o] = renumber(o)
        return 0

    lax.fori_loop(0, devices, clear, 0)
    rows[...] = jnp.full_like(rows, 255.0)
    acc[...] = jnp.zeros_like(acc)
    xs[...] = jnp.zeros_like(xs)
    full = flux[...].astype(F32)
    one = [full[:, f : f + 1] for f in range(fields)]
    heat = 0.2 * (one[1] + one[2] + one[3]) - 0.15 * one[5]
    salt = 0.2 * one[4] - 0.1 * one[5]
    heat_high = heat.astype(BF16).astype(F32)
    salt_high = salt.astype(BF16).astype(F32)
    mixed[...] = jnp.concatenate(
        [one[0], heat_high, salt_high, one[6], one[7], heat - heat_high, salt - salt_high, jnp.zeros_like(heat)], axis=1
    ).astype(BF16)

    low_rows = iota((fields, width), 0)
    low_rows = (low_rows == 1) | (low_rows == 2)

    def work(c, _):
        copy(c).wait()
        for b in range(0, batch, 2):
            k = c * batch + b
            left = jnp.concatenate([mixed[src[k]], mixed[src[k + 1]]], axis=0)
            both = dot(left, held[pl.ds(k, 2)].reshape(2 * width, width), NT)
            for z, part in enumerate((both[:fields, :width], both[fields:, width:])):
                part = part + jnp.where(low_rows, pltpu.roll(part, fields - 4, 0), 0.0)
                owner = own[0, k + z]
                at = counts[owner]
                counts[owner] = at + 1
                at = jnp.minimum(at, cap - 1)
                slots[k + z] = owner * cap + at
                slot = renumbered[owner] * cap + at
                acc[pl.ds(pl.multiple_of(slot * fields, fields), fields), :] = part
                rows[pl.ds(slot, 1), :] = jnp.full((1, width), dst[k + z].astype(F32), F32)
        return 0

    lax.fori_loop(0, parts, work, 0)

    lane = iota((cap, width), 1).astype(F32)
    sub = iota((cap, width), 0).astype(F32)
    row = iota((24, wide), 0)
    picks = {
        4: (0, 0), 5: (1, 0), 6: (3, 0), 7: (4, 0), 12: (0, last), 13: (1, last), 14: (3, last), 15: (4, last),
        20: (2, 0), 21: (3, 1), 22: (2, last), 23: (3, last - 1),
    }
    pick = jnp.full((24, wide), -1, jnp.int32)
    for at, (field, column) in picks.items():
        pick = jnp.where(row == at, field * width + column, pick)
    select = (iota((24, wide), 1) == pick).astype(F32).astype(BF16)
    row = iota((8, cap), 0)
    wanted = jnp.zeros((8, cap), F32)
    for at, x in enumerate((0, 1, last, last - 1, 0, 0, last, last)):
        wanted = jnp.where(row == at, float(x), wanted)
    group = 8

    def owners(g, _):
        ds = [g * group + j for j in range(group)]
        five = []
        for d in ds:
            x = [acc[pl.ds(d * cap * fields + f, cap, stride=fields), :] for f in range(SENT)]
            x = jnp.concatenate(x, axis=1)
            xs[d, 0:cap, :] = x
            five.append(x.astype(BF16))
        where = [rows[pl.ds(pl.multiple_of(d * cap, 8), cap), :] for d in ds]
        hot = [(lane == r).astype(F32).astype(BF16) for r in where]
        flat = [jnp.sum(jnp.where(lane == sub, r, 0.0), axis=0, keepdims=True) for r in where]
        flat = [jnp.where(lane[:1] < cap, f, 255.0) for f in flat]
        edge = [dot(select, x, NT).astype(BF16) for x in five]
        sides = [dot(e, h, NN) for e, h in zip(edge, hot)]
        ends = [dot((f[:, :cap] == wanted).astype(F32).astype(BF16), x, NN) for f, x in zip(flat, five)]
        for d, f, side, end in zip(ds, flat, sides, ends):
            here = lax.div(d, n_gx) ^ plane
            here = (lax.div(here, n_gy) * n_gx + (lax.rem(d, n_gx) ^ line)) * n_gy + lax.rem(here, n_gy)

            def at(offset):
                return renumbered[lax.rem(here + offset + 2 * devices, devices)]

            south_of, north_of, west_of, east_of = at(-n_gy), at(n_gy), at(-1), at(1)

            xs[south_of, first : first + 1, :] = end[0:1]
            xs[south_of, first + 1 : first + 2, 4 * width :] = end[1:2, 4 * width :]
            xs[north_of, first + 2 : first + 3, :] = end[2:3]
            xs[north_of, first + 3 : first + 4, 4 * width :] = end[3:4, 4 * width :]
            xs[at(-n_gy - 1), first + 4 : first + 5, 3 * width :] = end[4:5, 3 * width :]
            xs[at(-n_gy + 1), first + 5 : first + 6, 3 * width :] = end[5:6, 3 * width :]
            xs[at(n_gy - 1), first + 6 : first + 7, 3 * width :] = end[6:7, 3 * width :]
            xs[at(n_gy + 1), first + 7 : first + 8, 3 * width :] = end[7:8, 3 * width :]
            xs[west_of, first + 4 : first + 8, 0:width] = side[4:8]
            xs[east_of, first + 4 : first + 8, width : 2 * width] = side[12:16]
            xs[west_of, first + 4 : first + 6, 2 * width : 3 * width] = side[20:22]
            xs[east_of, first + 6 : first + 8, 2 * width : 3 * width] = side[22:24]
            xs[d, first + 1 : first + 2, 0:width] = f
        return 0

    lax.fori_loop(0, devices // group, owners, 0)

    for m, send in enumerate(sends):
        send[...] = xs[m * n_gx : (m + 1) * n_gx].astype(BF16)


def forward(flux, w, src, own, dst, grid, cap, parts=20):
    n_sec, n_gx, n_gy = grid
    devices = n_sec * n_gx * n_gy
    total, width, _ = w.shape
    chunk = up(cap + 8, 16)
    fields = flux.shape[1]
    wide = SENT * width
    return pl.pallas_call(
        functools.partial(forward_kernel, parts, cap, grid),
        in_specs=[SMEM, SMEM, SMEM, VMEM, ANY],
        out_specs=[VMEM] * (n_sec * n_gy) + [SMEM],
        scratch_shapes=[
            pltpu.VMEM(w.shape, BF16),
            pltpu.VMEM(flux.shape, BF16),
            pltpu.VMEM((devices * cap * fields, width), F32),
            pltpu.VMEM((devices * cap, width), F32),
            pltpu.VMEM((devices, chunk, wide), F32),
            pltpu.SMEM((devices,), jnp.int32),
            pltpu.SMEM((devices,), jnp.int32),
            pltpu.SemaphoreType.DMA((parts,)),
        ],
        out_shape=[jax.ShapeDtypeStruct((n_gx, chunk, wide), BF16)] * (n_sec * n_gy) + [jax.ShapeDtypeStruct((total,), jnp.int32)],
        compiler_params=kernel_params(58),
        cost_estimate=pl.CostEstimate(flops=2 * total * 8 * width * width, bytes_accessed=total * width * width * 2, transcendentals=0),
        name="forward_remap",
    )(src, own, dst, flux, w)


def merge_kernel(n_sources, *refs):
    sources, outs = refs[:n_sources], refs[n_sources:]
    chunk = sources[0].shape[1]
    height = outs[0].shape[0] - 8
    first = chunk - 8
    count = n_sources * chunk
    for z, out in enumerate(outs):
        ext = None
        where = []
        for source in sources:
            piece = source[z, first:chunk, :].astype(F32)
            where.append(piece[1:2, :chunk])
            ext = piece if ext is None else ext + piece
        where = jnp.concatenate(where, axis=1)
        hot = (iota((height, count), 0).astype(F32) == where).astype(F32).astype(BF16)
        sums = dot(hot, jnp.concatenate([source[z] for source in sources], axis=0), NN)
        row3 = jnp.concatenate([where, ext[3:4, count:]], axis=1)
        ext = jnp.where(iota((8, 1), 0) == 3, row3, ext)
        out[...] = jnp.concatenate([sums, ext], axis=0).astype(out.dtype)


def rows_kernel(tracers, currents, land, south, north):
    height, width = land.shape
    levels = tracers.shape[0] // 2 // height
    for out, edge, second in ((south, 0, 1), (north, height - 1, height - 2)):
        out[...] = jnp.concatenate(
            [
                tracers[pl.ds(edge, 2 * levels, stride=height), :],
                tracers[pl.ds(second, 2 * levels, stride=height), :],
                currents[pl.ds(edge, 2 * levels, stride=height), :],
                currents[pl.ds(levels * height + second, levels, stride=height), :],
                *[land[x : x + 1, :].astype(F32) for x in (edge, second)],
                jnp.zeros((out.shape[0] - 7 * levels - 2, width), F32),
            ],
            axis=0,
        ).astype(BF16)


def columns_kernel(tracers, currents, land, from_n, from_s, west, east, west_wide, east_wide):
    levels = tracers.shape[1]
    width = tracers.shape[3]
    last = width - 1
    lane = iota((1, width), 1)
    west_wide[...] = jnp.zeros_like(west_wide)
    east_wide[...] = jnp.zeros_like(east_wide)

    def put(plane, near, far):
        turned = plane.T
        for out, edge, second in ((west_wide, 0, 1), (east_wide, last, last - 1)):
            out[pl.ds(near, 1), :] = turned[edge : edge + 1]
            if far is not None:
                out[pl.ds(far, 1), :] = turned[second : second + 1]

    def level(l, _):
        for t in range(2):
            put(tracers[t, l], t * levels + l, (2 + t) * levels + l)
        put(currents[0, l], 4 * levels + l, 6 * levels + l)
        put(currents[1, l], 5 * levels + l, None)
        return 0

    lax.fori_loop(0, levels, level, 0, unroll=2)
    put(land[...].astype(F32), 7 * levels, 7 * levels + 1)
    base = 7 * levels + 8
    n_all, s_all = from_n[...].astype(F32), from_s[...].astype(F32)
    for start, stop, at in ((0, 2 * levels, 0), (4 * levels, 6 * levels, 2 * levels), (7 * levels, 7 * levels + 8, 4 * levels)):
        n, s = n_all[start:stop], s_all[start:stop]
        west_wide[base + at : base + at + stop - start] = jnp.where(lane == last, pltpu.roll(n, last, 1), s)
        east_wide[base + at : base + at + stop - start] = jnp.where(lane == last, n, pltpu.roll(s, 1, 1))
    west[...] = west_wide[...].astype(BF16)
    east[...] = east_wide[...].astype(BF16)


def plus_side(q, other, speed, speed_other, passable):
    return KH * passable * (other - q) - 0.25 * (speed + speed_other) * passable * (q + other)


def minus_side(q, other, speed, speed_other, passable):
    return KH * passable * (other - q) + 0.25 * (speed_other + speed) * passable * (other + q)


def level_profile(levels, width):
    depth = iota((levels, width), 0).astype(F32)
    return jnp.exp(-depth / 4.0) * (1.0 - jnp.exp(jnp.full((levels, width), -0.25, F32)))


def strip_step(q, q_plus, q_minus, across, across_plus, across_minus, along, corner_q, corner_along, wet, wet_plus, wet_minus, corner_wet, forcing):
    levels, width = q.shape
    lane = iota((1, width), 1)
    row = iota((levels, 1), 0)

    def ahead(x, corner):
        return jnp.where(lane == width - 1, corner, pltpu.roll(x, width - 1, 1))

    def behind(x, corner):
        return jnp.where(lane == 0, corner, pltpu.roll(x, 1, 1))

    total = plus_side(q, q_plus, across, across_plus, wet * wet_plus)
    total += minus_side(q, q_minus, across, across_minus, wet * wet_minus)
    total += plus_side(q, ahead(q, corner_q), along, ahead(along, corner_along), wet * ahead(wet, corner_wet))
    total += minus_side(q, behind(q, corner_q), along, behind(along, corner_along), wet * behind(wet, corner_wet))
    below = jnp.where(row < levels - 1, pltpu.roll(q, levels - 1, 0) - q, 0.0)
    above = jnp.where(row > 0, q - pltpu.roll(q, 1, 0), 0.0)
    return q + total + wet * (KV * (below - above) + forcing)


def strips(tracer, levels, inner, outer, flux):
    width = outer[0].shape[1]
    lane = iota((1, width), 1)
    base = 7 * levels + 8
    north, south, east, west = outer

    def part(x, at, count=levels):
        return x[at : at + count]

    def corners(at, count):
        e, w = part(east, base + at, count), part(west, base + at, count)
        n = jnp.where(lane == width - 1, e, pltpu.roll(w, 1, 1))
        s = jnp.where(lane == width - 1, pltpu.roll(e, width - 1, 1), w)
        return n, s, e, w

    corner_q = corners(tracer * levels, levels)
    corner_u = corners(2 * levels, levels)
    corner_v = corners(3 * levels, levels)
    corner_wet = corners(4 * levels, 1)
    top = (iota((levels, 1), 0) == 0).astype(F32)
    profile = level_profile(levels, width)
    results = []
    for side in range(4):
        near, far = inner[side], outer[side]
        beside, out = part(near, tracer * levels), part(far, (2 + tracer) * levels)
        mid = part(far, tracer * levels)
        speed = 5 if side < 2 else 4
        along = part(far, (9 - speed) * levels)
        corner_along = (corner_u if side < 2 else corner_v)[side]
        across, across_in, across_out = part(far, speed * levels), part(near, speed * levels), part(far, 6 * levels)
        wet, wet_in, wet_out = part(far, 7 * levels, 1), part(near, 7 * levels, 1), part(far, 7 * levels + 1, 1)
        shortwave, heat, salt = flux[side]
        forcing = 0.3 * profile * shortwave + top * heat if tracer == 0 else top * salt
        if side % 2 == 0:
            pairs = (out, beside, across, across_out, across_in)
            wets = (wet, wet_out, wet_in)
        else:
            pairs = (beside, out, across, across_in, across_out)
            wets = (wet, wet_in, wet_out)
        results.append(strip_step(mid, *pairs, along, corner_q[side], corner_along, *wets, corner_wet[side], forcing))
    return results


def shifts(plane, north, south, east, west):
    height, width = plane.shape
    lane, row = iota(plane.shape, 1), iota(plane.shape, 0)
    return (
        jnp.where(lane == width - 1, east, pltpu.roll(plane, width - 1, 1)),
        jnp.where(lane == 0, west, pltpu.roll(plane, 1, 1)),
        jnp.where(row == height - 1, north, pltpu.roll(plane, height - 1, 0)),
        jnp.where(row == 0, south, pltpu.roll(plane, 1, 0)),
    )


def wet_products(wet, north, south, east, west):
    return [wet * other for other in shifts(wet, north, south, east, west)]


def coefficients(u, v, u_east, u_west, v_north, v_south, passable):
    east, west, north, south = passable
    height, width = u.shape
    lane, row = iota(u.shape, 1), iota(u.shape, 0)
    e = jnp.where(lane == width - 1, u_east, pltpu.roll(u, width - 1, 1))
    w = jnp.where(lane == 0, u_west, pltpu.roll(u, 1, 1))
    n = jnp.where(row == height - 1, v_north, pltpu.roll(v, height - 1, 0))
    s = jnp.where(row == 0, v_south, pltpu.roll(v, 1, 0))
    flow_e, flow_w = 0.25 * (u + e) * east, 0.25 * (w + u) * west
    flow_n, flow_s = 0.25 * (v + n) * north, 0.25 * (s + v) * south
    own = 1.0 + (flow_w - flow_e) + (flow_s - flow_n) - KH * (east + west + north + south)
    return own, KH * east - flow_e, KH * west + flow_w, KH * north - flow_n, KH * south + flow_s


def column(turned, index, lane):
    return pltpu.roll(turned, lax.rem(lane - index + 2 * turned.shape[1], turned.shape[1]), 1)


def corrected(edge, x_rows):
    row = iota((edge.shape[0], 1), 0)
    for at, x in x_rows:
        edge = edge + jnp.where(row == at, 0.1 * x, 0.0)
    return edge


def corrected_edges(levels, ext, stress_u, stress_v, near, far):
    height, width = stress_u.shape
    last = width - 1
    lane = iota((1, width), 1)

    def block(r, b):
        return ext[r : r + 1, b * width : (b + 1) * width]

    u, v, second = 4 * levels, 5 * levels, 6 * levels
    base = 7 * levels + 8
    corners = []
    for b in (3, 4):
        ne, nw, se, sw = [block(r, b) for r in (4, 5, 6, 7)]
        corners.append((jnp.where(lane == last, pltpu.roll(ne, last, 1), se), jnp.where(lane == last, nw, pltpu.roll(sw, 1, 1))))
    turned = stress_u.T
    own = [[(v, stress_v[last:])], [(v, stress_v[0:1])], [(u, turned[last:])], [(u, turned[0:1])]]
    beside = [
        [(u, block(0, 3)), (v, block(0, 4)), (second, block(1, 4))],
        [(u, block(2, 3)), (v, block(2, 4)), (second, block(3, 4))],
        [(u, block(6, 0)), (v, block(7, 0)), (second, block(5, 2)), (base + 2 * levels, corners[0][0]), (base + 3 * levels, corners[1][0])],
        [(u, block(6, 1)), (v, block(7, 1)), (second, block(7, 2)), (base + 2 * levels, corners[0][1]), (base + 3 * levels, corners[1][1])],
    ]
    near = [corrected(edge[...].astype(F32), x) for edge, x in zip(near, own)]
    return near, [corrected(edge[...].astype(F32), x) for edge, x in zip(far, beside)]


def surface_kernel(grid, chunk, levels, *refs):
    n_sec, n_gx, n_gy = grid
    planes = n_sec * n_gy
    parts, refs = refs[:n_gx], refs[n_gx:]
    tracers, currents, land, own_n, own_s, own_e, own_w, from_n, from_s, from_e, from_w, *refs = refs
    back, flux, rim = refs
    height, width = land.shape
    last = width - 1
    lane = iota((1, width), 1)
    sums = parts[0][...]
    for part in parts[1:]:
        sums = sums + part[...].astype(F32)
    sums, ext = sums[:height], sums[height : height + 8]
    shortwave, heat, salt, stress_u, stress_v = [sums[:, f * width : (f + 1) * width] for f in range(SENT)]
    wet = land[...].astype(F32)
    u0 = currents[0, 0] + 0.1 * stress_u
    v0 = currents[1, 0] + 0.1 * stress_v
    flux[0], flux[1], flux[2], flux[3], flux[4] = shortwave, heat, salt, stress_u, stress_v
    rim[...] = ext

    near, far = corrected_edges(levels, ext, stress_u, stress_v, (own_n, own_s, own_e, own_w), (from_n, from_s, from_e, from_w))
    far_n, far_s, far_e, far_w = far
    e_turned, w_turned = far_e[:width].T, far_w[:width].T
    east = lambda index: column(e_turned, index, last)
    west = lambda index: column(w_turned, index, 0)
    passable = wet_products(
        wet, far_n[7 * levels : 7 * levels + 1], far_s[7 * levels : 7 * levels + 1], east(7 * levels), west(7 * levels)
    )
    lines = strips(0, levels, near, far, rim_flux(ext, width))
    profile = level_profile(levels, width)
    mix = KV * wet
    warm = 0.3 * wet * shortwave

    def weights(l, u, v):
        v_n, v_s = [x[5 * levels + l : 5 * levels + l + 1] for x in (far_n, far_s)]
        return coefficients(u, v, east(4 * levels + l), west(4 * levels + l), v_n, v_s, passable)

    def horizontal(c, q, halo):
        e, w, n, s = shifts(q, *halo)
        return c[0] * q + c[1] * e + c[2] * w + c[3] * n + c[4] * s

    def start(l):
        return far_n[l : l + 1], far_s[l : l + 1], east(l), west(l)

    q0, q1, q2 = tracers[0, 0], tracers[0, 1], tracers[0, 2]
    c0 = weights(0, u0, v0)
    c1 = weights(1, currents[0, 1], currents[1, 1])
    t0 = horizontal(c0, q0, start(0)) + mix * (q1 - q0) + warm * profile[0:1] + wet * heat
    t1 = horizontal(c1, q1, start(1)) + mix * ((q2 - q1) - (q1 - q0)) + warm * profile[1:2]
    sides = jnp.concatenate([lines[2][0:8], lines[3][0:8], jnp.zeros((width - 16, width), F32)], axis=0).T
    halo = lines[0][0:1], lines[1][0:1], column(sides, 0, last), column(sides, 8, 0)
    t0 = horizontal(c0, t0, halo) + mix * (t1 - t0) + warm * profile[0:1] + wet * heat
    sst = t0.astype(BF16)
    plane = lax.axis_index("sec") * n_gy + lax.axis_index("gy")
    line = lax.axis_index("gx")
    for z, part in enumerate(parts):
        where = part[height + 3 : height + 4, : planes * chunk].astype(F32)
        hot = (iota((height, planes * chunk), 0).astype(F32) == where).astype(F32)
        picked = dot(hot.T.astype(BF16), sst, NN).reshape(planes, chunk, width)
        for m in range(planes):
            there = plane ^ m
            device = (lax.div(there, n_gy) * n_gx + (line ^ z)) * n_gy + lax.rem(there, n_gy)
            back[device] = picked[m, : back.shape[1]].astype(BF16)


def rim_flux(ext, width):
    def block(r, b):
        return ext[r : r + 1, b * width : (b + 1) * width]

    return (
        (block(0, 0), block(0, 1), block(0, 2)),
        (block(2, 0), block(2, 1), block(2, 2)),
        (block(4, 0), block(5, 0), block(4, 2)),
        (block(4, 1), block(5, 1), block(6, 2)),
    )


def stencil_kernel(
    tracers_in, currents_in, land, flux, rim, own_n, own_s, own_e, own_w, from_n, from_s, from_e, from_w,
    result, tracers, currents, out, held, weights, edge_n, edge_s, line_n, line_s, depth, forced, passing, sems,
):
    copies = [
        pltpu.make_async_copy(tracers_in, tracers, sems.at[0]),
        pltpu.make_async_copy(currents_in, currents, sems.at[1]),
    ]
    for copy in copies:
        copy.start()
    levels = tracers.shape[1]

    def send(l):
        return pltpu.make_async_copy(out.at[:, l], result.at[:, l], sems.at[2 + l])

    height, width = land.shape
    last = width - 1
    wet = land[...].astype(F32)
    near, far = corrected_edges(
        levels, rim[...], flux[3], flux[4], (own_n, own_s, own_e, own_w), (from_n, from_s, from_e, from_w)
    )
    far_n, far_s, far_e, far_w = far
    edge_n[...], edge_s[...] = far_n, far_s
    e_turned, w_turned = far_e[:width].T, far_w[:width].T
    at = 7 * levels
    for i, x in enumerate(
        wet_products(wet, far_n[at : at + 1], far_s[at : at + 1], column(e_turned, at, last), column(w_turned, at, 0))
    ):
        passing[i] = x
    forced[0], forced[1], forced[2] = 0.3 * wet * flux[0], wet * flux[1], wet * flux[2]
    depth[...] = level_profile(levels, width)
    columns = []
    for tracer in range(2):
        lines = strips(
            tracer, levels, near, far, rim_flux(rim[...], width)
        )
        line_n[tracer * levels : (tracer + 1) * levels] = lines[0]
        line_s[tracer * levels : (tracer + 1) * levels] = lines[1]
        columns.append(lines[2:])
    blank = jnp.zeros((width - 2 * levels, width), F32)
    e_later, w_later = [jnp.concatenate([columns[0][i], columns[1][i], blank], axis=0).T for i in range(2)]

    def update(c, q, halo, under, over, forcing):
        e, w, n, s = shifts(q, *halo)
        mixed = KV * land[...].astype(F32) * ((under - q) - (q - over))
        return c[0] * q + c[1] * e + c[2] * w + c[3] * n + c[4] * s + mixed + forcing

    def forcing(tracer, l):
        top = jnp.where(l == 0, 1.0, 0.0)
        if tracer == 0:
            return forced[0] * depth[pl.ds(l, 1), :] + top * forced[1]
        return top * forced[2]

    for copy in copies:
        copy.wait()
    currents[0, 0] = currents[0, 0] + 0.1 * flux[3]
    currents[1, 0] = currents[1, 0] + 0.1 * flux[4]

    def first_step(l, _):
        u, v = currents[0, l], currents[1, l]
        row = 5 * levels + l
        c = coefficients(
            u, v, column(e_turned, 4 * levels + l, last), column(w_turned, 4 * levels + l, 0),
            edge_n[pl.ds(row, 1), :], edge_s[pl.ds(row, 1), :], [passing[i] for i in range(4)],
        )
        for i, x in enumerate(c):
            weights[i, l] = x
        for tracer in range(2):
            row = tracer * levels + l
            halo = edge_n[pl.ds(row, 1), :], edge_s[pl.ds(row, 1), :], column(e_turned, row, last), column(w_turned, row, 0)
            under, over = tracers[tracer, jnp.minimum(l + 1, levels - 1)], tracers[tracer, jnp.maximum(l - 1, 0)]
            held[tracer, l] = update(c, tracers[tracer, l], halo, under, over, forcing(tracer, l))
        return 0

    lax.fori_loop(0, levels, first_step, 0)

    def second_step(l, _):
        c = [weights[i, l] for i in range(5)]
        for tracer in range(2):
            row = tracer * levels + l
            halo = line_n[pl.ds(row, 1), :], line_s[pl.ds(row, 1), :], column(e_later, row, last), column(w_later, row, 0)
            under, over = held[tracer, jnp.minimum(l + 1, levels - 1)], held[tracer, jnp.maximum(l - 1, 0)]
            out[tracer, l] = update(c, held[tracer, l], halo, under, over, forcing(tracer, l))
        send(l).start()
        return 0

    lax.fori_loop(0, levels, second_step, 0)
    for l in range(levels):
        send(l).wait()


def backward_kernel(parts, slots_in, src, back, w, out, held, wide, picked, terms, slots, sems):
    total, width = terms.shape
    blocks = out.shape[0]
    batch = total // parts

    def copy(c):
        return pltpu.make_async_copy(w.at[pl.ds(c * batch, batch)], held.at[pl.ds(c * batch, batch)], sems.at[c])

    slots_copy = pltpu.make_async_copy(slots_in, slots, sems.at[parts])
    slots_copy.start()
    for c in range(parts):
        copy(c).start()
    slots_copy.wait()
    wide[...] = back[...].astype(F32).reshape(wide.shape)

    def pick(i, _):
        for j in range(16):
            picked[pl.ds(i * 16 + j, 1), :] = wide[pl.ds(slots[i * 16 + j], 1), :]
        return 0

    lax.fori_loop(0, total // 16, pick, 0, unroll=2)
    row = iota((16, width), 0)

    def work(c, _):
        copy(c).wait()
        for g in range(batch // 16):
            at = pl.multiple_of(c * batch + g * 16, 16)
            rows = picked[pl.ds(at, 16), :]
            left = [jnp.where((row == r) | (row == 8 + r), rows, 0.0).astype(BF16) for r in range(8)]
            block = held[pl.ds(at, 16)].reshape(2, 8 * width, width)
            both = dot(jnp.concatenate(left, axis=1), jnp.concatenate([block[0], block[1]], axis=1), NN)
            terms[pl.ds(at, 8), :] = both[:8, :width]
            terms[pl.ds(at + 8, 8), :] = both[8:, width:]
        return 0

    lax.fori_loop(0, parts, work, 0)
    hot = (iota((blocks, total), 0) == src[...]).astype(F32).astype(BF16)
    value = terms[...]
    high = value.astype(BF16)
    low = (value - high.astype(F32)).astype(BF16)
    both = dot(hot, jnp.concatenate([high, low], axis=1), NN)
    out[...] = both[:, :width] + both[:, width:]


def backward(back, w, src, slots, blocks, parts=20):
    total, width, _ = w.shape
    devices, cap, _ = back.shape
    return pl.pallas_call(
        functools.partial(backward_kernel, parts),
        in_specs=[ANY, VMEM, VMEM, ANY],
        out_specs=VMEM,
        scratch_shapes=[
            pltpu.VMEM(w.shape, BF16),
            pltpu.VMEM((devices * cap, width), F32),
            pltpu.VMEM((total, width), F32),
            pltpu.VMEM((total, width), F32),
            pltpu.SMEM((total,), jnp.int32),
            pltpu.SemaphoreType.DMA((parts + 1,)),
        ],
        out_shape=jax.ShapeDtypeStruct((blocks, width), F32),
        compiler_params=kernel_params(58),
        cost_estimate=pl.CostEstimate(flops=2 * total * 8 * width * width, bytes_accessed=total * width * width * 2, transcendentals=0),
        name="backward_remap",
    )(slots, src.reshape(1, total), back, w)


def kernel(body, outs, name, mebibytes, bytes_accessed, scratch=(), **specs):
    return pl.pallas_call(
        body,
        out_shape=[jax.ShapeDtypeStruct(shape, dtype) for shape, dtype in outs],
        scratch_shapes=list(scratch),
        compiler_params=kernel_params(mebibytes),
        cost_estimate=pl.CostEstimate(flops=bytes_accessed, bytes_accessed=bytes_accessed, transcendentals=0),
        name=name,
        **specs,
    )


def neighbours(axis):
    count = lax.axis_size(axis)
    forward_pairs = [(i, i + 1) for i in range(count - 1)]
    return forward_pairs, [(b, a) for a, b in forward_pairs]


def swapped(array, axes, count, step):
    return lax.ppermute(array, axes, [(i, i ^ step) for i in range(count)])


def on_device(atm_flux, remap_weights, remap_src, remap_dst, remap_owner, tracers, currents, land_sea):
    grid = n_sec, n_gx, n_gy = [lax.axis_size(axis) for axis in EVERY]
    planes = n_sec * n_gy
    total, width, _ = remap_weights.shape
    _, levels, height, _ = tracers.shape
    cap = up(2 * total // (planes * n_gx), 8)
    wide = SENT * width

    *sends, slots = forward(atm_flux, remap_weights, remap_src, remap_owner.reshape(1, total), remap_dst, grid, cap)
    chunk = sends[0].shape[1]
    got = [sends[0]] + [swapped(sends[m], ("sec", "gy"), planes, m) for m in range(1, planes)]

    side = (width, width)
    end = (7 * levels + 80, width)
    to_north, to_south = neighbours(NORTH)
    to_east, to_west = neighbours("gy")
    got[1], tracers_there, currents_there = lax.optimization_barrier((got[1], tracers, currents))
    own_s, own_n = kernel(rows_kernel, [(side, BF16)] * 2, "edge_rows", 16, 1 << 20)(
        tracers_there.reshape(-1, width), currents_there.reshape(-1, width), land_sea
    )
    from_n = lax.ppermute(own_s, NORTH, to_south)
    from_s = lax.ppermute(own_n, NORTH, to_north)
    got, from_n, from_s = lax.optimization_barrier((got, from_n, from_s))
    own_w, own_e = kernel(columns_kernel, [(end, BF16)] * 2, "edge_columns", 16, 1 << 22, [pltpu.VMEM(end, F32)] * 2)(
        tracers, currents, land_sea, from_n, from_s
    )
    from_e = lax.ppermute(own_w, "gy", to_west)
    from_w = lax.ppermute(own_e, "gy", to_east)
    part = (height + 8, wide)
    merged = kernel(functools.partial(merge_kernel, planes), [(part, F32)] + [(part, BF16)] * (n_gx - 1), "merge", 24, 1 << 22)(*got)
    parts = [merged[0]] + [swapped(merged[m], "gx", n_gx, m) for m in range(1, n_gx)]

    edges = own_n, own_s, own_e, own_w, from_n, from_s, from_e, from_w
    back, flux, rim = kernel(
        functools.partial(surface_kernel, grid, chunk, levels),
        [((planes * n_gx, cap, width), BF16), ((5, height, width), F32), ((8, wide), F32)],
        "surface",
        58,
        1 << 22,
    )(*parts, tracers[0:1, 0:3], currents[:, 0:2], land_sea, *edges)
    returned = lax.all_to_all(back, EVERY, split_axis=0, concat_axis=0, tiled=True)

    plane = (height, width)
    (tracers_out,) = kernel(
        stencil_kernel,
        [(tracers.shape, F32)],
        "substeps",
        58,
        1 << 24,
        [
            pltpu.VMEM(tracers.shape, F32),
            pltpu.VMEM(currents.shape, F32),
            pltpu.VMEM(tracers.shape, F32),
            pltpu.VMEM(tracers.shape, F32),
            pltpu.VMEM((5, levels) + plane, F32),
            pltpu.VMEM(side, F32),
            pltpu.VMEM(side, F32),
            pltpu.VMEM((2 * levels, width), F32),
            pltpu.VMEM((2 * levels, width), F32),
            pltpu.VMEM((levels, width), F32),
            pltpu.VMEM((3,) + plane, F32),
            pltpu.VMEM((4,) + plane, F32),
            pltpu.SemaphoreType.DMA((2 + levels,)),
        ],
        in_specs=[ANY, ANY] + [VMEM] * 11,
        out_specs=[ANY],
    )(tracers, currents, land_sea, flux, rim, *edges)
    return tracers_out, backward(returned, remap_weights, remap_src, slots, atm_flux.shape[0])


def solution(mesh):
    return jax.shard_map(
        on_device,
        mesh=mesh,
        in_specs=(
            P(EVERY, None, None),
            P(EVERY, None, None),
            P(EVERY),
            P(EVERY),
            P(EVERY, None),
            P(None, None, NORTH, "gy"),
            P(None, None, NORTH, "gy"),
            P(NORTH, "gy"),
        ),
        out_specs=(P(None, None, NORTH, "gy"), P(EVERY, None)),
        check_vma=False,
    )
```

```python
import functools

import jax
import jax.numpy as jnp
from jax import lax
from jax.experimental import pallas as pl
from jax.experimental.pallas import tpu as pltpu
from jax.sharding import PartitionSpec as P

F32 = jnp.float32
BF16 = jnp.bfloat16
NT = (((1,), (1,)), ((), ()))
NN = (((1,), (0,)), ((), ()))
TN = (((0,), (0,)), ((), ()))
EVERY = ("sec", "gx", "gy")
NORTH = ("sec", "gx")
SENT = 5
KH = 0.1
KV = 0.1


def dot(left, right, dims):
    return lax.dot_general(left, right, dims, preferred_element_type=F32)


def iota(shape, dim):
    return lax.broadcasted_iota(jnp.int32, shape, dim)


def up(number, step):
    return -(-number // step) * step


def kernel_params(mebibytes):
    return pltpu.CompilerParams(vmem_limit_bytes=mebibytes << 20)


VMEM = pl.BlockSpec(memory_space=pltpu.VMEM)
SMEM = pl.BlockSpec(memory_space=pltpu.SMEM)
ANY = pl.BlockSpec(memory_space=pl.ANY)


def forward_kernel(parts, cap, grid, src, own, dst, flux, w, *refs):
    sends, (slots, held, mixed, acc, rows, xs, counts, renumbered, sems) = refs[:-9], refs[-9:]
    n_sec, n_gx, n_gy = grid
    devices, chunk, wide = xs.shape
    total, width, _ = held.shape
    batch = total // parts
    fields = flux.shape[1]
    first = chunk - 8
    last = width - 1

    def copy(c):
        return pltpu.make_async_copy(w.at[pl.ds(c * batch, batch)], held.at[pl.ds(c * batch, batch)], sems.at[c])

    for c in range(parts):
        copy(c).start()

    plane = lax.axis_index("sec") * n_gy + lax.axis_index("gy")
    line = lax.axis_index("gx")

    def renumber(owner):
        x = lax.div(owner, n_gy)
        there = lax.div(x, n_gx) * n_gy + lax.rem(owner, n_gy)
        return (there ^ plane) * n_gx + (lax.rem(x, n_gx) ^ line)

    def clear(o, _):
        counts[o] = 0
        renumbered[o] = renumber(o)
        return 0

    lax.fori_loop(0, devices, clear, 0)
    rows[...] = jnp.full_like(rows, 255.0)
    acc[...] = jnp.zeros_like(acc)
    xs[...] = jnp.zeros_like(xs)
    full = flux[...].astype(F32)
    one = [full[:, f : f + 1] for f in range(fields)]
    heat = 0.2 * (one[1] + one[2] + one[3]) - 0.15 * one[5]
    salt = 0.2 * one[4] - 0.1 * one[5]
    heat_high = heat.astype(BF16).astype(F32)
    salt_high = salt.astype(BF16).astype(F32)
    mixed[...] = jnp.concatenate(
        [one[0], heat_high, salt_high, one[6], one[7], heat - heat_high, salt - salt_high, jnp.zeros_like(heat)], axis=1
    ).astype(BF16)

    low_rows = iota((fields, width), 0)
    low_rows = (low_rows == 1) | (low_rows == 2)

    def work(c, _):
        copy(c).wait()
        for b in range(0, batch, 2):
            k = c * batch + b
            left = jnp.concatenate([mixed[src[k]], mixed[src[k + 1]]], axis=0)
            both = dot(left, held[pl.ds(k, 2)].reshape(2 * width, width), NT)
            for z, part in enumerate((both[:fields, :width], both[fields:, width:])):
                part = part + jnp.where(low_rows, pltpu.roll(part, fields - 4, 0), 0.0)
                owner = own[0, k + z]
                at = counts[owner]
                counts[owner] = at + 1
                at = jnp.minimum(at, cap - 1)
                slots[k + z] = owner * cap + at
                slot = renumbered[owner] * cap + at
                acc[pl.ds(pl.multiple_of(slot * fields, fields), fields), :] = part
                rows[pl.ds(slot, 1), :] = jnp.full((1, width), dst[k + z].astype(F32), F32)
        return 0

    lax.fori_loop(0, parts, work, 0)

    lane = iota((cap, width), 1).astype(F32)
    sub = iota((cap, width), 0).astype(F32)
    row = iota((24, wide), 0)
    picks = {
        4: (0, 0), 5: (1, 0), 6: (3, 0), 7: (4, 0), 12: (0, last), 13: (1, last), 14: (3, last), 15: (4, last),
        20: (2, 0), 21: (3, 1), 22: (2, last), 23: (3, last - 1),
    }
    pick = jnp.full((24, wide), -1, jnp.int32)
    for at, (field, column) in picks.items():
        pick = jnp.where(row == at, field * width + column, pick)
    select = (iota((24, wide), 1) == pick).astype(F32).astype(BF16)
    row = iota((8, cap), 0)
    wanted = jnp.zeros((8, cap), F32)
    for at, x in enumerate((0, 1, last, last - 1, 0, 0, last, last)):
        wanted = jnp.where(row == at, float(x), wanted)
    group = 8

    def owners(g, _):
        ds = [g * group + j for j in range(group)]
        five = []
        for d in ds:
            x = [acc[pl.ds(d * cap * fields + f, cap, stride=fields), :] for f in range(SENT)]
            x = jnp.concatenate(x, axis=1)
            xs[d, 0:cap, :] = x
            five.append(x.astype(BF16))
        where = [rows[pl.ds(pl.multiple_of(d * cap, 8), cap), :] for d in ds]
        hot = [(lane == r).astype(F32).astype(BF16) for r in where]
        flat = [jnp.sum(jnp.where(lane == sub, r, 0.0), axis=0, keepdims=True) for r in where]
        flat = [jnp.where(lane[:1] < cap, f, 255.0) for f in flat]
        edge = [dot(select, x, NT).astype(BF16) for x in five]
        sides = [dot(e, h, NN) for e, h in zip(edge, hot)]
        ends = [dot((f[:, :cap] == wanted).astype(F32).astype(BF16), x, NN) for f, x in zip(flat, five)]
        for d, f, side, end in zip(ds, flat, sides, ends):
            here = lax.div(d, n_gx) ^ plane
            here = (lax.div(here, n_gy) * n_gx + (lax.rem(d, n_gx) ^ line)) * n_gy + lax.rem(here, n_gy)

            def at(offset):
                return renumbered[lax.rem(here + offset + 2 * devices, devices)]

            south_of, north_of, west_of, east_of = at(-n_gy), at(n_gy), at(-1), at(1)

            xs[south_of, first : first + 1, :] = end[0:1]
            xs[south_of, first + 1 : first + 2, 4 * width :] = end[1:2, 4 * width :]
            xs[north_of, first + 2 : first + 3, :] = end[2:3]
            xs[north_of, first + 3 : first + 4, 4 * width :] = end[3:4, 4 * width :]
            xs[at(-n_gy - 1), first + 4 : first + 5, 3 * width :] = end[4:5, 3 * width :]
            xs[at(-n_gy + 1), first + 5 : first + 6, 3 * width :] = end[5:6, 3 * width :]
            xs[at(n_gy - 1), first + 6 : first + 7, 3 * width :] = end[6:7, 3 * width :]
            xs[at(n_gy + 1), first + 7 : first + 8, 3 * width :] = end[7:8, 3 * width :]
            xs[west_of, first + 4 : first + 8, 0:width] = side[4:8]
            xs[east_of, first + 4 : first + 8, width : 2 * width] = side[12:16]
            xs[west_of, first + 4 : first + 6, 2 * width : 3 * width] = side[20:22]
            xs[east_of, first + 6 : first + 8, 2 * width : 3 * width] = side[22:24]
            xs[d, first + 1 : first + 2, 0:width] = f
        return 0

    lax.fori_loop(0, devices // group, owners, 0)

    half = n_gx // 2
    planes = n_sec * n_gy
    for m in range(planes):
        sends[m][...] = xs[m * n_gx + half : (m + 1) * n_gx].astype(BF16)
        sends[planes + m][...] = xs[m * n_gx : m * n_gx + half].astype(BF16)


def forward(flux, w, src, own, dst, grid, cap, parts=20):
    n_sec, n_gx, n_gy = grid
    devices = n_sec * n_gx * n_gy
    total, width, _ = w.shape
    chunk = up(cap + 8, 16)
    fields = flux.shape[1]
    wide = SENT * width
    return pl.pallas_call(
        functools.partial(forward_kernel, parts, cap, grid),
        in_specs=[SMEM, SMEM, SMEM, VMEM, ANY],
        out_specs=[VMEM] * (2 * n_sec * n_gy) + [SMEM],
        scratch_shapes=[
            pltpu.VMEM(w.shape, BF16),
            pltpu.VMEM(flux.shape, BF16),
            pltpu.VMEM((devices * cap * fields, width), F32),
            pltpu.VMEM((devices * cap, width), F32),
            pltpu.VMEM((devices, chunk, wide), F32),
            pltpu.SMEM((devices,), jnp.int32),
            pltpu.SMEM((devices,), jnp.int32),
            pltpu.SemaphoreType.DMA((parts,)),
        ],
        out_shape=[jax.ShapeDtypeStruct((n_gx // 2, chunk, wide), BF16)] * (2 * n_sec * n_gy) + [jax.ShapeDtypeStruct((total,), jnp.int32)],
        compiler_params=kernel_params(58),
        cost_estimate=pl.CostEstimate(flops=2 * total * 8 * width * width, bytes_accessed=total * width * width * 2, transcendentals=0),
        name="forward_remap",
    )(src, own, dst, flux, w)


def merge_kernel(n_sources, *refs):
    sources, outs = refs[:n_sources], refs[n_sources:]
    chunk = sources[0].shape[1]
    height = outs[0].shape[0] - 8
    first = chunk - 8
    count = n_sources * chunk
    for z, out in enumerate(outs):
        ext = None
        where = []
        for source in sources:
            piece = source[z, first:chunk, :].astype(F32)
            where.append(piece[1:2, :chunk])
            ext = piece if ext is None else ext + piece
        where = jnp.concatenate(where, axis=1)
        hot = (iota((height, count), 0).astype(F32) == where).astype(F32).astype(BF16)
        sums = dot(hot, jnp.concatenate([source[z] for source in sources], axis=0), NN)
        row3 = jnp.concatenate([where, ext[3:4, count:]], axis=1)
        ext = jnp.where(iota((8, 1), 0) == 3, row3, ext)
        out[...] = jnp.concatenate([sums, ext], axis=0).astype(out.dtype)


def rows_kernel(tracers, currents, land, south, north):
    height, width = land.shape
    levels = tracers.shape[0] // 2 // height
    for out, edge, second in ((south, 0, 1), (north, height - 1, height - 2)):
        out[...] = jnp.concatenate(
            [
                tracers[pl.ds(edge, 2 * levels, stride=height), :],
                tracers[pl.ds(second, 2 * levels, stride=height), :],
                currents[pl.ds(edge, 2 * levels, stride=height), :],
                currents[pl.ds(levels * height + second, levels, stride=height), :],
                *[land[x : x + 1, :].astype(F32) for x in (edge, second)],
                jnp.zeros((out.shape[0] - 7 * levels - 2, width), F32),
            ],
            axis=0,
        ).astype(BF16)


def columns_kernel(tracers, currents, land, from_n, from_s, west, east, west_wide, east_wide):
    levels = tracers.shape[1]
    width = tracers.shape[3]
    last = width - 1
    lane = iota((1, width), 1)
    west_wide[...] = jnp.zeros_like(west_wide)
    east_wide[...] = jnp.zeros_like(east_wide)

    def put(plane, near, far):
        turned = plane.T
        for out, edge, second in ((west_wide, 0, 1), (east_wide, last, last - 1)):
            out[pl.ds(near, 1), :] = turned[edge : edge + 1]
            if far is not None:
                out[pl.ds(far, 1), :] = turned[second : second + 1]

    def level(l, _):
        for t in range(2):
            put(tracers[t, l], t * levels + l, (2 + t) * levels + l)
        put(currents[0, l], 4 * levels + l, 6 * levels + l)
        put(currents[1, l], 5 * levels + l, None)
        return 0

    lax.fori_loop(0, levels, level, 0, unroll=2)
    put(land[...].astype(F32), 7 * levels, 7 * levels + 1)
    base = 7 * levels + 8
    n_all, s_all = from_n[...].astype(F32), from_s[...].astype(F32)
    for start, stop, at in ((0, 2 * levels, 0), (4 * levels, 6 * levels, 2 * levels), (7 * levels, 7 * levels + 8, 4 * levels)):
        n, s = n_all[start:stop], s_all[start:stop]
        west_wide[base + at : base + at + stop - start] = jnp.where(lane == last, pltpu.roll(n, last, 1), s)
        east_wide[base + at : base + at + stop - start] = jnp.where(lane == last, n, pltpu.roll(s, 1, 1))
    west[...] = west_wide[...].astype(BF16)
    east[...] = east_wide[...].astype(BF16)


def plus_side(q, other, speed, speed_other, passable):
    return KH * passable * (other - q) - 0.25 * (speed + speed_other) * passable * (q + other)


def minus_side(q, other, speed, speed_other, passable):
    return KH * passable * (other - q) + 0.25 * (speed_other + speed) * passable * (other + q)


def level_profile(levels, width):
    depth = iota((levels, width), 0).astype(F32)
    return jnp.exp(-depth / 4.0) * (1.0 - jnp.exp(jnp.full((levels, width), -0.25, F32)))


def strip_step(q, q_plus, q_minus, across, across_plus, across_minus, along, corner_q, corner_along, wet, wet_plus, wet_minus, corner_wet, forcing):
    levels, width = q.shape
    lane = iota((1, width), 1)
    row = iota((levels, 1), 0)

    def ahead(x, corner):
        return jnp.where(lane == width - 1, corner, pltpu.roll(x, width - 1, 1))

    def behind(x, corner):
        return jnp.where(lane == 0, corner, pltpu.roll(x, 1, 1))

    total = plus_side(q, q_plus, across, across_plus, wet * wet_plus)
    total += minus_side(q, q_minus, across, across_minus, wet * wet_minus)
    total += plus_side(q, ahead(q, corner_q), along, ahead(along, corner_along), wet * ahead(wet, corner_wet))
    total += minus_side(q, behind(q, corner_q), along, behind(along, corner_along), wet * behind(wet, corner_wet))
    below = jnp.where(row < levels - 1, pltpu.roll(q, levels - 1, 0) - q, 0.0)
    above = jnp.where(row > 0, q - pltpu.roll(q, 1, 0), 0.0)
    return q + total + wet * (KV * (below - above) + forcing)


def strips(tracer, levels, inner, outer, flux):
    width = outer[0].shape[1]
    lane = iota((1, width), 1)
    base = 7 * levels + 8
    north, south, east, west = outer

    def part(x, at, count=levels):
        return x[at : at + count]

    def corners(at, count):
        e, w = part(east, base + at, count), part(west, base + at, count)
        n = jnp.where(lane == width - 1, e, pltpu.roll(w, 1, 1))
        s = jnp.where(lane == width - 1, pltpu.roll(e, width - 1, 1), w)
        return n, s, e, w

    corner_q = corners(tracer * levels, levels)
    corner_u = corners(2 * levels, levels)
    corner_v = corners(3 * levels, levels)
    corner_wet = corners(4 * levels, 1)
    top = (iota((levels, 1), 0) == 0).astype(F32)
    profile = level_profile(levels, width)
    results = []
    for side in range(4):
        near, far = inner[side], outer[side]
        beside, out = part(near, tracer * levels), part(far, (2 + tracer) * levels)
        mid = part(far, tracer * levels)
        speed = 5 if side < 2 else 4
        along = part(far, (9 - speed) * levels)
        corner_along = (corner_u if side < 2 else corner_v)[side]
        across, across_in, across_out = part(far, speed * levels), part(near, speed * levels), part(far, 6 * levels)
        wet, wet_in, wet_out = part(far, 7 * levels, 1), part(near, 7 * levels, 1), part(far, 7 * levels + 1, 1)
        shortwave, heat, salt = flux[side]
        forcing = 0.3 * profile * shortwave + top * heat if tracer == 0 else top * salt
        if side % 2 == 0:
            pairs = (out, beside, across, across_out, across_in)
            wets = (wet, wet_out, wet_in)
        else:
            pairs = (beside, out, across, across_in, across_out)
            wets = (wet, wet_in, wet_out)
        results.append(strip_step(mid, *pairs, along, corner_q[side], corner_along, *wets, corner_wet[side], forcing))
    return results


def shifts(plane, north, south, east, west):
    height, width = plane.shape
    lane, row = iota(plane.shape, 1), iota(plane.shape, 0)
    return (
        jnp.where(lane == width - 1, east, pltpu.roll(plane, width - 1, 1)),
        jnp.where(lane == 0, west, pltpu.roll(plane, 1, 1)),
        jnp.where(row == height - 1, north, pltpu.roll(plane, height - 1, 0)),
        jnp.where(row == 0, south, pltpu.roll(plane, 1, 0)),
    )


def wet_products(wet, north, south, east, west):
    return [wet * other for other in shifts(wet, north, south, east, west)]


def coefficients(u, v, u_east, u_west, v_north, v_south, passable):
    east, west, north, south = passable
    height, width = u.shape
    lane, row = iota(u.shape, 1), iota(u.shape, 0)
    e = jnp.where(lane == width - 1, u_east, pltpu.roll(u, width - 1, 1))
    w = jnp.where(lane == 0, u_west, pltpu.roll(u, 1, 1))
    n = jnp.where(row == height - 1, v_north, pltpu.roll(v, height - 1, 0))
    s = jnp.where(row == 0, v_south, pltpu.roll(v, 1, 0))
    flow_e, flow_w = 0.25 * (u + e) * east, 0.25 * (w + u) * west
    flow_n, flow_s = 0.25 * (v + n) * north, 0.25 * (s + v) * south
    own = 1.0 + (flow_w - flow_e) + (flow_s - flow_n) - KH * (east + west + north + south)
    return own, KH * east - flow_e, KH * west + flow_w, KH * north - flow_n, KH * south + flow_s


def column(turned, index, lane):
    return pltpu.roll(turned, lax.rem(lane - index + 2 * turned.shape[1], turned.shape[1]), 1)


def corrected(edge, x_rows):
    row = iota((edge.shape[0], 1), 0)
    for at, x in x_rows:
        edge = edge + jnp.where(row == at, 0.1 * x, 0.0)
    return edge


def corrected_edges(levels, ext, stress_u, stress_v, near, far):
    height, width = stress_u.shape
    last = width - 1
    lane = iota((1, width), 1)

    def block(r, b):
        return ext[r : r + 1, b * width : (b + 1) * width]

    u, v, second = 4 * levels, 5 * levels, 6 * levels
    base = 7 * levels + 8
    corners = []
    for b in (3, 4):
        ne, nw, se, sw = [block(r, b) for r in (4, 5, 6, 7)]
        corners.append((jnp.where(lane == last, pltpu.roll(ne, last, 1), se), jnp.where(lane == last, nw, pltpu.roll(sw, 1, 1))))
    turned = stress_u.T
    own = [[(v, stress_v[last:])], [(v, stress_v[0:1])], [(u, turned[last:])], [(u, turned[0:1])]]
    beside = [
        [(u, block(0, 3)), (v, block(0, 4)), (second, block(1, 4))],
        [(u, block(2, 3)), (v, block(2, 4)), (second, block(3, 4))],
        [(u, block(6, 0)), (v, block(7, 0)), (second, block(5, 2)), (base + 2 * levels, corners[0][0]), (base + 3 * levels, corners[1][0])],
        [(u, block(6, 1)), (v, block(7, 1)), (second, block(7, 2)), (base + 2 * levels, corners[0][1]), (base + 3 * levels, corners[1][1])],
    ]
    near = [corrected(edge[...].astype(F32), x) for edge, x in zip(near, own)]
    return near, [corrected(edge[...].astype(F32), x) for edge, x in zip(far, beside)]


def surface_kernel(grid, chunk, levels, *refs):
    n_sec, n_gx, n_gy = grid
    planes = n_sec * n_gy
    parts, refs = refs[:n_gx], refs[n_gx:]
    tracers, currents, land, own_n, own_s, own_e, own_w, from_n, from_s, from_e, from_w, *refs = refs
    back, flux, rim = refs
    height, width = land.shape
    last = width - 1
    lane = iota((1, width), 1)
    sums = parts[0][...]
    for part in parts[1:]:
        sums = sums + part[...].astype(F32)
    sums, ext = sums[:height], sums[height : height + 8]
    shortwave, heat, salt, stress_u, stress_v = [sums[:, f * width : (f + 1) * width] for f in range(SENT)]
    wet = land[...].astype(F32)
    u0 = currents[0, 0] + 0.1 * stress_u
    v0 = currents[1, 0] + 0.1 * stress_v
    flux[0], flux[1], flux[2], flux[3], flux[4] = shortwave, heat, salt, stress_u, stress_v
    rim[...] = ext

    near, far = corrected_edges(levels, ext, stress_u, stress_v, (own_n, own_s, own_e, own_w), (from_n, from_s, from_e, from_w))
    far_n, far_s, far_e, far_w = far
    e_turned, w_turned = far_e[:width].T, far_w[:width].T
    east = lambda index: column(e_turned, index, last)
    west = lambda index: column(w_turned, index, 0)
    passable = wet_products(
        wet, far_n[7 * levels : 7 * levels + 1], far_s[7 * levels : 7 * levels + 1], east(7 * levels), west(7 * levels)
    )
    lines = strips(0, levels, near, far, rim_flux(ext, width))
    profile = level_profile(levels, width)
    mix = KV * wet
    warm = 0.3 * wet * shortwave

    def weights(l, u, v):
        v_n, v_s = [x[5 * levels + l : 5 * levels + l + 1] for x in (far_n, far_s)]
        return coefficients(u, v, east(4 * levels + l), west(4 * levels + l), v_n, v_s, passable)

    def horizontal(c, q, halo):
        e, w, n, s = shifts(q, *halo)
        return c[0] * q + c[1] * e + c[2] * w + c[3] * n + c[4] * s

    def start(l):
        return far_n[l : l + 1], far_s[l : l + 1], east(l), west(l)

    q0, q1, q2 = tracers[0, 0], tracers[0, 1], tracers[0, 2]
    c0 = weights(0, u0, v0)
    c1 = weights(1, currents[0, 1], currents[1, 1])
    t0 = horizontal(c0, q0, start(0)) + mix * (q1 - q0) + warm * profile[0:1] + wet * heat
    t1 = horizontal(c1, q1, start(1)) + mix * ((q2 - q1) - (q1 - q0)) + warm * profile[1:2]
    sides = jnp.concatenate([lines[2][0:8], lines[3][0:8], jnp.zeros((width - 16, width), F32)], axis=0).T
    halo = lines[0][0:1], lines[1][0:1], column(sides, 0, last), column(sides, 8, 0)
    t0 = horizontal(c0, t0, halo) + mix * (t1 - t0) + warm * profile[0:1] + wet * heat
    sst = t0.astype(BF16)
    plane = lax.axis_index("sec") * n_gy + lax.axis_index("gy")
    line = lax.axis_index("gx")
    for z, part in enumerate(parts):
        where = part[height + 3 : height + 4, : planes * chunk].astype(F32)
        hot = (iota((height, planes * chunk), 0).astype(F32) == where).astype(F32)
        picked = dot(hot.T.astype(BF16), sst, NN).reshape(planes, chunk, width)
        for m in range(planes):
            there = plane ^ m
            device = (lax.div(there, n_gy) * n_gx + (line ^ z)) * n_gy + lax.rem(there, n_gy)
            back[device] = picked[m, : back.shape[1]].astype(BF16)


def rim_flux(ext, width):
    def block(r, b):
        return ext[r : r + 1, b * width : (b + 1) * width]

    return (
        (block(0, 0), block(0, 1), block(0, 2)),
        (block(2, 0), block(2, 1), block(2, 2)),
        (block(4, 0), block(5, 0), block(4, 2)),
        (block(4, 1), block(5, 1), block(6, 2)),
    )


def stencil_kernel(
    tracers_in, currents_in, land, flux, rim, own_n, own_s, own_e, own_w, from_n, from_s, from_e, from_w,
    result, tracers, currents, out, held, weights, edge_n, edge_s, line_n, line_s, depth, forced, passing, sems,
):
    copies = [
        pltpu.make_async_copy(tracers_in, tracers, sems.at[0]),
        pltpu.make_async_copy(currents_in, currents, sems.at[1]),
    ]
    for copy in copies:
        copy.start()
    levels = tracers.shape[1]

    def send(l):
        return pltpu.make_async_copy(out.at[:, l], result.at[:, l], sems.at[2 + l])

    height, width = land.shape
    last = width - 1
    wet = land[...].astype(F32)
    near, far = corrected_edges(
        levels, rim[...], flux[3], flux[4], (own_n, own_s, own_e, own_w), (from_n, from_s, from_e, from_w)
    )
    far_n, far_s, far_e, far_w = far
    edge_n[...], edge_s[...] = far_n, far_s
    e_turned, w_turned = far_e[:width].T, far_w[:width].T
    at = 7 * levels
    for i, x in enumerate(
        wet_products(wet, far_n[at : at + 1], far_s[at : at + 1], column(e_turned, at, last), column(w_turned, at, 0))
    ):
        passing[i] = x
    forced[0], forced[1], forced[2] = 0.3 * wet * flux[0], wet * flux[1], wet * flux[2]
    depth[...] = level_profile(levels, width)
    columns = []
    for tracer in range(2):
        lines = strips(
            tracer, levels, near, far, rim_flux(rim[...], width)
        )
        line_n[tracer * levels : (tracer + 1) * levels] = lines[0]
        line_s[tracer * levels : (tracer + 1) * levels] = lines[1]
        columns.append(lines[2:])
    blank = jnp.zeros((width - 2 * levels, width), F32)
    e_later, w_later = [jnp.concatenate([columns[0][i], columns[1][i], blank], axis=0).T for i in range(2)]

    def update(c, q, halo, under, over, forcing):
        e, w, n, s = shifts(q, *halo)
        mixed = KV * land[...].astype(F32) * ((under - q) - (q - over))
        return c[0] * q + c[1] * e + c[2] * w + c[3] * n + c[4] * s + mixed + forcing

    def forcing(tracer, l):
        top = jnp.where(l == 0, 1.0, 0.0)
        if tracer == 0:
            return forced[0] * depth[pl.ds(l, 1), :] + top * forced[1]
        return top * forced[2]

    for copy in copies:
        copy.wait()
    currents[0, 0] = currents[0, 0] + 0.1 * flux[3]
    currents[1, 0] = currents[1, 0] + 0.1 * flux[4]

    def first_step(l, _):
        u, v = currents[0, l], currents[1, l]
        row = 5 * levels + l
        c = coefficients(
            u, v, column(e_turned, 4 * levels + l, last), column(w_turned, 4 * levels + l, 0),
            edge_n[pl.ds(row, 1), :], edge_s[pl.ds(row, 1), :], [passing[i] for i in range(4)],
        )
        for i, x in enumerate(c):
            weights[i, l] = x
        for tracer in range(2):
            row = tracer * levels + l
            halo = edge_n[pl.ds(row, 1), :], edge_s[pl.ds(row, 1), :], column(e_turned, row, last), column(w_turned, row, 0)
            under, over = tracers[tracer, jnp.minimum(l + 1, levels - 1)], tracers[tracer, jnp.maximum(l - 1, 0)]
            held[tracer, l] = update(c, tracers[tracer, l], halo, under, over, forcing(tracer, l))
        return 0

    lax.fori_loop(0, levels, first_step, 0)

    def second_step(l, _):
        c = [weights[i, l] for i in range(5)]
        for tracer in range(2):
            row = tracer * levels + l
            halo = line_n[pl.ds(row, 1), :], line_s[pl.ds(row, 1), :], column(e_later, row, last), column(w_later, row, 0)
            under, over = held[tracer, jnp.minimum(l + 1, levels - 1)], held[tracer, jnp.maximum(l - 1, 0)]
            out[tracer, l] = update(c, held[tracer, l], halo, under, over, forcing(tracer, l))
        send(l).start()
        return 0

    lax.fori_loop(0, levels, second_step, 0)
    for l in range(levels):
        send(l).wait()


def backward_kernel(parts, slots_in, src, back, w, out, held, wide, picked, terms, slots, sems):
    total, width = terms.shape
    blocks = out.shape[0]
    batch = total // parts

    def copy(c):
        return pltpu.make_async_copy(w.at[pl.ds(c * batch, batch)], held.at[pl.ds(c * batch, batch)], sems.at[c])

    slots_copy = pltpu.make_async_copy(slots_in, slots, sems.at[parts])
    slots_copy.start()
    for c in range(parts):
        copy(c).start()
    slots_copy.wait()
    wide[...] = back[...].astype(F32).reshape(wide.shape)

    def pick(i, _):
        for j in range(16):
            picked[pl.ds(i * 16 + j, 1), :] = wide[pl.ds(slots[i * 16 + j], 1), :]
        return 0

    lax.fori_loop(0, total // 16, pick, 0, unroll=2)
    row = iota((16, width), 0)

    def work(c, _):
        copy(c).wait()
        for g in range(batch // 16):
            at = pl.multiple_of(c * batch + g * 16, 16)
            rows = picked[pl.ds(at, 16), :]
            left = [jnp.where((row == r) | (row == 8 + r), rows, 0.0).astype(BF16) for r in range(8)]
            block = held[pl.ds(at, 16)].reshape(2, 8 * width, width)
            both = dot(jnp.concatenate(left, axis=1), jnp.concatenate([block[0], block[1]], axis=1), NN)
            terms[pl.ds(at, 8), :] = both[:8, :width]
            terms[pl.ds(at + 8, 8), :] = both[8:, width:]
        return 0

    lax.fori_loop(0, parts, work, 0)
    hot = (iota((blocks, total), 0) == src[...]).astype(F32).astype(BF16)
    value = terms[...]
    high = value.astype(BF16)
    low = (value - high.astype(F32)).astype(BF16)
    both = dot(hot, jnp.concatenate([high, low], axis=1), NN)
    out[...] = both[:, :width] + both[:, width:]


def backward(back, w, src, slots, blocks, parts=20):
    total, width, _ = w.shape
    devices, cap, _ = back.shape
    return pl.pallas_call(
        functools.partial(backward_kernel, parts),
        in_specs=[ANY, VMEM, VMEM, ANY],
        out_specs=VMEM,
        scratch_shapes=[
            pltpu.VMEM(w.shape, BF16),
            pltpu.VMEM((devices * cap, width), F32),
            pltpu.VMEM((total, width), F32),
            pltpu.VMEM((total, width), F32),
            pltpu.SMEM((total,), jnp.int32),
            pltpu.SemaphoreType.DMA((parts + 1,)),
        ],
        out_shape=jax.ShapeDtypeStruct((blocks, width), F32),
        compiler_params=kernel_params(46),
        cost_estimate=pl.CostEstimate(flops=2 * total * 8 * width * width, bytes_accessed=total * width * width * 2, transcendentals=0),
        name="backward_remap",
    )(slots, src.reshape(1, total), back, w)


def kernel(body, outs, name, mebibytes, bytes_accessed, scratch=(), **specs):
    return pl.pallas_call(
        body,
        out_shape=[jax.ShapeDtypeStruct(shape, dtype) for shape, dtype in outs],
        scratch_shapes=list(scratch),
        compiler_params=kernel_params(mebibytes),
        cost_estimate=pl.CostEstimate(flops=bytes_accessed, bytes_accessed=bytes_accessed, transcendentals=0),
        name=name,
        **specs,
    )


def neighbours(axis):
    count = lax.axis_size(axis)
    forward_pairs = [(i, i + 1) for i in range(count - 1)]
    return forward_pairs, [(b, a) for a, b in forward_pairs]


def swapped(array, axes, count, step):
    return lax.ppermute(array, axes, [(i, i ^ step) for i in range(count)])


def on_device(atm_flux, remap_weights, remap_src, remap_dst, remap_owner, tracers, currents, land_sea):
    grid = n_sec, n_gx, n_gy = [lax.axis_size(axis) for axis in EVERY]
    planes = n_sec * n_gy
    total, width, _ = remap_weights.shape
    _, levels, height, _ = tracers.shape
    cap = up(2 * total // (planes * n_gx), 8)
    wide = SENT * width

    *sends, slots = forward(atm_flux, remap_weights, remap_src, remap_owner.reshape(1, total), remap_dst, grid, cap)
    chunk = sends[0].shape[1]
    far_sends, near_sends = sends[:planes], sends[planes:]

    def in_plane(chunks):
        return [chunks[0]] + [swapped(chunks[m], ("sec", "gy"), planes, m) for m in range(1, planes)]

    def merge(chunks, dtypes):
        outs = [((height + 8, wide), dtype) for dtype in dtypes]
        return kernel(functools.partial(merge_kernel, planes), outs, "merge", 24, 1 << 22)(*chunks)

    far = in_plane(far_sends)
    far[1], near_sends, tracers_there, currents_there = lax.optimization_barrier((far[1], near_sends, tracers, currents))
    near = in_plane(near_sends)

    side = (width, width)
    end = (7 * levels + 80, width)
    to_north, to_south = neighbours(NORTH)
    to_east, to_west = neighbours("gy")
    own_s, own_n = kernel(rows_kernel, [(side, BF16)] * 2, "edge_rows", 16, 1 << 20)(
        tracers_there.reshape(-1, width), currents_there.reshape(-1, width), land_sea
    )
    from_n = lax.ppermute(own_s, NORTH, to_south)
    from_s = lax.ppermute(own_n, NORTH, to_north)
    far = merge(far, [BF16] * (n_gx // 2))
    far, from_n, from_s = lax.optimization_barrier((far, from_n, from_s))
    far = [swapped(part, "gx", n_gx, n_gx // 2 + m) for m, part in enumerate(far)]
    own_w, own_e = kernel(columns_kernel, [(end, BF16)] * 2, "edge_columns", 16, 1 << 22, [pltpu.VMEM(end, F32)] * 2)(
        tracers, currents, land_sea, from_n, from_s
    )
    from_e = lax.ppermute(own_w, "gy", to_west)
    from_w = lax.ppermute(own_e, "gy", to_east)
    near = merge(near, [F32] + [BF16] * (n_gx // 2 - 1))
    parts = [near[0]] + [swapped(near[m], "gx", n_gx, m) for m in range(1, n_gx // 2)] + far

    edges = own_n, own_s, own_e, own_w, from_n, from_s, from_e, from_w
    back, flux, rim = kernel(
        functools.partial(surface_kernel, grid, chunk, levels),
        [((planes * n_gx, cap, width), BF16), ((5, height, width), F32), ((8, wide), F32)],
        "surface",
        58,
        1 << 22,
    )(*parts, tracers[0:1, 0:3], currents[:, 0:2], land_sea, *edges)
    returned = lax.all_to_all(back, EVERY, split_axis=0, concat_axis=0, tiled=True)

    plane = (height, width)
    (tracers_out,) = kernel(
        stencil_kernel,
        [(tracers.shape, F32)],
        "substeps",
        58,
        1 << 24,
        [
            pltpu.VMEM(tracers.shape, F32),
            pltpu.VMEM(currents.shape, F32),
            pltpu.VMEM(tracers.shape, F32),
            pltpu.VMEM(tracers.shape, F32),
            pltpu.VMEM((5, levels) + plane, F32),
            pltpu.VMEM(side, F32),
            pltpu.VMEM(side, F32),
            pltpu.VMEM((2 * levels, width), F32),
            pltpu.VMEM((2 * levels, width), F32),
            pltpu.VMEM((levels, width), F32),
            pltpu.VMEM((3,) + plane, F32),
            pltpu.VMEM((4,) + plane, F32),
            pltpu.SemaphoreType.DMA((2 + levels,)),
        ],
        in_specs=[ANY, ANY] + [VMEM] * 11,
        out_specs=[ANY],
    )(tracers, currents, land_sea, flux, rim, *edges)
    return tracers_out, backward(returned, remap_weights, remap_src, slots, atm_flux.shape[0])


def solution(mesh):
    return jax.shard_map(
        on_device,
        mesh=mesh,
        in_specs=(
            P(EVERY, None, None),
            P(EVERY, None, None),
            P(EVERY),
            P(EVERY),
            P(EVERY, None),
            P(None, None, NORTH, "gy"),
            P(None, None, NORTH, "gy"),
            P(NORTH, "gy"),
        ),
        out_specs=(P(None, None, NORTH, "gy"), P(EVERY, None)),
        check_vma=False,
    )
```

```python
import functools

import jax
import jax.numpy as jnp
from jax import lax
from jax.experimental import pallas as pl
from jax.experimental.pallas import tpu as pltpu
from jax.sharding import PartitionSpec as P

F32 = jnp.float32
BF16 = jnp.bfloat16
NT = (((1,), (1,)), ((), ()))
NN = (((1,), (0,)), ((), ()))
TN = (((0,), (0,)), ((), ()))
EVERY = ("sec", "gx", "gy")
NORTH = ("sec", "gx")
SENT = 5
KH = 0.1
KV = 0.1


def dot(left, right, dims):
    return lax.dot_general(left, right, dims, preferred_element_type=F32)


def iota(shape, dim):
    return lax.broadcasted_iota(jnp.int32, shape, dim)


def up(number, step):
    return -(-number // step) * step


def kernel_params(mebibytes):
    return pltpu.CompilerParams(vmem_limit_bytes=mebibytes << 20)


VMEM = pl.BlockSpec(memory_space=pltpu.VMEM)
SMEM = pl.BlockSpec(memory_space=pltpu.SMEM)
ANY = pl.BlockSpec(memory_space=pl.ANY)


def forward_kernel(parts, cap, grid, src, own, dst, flux, w, *refs):
    sends, (slots, held, mixed, acc, rows, xs, counts, renumbered, sems) = refs[:-9], refs[-9:]
    n_sec, n_gx, n_gy = grid
    devices, chunk, wide = xs.shape
    total, width, _ = held.shape
    batch = total // parts
    fields = flux.shape[1]
    first = chunk - 8
    last = width - 1

    def copy(c):
        return pltpu.make_async_copy(w.at[pl.ds(c * batch, batch)], held.at[pl.ds(c * batch, batch)], sems.at[c])

    for c in range(parts):
        copy(c).start()

    plane = lax.axis_index("sec") * n_gy + lax.axis_index("gy")
    line = lax.axis_index("gx")

    def renumber(owner):
        x = lax.div(owner, n_gy)
        there = lax.div(x, n_gx) * n_gy + lax.rem(owner, n_gy)
        return (there ^ plane) * n_gx + (lax.rem(x, n_gx) ^ line)

    def clear(o, _):
        counts[o] = 0
        renumbered[o] = renumber(o)
        return 0

    lax.fori_loop(0, devices, clear, 0)
    rows[...] = jnp.full_like(rows, 255.0)
    acc[...] = jnp.zeros_like(acc)
    xs[...] = jnp.zeros_like(xs)
    full = flux[...].astype(F32)
    one = [full[:, f : f + 1] for f in range(fields)]
    heat = 0.2 * (one[1] + one[2] + one[3]) - 0.15 * one[5]
    salt = 0.2 * one[4] - 0.1 * one[5]
    heat_high = heat.astype(BF16).astype(F32)
    salt_high = salt.astype(BF16).astype(F32)
    mixed[...] = jnp.concatenate(
        [one[0], heat_high, salt_high, one[6], one[7], heat - heat_high, salt - salt_high, jnp.zeros_like(heat)], axis=1
    ).astype(BF16)

    low_rows = iota((fields, width), 0)
    low_rows = (low_rows == 1) | (low_rows == 2)

    def work(c, _):
        copy(c).wait()
        for b in range(0, batch, 2):
            k = c * batch + b
            left = jnp.concatenate([mixed[src[k]], mixed[src[k + 1]]], axis=0)
            both = dot(left, held[pl.ds(k, 2)].reshape(2 * width, width), NT)
            for z, part in enumerate((both[:fields, :width], both[fields:, width:])):
                part = part + jnp.where(low_rows, pltpu.roll(part, fields - 4, 0), 0.0)
                owner = own[0, k + z]
                at = counts[owner]
                counts[owner] = at + 1
                at = jnp.minimum(at, cap - 1)
                slots[k + z] = owner * cap + at
                slot = renumbered[owner] * cap + at
                acc[pl.ds(pl.multiple_of(slot * fields, fields), fields), :] = part
                rows[pl.ds(slot, 1), :] = jnp.full((1, width), dst[k + z].astype(F32), F32)
        return 0

    lax.fori_loop(0, parts, work, 0)

    lane = iota((cap, width), 1).astype(F32)
    sub = iota((cap, width), 0).astype(F32)
    row = iota((24, wide), 0)
    picks = {
        4: (0, 0), 5: (1, 0), 6: (3, 0), 7: (4, 0), 12: (0, last), 13: (1, last), 14: (3, last), 15: (4, last),
        20: (2, 0), 21: (3, 1), 22: (2, last), 23: (3, last - 1),
    }
    pick = jnp.full((24, wide), -1, jnp.int32)
    for at, (field, column) in picks.items():
        pick = jnp.where(row == at, field * width + column, pick)
    select = (iota((24, wide), 1) == pick).astype(F32).astype(BF16)
    row = iota((8, cap), 0)
    wanted = jnp.zeros((8, cap), F32)
    for at, x in enumerate((0, 1, last, last - 1, 0, 0, last, last)):
        wanted = jnp.where(row == at, float(x), wanted)
    group = 16

    def owners(g, _):
        ds = [g * group + j for j in range(group)]
        five = []
        for d in ds:
            x = [acc[pl.ds(d * cap * fields + f, cap, stride=fields), :] for f in range(SENT)]
            x = jnp.concatenate(x, axis=1)
            xs[d, 0:cap, :] = x
            five.append(x.astype(BF16))
        where = [rows[pl.ds(pl.multiple_of(d * cap, 8), cap), :] for d in ds]
        hot = [(lane == r).astype(F32).astype(BF16) for r in where]
        flat = [jnp.sum(jnp.where(lane == sub, r, 0.0), axis=0, keepdims=True) for r in where]
        flat = [jnp.where(lane[:1] < cap, f, 255.0) for f in flat]
        edge = [dot(select, x, NT).astype(BF16) for x in five]
        sides = [dot(e, h, NN) for e, h in zip(edge, hot)]
        ends = [dot((f[:, :cap] == wanted).astype(F32).astype(BF16), x, NN) for f, x in zip(flat, five)]
        for d, f, side, end in zip(ds, flat, sides, ends):
            here = lax.div(d, n_gx) ^ plane
            here = (lax.div(here, n_gy) * n_gx + (lax.rem(d, n_gx) ^ line)) * n_gy + lax.rem(here, n_gy)

            def at(offset):
                return renumbered[lax.rem(here + offset + 2 * devices, devices)]

            south_of, north_of, west_of, east_of = at(-n_gy), at(n_gy), at(-1), at(1)

            xs[south_of, first : first + 1, :] = end[0:1]
            xs[south_of, first + 1 : first + 2, 4 * width :] = end[1:2, 4 * width :]
            xs[north_of, first + 2 : first + 3, :] = end[2:3]
            xs[north_of, first + 3 : first + 4, 4 * width :] = end[3:4, 4 * width :]
            xs[at(-n_gy - 1), first + 4 : first + 5, 3 * width :] = end[4:5, 3 * width :]
            xs[at(-n_gy + 1), first + 5 : first + 6, 3 * width :] = end[5:6, 3 * width :]
            xs[at(n_gy - 1), first + 6 : first + 7, 3 * width :] = end[6:7, 3 * width :]
            xs[at(n_gy + 1), first + 7 : first + 8, 3 * width :] = end[7:8, 3 * width :]
            xs[west_of, first + 4 : first + 8, 0:width] = side[4:8]
            xs[east_of, first + 4 : first + 8, width : 2 * width] = side[12:16]
            xs[west_of, first + 4 : first + 6, 2 * width : 3 * width] = side[20:22]
            xs[east_of, first + 6 : first + 8, 2 * width : 3 * width] = side[22:24]
            xs[d, first + 1 : first + 2, 0:width] = f
        return 0

    lax.fori_loop(0, devices // group, owners, 0)

    for m, send in enumerate(sends):
        send[...] = xs[m * n_gx : (m + 1) * n_gx].astype(BF16)


def forward(flux, w, src, own, dst, grid, cap, parts=8):
    n_sec, n_gx, n_gy = grid
    devices = n_sec * n_gx * n_gy
    total, width, _ = w.shape
    chunk = up(cap + 8, 16)
    fields = flux.shape[1]
    wide = SENT * width
    return pl.pallas_call(
        functools.partial(forward_kernel, parts, cap, grid),
        in_specs=[SMEM, SMEM, SMEM, VMEM, ANY],
        out_specs=[VMEM] * (n_sec * n_gy) + [SMEM],
        scratch_shapes=[
            pltpu.VMEM(w.shape, BF16),
            pltpu.VMEM(flux.shape, BF16),
            pltpu.VMEM((devices * cap * fields, width), F32),
            pltpu.VMEM((devices * cap, width), F32),
            pltpu.VMEM((devices, chunk, wide), F32),
            pltpu.SMEM((devices,), jnp.int32),
            pltpu.SMEM((devices,), jnp.int32),
            pltpu.SemaphoreType.DMA((parts,)),
        ],
        out_shape=[jax.ShapeDtypeStruct((n_gx, chunk, wide), BF16)] * (n_sec * n_gy) + [jax.ShapeDtypeStruct((total,), jnp.int32)],
        compiler_params=kernel_params(58),
        cost_estimate=pl.CostEstimate(flops=2 * total * 8 * width * width, bytes_accessed=total * width * width * 2, transcendentals=0),
        name="forward_remap",
    )(src, own, dst, flux, w)


def merge_kernel(n_sources, *refs):
    sources, outs = refs[:n_sources], refs[n_sources:]
    chunk = sources[0].shape[1]
    height = outs[0].shape[0] - 8
    first = chunk - 8
    count = n_sources * chunk
    for z, out in enumerate(outs):
        ext = None
        where = []
        for source in sources:
            piece = source[z, first:chunk, :].astype(F32)
            where.append(piece[1:2, :chunk])
            ext = piece if ext is None else ext + piece
        where = jnp.concatenate(where, axis=1)
        hot = (iota((height, count), 0).astype(F32) == where).astype(F32).astype(BF16)
        sums = dot(hot, jnp.concatenate([source[z] for source in sources], axis=0), NN)
        row3 = jnp.concatenate([where, ext[3:4, count:]], axis=1)
        ext = jnp.where(iota((8, 1), 0) == 3, row3, ext)
        out[...] = jnp.concatenate([sums, ext], axis=0).astype(out.dtype)


def rows_kernel(tracers, currents, land, south, north):
    height, width = land.shape
    levels = tracers.shape[0] // 2 // height
    for out, edge, second in ((south, 0, 1), (north, height - 1, height - 2)):
        out[...] = jnp.concatenate(
            [
                tracers[pl.ds(edge, 2 * levels, stride=height), :],
                tracers[pl.ds(second, 2 * levels, stride=height), :],
                currents[pl.ds(edge, 2 * levels, stride=height), :],
                currents[pl.ds(levels * height + second, levels, stride=height), :],
                *[land[x : x + 1, :].astype(F32) for x in (edge, second)],
                jnp.zeros((out.shape[0] - 7 * levels - 2, width), F32),
            ],
            axis=0,
        ).astype(BF16)


def columns_kernel(tracers, currents, land, from_n, from_s, west, east, west_wide, east_wide):
    levels = tracers.shape[1]
    width = tracers.shape[3]
    last = width - 1
    lane = iota((1, width), 1)
    west_wide[...] = jnp.zeros_like(west_wide)
    east_wide[...] = jnp.zeros_like(east_wide)

    def put(plane, near, far):
        turned = plane.T
        for out, edge, second in ((west_wide, 0, 1), (east_wide, last, last - 1)):
            out[pl.ds(near, 1), :] = turned[edge : edge + 1]
            if far is not None:
                out[pl.ds(far, 1), :] = turned[second : second + 1]

    def level(l, _):
        for t in range(2):
            put(tracers[t, l], t * levels + l, (2 + t) * levels + l)
        put(currents[0, l], 4 * levels + l, 6 * levels + l)
        put(currents[1, l], 5 * levels + l, None)
        return 0

    lax.fori_loop(0, levels, level, 0, unroll=2)
    put(land[...].astype(F32), 7 * levels, 7 * levels + 1)
    base = 7 * levels + 8
    n_all, s_all = from_n[...].astype(F32), from_s[...].astype(F32)
    for start, stop, at in ((0, 2 * levels, 0), (4 * levels, 6 * levels, 2 * levels), (7 * levels, 7 * levels + 8, 4 * levels)):
        n, s = n_all[start:stop], s_all[start:stop]
        west_wide[base + at : base + at + stop - start] = jnp.where(lane == last, pltpu.roll(n, last, 1), s)
        east_wide[base + at : base + at + stop - start] = jnp.where(lane == last, n, pltpu.roll(s, 1, 1))
    west[...] = west_wide[...].astype(BF16)
    east[...] = east_wide[...].astype(BF16)


def plus_side(q, other, speed, speed_other, passable):
    return KH * passable * (other - q) - 0.25 * (speed + speed_other) * passable * (q + other)


def minus_side(q, other, speed, speed_other, passable):
    return KH * passable * (other - q) + 0.25 * (speed_other + speed) * passable * (other + q)


def level_profile(levels, width):
    depth = iota((levels, width), 0).astype(F32)
    return jnp.exp(-depth / 4.0) * (1.0 - jnp.exp(jnp.full((levels, width), -0.25, F32)))


def strip_step(q, q_plus, q_minus, across, across_plus, across_minus, along, corner_q, corner_along, wet, wet_plus, wet_minus, corner_wet, forcing):
    levels, width = q.shape
    lane = iota((1, width), 1)
    row = iota((levels, 1), 0)

    def ahead(x, corner):
        return jnp.where(lane == width - 1, corner, pltpu.roll(x, width - 1, 1))

    def behind(x, corner):
        return jnp.where(lane == 0, corner, pltpu.roll(x, 1, 1))

    total = plus_side(q, q_plus, across, across_plus, wet * wet_plus)
    total += minus_side(q, q_minus, across, across_minus, wet * wet_minus)
    total += plus_side(q, ahead(q, corner_q), along, ahead(along, corner_along), wet * ahead(wet, corner_wet))
    total += minus_side(q, behind(q, corner_q), along, behind(along, corner_along), wet * behind(wet, corner_wet))
    below = jnp.where(row < levels - 1, pltpu.roll(q, levels - 1, 0) - q, 0.0)
    above = jnp.where(row > 0, q - pltpu.roll(q, 1, 0), 0.0)
    return q + total + wet * (KV * (below - above) + forcing)


def strips(tracer, levels, inner, outer, flux):
    width = outer[0].shape[1]
    lane = iota((1, width), 1)
    base = 7 * levels + 8
    north, south, east, west = outer

    def part(x, at, count=levels):
        return x[at : at + count]

    def corners(at, count):
        e, w = part(east, base + at, count), part(west, base + at, count)
        n = jnp.where(lane == width - 1, e, pltpu.roll(w, 1, 1))
        s = jnp.where(lane == width - 1, pltpu.roll(e, width - 1, 1), w)
        return n, s, e, w

    corner_q = corners(tracer * levels, levels)
    corner_u = corners(2 * levels, levels)
    corner_v = corners(3 * levels, levels)
    corner_wet = corners(4 * levels, 1)
    top = (iota((levels, 1), 0) == 0).astype(F32)
    profile = level_profile(levels, width)
    results = []
    for side in range(4):
        near, far = inner[side], outer[side]
        beside, out = part(near, tracer * levels), part(far, (2 + tracer) * levels)
        mid = part(far, tracer * levels)
        speed = 5 if side < 2 else 4
        along = part(far, (9 - speed) * levels)
        corner_along = (corner_u if side < 2 else corner_v)[side]
        across, across_in, across_out = part(far, speed * levels), part(near, speed * levels), part(far, 6 * levels)
        wet, wet_in, wet_out = part(far, 7 * levels, 1), part(near, 7 * levels, 1), part(far, 7 * levels + 1, 1)
        shortwave, heat, salt = flux[side]
        forcing = 0.3 * profile * shortwave + top * heat if tracer == 0 else top * salt
        if side % 2 == 0:
            pairs = (out, beside, across, across_out, across_in)
            wets = (wet, wet_out, wet_in)
        else:
            pairs = (beside, out, across, across_in, across_out)
            wets = (wet, wet_in, wet_out)
        results.append(strip_step(mid, *pairs, along, corner_q[side], corner_along, *wets, corner_wet[side], forcing))
    return results


def shifts(plane, north, south, east, west):
    height, width = plane.shape
    lane, row = iota(plane.shape, 1), iota(plane.shape, 0)
    return (
        jnp.where(lane == width - 1, east, pltpu.roll(plane, width - 1, 1)),
        jnp.where(lane == 0, west, pltpu.roll(plane, 1, 1)),
        jnp.where(row == height - 1, north, pltpu.roll(plane, height - 1, 0)),
        jnp.where(row == 0, south, pltpu.roll(plane, 1, 0)),
    )


def wet_products(wet, north, south, east, west):
    return [wet * other for other in shifts(wet, north, south, east, west)]


def coefficients(u, v, u_east, u_west, v_north, v_south, passable):
    east, west, north, south = passable
    height, width = u.shape
    lane, row = iota(u.shape, 1), iota(u.shape, 0)
    e = jnp.where(lane == width - 1, u_east, pltpu.roll(u, width - 1, 1))
    w = jnp.where(lane == 0, u_west, pltpu.roll(u, 1, 1))
    n = jnp.where(row == height - 1, v_north, pltpu.roll(v, height - 1, 0))
    s = jnp.where(row == 0, v_south, pltpu.roll(v, 1, 0))
    flow_e, flow_w = 0.25 * (u + e) * east, 0.25 * (w + u) * west
    flow_n, flow_s = 0.25 * (v + n) * north, 0.25 * (s + v) * south
    own = 1.0 + (flow_w - flow_e) + (flow_s - flow_n) - KH * (east + west + north + south)
    return own, KH * east - flow_e, KH * west + flow_w, KH * north - flow_n, KH * south + flow_s


def column(turned, index, lane):
    return pltpu.roll(turned, lax.rem(lane - index + 2 * turned.shape[1], turned.shape[1]), 1)


def corrected(edge, x_rows):
    row = iota((edge.shape[0], 1), 0)
    for at, x in x_rows:
        edge = edge + jnp.where(row == at, 0.1 * x, 0.0)
    return edge


def corrected_edges(levels, ext, stress_u, stress_v, near, far):
    height, width = stress_u.shape
    last = width - 1
    lane = iota((1, width), 1)

    def block(r, b):
        return ext[r : r + 1, b * width : (b + 1) * width]

    u, v, second = 4 * levels, 5 * levels, 6 * levels
    base = 7 * levels + 8
    corners = []
    for b in (3, 4):
        ne, nw, se, sw = [block(r, b) for r in (4, 5, 6, 7)]
        corners.append((jnp.where(lane == last, pltpu.roll(ne, last, 1), se), jnp.where(lane == last, nw, pltpu.roll(sw, 1, 1))))
    turned = stress_u.T
    own = [[(v, stress_v[last:])], [(v, stress_v[0:1])], [(u, turned[last:])], [(u, turned[0:1])]]
    beside = [
        [(u, block(0, 3)), (v, block(0, 4)), (second, block(1, 4))],
        [(u, block(2, 3)), (v, block(2, 4)), (second, block(3, 4))],
        [(u, block(6, 0)), (v, block(7, 0)), (second, block(5, 2)), (base + 2 * levels, corners[0][0]), (base + 3 * levels, corners[1][0])],
        [(u, block(6, 1)), (v, block(7, 1)), (second, block(7, 2)), (base + 2 * levels, corners[0][1]), (base + 3 * levels, corners[1][1])],
    ]
    near = [corrected(edge[...].astype(F32), x) for edge, x in zip(near, own)]
    return near, [corrected(edge[...].astype(F32), x) for edge, x in zip(far, beside)]


def surface_kernel(grid, chunk, levels, *refs):
    n_sec, n_gx, n_gy = grid
    planes = n_sec * n_gy
    parts, refs = refs[:n_gx], refs[n_gx:]
    tracers, currents, land, own_n, own_s, own_e, own_w, from_n, from_s, from_e, from_w, *refs = refs
    back, flux, rim = refs
    height, width = land.shape
    last = width - 1
    lane = iota((1, width), 1)
    sums = parts[0][...]
    for part in parts[1:]:
        sums = sums + part[...].astype(F32)
    sums, ext = sums[:height], sums[height : height + 8]
    shortwave, heat, salt, stress_u, stress_v = [sums[:, f * width : (f + 1) * width] for f in range(SENT)]
    wet = land[...].astype(F32)
    u0 = currents[0, 0] + 0.1 * stress_u
    v0 = currents[1, 0] + 0.1 * stress_v
    flux[0], flux[1], flux[2], flux[3], flux[4] = shortwave, heat, salt, stress_u, stress_v
    rim[...] = ext

    near, far = corrected_edges(levels, ext, stress_u, stress_v, (own_n, own_s, own_e, own_w), (from_n, from_s, from_e, from_w))
    far_n, far_s, far_e, far_w = far
    e_turned, w_turned = far_e[:width].T, far_w[:width].T
    east = lambda index: column(e_turned, index, last)
    west = lambda index: column(w_turned, index, 0)
    passable = wet_products(
        wet, far_n[7 * levels : 7 * levels + 1], far_s[7 * levels : 7 * levels + 1], east(7 * levels), west(7 * levels)
    )
    lines = strips(0, levels, near, far, rim_flux(ext, width))
    profile = level_profile(levels, width)
    mix = KV * wet
    warm = 0.3 * wet * shortwave

    def weights(l, u, v):
        v_n, v_s = [x[5 * levels + l : 5 * levels + l + 1] for x in (far_n, far_s)]
        return coefficients(u, v, east(4 * levels + l), west(4 * levels + l), v_n, v_s, passable)

    def horizontal(c, q, halo):
        e, w, n, s = shifts(q, *halo)
        return c[0] * q + c[1] * e + c[2] * w + c[3] * n + c[4] * s

    def start(l):
        return far_n[l : l + 1], far_s[l : l + 1], east(l), west(l)

    q0, q1, q2 = tracers[0, 0], tracers[0, 1], tracers[0, 2]
    c0 = weights(0, u0, v0)
    c1 = weights(1, currents[0, 1], currents[1, 1])
    t0 = horizontal(c0, q0, start(0)) + mix * (q1 - q0) + warm * profile[0:1] + wet * heat
    t1 = horizontal(c1, q1, start(1)) + mix * ((q2 - q1) - (q1 - q0)) + warm * profile[1:2]
    sides = jnp.concatenate([lines[2][0:8], lines[3][0:8], jnp.zeros((width - 16, width), F32)], axis=0).T
    halo = lines[0][0:1], lines[1][0:1], column(sides, 0, last), column(sides, 8, 0)
    t0 = horizontal(c0, t0, halo) + mix * (t1 - t0) + warm * profile[0:1] + wet * heat
    sst = t0.astype(BF16)
    plane = lax.axis_index("sec") * n_gy + lax.axis_index("gy")
    line = lax.axis_index("gx")
    for z, part in enumerate(parts):
        where = part[height + 3 : height + 4, : planes * chunk].astype(F32)
        hot = (iota((height, planes * chunk), 0).astype(F32) == where).astype(F32)
        picked = dot(hot.T.astype(BF16), sst, NN).reshape(planes, chunk, width)
        for m in range(planes):
            there = plane ^ m
            device = (lax.div(there, n_gy) * n_gx + (line ^ z)) * n_gy + lax.rem(there, n_gy)
            back[device] = picked[m, : back.shape[1]].astype(BF16)


def rim_flux(ext, width):
    def block(r, b):
        return ext[r : r + 1, b * width : (b + 1) * width]

    return (
        (block(0, 0), block(0, 1), block(0, 2)),
        (block(2, 0), block(2, 1), block(2, 2)),
        (block(4, 0), block(5, 0), block(4, 2)),
        (block(4, 1), block(5, 1), block(6, 2)),
    )


def stencil_kernel(
    tracers_in, currents_in, land, flux, rim, own_n, own_s, own_e, own_w, from_n, from_s, from_e, from_w,
    result, tracers, currents, out, held, weights, edge_n, edge_s, line_n, line_s, depth, forced, passing, sems,
):
    copies = [
        pltpu.make_async_copy(tracers_in, tracers, sems.at[0]),
        pltpu.make_async_copy(currents_in, currents, sems.at[1]),
    ]
    for copy in copies:
        copy.start()
    levels = tracers.shape[1]

    def send(l):
        return pltpu.make_async_copy(out.at[:, l], result.at[:, l], sems.at[2 + l])

    height, width = land.shape
    last = width - 1
    wet = land[...].astype(F32)
    near, far = corrected_edges(
        levels, rim[...], flux[3], flux[4], (own_n, own_s, own_e, own_w), (from_n, from_s, from_e, from_w)
    )
    far_n, far_s, far_e, far_w = far
    edge_n[...], edge_s[...] = far_n, far_s
    e_turned, w_turned = far_e[:width].T, far_w[:width].T
    at = 7 * levels
    for i, x in enumerate(
        wet_products(wet, far_n[at : at + 1], far_s[at : at + 1], column(e_turned, at, last), column(w_turned, at, 0))
    ):
        passing[i] = x
    forced[0], forced[1], forced[2] = 0.3 * wet * flux[0], wet * flux[1], wet * flux[2]
    depth[...] = level_profile(levels, width)
    columns = []
    for tracer in range(2):
        lines = strips(
            tracer, levels, near, far, rim_flux(rim[...], width)
        )
        line_n[tracer * levels : (tracer + 1) * levels] = lines[0]
        line_s[tracer * levels : (tracer + 1) * levels] = lines[1]
        columns.append(lines[2:])
    blank = jnp.zeros((width - 2 * levels, width), F32)
    e_later, w_later = [jnp.concatenate([columns[0][i], columns[1][i], blank], axis=0).T for i in range(2)]

    def update(c, q, halo, under, over, forcing):
        e, w, n, s = shifts(q, *halo)
        mixed = KV * land[...].astype(F32) * ((under - q) - (q - over))
        return c[0] * q + c[1] * e + c[2] * w + c[3] * n + c[4] * s + mixed + forcing

    def forcing(tracer, l):
        top = jnp.where(l == 0, 1.0, 0.0)
        if tracer == 0:
            return forced[0] * depth[pl.ds(l, 1), :] + top * forced[1]
        return top * forced[2]

    for copy in copies:
        copy.wait()
    currents[0, 0] = currents[0, 0] + 0.1 * flux[3]
    currents[1, 0] = currents[1, 0] + 0.1 * flux[4]

    def first_step(l, _):
        u, v = currents[0, l], currents[1, l]
        row = 5 * levels + l
        c = coefficients(
            u, v, column(e_turned, 4 * levels + l, last), column(w_turned, 4 * levels + l, 0),
            edge_n[pl.ds(row, 1), :], edge_s[pl.ds(row, 1), :], [passing[i] for i in range(4)],
        )
        for i, x in enumerate(c):
            weights[i, l] = x
        for tracer in range(2):
            row = tracer * levels + l
            halo = edge_n[pl.ds(row, 1), :], edge_s[pl.ds(row, 1), :], column(e_turned, row, last), column(w_turned, row, 0)
            under, over = tracers[tracer, jnp.minimum(l + 1, levels - 1)], tracers[tracer, jnp.maximum(l - 1, 0)]
            held[tracer, l] = update(c, tracers[tracer, l], halo, under, over, forcing(tracer, l))
        return 0

    lax.fori_loop(0, levels, first_step, 0, unroll=4)

    def second_step(l, _):
        c = [weights[i, l] for i in range(5)]
        for tracer in range(2):
            row = tracer * levels + l
            halo = line_n[pl.ds(row, 1), :], line_s[pl.ds(row, 1), :], column(e_later, row, last), column(w_later, row, 0)
            under, over = held[tracer, jnp.minimum(l + 1, levels - 1)], held[tracer, jnp.maximum(l - 1, 0)]
            out[tracer, l] = update(c, held[tracer, l], halo, under, over, forcing(tracer, l))
        send(l).start()
        return 0

    lax.fori_loop(0, levels, second_step, 0, unroll=4)
    for l in range(levels):
        send(l).wait()


def backward_kernel(parts, slots_in, src, back, w, out, held, wide, picked, terms, slots, sems):
    total, width = terms.shape
    blocks = out.shape[0]
    batch = total // parts

    def copy(c):
        return pltpu.make_async_copy(w.at[pl.ds(c * batch, batch)], held.at[pl.ds(c * batch, batch)], sems.at[c])

    slots_copy = pltpu.make_async_copy(slots_in, slots, sems.at[parts])
    slots_copy.start()
    for c in range(parts):
        copy(c).start()
    slots_copy.wait()
    wide[...] = back[...].astype(F32).reshape(wide.shape)

    def pick(i, _):
        for j in range(16):
            picked[pl.ds(i * 16 + j, 1), :] = wide[pl.ds(slots[i * 16 + j], 1), :]
        return 0

    lax.fori_loop(0, total // 16, pick, 0, unroll=2)
    row = iota((16, width), 0)

    def work(c, _):
        copy(c).wait()
        for g in range(batch // 16):
            at = pl.multiple_of(c * batch + g * 16, 16)
            rows = picked[pl.ds(at, 16), :]
            left = [jnp.where((row == r) | (row == 8 + r), rows, 0.0).astype(BF16) for r in range(8)]
            block = held[pl.ds(at, 16)].reshape(2, 8 * width, width)
            both = dot(jnp.concatenate(left, axis=1), jnp.concatenate([block[0], block[1]], axis=1), NN)
            terms[pl.ds(at, 8), :] = both[:8, :width]
            terms[pl.ds(at + 8, 8), :] = both[8:, width:]
        return 0

    lax.fori_loop(0, parts, work, 0)
    hot = (iota((blocks, total), 0) == src[...]).astype(F32).astype(BF16)
    value = terms[...]
    high = value.astype(BF16)
    low = (value - high.astype(F32)).astype(BF16)
    both = dot(hot, jnp.concatenate([high, low], axis=1), NN)
    out[...] = both[:, :width] + both[:, width:]


def backward(back, w, src, slots, blocks, parts=10):
    total, width, _ = w.shape
    devices, cap, _ = back.shape
    return pl.pallas_call(
        functools.partial(backward_kernel, parts),
        in_specs=[ANY, VMEM, VMEM, ANY],
        out_specs=VMEM,
        scratch_shapes=[
            pltpu.VMEM(w.shape, BF16),
            pltpu.VMEM((devices * cap, width), F32),
            pltpu.VMEM((total, width), F32),
            pltpu.VMEM((total, width), F32),
            pltpu.SMEM((total,), jnp.int32),
            pltpu.SemaphoreType.DMA((parts + 1,)),
        ],
        out_shape=jax.ShapeDtypeStruct((blocks, width), F32),
        compiler_params=kernel_params(46),
        cost_estimate=pl.CostEstimate(flops=2 * total * 8 * width * width, bytes_accessed=total * width * width * 2, transcendentals=0),
        name="backward_remap",
    )(slots, src.reshape(1, total), back, w)


def kernel(body, outs, name, mebibytes, bytes_accessed, scratch=(), **specs):
    return pl.pallas_call(
        body,
        out_shape=[jax.ShapeDtypeStruct(shape, dtype) for shape, dtype in outs],
        scratch_shapes=list(scratch),
        compiler_params=kernel_params(mebibytes),
        cost_estimate=pl.CostEstimate(flops=bytes_accessed, bytes_accessed=bytes_accessed, transcendentals=0),
        name=name,
        **specs,
    )


def neighbours(axis):
    count = lax.axis_size(axis)
    forward_pairs = [(i, i + 1) for i in range(count - 1)]
    return forward_pairs, [(b, a) for a, b in forward_pairs]


def swapped(array, axes, count, step):
    return lax.ppermute(array, axes, [(i, i ^ step) for i in range(count)])


def on_device(atm_flux, remap_weights, remap_src, remap_dst, remap_owner, tracers, currents, land_sea):
    grid = n_sec, n_gx, n_gy = [lax.axis_size(axis) for axis in EVERY]
    planes = n_sec * n_gy
    total, width, _ = remap_weights.shape
    _, levels, height, _ = tracers.shape
    cap = up(2 * total // (planes * n_gx), 8)
    wide = SENT * width

    *sends, slots = forward(atm_flux, remap_weights, remap_src, remap_owner.reshape(1, total), remap_dst, grid, cap)
    chunk = sends[0].shape[1]
    got = [sends[0]] + [swapped(sends[m], ("sec", "gy"), planes, m) for m in range(1, planes)]

    side = (width, width)
    end = (7 * levels + 80, width)
    to_north, to_south = neighbours(NORTH)
    to_east, to_west = neighbours("gy")
    got[1], tracers_there, currents_there = lax.optimization_barrier((got[1], tracers, currents))
    own_s, own_n = kernel(rows_kernel, [(side, BF16)] * 2, "edge_rows", 16, 1 << 20)(
        tracers_there.reshape(-1, width), currents_there.reshape(-1, width), land_sea
    )
    from_n = lax.ppermute(own_s, NORTH, to_south)
    from_s = lax.ppermute(own_n, NORTH, to_north)
    got, from_n, from_s = lax.optimization_barrier((got, from_n, from_s))
    own_w, own_e = kernel(columns_kernel, [(end, BF16)] * 2, "edge_columns", 16, 1 << 22, [pltpu.VMEM(end, F32)] * 2)(
        tracers, currents, land_sea, from_n, from_s
    )
    from_e = lax.ppermute(own_w, "gy", to_west)
    from_w = lax.ppermute(own_e, "gy", to_east)
    part = (height + 8, wide)
    merged = kernel(functools.partial(merge_kernel, planes), [(part, F32)] + [(part, BF16)] * (n_gx - 1), "merge", 24, 1 << 22)(*got)
    parts = [merged[0]] + [swapped(merged[m], "gx", n_gx, m) for m in range(1, n_gx)]

    edges = own_n, own_s, own_e, own_w, from_n, from_s, from_e, from_w
    back, flux, rim = kernel(
        functools.partial(surface_kernel, grid, chunk, levels),
        [((planes * n_gx, cap, width), BF16), ((5, height, width), F32), ((8, wide), F32)],
        "surface",
        24,
        1 << 22,
    )(*parts, tracers[0:1, 0:3], currents[:, 0:2], land_sea, *edges)
    returned = lax.all_to_all(back, EVERY, split_axis=0, concat_axis=0, tiled=True)

    plane = (height, width)
    (tracers_out,) = kernel(
        stencil_kernel,
        [(tracers.shape, F32)],
        "substeps",
        58,
        1 << 24,
        [
            pltpu.VMEM(tracers.shape, F32),
            pltpu.VMEM(currents.shape, F32),
            pltpu.VMEM(tracers.shape, F32),
            pltpu.VMEM(tracers.shape, F32),
            pltpu.VMEM((5, levels) + plane, F32),
            pltpu.VMEM(side, F32),
            pltpu.VMEM(side, F32),
            pltpu.VMEM((2 * levels, width), F32),
            pltpu.VMEM((2 * levels, width), F32),
            pltpu.VMEM((levels, width), F32),
            pltpu.VMEM((3,) + plane, F32),
            pltpu.VMEM((4,) + plane, F32),
            pltpu.SemaphoreType.DMA((2 + levels,)),
        ],
        in_specs=[ANY, ANY] + [VMEM] * 11,
        out_specs=[ANY],
    )(tracers, currents, land_sea, flux, rim, *edges)
    return tracers_out, backward(returned, remap_weights, remap_src, slots, atm_flux.shape[0])


def solution(mesh):
    return jax.shard_map(
        on_device,
        mesh=mesh,
        in_specs=(
            P(EVERY, None, None),
            P(EVERY, None, None),
            P(EVERY),
            P(EVERY),
            P(EVERY, None),
            P(None, None, NORTH, "gy"),
            P(None, None, NORTH, "gy"),
            P(NORTH, "gy"),
        ),
        out_specs=(P(None, None, NORTH, "gy"), P(EVERY, None)),
        check_vma=False,
    )
```

```python
import functools

import jax
import jax.numpy as jnp
from jax import lax
from jax.experimental import pallas as pl
from jax.experimental.pallas import tpu as pltpu
from jax.sharding import PartitionSpec as P

F32 = jnp.float32
BF16 = jnp.bfloat16
NT = (((1,), (1,)), ((), ()))
NN = (((1,), (0,)), ((), ()))
TN = (((0,), (0,)), ((), ()))
EVERY = ("sec", "gx", "gy")
NORTH = ("sec", "gx")
SENT = 5
KH = 0.1
KV = 0.1


def dot(left, right, dims):
    return lax.dot_general(left, right, dims, preferred_element_type=F32)


def iota(shape, dim):
    return lax.broadcasted_iota(jnp.int32, shape, dim)


def up(number, step):
    return -(-number // step) * step


def kernel_params(mebibytes):
    return pltpu.CompilerParams(vmem_limit_bytes=mebibytes << 20)


VMEM = pl.BlockSpec(memory_space=pltpu.VMEM)
SMEM = pl.BlockSpec(memory_space=pltpu.SMEM)
ANY = pl.BlockSpec(memory_space=pl.ANY)


def forward_kernel(parts, cap, grid, src, own, dst, flux, w, *refs):
    sends, (slots, held, mixed, acc, rows, xs, counts, renumbered, sems) = refs[:-9], refs[-9:]
    n_sec, n_gx, n_gy = grid
    devices, _, wide = xs.shape
    total, width, _ = held.shape
    batch = total // parts
    fields = flux.shape[1]
    main = sends[0].shape[1] - 16
    first = 8
    last = width - 1

    def copy(c):
        return pltpu.make_async_copy(w.at[pl.ds(c * batch, batch)], held.at[pl.ds(c * batch, batch)], sems.at[c])

    for c in range(parts):
        copy(c).start()

    plane = lax.axis_index("sec") * n_gy + lax.axis_index("gy")
    line = lax.axis_index("gx")

    def renumber(owner):
        x = lax.div(owner, n_gy)
        there = lax.div(x, n_gx) * n_gy + lax.rem(owner, n_gy)
        return (there ^ plane) * n_gx + (lax.rem(x, n_gx) ^ line)

    def clear(o, _):
        counts[o] = 0
        renumbered[o] = renumber(o)
        return 0

    lax.fori_loop(0, devices, clear, 0)
    rows[...] = jnp.full_like(rows, 255.0)
    acc[...] = jnp.zeros_like(acc)
    xs[...] = jnp.zeros_like(xs)
    full = flux[...].astype(F32)
    one = [full[:, f : f + 1] for f in range(fields)]
    heat = 0.2 * (one[1] + one[2] + one[3]) - 0.15 * one[5]
    salt = 0.2 * one[4] - 0.1 * one[5]
    heat_high = heat.astype(BF16).astype(F32)
    salt_high = salt.astype(BF16).astype(F32)
    mixed[...] = jnp.concatenate(
        [one[0], heat_high, salt_high, one[6], one[7], heat - heat_high, salt - salt_high, jnp.zeros_like(heat)], axis=1
    ).astype(BF16)

    low_rows = iota((fields, width), 0)
    low_rows = (low_rows == 1) | (low_rows == 2)

    def work(c, _):
        copy(c).wait()
        for b in range(0, batch, 2):
            k = c * batch + b
            left = jnp.concatenate([mixed[src[k]], mixed[src[k + 1]]], axis=0)
            both = dot(left, held[pl.ds(k, 2)].reshape(2 * width, width), NT)
            for z, part in enumerate((both[:fields, :width], both[fields:, width:])):
                part = part + jnp.where(low_rows, pltpu.roll(part, fields - 4, 0), 0.0)
                owner = own[0, k + z]
                at = counts[owner]
                counts[owner] = at + 1
                at = jnp.minimum(at, cap - 1)
                slots[k + z] = owner * cap + at
                slot = renumbered[owner] * cap + at
                acc[pl.ds(pl.multiple_of(slot * fields, fields), fields), :] = part
                rows[pl.ds(slot, 1), :] = jnp.full((1, width), dst[k + z].astype(F32), F32)
        return 0

    lax.fori_loop(0, parts, work, 0)

    lane = iota((cap, width), 1).astype(F32)
    sub = iota((cap, width), 0).astype(F32)
    row = iota((24, wide), 0)
    picks = {
        4: (0, 0), 5: (1, 0), 6: (3, 0), 7: (4, 0), 12: (0, last), 13: (1, last), 14: (3, last), 15: (4, last),
        20: (2, 0), 21: (3, 1), 22: (2, last), 23: (3, last - 1),
    }
    pick = jnp.full((24, wide), -1, jnp.int32)
    for at, (field, column) in picks.items():
        pick = jnp.where(row == at, field * width + column, pick)
    select = (iota((24, wide), 1) == pick).astype(F32).astype(BF16)
    row = iota((8, cap), 0)
    wanted = jnp.zeros((8, cap), F32)
    for at, x in enumerate((0, 1, last, last - 1, 0, 0, last, last)):
        wanted = jnp.where(row == at, float(x), wanted)
    group = 16

    def owners(g):
        ds = [g * group + j for j in range(group)]
        five = []
        for d in ds:
            x = [acc[pl.ds(d * cap * fields + f, cap, stride=fields), :] for f in range(SENT)]
            x = jnp.concatenate(x, axis=1)
            if cap > main:
                xs[d, 0 : cap - main, :] = x[main:]
            x = x.astype(BF16)
            sends[d // n_gx][d % n_gx, 0:main, :] = x[:main]
            five.append(x)
        where = [rows[pl.ds(pl.multiple_of(d * cap, 8), cap), :] for d in ds]
        hot = [(lane == r).astype(F32).astype(BF16) for r in where]
        flat = [jnp.sum(jnp.where(lane == sub, r, 0.0), axis=0, keepdims=True) for r in where]
        flat = [jnp.where(lane[:1] < cap, f, 255.0) for f in flat]
        edge = [dot(select, x, NT).astype(BF16) for x in five]
        sides = [dot(e, h, NN) for e, h in zip(edge, hot)]
        ends = [dot((f[:, :cap] == wanted).astype(F32).astype(BF16), x, NN) for f, x in zip(flat, five)]
        for d, f, side, end in zip(ds, flat, sides, ends):
            here = (d // n_gx) ^ plane
            here = (lax.div(here, n_gy) * n_gx + ((d % n_gx) ^ line)) * n_gy + lax.rem(here, n_gy)

            def at(offset):
                return renumbered[lax.rem(here + offset + 2 * devices, devices)]

            south_of, north_of, west_of, east_of = at(-n_gy), at(n_gy), at(-1), at(1)

            xs[south_of, first : first + 1, :] = end[0:1]
            xs[south_of, first + 1 : first + 2, 4 * width :] = end[1:2, 4 * width :]
            xs[north_of, first + 2 : first + 3, :] = end[2:3]
            xs[north_of, first + 3 : first + 4, 4 * width :] = end[3:4, 4 * width :]
            xs[at(-n_gy - 1), first + 4 : first + 5, 3 * width :] = end[4:5, 3 * width :]
            xs[at(-n_gy + 1), first + 5 : first + 6, 3 * width :] = end[5:6, 3 * width :]
            xs[at(n_gy - 1), first + 6 : first + 7, 3 * width :] = end[6:7, 3 * width :]
            xs[at(n_gy + 1), first + 7 : first + 8, 3 * width :] = end[7:8, 3 * width :]
            xs[west_of, first + 4 : first + 8, 0:width] = side[4:8]
            xs[east_of, first + 4 : first + 8, width : 2 * width] = side[12:16]
            xs[west_of, first + 4 : first + 6, 2 * width : 3 * width] = side[20:22]
            xs[east_of, first + 6 : first + 8, 2 * width : 3 * width] = side[22:24]
            xs[d, first + 1 : first + 2, 0:width] = f

    for g in range(devices // group):
        owners(g)

    for m, send in enumerate(sends):
        send[:, main:, :] = xs[m * n_gx : (m + 1) * n_gx].astype(BF16)


def forward(flux, w, src, own, dst, grid, cap, parts=8):
    n_sec, n_gx, n_gy = grid
    devices = n_sec * n_gx * n_gy
    total, width, _ = w.shape
    chunk = up(cap + 8, 16)
    fields = flux.shape[1]
    wide = SENT * width
    return pl.pallas_call(
        functools.partial(forward_kernel, parts, cap, grid),
        in_specs=[SMEM, SMEM, SMEM, VMEM, ANY],
        out_specs=[VMEM] * (n_sec * n_gy) + [SMEM],
        scratch_shapes=[
            pltpu.VMEM(w.shape, BF16),
            pltpu.VMEM(flux.shape, BF16),
            pltpu.VMEM((devices * cap * fields, width), F32),
            pltpu.VMEM((devices * cap, width), F32),
            pltpu.VMEM((devices, 16, wide), F32),
            pltpu.SMEM((devices,), jnp.int32),
            pltpu.SMEM((devices,), jnp.int32),
            pltpu.SemaphoreType.DMA((parts,)),
        ],
        out_shape=[jax.ShapeDtypeStruct((n_gx, chunk, wide), BF16)] * (n_sec * n_gy) + [jax.ShapeDtypeStruct((total,), jnp.int32)],
        compiler_params=kernel_params(58),
        cost_estimate=pl.CostEstimate(flops=2 * total * 8 * width * width, bytes_accessed=total * width * width * 2, transcendentals=0),
        name="forward_remap",
    )(src, own, dst, flux, w)


def merge_kernel(n_sources, *refs):
    sources, outs = refs[:n_sources], refs[n_sources:]
    chunk = sources[0].shape[1]
    height = outs[0].shape[0] - 8
    first = chunk - 8
    count = n_sources * chunk
    for z, out in enumerate(outs):
        ext = None
        where = []
        for source in sources:
            piece = source[z, first:chunk, :].astype(F32)
            where.append(piece[1:2, :chunk])
            ext = piece if ext is None else ext + piece
        where = jnp.concatenate(where, axis=1)
        hot = (iota((height, count), 0).astype(F32) == where).astype(F32).astype(BF16)
        sums = dot(hot, jnp.concatenate([source[z] for source in sources], axis=0), NN)
        row3 = jnp.concatenate([where, ext[3:4, count:]], axis=1)
        ext = jnp.where(iota((8, 1), 0) == 3, row3, ext)
        out[...] = jnp.concatenate([sums, ext], axis=0).astype(out.dtype)


def rows_kernel(tracers, currents, land, south, north):
    height, width = land.shape
    levels = tracers.shape[0] // 2 // height
    for out, edge, second in ((south, 0, 1), (north, height - 1, height - 2)):
        out[...] = jnp.concatenate(
            [
                tracers[pl.ds(edge, 2 * levels, stride=height), :],
                tracers[pl.ds(second, 2 * levels, stride=height), :],
                currents[pl.ds(edge, 2 * levels, stride=height), :],
                currents[pl.ds(levels * height + second, levels, stride=height), :],
                *[land[x : x + 1, :].astype(F32) for x in (edge, second)],
                jnp.zeros((out.shape[0] - 7 * levels - 2, width), F32),
            ],
            axis=0,
        ).astype(BF16)


def columns_kernel(tracers, currents, land, from_n, from_s, west, east, west_wide, east_wide):
    levels = tracers.shape[1]
    width = tracers.shape[3]
    last = width - 1
    lane = iota((1, width), 1)
    west_wide[...] = jnp.zeros_like(west_wide)
    east_wide[...] = jnp.zeros_like(east_wide)

    def put(plane, near, far):
        turned = plane.T
        for out, edge, second in ((west_wide, 0, 1), (east_wide, last, last - 1)):
            out[pl.ds(near, 1), :] = turned[edge : edge + 1]
            if far is not None:
                out[pl.ds(far, 1), :] = turned[second : second + 1]

    def level(l, _):
        for t in range(2):
            put(tracers[t, l], t * levels + l, (2 + t) * levels + l)
        put(currents[0, l], 4 * levels + l, 6 * levels + l)
        put(currents[1, l], 5 * levels + l, None)
        return 0

    lax.fori_loop(0, levels, level, 0, unroll=2)
    put(land[...].astype(F32), 7 * levels, 7 * levels + 1)
    base = 7 * levels + 8
    n_all, s_all = from_n[...].astype(F32), from_s[...].astype(F32)
    for start, stop, at in ((0, 2 * levels, 0), (4 * levels, 6 * levels, 2 * levels), (7 * levels, 7 * levels + 8, 4 * levels)):
        n, s = n_all[start:stop], s_all[start:stop]
        west_wide[base + at : base + at + stop - start] = jnp.where(lane == last, pltpu.roll(n, last, 1), s)
        east_wide[base + at : base + at + stop - start] = jnp.where(lane == last, n, pltpu.roll(s, 1, 1))
    west[...] = west_wide[...].astype(BF16)
    east[...] = east_wide[...].astype(BF16)


def plus_side(q, other, speed, speed_other, passable):
    return KH * passable * (other - q) - 0.25 * (speed + speed_other) * passable * (q + other)


def minus_side(q, other, speed, speed_other, passable):
    return KH * passable * (other - q) + 0.25 * (speed_other + speed) * passable * (other + q)


def level_profile(levels, width):
    depth = iota((levels, width), 0).astype(F32)
    return jnp.exp(-depth / 4.0) * (1.0 - jnp.exp(jnp.full((levels, width), -0.25, F32)))


def strip_step(q, q_plus, q_minus, across, across_plus, across_minus, along, corner_q, corner_along, wet, wet_plus, wet_minus, corner_wet, forcing):
    levels, width = q.shape
    lane = iota((1, width), 1)
    row = iota((levels, 1), 0)

    def ahead(x, corner):
        return jnp.where(lane == width - 1, corner, pltpu.roll(x, width - 1, 1))

    def behind(x, corner):
        return jnp.where(lane == 0, corner, pltpu.roll(x, 1, 1))

    total = plus_side(q, q_plus, across, across_plus, wet * wet_plus)
    total += minus_side(q, q_minus, across, across_minus, wet * wet_minus)
    total += plus_side(q, ahead(q, corner_q), along, ahead(along, corner_along), wet * ahead(wet, corner_wet))
    total += minus_side(q, behind(q, corner_q), along, behind(along, corner_along), wet * behind(wet, corner_wet))
    below = jnp.where(row < levels - 1, pltpu.roll(q, levels - 1, 0) - q, 0.0)
    above = jnp.where(row > 0, q - pltpu.roll(q, 1, 0), 0.0)
    return q + total + wet * (KV * (below - above) + forcing)


def strips(tracer, levels, inner, outer, flux):
    width = outer[0].shape[1]
    lane = iota((1, width), 1)
    base = 7 * levels + 8
    north, south, east, west = outer

    def part(x, at, count=levels):
        return x[at : at + count]

    def corners(at, count):
        e, w = part(east, base + at, count), part(west, base + at, count)
        n = jnp.where(lane == width - 1, e, pltpu.roll(w, 1, 1))
        s = jnp.where(lane == width - 1, pltpu.roll(e, width - 1, 1), w)
        return n, s, e, w

    corner_q = corners(tracer * levels, levels)
    corner_u = corners(2 * levels, levels)
    corner_v = corners(3 * levels, levels)
    corner_wet = corners(4 * levels, 1)
    top = (iota((levels, 1), 0) == 0).astype(F32)
    profile = level_profile(levels, width)
    results = []
    for side in range(4):
        near, far = inner[side], outer[side]
        beside, out = part(near, tracer * levels), part(far, (2 + tracer) * levels)
        mid = part(far, tracer * levels)
        speed = 5 if side < 2 else 4
        along = part(far, (9 - speed) * levels)
        corner_along = (corner_u if side < 2 else corner_v)[side]
        across, across_in, across_out = part(far, speed * levels), part(near, speed * levels), part(far, 6 * levels)
        wet, wet_in, wet_out = part(far, 7 * levels, 1), part(near, 7 * levels, 1), part(far, 7 * levels + 1, 1)
        shortwave, heat, salt = flux[side]
        forcing = 0.3 * profile * shortwave + top * heat if tracer == 0 else top * salt
        if side % 2 == 0:
            pairs = (out, beside, across, across_out, across_in)
            wets = (wet, wet_out, wet_in)
        else:
            pairs = (beside, out, across, across_in, across_out)
            wets = (wet, wet_in, wet_out)
        results.append(strip_step(mid, *pairs, along, corner_q[side], corner_along, *wets, corner_wet[side], forcing))
    return results


def shifts(plane, north, south, east, west):
    height, width = plane.shape
    lane, row = iota(plane.shape, 1), iota(plane.shape, 0)
    return (
        jnp.where(lane == width - 1, east, pltpu.roll(plane, width - 1, 1)),
        jnp.where(lane == 0, west, pltpu.roll(plane, 1, 1)),
        jnp.where(row == height - 1, north, pltpu.roll(plane, height - 1, 0)),
        jnp.where(row == 0, south, pltpu.roll(plane, 1, 0)),
    )


def wet_products(wet, north, south, east, west):
    return [wet * other for other in shifts(wet, north, south, east, west)]


def coefficients(u, v, u_east, u_west, v_north, v_south, passable):
    east, west, north, south = passable
    height, width = u.shape
    lane, row = iota(u.shape, 1), iota(u.shape, 0)
    e = jnp.where(lane == width - 1, u_east, pltpu.roll(u, width - 1, 1))
    w = jnp.where(lane == 0, u_west, pltpu.roll(u, 1, 1))
    n = jnp.where(row == height - 1, v_north, pltpu.roll(v, height - 1, 0))
    s = jnp.where(row == 0, v_south, pltpu.roll(v, 1, 0))
    flow_e, flow_w = 0.25 * (u + e) * east, 0.25 * (w + u) * west
    flow_n, flow_s = 0.25 * (v + n) * north, 0.25 * (s + v) * south
    own = 1.0 + (flow_w - flow_e) + (flow_s - flow_n) - KH * (east + west + north + south)
    return own, KH * east - flow_e, KH * west + flow_w, KH * north - flow_n, KH * south + flow_s


def column(turned, index, lane):
    return pltpu.roll(turned, lax.rem(lane - index + 2 * turned.shape[1], turned.shape[1]), 1)


def corrected(edge, x_rows):
    row = iota((edge.shape[0], 1), 0)
    for at, x in x_rows:
        edge = edge + jnp.where(row == at, 0.1 * x, 0.0)
    return edge


def owner_sums(height, width, parts):
    sums = parts[0][...]
    for part in parts[1:]:
        sums = sums + part[...].astype(F32)
    return [sums[:height, f * width : (f + 1) * width] for f in range(SENT)], sums[height : height + 8]


def corrected_edges(levels, ext, stress_u, stress_v, near, far):
    height, width = stress_u.shape
    last = width - 1
    lane = iota((1, width), 1)

    def block(r, b):
        return ext[r : r + 1, b * width : (b + 1) * width]

    u, v, second = 4 * levels, 5 * levels, 6 * levels
    base = 7 * levels + 8
    corners = []
    for b in (3, 4):
        ne, nw, se, sw = [block(r, b) for r in (4, 5, 6, 7)]
        corners.append((jnp.where(lane == last, pltpu.roll(ne, last, 1), se), jnp.where(lane == last, nw, pltpu.roll(sw, 1, 1))))
    turned = stress_u.T
    own = [[(v, stress_v[last:])], [(v, stress_v[0:1])], [(u, turned[last:])], [(u, turned[0:1])]]
    beside = [
        [(u, block(0, 3)), (v, block(0, 4)), (second, block(1, 4))],
        [(u, block(2, 3)), (v, block(2, 4)), (second, block(3, 4))],
        [(u, block(6, 0)), (v, block(7, 0)), (second, block(5, 2)), (base + 2 * levels, corners[0][0]), (base + 3 * levels, corners[1][0])],
        [(u, block(6, 1)), (v, block(7, 1)), (second, block(7, 2)), (base + 2 * levels, corners[0][1]), (base + 3 * levels, corners[1][1])],
    ]
    near = [corrected(edge[...].astype(F32), x) for edge, x in zip(near, own)]
    return near, [corrected(edge[...].astype(F32), x) for edge, x in zip(far, beside)]


def surface_kernel(grid, chunk, levels, *refs):
    n_sec, n_gx, n_gy = grid
    planes = n_sec * n_gy
    parts, refs = refs[:n_gx], refs[n_gx:]
    tracers, currents, land, own_n, own_s, own_e, own_w, from_n, from_s, from_e, from_w, *refs = refs
    (back,) = refs
    height, width = land.shape
    last = width - 1
    lane = iota((1, width), 1)
    (shortwave, heat, salt, stress_u, stress_v), ext = owner_sums(height, width, parts)
    wet = land[...].astype(F32)
    u0 = currents[0, 0] + 0.1 * stress_u
    v0 = currents[1, 0] + 0.1 * stress_v
    near, far = corrected_edges(levels, ext, stress_u, stress_v, (own_n, own_s, own_e, own_w), (from_n, from_s, from_e, from_w))
    far_n, far_s, far_e, far_w = far
    e_turned, w_turned = far_e[:width].T, far_w[:width].T
    east = lambda index: column(e_turned, index, last)
    west = lambda index: column(w_turned, index, 0)
    passable = wet_products(
        wet, far_n[7 * levels : 7 * levels + 1], far_s[7 * levels : 7 * levels + 1], east(7 * levels), west(7 * levels)
    )
    lines = strips(0, levels, near, far, rim_flux(ext, width))
    profile = level_profile(levels, width)
    mix = KV * wet
    warm = 0.3 * wet * shortwave

    def weights(l, u, v):
        v_n, v_s = [x[5 * levels + l : 5 * levels + l + 1] for x in (far_n, far_s)]
        return coefficients(u, v, east(4 * levels + l), west(4 * levels + l), v_n, v_s, passable)

    def horizontal(c, q, halo):
        e, w, n, s = shifts(q, *halo)
        return c[0] * q + c[1] * e + c[2] * w + c[3] * n + c[4] * s

    def start(l):
        return far_n[l : l + 1], far_s[l : l + 1], east(l), west(l)

    q0, q1, q2 = tracers[0, 0], tracers[0, 1], tracers[0, 2]
    c0 = weights(0, u0, v0)
    c1 = weights(1, currents[0, 1], currents[1, 1])
    t0 = horizontal(c0, q0, start(0)) + mix * (q1 - q0) + warm * profile[0:1] + wet * heat
    t1 = horizontal(c1, q1, start(1)) + mix * ((q2 - q1) - (q1 - q0)) + warm * profile[1:2]
    sides = jnp.concatenate([lines[2][0:8], lines[3][0:8], jnp.zeros((width - 16, width), F32)], axis=0).T
    halo = lines[0][0:1], lines[1][0:1], column(sides, 0, last), column(sides, 8, 0)
    t0 = horizontal(c0, t0, halo) + mix * (t1 - t0) + warm * profile[0:1] + wet * heat
    sst = t0.astype(BF16)
    plane = lax.axis_index("sec") * n_gy + lax.axis_index("gy")
    line = lax.axis_index("gx")
    for z, part in enumerate(parts):
        where = part[height + 3 : height + 4, : planes * chunk].astype(F32)
        hot = (iota((height, planes * chunk), 0).astype(F32) == where).astype(F32)
        picked = dot(hot.T.astype(BF16), sst, NN).reshape(planes, chunk, width)
        for i, m in enumerate(swap_order(planes)):
            there = plane ^ m
            device = (lax.div(there, n_gy) * n_gx + (line ^ z)) * n_gy + lax.rem(there, n_gy)
            back[device] = picked[i, : back.shape[1]].astype(BF16)


def rim_flux(ext, width):
    def block(r, b):
        return ext[r : r + 1, b * width : (b + 1) * width]

    return (
        (block(0, 0), block(0, 1), block(0, 2)),
        (block(2, 0), block(2, 1), block(2, 2)),
        (block(4, 0), block(5, 0), block(4, 2)),
        (block(4, 1), block(5, 1), block(6, 2)),
    )


def stencil_kernel(n_gx, tracers_in, currents_in, land, *refs):
    parts, edges, refs = refs[:n_gx], refs[n_gx : n_gx + 8], refs[n_gx + 8 :]
    result, tracers, currents, out, held, weights, edge_n, edge_s, line_n, line_s, depth, forced, passing, sems = refs
    copies = [
        pltpu.make_async_copy(tracers_in, tracers, sems.at[0]),
        pltpu.make_async_copy(currents_in, currents, sems.at[1]),
    ]
    for copy in copies:
        copy.start()
    levels = tracers.shape[1]

    def send(l):
        return pltpu.make_async_copy(out.at[:, l], result.at[:, l], sems.at[2 + l])

    height, width = land.shape
    last = width - 1
    wet = land[...].astype(F32)
    (shortwave, heat, salt, stress_u, stress_v), ext = owner_sums(height, width, parts)
    near, far = corrected_edges(levels, ext, stress_u, stress_v, edges[:4], edges[4:])
    far_n, far_s, far_e, far_w = far
    edge_n[...], edge_s[...] = far_n, far_s
    e_turned, w_turned = far_e[:width].T, far_w[:width].T
    at = 7 * levels
    for i, x in enumerate(
        wet_products(wet, far_n[at : at + 1], far_s[at : at + 1], column(e_turned, at, last), column(w_turned, at, 0))
    ):
        passing[i] = x
    forced[0], forced[1], forced[2] = 0.3 * wet * shortwave, wet * heat, wet * salt
    depth[...] = level_profile(levels, width)
    columns = []
    for tracer in range(2):
        lines = strips(
            tracer, levels, near, far, rim_flux(ext, width)
        )
        line_n[tracer * levels : (tracer + 1) * levels] = lines[0]
        line_s[tracer * levels : (tracer + 1) * levels] = lines[1]
        columns.append(lines[2:])
    blank = jnp.zeros((width - 2 * levels, width), F32)
    e_later, w_later = [jnp.concatenate([columns[0][i], columns[1][i], blank], axis=0).T for i in range(2)]

    def update(c, q, halo, under, over, forcing):
        e, w, n, s = shifts(q, *halo)
        mixed = KV * land[...].astype(F32) * ((under - q) - (q - over))
        return c[0] * q + c[1] * e + c[2] * w + c[3] * n + c[4] * s + mixed + forcing

    def forcing(tracer, l):
        top = jnp.where(l == 0, 1.0, 0.0)
        if tracer == 0:
            return forced[0] * depth[pl.ds(l, 1), :] + top * forced[1]
        return top * forced[2]

    for copy in copies:
        copy.wait()
    currents[0, 0] = currents[0, 0] + 0.1 * stress_u
    currents[1, 0] = currents[1, 0] + 0.1 * stress_v

    def first_step(l, _):
        u, v = currents[0, l], currents[1, l]
        row = 5 * levels + l
        c = coefficients(
            u, v, column(e_turned, 4 * levels + l, last), column(w_turned, 4 * levels + l, 0),
            edge_n[pl.ds(row, 1), :], edge_s[pl.ds(row, 1), :], [passing[i] for i in range(4)],
        )
        for i, x in enumerate(c):
            weights[i, l] = x
        for tracer in range(2):
            row = tracer * levels + l
            halo = edge_n[pl.ds(row, 1), :], edge_s[pl.ds(row, 1), :], column(e_turned, row, last), column(w_turned, row, 0)
            under, over = tracers[tracer, jnp.minimum(l + 1, levels - 1)], tracers[tracer, jnp.maximum(l - 1, 0)]
            held[tracer, l] = update(c, tracers[tracer, l], halo, under, over, forcing(tracer, l))
        return 0

    lax.fori_loop(0, levels, first_step, 0, unroll=4)

    def second_step(l, _):
        c = [weights[i, l] for i in range(5)]
        for tracer in range(2):
            row = tracer * levels + l
            halo = line_n[pl.ds(row, 1), :], line_s[pl.ds(row, 1), :], column(e_later, row, last), column(w_later, row, 0)
            under, over = held[tracer, jnp.minimum(l + 1, levels - 1)], held[tracer, jnp.maximum(l - 1, 0)]
            out[tracer, l] = update(c, held[tracer, l], halo, under, over, forcing(tracer, l))
        send(l).start()
        return 0

    lax.fori_loop(0, levels, second_step, 0, unroll=4)
    for l in range(levels):
        send(l).wait()


def backward_kernel(parts, slots_in, src, back, w, out, held, wide, picked, terms, slots, sems):
    total, width = terms.shape
    blocks = out.shape[0]
    batch = total // parts

    def copy(c):
        return pltpu.make_async_copy(w.at[pl.ds(c * batch, batch)], held.at[pl.ds(c * batch, batch)], sems.at[c])

    slots_copy = pltpu.make_async_copy(slots_in, slots, sems.at[parts])
    slots_copy.start()
    for c in range(parts):
        copy(c).start()
    slots_copy.wait()
    wide[...] = back[...].astype(F32).reshape(wide.shape)

    def pick(i, _):
        for j in range(16):
            picked[pl.ds(i * 16 + j, 1), :] = wide[pl.ds(slots[i * 16 + j], 1), :]
        return 0

    lax.fori_loop(0, total // 16, pick, 0, unroll=2)
    row = iota((16, width), 0)

    def work(c, _):
        copy(c).wait()
        for g in range(batch // 16):
            at = pl.multiple_of(c * batch + g * 16, 16)
            rows = picked[pl.ds(at, 16), :]
            left = [jnp.where((row == r) | (row == 8 + r), rows, 0.0).astype(BF16) for r in range(8)]
            block = held[pl.ds(at, 16)].reshape(2, 8 * width, width)
            both = dot(jnp.concatenate(left, axis=1), jnp.concatenate([block[0], block[1]], axis=1), NN)
            terms[pl.ds(at, 8), :] = both[:8, :width]
            terms[pl.ds(at + 8, 8), :] = both[8:, width:]
        return 0

    lax.fori_loop(0, parts, work, 0)
    hot = (iota((blocks, total), 0) == src[...]).astype(F32).astype(BF16)
    value = terms[...]
    high = value.astype(BF16)
    low = (value - high.astype(F32)).astype(BF16)
    both = dot(hot, jnp.concatenate([high, low], axis=1), NN)
    out[...] = both[:, :width] + both[:, width:]


def backward(back, w, src, slots, blocks, parts=10):
    total, width, _ = w.shape
    devices, cap, _ = back.shape
    return pl.pallas_call(
        functools.partial(backward_kernel, parts),
        in_specs=[ANY, VMEM, VMEM, ANY],
        out_specs=VMEM,
        scratch_shapes=[
            pltpu.VMEM(w.shape, BF16),
            pltpu.VMEM((devices * cap, width), F32),
            pltpu.VMEM((total, width), F32),
            pltpu.VMEM((total, width), F32),
            pltpu.SMEM((total,), jnp.int32),
            pltpu.SemaphoreType.DMA((parts + 1,)),
        ],
        out_shape=jax.ShapeDtypeStruct((blocks, width), F32),
        compiler_params=kernel_params(46),
        cost_estimate=pl.CostEstimate(flops=2 * total * 8 * width * width, bytes_accessed=total * width * width * 2, transcendentals=0),
        name="backward_remap",
    )(slots, src.reshape(1, total), back, w)


def kernel(body, outs, name, mebibytes, bytes_accessed, scratch=(), **specs):
    return pl.pallas_call(
        body,
        out_shape=[jax.ShapeDtypeStruct(shape, dtype) for shape, dtype in outs],
        scratch_shapes=list(scratch),
        compiler_params=kernel_params(mebibytes),
        cost_estimate=pl.CostEstimate(flops=bytes_accessed, bytes_accessed=bytes_accessed, transcendentals=0),
        name=name,
        **specs,
    )


def neighbours(axis):
    count = lax.axis_size(axis)
    forward_pairs = [(i, i + 1) for i in range(count - 1)]
    return forward_pairs, [(b, a) for a, b in forward_pairs]


def swap_order(count):
    return [0, count - 1, count - 2, 1] + list(range(count - 3, 1, -1))


def swapped(array, axes, count, step):
    return lax.ppermute(array, axes, [(i, i ^ step) for i in range(count)])


def on_device(atm_flux, remap_weights, remap_src, remap_dst, remap_owner, tracers, currents, land_sea):
    grid = n_sec, n_gx, n_gy = [lax.axis_size(axis) for axis in EVERY]
    planes = n_sec * n_gy
    total, width, _ = remap_weights.shape
    _, levels, height, _ = tracers.shape
    cap = up(2 * total // (planes * n_gx), 8)
    wide = SENT * width

    *sends, slots = forward(atm_flux, remap_weights, remap_src, remap_owner.reshape(1, total), remap_dst, grid, cap)
    chunk = sends[0].shape[1]
    order = swap_order(planes)
    got = [sends[0]] + [swapped(sends[m], ("sec", "gy"), planes, m) for m in order[1:]]
    early = order.index(1)

    side = (width, width)
    end = (7 * levels + 80, width)
    to_north, to_south = neighbours(NORTH)
    to_east, to_west = neighbours("gy")
    got[early], tracers_there, currents_there = lax.optimization_barrier((got[early], tracers, currents))
    own_s, own_n = kernel(rows_kernel, [(side, BF16)] * 2, "edge_rows", 16, 1 << 20)(
        tracers_there.reshape(-1, width), currents_there.reshape(-1, width), land_sea
    )
    from_n = lax.ppermute(own_s, NORTH, to_south)
    from_s = lax.ppermute(own_n, NORTH, to_north)
    got, from_n, from_s = lax.optimization_barrier((got, from_n, from_s))
    own_w, own_e = kernel(columns_kernel, [(end, BF16)] * 2, "edge_columns", 16, 1 << 22, [pltpu.VMEM(end, F32)] * 2)(
        tracers, currents, land_sea, from_n, from_s
    )
    from_e = lax.ppermute(own_w, "gy", to_west)
    from_w = lax.ppermute(own_e, "gy", to_east)
    part = (height + 8, wide)
    merged = kernel(functools.partial(merge_kernel, planes), [(part, F32)] + [(part, BF16)] * (n_gx - 1), "merge", 24, 1 << 22)(*got)
    parts = [merged[0]] + [swapped(merged[m], "gx", n_gx, m) for m in range(1, n_gx)]

    edges = own_n, own_s, own_e, own_w, from_n, from_s, from_e, from_w
    (back,) = kernel(
        functools.partial(surface_kernel, grid, chunk, levels),
        [((planes * n_gx, cap, width), BF16)],
        "surface",
        24,
        1 << 22,
    )(*parts, tracers[0:1, 0:3], currents[:, 0:2], land_sea, *edges)
    returned = lax.all_to_all(back, EVERY, split_axis=0, concat_axis=0, tiled=True)

    plane = (height, width)
    (tracers_out,) = kernel(
        functools.partial(stencil_kernel, n_gx),
        [(tracers.shape, F32)],
        "substeps",
        58,
        1 << 24,
        [
            pltpu.VMEM(tracers.shape, F32),
            pltpu.VMEM(currents.shape, F32),
            pltpu.VMEM(tracers.shape, F32),
            pltpu.VMEM(tracers.shape, F32),
            pltpu.VMEM((5, levels) + plane, F32),
            pltpu.VMEM(side, F32),
            pltpu.VMEM(side, F32),
            pltpu.VMEM((2 * levels, width), F32),
            pltpu.VMEM((2 * levels, width), F32),
            pltpu.VMEM((levels, width), F32),
            pltpu.VMEM((3,) + plane, F32),
            pltpu.VMEM((4,) + plane, F32),
            pltpu.SemaphoreType.DMA((2 + levels,)),
        ],
        in_specs=[ANY, ANY] + [VMEM] * (n_gx + 9),
        out_specs=[ANY],
    )(tracers, currents, land_sea, *parts, *edges)
    return tracers_out, backward(returned, remap_weights, remap_src, slots, atm_flux.shape[0])


def solution(mesh):
    return jax.shard_map(
        on_device,
        mesh=mesh,
        in_specs=(
            P(EVERY, None, None),
            P(EVERY, None, None),
            P(EVERY),
            P(EVERY),
            P(EVERY, None),
            P(None, None, NORTH, "gy"),
            P(None, None, NORTH, "gy"),
            P(NORTH, "gy"),
        ),
        out_specs=(P(None, None, NORTH, "gy"), P(EVERY, None)),
        check_vma=False,
    )
```

```python
import functools

import jax
import jax.numpy as jnp
from jax import lax
from jax.experimental import pallas as pl
from jax.experimental.pallas import tpu as pltpu
from jax.sharding import PartitionSpec as P

F32 = jnp.float32
BF16 = jnp.bfloat16
NT = (((1,), (1,)), ((), ()))
NN = (((1,), (0,)), ((), ()))
TN = (((0,), (0,)), ((), ()))
EVERY = ("sec", "gx", "gy")
NORTH = ("sec", "gx")
SENT = 5
KH = 0.1
KV = 0.1


def dot(left, right, dims):
    return lax.dot_general(left, right, dims, preferred_element_type=F32)


def iota(shape, dim):
    return lax.broadcasted_iota(jnp.int32, shape, dim)


def up(number, step):
    return -(-number // step) * step


def kernel_params(mebibytes):
    return pltpu.CompilerParams(vmem_limit_bytes=mebibytes << 20)


VMEM = pl.BlockSpec(memory_space=pltpu.VMEM)
SMEM = pl.BlockSpec(memory_space=pltpu.SMEM)
ANY = pl.BlockSpec(memory_space=pl.ANY)


def forward_kernel(parts, cap, grid, src_in, own_in, dst_in, flux_in, w, *refs):
    sends, (slots, held, mixed, acc, rows, xs, counts, renumbered, sems, src, own, dst, flux) = refs[:-13], refs[-13:]
    n_sec, n_gx, n_gy = grid
    devices, _, wide = xs.shape
    total, width, _ = held.shape
    batch = total // parts
    fields = flux.shape[1]
    main = sends[0].shape[1] - 16
    first = 8
    last = width - 1

    def copy(c):
        return pltpu.make_async_copy(w.at[pl.ds(c * batch, batch)], held.at[pl.ds(c * batch, batch)], sems.at[c])

    small = [(src_in, src), (own_in, own), (dst_in, dst), (flux_in, flux)]
    small = [pltpu.make_async_copy(there, here, sems.at[parts + i]) for i, (there, here) in enumerate(small)]
    for load in small:
        load.start()
    for c in range(parts):
        copy(c).start()

    plane = lax.axis_index("sec") * n_gy + lax.axis_index("gy")
    line = lax.axis_index("gx")

    def renumber(owner):
        x = lax.div(owner, n_gy)
        there = lax.div(x, n_gx) * n_gy + lax.rem(owner, n_gy)
        return (there ^ plane) * n_gx + (lax.rem(x, n_gx) ^ line)

    def clear(o, _):
        counts[o] = 0
        renumbered[o] = renumber(o)
        return 0

    lax.fori_loop(0, devices, clear, 0)
    rows[...] = jnp.full_like(rows, 255.0)
    acc[...] = jnp.zeros_like(acc)
    xs[...] = jnp.zeros_like(xs)
    for load in small:
        load.wait()
    full = flux[...].astype(F32)
    one = [full[:, f : f + 1] for f in range(fields)]
    heat = 0.2 * (one[1] + one[2] + one[3]) - 0.15 * one[5]
    salt = 0.2 * one[4] - 0.1 * one[5]
    heat_high = heat.astype(BF16).astype(F32)
    salt_high = salt.astype(BF16).astype(F32)
    mixed[...] = jnp.concatenate(
        [one[0], heat_high, salt_high, one[6], one[7], heat - heat_high, salt - salt_high, jnp.zeros_like(heat)], axis=1
    ).astype(BF16)

    low_rows = iota((fields, width), 0)
    low_rows = (low_rows == 1) | (low_rows == 2)

    def work(c, _):
        copy(c).wait()
        for b in range(0, batch, 2):
            k = c * batch + b
            left = jnp.concatenate([mixed[src[k]], mixed[src[k + 1]]], axis=0)
            both = dot(left, held[pl.ds(k, 2)].reshape(2 * width, width), NT)
            for z, part in enumerate((both[:fields, :width], both[fields:, width:])):
                part = part + jnp.where(low_rows, pltpu.roll(part, fields - 4, 0), 0.0)
                owner = own[0, k + z]
                at = counts[owner]
                counts[owner] = at + 1
                at = jnp.minimum(at, cap - 1)
                slots[k + z] = owner * cap + at
                slot = renumbered[owner] * cap + at
                acc[pl.ds(pl.multiple_of(slot * fields, fields), fields), :] = part
                rows[pl.ds(slot, 1), :] = jnp.full((1, width), dst[k + z].astype(F32), F32)
        return 0

    lax.fori_loop(0, parts, work, 0)

    lane = iota((cap, width), 1).astype(F32)
    sub = iota((cap, width), 0).astype(F32)
    row = iota((24, wide), 0)
    picks = {
        4: (0, 0), 5: (1, 0), 6: (3, 0), 7: (4, 0), 12: (0, last), 13: (1, last), 14: (3, last), 15: (4, last),
        20: (2, 0), 21: (3, 1), 22: (2, last), 23: (3, last - 1),
    }
    pick = jnp.full((24, wide), -1, jnp.int32)
    for at, (field, column) in picks.items():
        pick = jnp.where(row == at, field * width + column, pick)
    select = (iota((24, wide), 1) == pick).astype(F32).astype(BF16)
    row = iota((8, cap), 0)
    wanted = jnp.zeros((8, cap), F32)
    for at, x in enumerate((0, 1, last, last - 1, 0, 0, last, last)):
        wanted = jnp.where(row == at, float(x), wanted)
    group = 16

    def owners(g):
        ds = [g * group + j for j in range(group)]
        five = []
        for d in ds:
            x = [acc[pl.ds(d * cap * fields + f, cap, stride=fields), :] for f in range(SENT)]
            x = jnp.concatenate(x, axis=1)
            if cap > main:
                xs[d, 0 : cap - main, :] = x[main:]
            x = x.astype(BF16)
            sends[d // n_gx][d % n_gx, 0:main, :] = x[:main]
            five.append(x)
        where = [rows[pl.ds(pl.multiple_of(d * cap, 8), cap), :] for d in ds]
        hot = [(lane == r).astype(F32).astype(BF16) for r in where]
        flat = [jnp.sum(jnp.where(lane == sub, r, 0.0), axis=0, keepdims=True) for r in where]
        flat = [jnp.where(lane[:1] < cap, f, 255.0) for f in flat]
        edge = [dot(select, x, NT).astype(BF16) for x in five]
        sides = [dot(e, h, NN) for e, h in zip(edge, hot)]
        ends = [dot((f[:, :cap] == wanted).astype(F32).astype(BF16), x, NN) for f, x in zip(flat, five)]
        for d, f, side, end in zip(ds, flat, sides, ends):
            here = (d // n_gx) ^ plane
            here = (lax.div(here, n_gy) * n_gx + ((d % n_gx) ^ line)) * n_gy + lax.rem(here, n_gy)

            def at(offset):
                return renumbered[lax.rem(here + offset + 2 * devices, devices)]

            south_of, north_of, west_of, east_of = at(-n_gy), at(n_gy), at(-1), at(1)

            xs[south_of, first : first + 1, :] = end[0:1]
            xs[south_of, first + 1 : first + 2, 4 * width :] = end[1:2, 4 * width :]
            xs[north_of, first + 2 : first + 3, :] = end[2:3]
            xs[north_of, first + 3 : first + 4, 4 * width :] = end[3:4, 4 * width :]
            xs[at(-n_gy - 1), first + 4 : first + 5, 3 * width :] = end[4:5, 3 * width :]
            xs[at(-n_gy + 1), first + 5 : first + 6, 3 * width :] = end[5:6, 3 * width :]
            xs[at(n_gy - 1), first + 6 : first + 7, 3 * width :] = end[6:7, 3 * width :]
            xs[at(n_gy + 1), first + 7 : first + 8, 3 * width :] = end[7:8, 3 * width :]
            xs[west_of, first + 4 : first + 8, 0:width] = side[4:8]
            xs[east_of, first + 4 : first + 8, width : 2 * width] = side[12:16]
            xs[west_of, first + 4 : first + 6, 2 * width : 3 * width] = side[20:22]
            xs[east_of, first + 6 : first + 8, 2 * width : 3 * width] = side[22:24]
            xs[d, first + 1 : first + 2, 0:width] = f

    for g in range(devices // group):
        owners(g)

    for m, send in enumerate(sends):
        send[:, main:, :] = xs[m * n_gx : (m + 1) * n_gx].astype(BF16)


def forward(flux, w, src, own, dst, grid, cap, parts=8):
    n_sec, n_gx, n_gy = grid
    devices = n_sec * n_gx * n_gy
    total, width, _ = w.shape
    chunk = up(cap + 8, 16)
    fields = flux.shape[1]
    wide = SENT * width
    return pl.pallas_call(
        functools.partial(forward_kernel, parts, cap, grid),
        in_specs=[ANY] * 5,
        out_specs=[VMEM] * (n_sec * n_gy) + [SMEM],
        scratch_shapes=[
            pltpu.VMEM(w.shape, BF16),
            pltpu.VMEM(flux.shape, BF16),
            pltpu.VMEM((devices * cap * fields, width), F32),
            pltpu.VMEM((devices * cap, width), F32),
            pltpu.VMEM((devices, 16, wide), F32),
            pltpu.SMEM((devices,), jnp.int32),
            pltpu.SMEM((devices,), jnp.int32),
            pltpu.SemaphoreType.DMA((parts + 4,)),
            pltpu.SMEM(src.shape, jnp.int32),
            pltpu.SMEM(own.shape, jnp.int32),
            pltpu.SMEM(dst.shape, jnp.int32),
            pltpu.VMEM(flux.shape, BF16),
        ],
        out_shape=[jax.ShapeDtypeStruct((n_gx, chunk, wide), BF16)] * (n_sec * n_gy) + [jax.ShapeDtypeStruct((total,), jnp.int32)],
        compiler_params=kernel_params(58),
        cost_estimate=pl.CostEstimate(flops=2 * total * 8 * width * width, bytes_accessed=total * width * width * 2, transcendentals=0),
        name="forward_remap",
    )(src, own, dst, flux, w)


def merge_kernel(n_sources, *refs):
    sources, outs = refs[:n_sources], refs[n_sources:]
    chunk = sources[0].shape[1]
    height = outs[0].shape[0] - 8
    first = chunk - 8
    count = n_sources * chunk
    for z, out in enumerate(outs):
        ext = None
        where = []
        for source in sources:
            piece = source[z, first:chunk, :].astype(F32)
            where.append(piece[1:2, :chunk])
            ext = piece if ext is None else ext + piece
        where = jnp.concatenate(where, axis=1)
        hot = (iota((height, count), 0).astype(F32) == where).astype(F32).astype(BF16)
        sums = dot(hot, jnp.concatenate([source[z] for source in sources], axis=0), NN)
        row3 = jnp.concatenate([where, ext[3:4, count:]], axis=1)
        ext = jnp.where(iota((8, 1), 0) == 3, row3, ext)
        out[...] = jnp.concatenate([sums, ext], axis=0).astype(out.dtype)


def rows_kernel(tracers, currents, land, south, north):
    height, width = land.shape
    levels = tracers.shape[0] // 2 // height
    for out, edge, second in ((south, 0, 1), (north, height - 1, height - 2)):
        out[...] = jnp.concatenate(
            [
                tracers[pl.ds(edge, 2 * levels, stride=height), :],
                tracers[pl.ds(second, 2 * levels, stride=height), :],
                currents[pl.ds(edge, 2 * levels, stride=height), :],
                currents[pl.ds(levels * height + second, levels, stride=height), :],
                *[land[x : x + 1, :].astype(F32) for x in (edge, second)],
                jnp.zeros((out.shape[0] - 7 * levels - 2, width), F32),
            ],
            axis=0,
        ).astype(BF16)


def columns_kernel(tracers, currents, land, from_n, from_s, west, east, west_wide, east_wide):
    levels = tracers.shape[1]
    width = tracers.shape[3]
    last = width - 1
    lane = iota((1, width), 1)
    west_wide[...] = jnp.zeros_like(west_wide)
    east_wide[...] = jnp.zeros_like(east_wide)

    def put(plane, near, far):
        turned = plane.T
        for out, edge, second in ((west_wide, 0, 1), (east_wide, last, last - 1)):
            out[pl.ds(near, 1), :] = turned[edge : edge + 1]
            if far is not None:
                out[pl.ds(far, 1), :] = turned[second : second + 1]

    def level(l, _):
        for t in range(2):
            put(tracers[t, l], t * levels + l, (2 + t) * levels + l)
        put(currents[0, l], 4 * levels + l, 6 * levels + l)
        put(currents[1, l], 5 * levels + l, None)
        return 0

    lax.fori_loop(0, levels, level, 0, unroll=2)
    put(land[...].astype(F32), 7 * levels, 7 * levels + 1)
    base = 7 * levels + 8
    n_all, s_all = from_n[...].astype(F32), from_s[...].astype(F32)
    for start, stop, at in ((0, 2 * levels, 0), (4 * levels, 6 * levels, 2 * levels), (7 * levels, 7 * levels + 8, 4 * levels)):
        n, s = n_all[start:stop], s_all[start:stop]
        west_wide[base + at : base + at + stop - start] = jnp.where(lane == last, pltpu.roll(n, last, 1), s)
        east_wide[base + at : base + at + stop - start] = jnp.where(lane == last, n, pltpu.roll(s, 1, 1))
    west[...] = west_wide[...].astype(BF16)
    east[...] = east_wide[...].astype(BF16)


def plus_side(q, other, speed, speed_other, passable):
    return KH * passable * (other - q) - 0.25 * (speed + speed_other) * passable * (q + other)


def minus_side(q, other, speed, speed_other, passable):
    return KH * passable * (other - q) + 0.25 * (speed_other + speed) * passable * (other + q)


def level_profile(levels, width):
    depth = iota((levels, width), 0).astype(F32)
    return jnp.exp(-depth / 4.0) * (1.0 - jnp.exp(jnp.full((levels, width), -0.25, F32)))


def strip_step(q, q_plus, q_minus, across, across_plus, across_minus, along, corner_q, corner_along, wet, wet_plus, wet_minus, corner_wet, forcing):
    levels, width = q.shape
    lane = iota((1, width), 1)
    row = iota((levels, 1), 0)

    def ahead(x, corner):
        return jnp.where(lane == width - 1, corner, pltpu.roll(x, width - 1, 1))

    def behind(x, corner):
        return jnp.where(lane == 0, corner, pltpu.roll(x, 1, 1))

    total = plus_side(q, q_plus, across, across_plus, wet * wet_plus)
    total += minus_side(q, q_minus, across, across_minus, wet * wet_minus)
    total += plus_side(q, ahead(q, corner_q), along, ahead(along, corner_along), wet * ahead(wet, corner_wet))
    total += minus_side(q, behind(q, corner_q), along, behind(along, corner_along), wet * behind(wet, corner_wet))
    below = jnp.where(row < levels - 1, pltpu.roll(q, levels - 1, 0) - q, 0.0)
    above = jnp.where(row > 0, q - pltpu.roll(q, 1, 0), 0.0)
    return q + total + wet * (KV * (below - above) + forcing)


def strips(tracer, levels, inner, outer, flux):
    width = outer[0].shape[1]
    lane = iota((1, width), 1)
    base = 7 * levels + 8
    north, south, east, west = outer

    def part(x, at, count=levels):
        return x[at : at + count]

    def corners(at, count):
        e, w = part(east, base + at, count), part(west, base + at, count)
        n = jnp.where(lane == width - 1, e, pltpu.roll(w, 1, 1))
        s = jnp.where(lane == width - 1, pltpu.roll(e, width - 1, 1), w)
        return n, s, e, w

    corner_q = corners(tracer * levels, levels)
    corner_u = corners(2 * levels, levels)
    corner_v = corners(3 * levels, levels)
    corner_wet = corners(4 * levels, 1)
    top = (iota((levels, 1), 0) == 0).astype(F32)
    profile = level_profile(levels, width)
    results = []
    for side in range(4):
        near, far = inner[side], outer[side]
        beside, out = part(near, tracer * levels), part(far, (2 + tracer) * levels)
        mid = part(far, tracer * levels)
        speed = 5 if side < 2 else 4
        along = part(far, (9 - speed) * levels)
        corner_along = (corner_u if side < 2 else corner_v)[side]
        across, across_in, across_out = part(far, speed * levels), part(near, speed * levels), part(far, 6 * levels)
        wet, wet_in, wet_out = part(far, 7 * levels, 1), part(near, 7 * levels, 1), part(far, 7 * levels + 1, 1)
        shortwave, heat, salt = flux[side]
        forcing = 0.3 * profile * shortwave + top * heat if tracer == 0 else top * salt
        if side % 2 == 0:
            pairs = (out, beside, across, across_out, across_in)
            wets = (wet, wet_out, wet_in)
        else:
            pairs = (beside, out, across, across_in, across_out)
            wets = (wet, wet_in, wet_out)
        results.append(strip_step(mid, *pairs, along, corner_q[side], corner_along, *wets, corner_wet[side], forcing))
    return results


def shifts(plane, north, south, east, west):
    height, width = plane.shape
    lane, row = iota(plane.shape, 1), iota(plane.shape, 0)
    return (
        jnp.where(lane == width - 1, east, pltpu.roll(plane, width - 1, 1)),
        jnp.where(lane == 0, west, pltpu.roll(plane, 1, 1)),
        jnp.where(row == height - 1, north, pltpu.roll(plane, height - 1, 0)),
        jnp.where(row == 0, south, pltpu.roll(plane, 1, 0)),
    )


def wet_products(wet, north, south, east, west):
    return [wet * other for other in shifts(wet, north, south, east, west)]


def coefficients(u, v, u_east, u_west, v_north, v_south, passable):
    east, west, north, south = passable
    height, width = u.shape
    lane, row = iota(u.shape, 1), iota(u.shape, 0)
    e = jnp.where(lane == width - 1, u_east, pltpu.roll(u, width - 1, 1))
    w = jnp.where(lane == 0, u_west, pltpu.roll(u, 1, 1))
    n = jnp.where(row == height - 1, v_north, pltpu.roll(v, height - 1, 0))
    s = jnp.where(row == 0, v_south, pltpu.roll(v, 1, 0))
    flow_e, flow_w = 0.25 * (u + e) * east, 0.25 * (w + u) * west
    flow_n, flow_s = 0.25 * (v + n) * north, 0.25 * (s + v) * south
    own = 1.0 + (flow_w - flow_e) + (flow_s - flow_n) - KH * (east + west + north + south)
    return own, KH * east - flow_e, KH * west + flow_w, KH * north - flow_n, KH * south + flow_s


def column(turned, index, lane):
    return pltpu.roll(turned, lax.rem(lane - index + 2 * turned.shape[1], turned.shape[1]), 1)


def corrected(edge, x_rows):
    row = iota((edge.shape[0], 1), 0)
    for at, x in x_rows:
        edge = edge + jnp.where(row == at, 0.1 * x, 0.0)
    return edge


def owner_sums(height, width, parts):
    sums = parts[0][...]
    for part in parts[1:]:
        sums = sums + part[...].astype(F32)
    return [sums[:height, f * width : (f + 1) * width] for f in range(SENT)], sums[height : height + 8]


def corrected_edges(levels, ext, stress_u, stress_v, near, far):
    height, width = stress_u.shape
    last = width - 1
    lane = iota((1, width), 1)

    def block(r, b):
        return ext[r : r + 1, b * width : (b + 1) * width]

    u, v, second = 4 * levels, 5 * levels, 6 * levels
    base = 7 * levels + 8
    corners = []
    for b in (3, 4):
        ne, nw, se, sw = [block(r, b) for r in (4, 5, 6, 7)]
        corners.append((jnp.where(lane == last, pltpu.roll(ne, last, 1), se), jnp.where(lane == last, nw, pltpu.roll(sw, 1, 1))))
    turned = stress_u.T
    own = [[(v, stress_v[last:])], [(v, stress_v[0:1])], [(u, turned[last:])], [(u, turned[0:1])]]
    beside = [
        [(u, block(0, 3)), (v, block(0, 4)), (second, block(1, 4))],
        [(u, block(2, 3)), (v, block(2, 4)), (second, block(3, 4))],
        [(u, block(6, 0)), (v, block(7, 0)), (second, block(5, 2)), (base + 2 * levels, corners[0][0]), (base + 3 * levels, corners[1][0])],
        [(u, block(6, 1)), (v, block(7, 1)), (second, block(7, 2)), (base + 2 * levels, corners[0][1]), (base + 3 * levels, corners[1][1])],
    ]
    near = [corrected(edge[...].astype(F32), x) for edge, x in zip(near, own)]
    return near, [corrected(edge[...].astype(F32), x) for edge, x in zip(far, beside)]


def surface_kernel(grid, chunk, levels, *refs):
    n_sec, n_gx, n_gy = grid
    planes = n_sec * n_gy
    parts, refs = refs[:n_gx], refs[n_gx:]
    tracers, currents, land, own_n, own_s, own_e, own_w, from_n, from_s, from_e, from_w, *refs = refs
    (back,) = refs
    height, width = land.shape
    last = width - 1
    lane = iota((1, width), 1)
    (shortwave, heat, salt, stress_u, stress_v), ext = owner_sums(height, width, parts)
    wet = land[...].astype(F32)
    u0 = currents[0, 0] + 0.1 * stress_u
    v0 = currents[1, 0] + 0.1 * stress_v
    near, far = corrected_edges(levels, ext, stress_u, stress_v, (own_n, own_s, own_e, own_w), (from_n, from_s, from_e, from_w))
    far_n, far_s, far_e, far_w = far
    e_turned, w_turned = far_e[:width].T, far_w[:width].T
    east = lambda index: column(e_turned, index, last)
    west = lambda index: column(w_turned, index, 0)
    passable = wet_products(
        wet, far_n[7 * levels : 7 * levels + 1], far_s[7 * levels : 7 * levels + 1], east(7 * levels), west(7 * levels)
    )
    lines = strips(0, levels, near, far, rim_flux(ext, width))
    profile = level_profile(levels, width)
    mix = KV * wet
    warm = 0.3 * wet * shortwave

    def weights(l, u, v):
        v_n, v_s = [x[5 * levels + l : 5 * levels + l + 1] for x in (far_n, far_s)]
        return coefficients(u, v, east(4 * levels + l), west(4 * levels + l), v_n, v_s, passable)

    def horizontal(c, q, halo):
        e, w, n, s = shifts(q, *halo)
        return c[0] * q + c[1] * e + c[2] * w + c[3] * n + c[4] * s

    def start(l):
        return far_n[l : l + 1], far_s[l : l + 1], east(l), west(l)

    q0, q1, q2 = tracers[0, 0], tracers[0, 1], tracers[0, 2]
    c0 = weights(0, u0, v0)
    c1 = weights(1, currents[0, 1], currents[1, 1])
    t0 = horizontal(c0, q0, start(0)) + mix * (q1 - q0) + warm * profile[0:1] + wet * heat
    t1 = horizontal(c1, q1, start(1)) + mix * ((q2 - q1) - (q1 - q0)) + warm * profile[1:2]
    sides = jnp.concatenate([lines[2][0:8], lines[3][0:8], jnp.zeros((width - 16, width), F32)], axis=0).T
    halo = lines[0][0:1], lines[1][0:1], column(sides, 0, last), column(sides, 8, 0)
    t0 = horizontal(c0, t0, halo) + mix * (t1 - t0) + warm * profile[0:1] + wet * heat
    sst = t0.astype(BF16)
    plane = lax.axis_index("sec") * n_gy + lax.axis_index("gy")
    line = lax.axis_index("gx")
    for z, part in enumerate(parts):
        where = part[height + 3 : height + 4, : planes * chunk].astype(F32)
        hot = (iota((height, planes * chunk), 0).astype(F32) == where).astype(F32)
        picked = dot(hot.T.astype(BF16), sst, NN).reshape(planes, chunk, width)
        for i, m in enumerate(swap_order(planes)):
            there = plane ^ m
            device = (lax.div(there, n_gy) * n_gx + (line ^ z)) * n_gy + lax.rem(there, n_gy)
            back[device] = picked[i, : back.shape[1]].astype(BF16)


def rim_flux(ext, width):
    def block(r, b):
        return ext[r : r + 1, b * width : (b + 1) * width]

    return (
        (block(0, 0), block(0, 1), block(0, 2)),
        (block(2, 0), block(2, 1), block(2, 2)),
        (block(4, 0), block(5, 0), block(4, 2)),
        (block(4, 1), block(5, 1), block(6, 2)),
    )


def stencil_kernel(n_gx, *refs):
    count = n_gx + 11
    given, result, here, refs = refs[:count], refs[count], refs[count + 1 : 2 * count + 1], refs[2 * count + 1 :]
    out, held, weights, edge_n, edge_s, line_n, line_s, depth, forced, passing, sems = refs
    parts, edges, (land, tracers, currents) = here[:n_gx], here[n_gx : n_gx + 8], here[n_gx + 8 :]
    copies = [pltpu.make_async_copy(x, y, sems.at[i]) for i, (x, y) in enumerate(zip(given, here))]
    for copy in copies:
        copy.start()
    for copy in copies[:-2]:
        copy.wait()
    levels = tracers.shape[1]

    def send(l):
        return pltpu.make_async_copy(out.at[:, l], result.at[:, l], sems.at[count + l])

    height, width = land.shape
    last = width - 1
    wet = land[...].astype(F32)
    (shortwave, heat, salt, stress_u, stress_v), ext = owner_sums(height, width, parts)
    near, far = corrected_edges(levels, ext, stress_u, stress_v, edges[:4], edges[4:])
    far_n, far_s, far_e, far_w = far
    edge_n[...], edge_s[...] = far_n, far_s
    e_turned, w_turned = far_e[:width].T, far_w[:width].T
    at = 7 * levels
    for i, x in enumerate(
        wet_products(wet, far_n[at : at + 1], far_s[at : at + 1], column(e_turned, at, last), column(w_turned, at, 0))
    ):
        passing[i] = x
    forced[0], forced[1], forced[2] = 0.3 * wet * shortwave, wet * heat, wet * salt
    depth[...] = level_profile(levels, width)
    columns = []
    for tracer in range(2):
        lines = strips(
            tracer, levels, near, far, rim_flux(ext, width)
        )
        line_n[tracer * levels : (tracer + 1) * levels] = lines[0]
        line_s[tracer * levels : (tracer + 1) * levels] = lines[1]
        columns.append(lines[2:])
    blank = jnp.zeros((width - 2 * levels, width), F32)
    e_later, w_later = [jnp.concatenate([columns[0][i], columns[1][i], blank], axis=0).T for i in range(2)]

    def update(c, q, halo, under, over, forcing):
        e, w, n, s = shifts(q, *halo)
        mixed = KV * land[...].astype(F32) * ((under - q) - (q - over))
        return c[0] * q + c[1] * e + c[2] * w + c[3] * n + c[4] * s + mixed + forcing

    def forcing(tracer, l):
        top = jnp.where(l == 0, 1.0, 0.0)
        if tracer == 0:
            return forced[0] * depth[pl.ds(l, 1), :] + top * forced[1]
        return top * forced[2]

    for copy in copies[-2:]:
        copy.wait()
    currents[0, 0] = currents[0, 0] + 0.1 * stress_u
    currents[1, 0] = currents[1, 0] + 0.1 * stress_v

    def first_step(l, _):
        u, v = currents[0, l], currents[1, l]
        row = 5 * levels + l
        c = coefficients(
            u, v, column(e_turned, 4 * levels + l, last), column(w_turned, 4 * levels + l, 0),
            edge_n[pl.ds(row, 1), :], edge_s[pl.ds(row, 1), :], [passing[i] for i in range(4)],
        )
        for i, x in enumerate(c):
            weights[i, l] = x
        for tracer in range(2):
            row = tracer * levels + l
            halo = edge_n[pl.ds(row, 1), :], edge_s[pl.ds(row, 1), :], column(e_turned, row, last), column(w_turned, row, 0)
            under, over = tracers[tracer, jnp.minimum(l + 1, levels - 1)], tracers[tracer, jnp.maximum(l - 1, 0)]
            held[tracer, l] = update(c, tracers[tracer, l], halo, under, over, forcing(tracer, l))
        return 0

    lax.fori_loop(0, levels, first_step, 0, unroll=8)

    def second_step(l, _):
        c = [weights[i, l] for i in range(5)]
        for tracer in range(2):
            row = tracer * levels + l
            halo = line_n[pl.ds(row, 1), :], line_s[pl.ds(row, 1), :], column(e_later, row, last), column(w_later, row, 0)
            under, over = held[tracer, jnp.minimum(l + 1, levels - 1)], held[tracer, jnp.maximum(l - 1, 0)]
            out[tracer, l] = update(c, held[tracer, l], halo, under, over, forcing(tracer, l))
        send(l).start()
        return 0

    lax.fori_loop(0, levels, second_step, 0, unroll=8)
    for l in range(levels):
        send(l).wait()


def backward_kernel(parts, slots_in, src_in, back, w, out, held, wide, picked, terms, slots, src, sems):
    total, width = terms.shape
    blocks = out.shape[0]
    batch = total // parts

    def copy(c):
        return pltpu.make_async_copy(w.at[pl.ds(c * batch, batch)], held.at[pl.ds(c * batch, batch)], sems.at[c])

    slots_copy = pltpu.make_async_copy(slots_in, slots, sems.at[parts])
    src_copy = pltpu.make_async_copy(src_in, src, sems.at[parts + 1])
    slots_copy.start()
    src_copy.start()
    for c in range(parts):
        copy(c).start()
    slots_copy.wait()
    wide[...] = back[...].astype(F32).reshape(wide.shape)

    def pick(i, _):
        for j in range(16):
            picked[pl.ds(i * 16 + j, 1), :] = wide[pl.ds(slots[i * 16 + j], 1), :]
        return 0

    lax.fori_loop(0, total // 16, pick, 0, unroll=2)
    row = iota((16, width), 0)

    def work(c, _):
        copy(c).wait()
        for g in range(batch // 16):
            at = pl.multiple_of(c * batch + g * 16, 16)
            rows = picked[pl.ds(at, 16), :]
            left = [jnp.where((row == r) | (row == 8 + r), rows, 0.0).astype(BF16) for r in range(8)]
            block = held[pl.ds(at, 16)].reshape(2, 8 * width, width)
            both = dot(jnp.concatenate(left, axis=1), jnp.concatenate([block[0], block[1]], axis=1), NN)
            terms[pl.ds(at, 8), :] = both[:8, :width]
            terms[pl.ds(at + 8, 8), :] = both[8:, width:]
        return 0

    lax.fori_loop(0, parts, work, 0)
    src_copy.wait()
    hot = (iota((blocks, total), 0) == src[...]).astype(F32).astype(BF16)
    value = terms[...]
    high = value.astype(BF16)
    low = (value - high.astype(F32)).astype(BF16)
    both = dot(hot, jnp.concatenate([high, low], axis=1), NN)
    out[...] = both[:, :width] + both[:, width:]


def backward(back, w, src, slots, blocks, parts=10):
    total, width, _ = w.shape
    devices, cap, _ = back.shape
    return pl.pallas_call(
        functools.partial(backward_kernel, parts),
        in_specs=[ANY, ANY, VMEM, ANY],
        out_specs=VMEM,
        scratch_shapes=[
            pltpu.VMEM(w.shape, BF16),
            pltpu.VMEM((devices * cap, width), F32),
            pltpu.VMEM((total, width), F32),
            pltpu.VMEM((total, width), F32),
            pltpu.SMEM((total,), jnp.int32),
            pltpu.VMEM((1, total), jnp.int32),
            pltpu.SemaphoreType.DMA((parts + 2,)),
        ],
        out_shape=jax.ShapeDtypeStruct((blocks, width), F32),
        compiler_params=kernel_params(46),
        cost_estimate=pl.CostEstimate(flops=2 * total * 8 * width * width, bytes_accessed=total * width * width * 2, transcendentals=0),
        name="backward_remap",
    )(slots, src.reshape(1, total), back, w)


def kernel(body, outs, name, mebibytes, bytes_accessed, scratch=(), **specs):
    return pl.pallas_call(
        body,
        out_shape=[jax.ShapeDtypeStruct(shape, dtype) for shape, dtype in outs],
        scratch_shapes=list(scratch),
        compiler_params=kernel_params(mebibytes),
        cost_estimate=pl.CostEstimate(flops=bytes_accessed, bytes_accessed=bytes_accessed, transcendentals=0),
        name=name,
        **specs,
    )


def neighbours(axis):
    count = lax.axis_size(axis)
    forward_pairs = [(i, i + 1) for i in range(count - 1)]
    return forward_pairs, [(b, a) for a, b in forward_pairs]


def swap_order(count):
    return [0, count - 1, count - 2, 1] + list(range(count - 3, 1, -1))


def swapped(array, axes, count, step):
    return lax.ppermute(array, axes, [(i, i ^ step) for i in range(count)])


def on_device(atm_flux, remap_weights, remap_src, remap_dst, remap_owner, tracers, currents, land_sea):
    grid = n_sec, n_gx, n_gy = [lax.axis_size(axis) for axis in EVERY]
    planes = n_sec * n_gy
    total, width, _ = remap_weights.shape
    _, levels, height, _ = tracers.shape
    cap = up(2 * total // (planes * n_gx), 8)
    wide = SENT * width

    *sends, slots = forward(atm_flux, remap_weights, remap_src, remap_owner.reshape(1, total), remap_dst, grid, cap)
    chunk = sends[0].shape[1]
    order = swap_order(planes)
    got = [sends[0]] + [swapped(sends[m], ("sec", "gy"), planes, m) for m in order[1:]]
    early = order.index(1)

    side = (width, width)
    end = (7 * levels + 80, width)
    to_north, to_south = neighbours(NORTH)
    to_east, to_west = neighbours("gy")
    got[early], tracers_there, currents_there = lax.optimization_barrier((got[early], tracers, currents))
    own_s, own_n = kernel(rows_kernel, [(side, BF16)] * 2, "edge_rows", 16, 1 << 20)(
        tracers_there.reshape(-1, width), currents_there.reshape(-1, width), land_sea
    )
    from_n = lax.ppermute(own_s, NORTH, to_south)
    from_s = lax.ppermute(own_n, NORTH, to_north)
    got, from_n, from_s = lax.optimization_barrier((got, from_n, from_s))
    own_w, own_e = kernel(columns_kernel, [(end, BF16)] * 2, "edge_columns", 16, 1 << 22, [pltpu.VMEM(end, F32)] * 2)(
        tracers, currents, land_sea, from_n, from_s
    )
    from_e = lax.ppermute(own_w, "gy", to_west)
    from_w = lax.ppermute(own_e, "gy", to_east)
    part = (height + 8, wide)
    merged = kernel(functools.partial(merge_kernel, planes), [(part, F32)] + [(part, BF16)] * (n_gx - 1), "merge", 24, 1 << 22)(*got)
    parts = [merged[0]] + [swapped(merged[m], "gx", n_gx, m) for m in range(1, n_gx)]

    edges = own_n, own_s, own_e, own_w, from_n, from_s, from_e, from_w
    (back,) = kernel(
        functools.partial(surface_kernel, grid, chunk, levels),
        [((planes * n_gx, cap, width), BF16)],
        "surface",
        24,
        1 << 22,
    )(*parts, tracers[0:1, 0:3], currents[:, 0:2], land_sea, *edges)
    returned = lax.all_to_all(back, EVERY, split_axis=0, concat_axis=0, tiled=True)

    plane = (height, width)
    given = (*parts, *edges, land_sea, tracers, currents)
    (tracers_out,) = kernel(
        functools.partial(stencil_kernel, n_gx),
        [(tracers.shape, F32)],
        "substeps",
        58,
        1 << 24,
        [pltpu.VMEM(x.shape, x.dtype) for x in given]
        + [
            pltpu.VMEM(tracers.shape, F32),
            pltpu.VMEM(tracers.shape, F32),
            pltpu.VMEM((5, levels) + plane, F32),
            pltpu.VMEM(side, F32),
            pltpu.VMEM(side, F32),
            pltpu.VMEM((2 * levels, width), F32),
            pltpu.VMEM((2 * levels, width), F32),
            pltpu.VMEM((levels, width), F32),
            pltpu.VMEM((3,) + plane, F32),
            pltpu.VMEM((4,) + plane, F32),
            pltpu.SemaphoreType.DMA((len(given) + levels,)),
        ],
        in_specs=[ANY] * len(given),
        out_specs=[ANY],
    )(*given)
    return tracers_out, backward(returned, remap_weights, remap_src, slots, atm_flux.shape[0])


def solution(mesh):
    return jax.shard_map(
        on_device,
        mesh=mesh,
        in_specs=(
            P(EVERY, None, None),
            P(EVERY, None, None),
            P(EVERY),
            P(EVERY),
            P(EVERY, None),
            P(None, None, NORTH, "gy"),
            P(None, None, NORTH, "gy"),
            P(NORTH, "gy"),
        ),
        out_specs=(P(None, None, NORTH, "gy"), P(EVERY, None)),
        check_vma=False,
    )
```

```python
import functools

import jax
import jax.numpy as jnp
from jax import lax
from jax.experimental import pallas as pl
from jax.experimental.pallas import tpu as pltpu
from jax.sharding import PartitionSpec as P

F32 = jnp.float32
BF16 = jnp.bfloat16
NT = (((1,), (1,)), ((), ()))
NN = (((1,), (0,)), ((), ()))
TN = (((0,), (0,)), ((), ()))
EVERY = ("sec", "gx", "gy")
NORTH = ("sec", "gx")
SENT = 5
KH = 0.1
KV = 0.1


def dot(left, right, dims):
    return lax.dot_general(left, right, dims, preferred_element_type=F32)


def iota(shape, dim):
    return lax.broadcasted_iota(jnp.int32, shape, dim)


def up(number, step):
    return -(-number // step) * step


def kernel_params(mebibytes):
    return pltpu.CompilerParams(vmem_limit_bytes=mebibytes << 20)


VMEM = pl.BlockSpec(memory_space=pltpu.VMEM)
SMEM = pl.BlockSpec(memory_space=pltpu.SMEM)
ANY = pl.BlockSpec(memory_space=pl.ANY)


def place_of(device, grid):
    n_sec, n_gx, n_gy = grid
    x, y = lax.div(device, n_gy), lax.rem(device, n_gy)
    gx = lax.rem(x, n_gx)
    return (lax.div(x, n_gx) * (n_gx // 2) + lax.rem(gx, n_gx // 2)) * n_gy + y, lax.div(gx, n_gx // 2)


def device_at(index, half, grid):
    n_sec, n_gx, n_gy = grid
    x = lax.div(index, n_gy)
    gx = half * (n_gx // 2) + lax.rem(x, n_gx // 2)
    return (lax.div(x, n_gx // 2) * n_gx + gx) * n_gy + lax.rem(index, n_gy)


def this_device(grid):
    n_sec, n_gx, n_gy = grid
    return (lax.axis_index("sec") * n_gx + lax.axis_index("gx")) * n_gy + lax.axis_index("gy")


def swap_order(count):
    return [0, count - 1, count - 2, 1] + list(range(count - 3, 1, -1))


def swapped(array, grid, index, half):
    n_sec, n_gx, n_gy = grid
    x = index // n_gy
    bits = (x // (n_gx // 2) * n_gx + half * (n_gx // 2) + x % (n_gx // 2)) * n_gy + index % n_gy
    return lax.ppermute(array, EVERY, [(i, i ^ bits) for i in range(n_sec * n_gx * n_gy)])


def forward_kernel(parts, cap, grid, src_in, own_in, dst_in, flux_in, w, *refs):
    sends, (slots, held, mixed, acc, rows, xs, counts, renumbered, sems, src, own, dst, flux) = refs[:-13], refs[-13:]
    n_sec, n_gx, n_gy = grid
    devices, _, wide = xs.shape
    total, width, _ = held.shape
    batch = total // parts
    fields = flux.shape[1]
    main = sends[0].shape[1] - 16
    first = 8
    last = width - 1

    def copy(c):
        return pltpu.make_async_copy(w.at[pl.ds(c * batch, batch)], held.at[pl.ds(c * batch, batch)], sems.at[c])

    small = [(src_in, src), (own_in, own), (dst_in, dst), (flux_in, flux)]
    small = [pltpu.make_async_copy(there, here, sems.at[parts + i]) for i, (there, here) in enumerate(small)]
    for load in small:
        load.start()
    for c in range(parts):
        copy(c).start()

    index, half = place_of(this_device(grid), grid)

    def renumber(owner):
        index_there, half_there = place_of(owner, grid)
        return (index_there ^ index) * 2 + (half_there ^ half)

    def clear(o, _):
        counts[o] = 0
        renumbered[o] = renumber(o)
        return 0

    lax.fori_loop(0, devices, clear, 0)
    rows[...] = jnp.full_like(rows, 255.0)
    acc[...] = jnp.zeros_like(acc)
    xs[...] = jnp.zeros_like(xs)
    for load in small:
        load.wait()
    full = flux[...].astype(F32)
    one = [full[:, f : f + 1] for f in range(fields)]
    heat = 0.2 * (one[1] + one[2] + one[3]) - 0.15 * one[5]
    salt = 0.2 * one[4] - 0.1 * one[5]
    heat_high = heat.astype(BF16).astype(F32)
    salt_high = salt.astype(BF16).astype(F32)
    mixed[...] = jnp.concatenate(
        [one[0], heat_high, salt_high, one[6], one[7], heat - heat_high, salt - salt_high, jnp.zeros_like(heat)], axis=1
    ).astype(BF16)

    low_rows = iota((fields, width), 0)
    low_rows = (low_rows == 1) | (low_rows == 2)

    def work(c, _):
        copy(c).wait()
        for b in range(0, batch, 2):
            k = c * batch + b
            left = jnp.concatenate([mixed[src[k]], mixed[src[k + 1]]], axis=0)
            both = dot(left, held[pl.ds(k, 2)].reshape(2 * width, width), NT)
            for z, part in enumerate((both[:fields, :width], both[fields:, width:])):
                part = part + jnp.where(low_rows, pltpu.roll(part, fields - 4, 0), 0.0)
                owner = own[0, k + z]
                at = counts[owner]
                counts[owner] = at + 1
                at = jnp.minimum(at, cap - 1)
                slots[k + z] = owner * cap + at
                slot = renumbered[owner] * cap + at
                acc[pl.ds(pl.multiple_of(slot * fields, fields), fields), :] = part
                rows[pl.ds(slot, 1), :] = jnp.full((1, width), dst[k + z].astype(F32), F32)
        return 0

    lax.fori_loop(0, parts, work, 0)

    lane = iota((cap, width), 1).astype(F32)
    sub = iota((cap, width), 0).astype(F32)
    row = iota((24, wide), 0)
    picks = {
        4: (0, 0), 5: (1, 0), 6: (3, 0), 7: (4, 0), 12: (0, last), 13: (1, last), 14: (3, last), 15: (4, last),
        20: (2, 0), 21: (3, 1), 22: (2, last), 23: (3, last - 1),
    }
    pick = jnp.full((24, wide), -1, jnp.int32)
    for at, (field, column) in picks.items():
        pick = jnp.where(row == at, field * width + column, pick)
    select = (iota((24, wide), 1) == pick).astype(F32).astype(BF16)
    row = iota((8, cap), 0)
    wanted = jnp.zeros((8, cap), F32)
    for at, x in enumerate((0, 1, last, last - 1, 0, 0, last, last)):
        wanted = jnp.where(row == at, float(x), wanted)
    group = 16

    def owners(g):
        ds = [g * group + j for j in range(group)]
        five = []
        for d in ds:
            x = [acc[pl.ds(d * cap * fields + f, cap, stride=fields), :] for f in range(SENT)]
            x = jnp.concatenate(x, axis=1)
            if cap > main:
                xs[d, 0 : cap - main, :] = x[main:]
            x = x.astype(BF16)
            sends[d // 2][d % 2, 0:main, :] = x[:main]
            five.append(x)
        where = [rows[pl.ds(pl.multiple_of(d * cap, 8), cap), :] for d in ds]
        hot = [(lane == r).astype(F32).astype(BF16) for r in where]
        flat = [jnp.sum(jnp.where(lane == sub, r, 0.0), axis=0, keepdims=True) for r in where]
        flat = [jnp.where(lane[:1] < cap, f, 255.0) for f in flat]
        edge = [dot(select, x, NT).astype(BF16) for x in five]
        sides = [dot(e, h, NN) for e, h in zip(edge, hot)]
        ends = [dot((f[:, :cap] == wanted).astype(F32).astype(BF16), x, NN) for f, x in zip(flat, five)]
        for d, f, side, end in zip(ds, flat, sides, ends):
            here = device_at((d // 2) ^ index, (d % 2) ^ half, grid)

            def at(offset):
                return renumbered[lax.rem(here + offset + 2 * devices, devices)]

            south_of, north_of, west_of, east_of = at(-n_gy), at(n_gy), at(-1), at(1)

            xs[south_of, first : first + 1, :] = end[0:1]
            xs[south_of, first + 1 : first + 2, 4 * width :] = end[1:2, 4 * width :]
            xs[north_of, first + 2 : first + 3, :] = end[2:3]
            xs[north_of, first + 3 : first + 4, 4 * width :] = end[3:4, 4 * width :]
            xs[at(-n_gy - 1), first + 4 : first + 5, 3 * width :] = end[4:5, 3 * width :]
            xs[at(-n_gy + 1), first + 5 : first + 6, 3 * width :] = end[5:6, 3 * width :]
            xs[at(n_gy - 1), first + 6 : first + 7, 3 * width :] = end[6:7, 3 * width :]
            xs[at(n_gy + 1), first + 7 : first + 8, 3 * width :] = end[7:8, 3 * width :]
            xs[west_of, first + 4 : first + 8, 0:width] = side[4:8]
            xs[east_of, first + 4 : first + 8, width : 2 * width] = side[12:16]
            xs[west_of, first + 4 : first + 6, 2 * width : 3 * width] = side[20:22]
            xs[east_of, first + 6 : first + 8, 2 * width : 3 * width] = side[22:24]
            xs[d, first + 1 : first + 2, 0:width] = f

    for g in range(devices // group):
        owners(g)

    for m, send in enumerate(sends):
        send[:, main:, :] = xs[2 * m : 2 * m + 2].astype(BF16)


def forward(flux, w, src, own, dst, grid, cap, parts=8):
    n_sec, n_gx, n_gy = grid
    devices = n_sec * n_gx * n_gy
    total, width, _ = w.shape
    chunk = up(cap + 8, 16)
    fields = flux.shape[1]
    wide = SENT * width
    return pl.pallas_call(
        functools.partial(forward_kernel, parts, cap, grid),
        in_specs=[ANY] * 5,
        out_specs=[VMEM] * (devices // 2) + [SMEM],
        scratch_shapes=[
            pltpu.VMEM(w.shape, BF16),
            pltpu.VMEM(flux.shape, BF16),
            pltpu.VMEM((devices * cap * fields, width), F32),
            pltpu.VMEM((devices * cap, width), F32),
            pltpu.VMEM((devices, 16, wide), F32),
            pltpu.SMEM((devices,), jnp.int32),
            pltpu.SMEM((devices,), jnp.int32),
            pltpu.SemaphoreType.DMA((parts + 4,)),
            pltpu.SMEM(src.shape, jnp.int32),
            pltpu.SMEM(own.shape, jnp.int32),
            pltpu.SMEM(dst.shape, jnp.int32),
            pltpu.VMEM(flux.shape, BF16),
        ],
        out_shape=[jax.ShapeDtypeStruct((2, chunk, wide), BF16)] * (devices // 2) + [jax.ShapeDtypeStruct((total,), jnp.int32)],
        compiler_params=kernel_params(58),
        cost_estimate=pl.CostEstimate(flops=2 * total * 8 * width * width, bytes_accessed=total * width * width * 2, transcendentals=0),
        name="forward_remap",
    )(src, own, dst, flux, w)


def merge_kernel(n_sources, *refs):
    sources, outs = refs[:n_sources], refs[n_sources:]
    chunk = sources[0].shape[1]
    height, wide = outs[0].shape
    height -= 16
    first = chunk - 8
    count = n_sources * chunk
    for z, out in enumerate(outs):
        ext = None
        where = []
        for source in sources:
            piece = source[z, first:chunk, :].astype(F32)
            where.append(piece[1:2, :chunk])
            ext = piece if ext is None else ext + piece
        where = jnp.concatenate(where, axis=1)
        hot = (iota((height, count), 0).astype(F32) == where).astype(F32).astype(BF16)
        sums = dot(hot, jnp.concatenate([source[z] for source in sources], axis=0), NN)
        where = jnp.concatenate([where, jnp.zeros((1, up(count, wide) - count), F32)], axis=1)
        where = [where[:, at : at + wide] for at in range(0, count, wide)]
        blank = jnp.zeros((8 - len(where), wide), F32)
        out[...] = jnp.concatenate([sums, ext, *where, blank], axis=0).astype(out.dtype)


def rows_kernel(tracers, currents, land, south, north):
    height, width = land.shape
    levels = tracers.shape[0] // 2 // height
    for out, edge, second in ((south, 0, 1), (north, height - 1, height - 2)):
        out[...] = jnp.concatenate(
            [
                tracers[pl.ds(edge, 2 * levels, stride=height), :],
                tracers[pl.ds(second, 2 * levels, stride=height), :],
                currents[pl.ds(edge, 2 * levels, stride=height), :],
                currents[pl.ds(levels * height + second, levels, stride=height), :],
                *[land[x : x + 1, :].astype(F32) for x in (edge, second)],
                jnp.zeros((out.shape[0] - 7 * levels - 2, width), F32),
            ],
            axis=0,
        ).astype(BF16)


def columns_kernel(tracers, currents, land, from_n, from_s, west, east, west_wide, east_wide):
    levels = tracers.shape[1]
    width = tracers.shape[3]
    last = width - 1
    lane = iota((1, width), 1)
    west_wide[...] = jnp.zeros_like(west_wide)
    east_wide[...] = jnp.zeros_like(east_wide)

    def put(plane, near, far):
        turned = plane.T
        for out, edge, second in ((west_wide, 0, 1), (east_wide, last, last - 1)):
            out[pl.ds(near, 1), :] = turned[edge : edge + 1]
            if far is not None:
                out[pl.ds(far, 1), :] = turned[second : second + 1]

    def level(l, _):
        for t in range(2):
            put(tracers[t, l], t * levels + l, (2 + t) * levels + l)
        put(currents[0, l], 4 * levels + l, 6 * levels + l)
        put(currents[1, l], 5 * levels + l, None)
        return 0

    lax.fori_loop(0, levels, level, 0, unroll=2)
    put(land[...].astype(F32), 7 * levels, 7 * levels + 1)
    base = 7 * levels + 8
    n_all, s_all = from_n[...].astype(F32), from_s[...].astype(F32)
    for start, stop, at in ((0, 2 * levels, 0), (4 * levels, 6 * levels, 2 * levels), (7 * levels, 7 * levels + 8, 4 * levels)):
        n, s = n_all[start:stop], s_all[start:stop]
        west_wide[base + at : base + at + stop - start] = jnp.where(lane == last, pltpu.roll(n, last, 1), s)
        east_wide[base + at : base + at + stop - start] = jnp.where(lane == last, n, pltpu.roll(s, 1, 1))
    west[...] = west_wide[...].astype(BF16)
    east[...] = east_wide[...].astype(BF16)


def plus_side(q, other, speed, speed_other, passable):
    return KH * passable * (other - q) - 0.25 * (speed + speed_other) * passable * (q + other)


def minus_side(q, other, speed, speed_other, passable):
    return KH * passable * (other - q) + 0.25 * (speed_other + speed) * passable * (other + q)


def level_profile(levels, width):
    depth = iota((levels, width), 0).astype(F32)
    return jnp.exp(-depth / 4.0) * (1.0 - jnp.exp(jnp.full((levels, width), -0.25, F32)))


def strip_step(q, q_plus, q_minus, across, across_plus, across_minus, along, corner_q, corner_along, wet, wet_plus, wet_minus, corner_wet, forcing):
    levels, width = q.shape
    lane = iota((1, width), 1)
    row = iota((levels, 1), 0)

    def ahead(x, corner):
        return jnp.where(lane == width - 1, corner, pltpu.roll(x, width - 1, 1))

    def behind(x, corner):
        return jnp.where(lane == 0, corner, pltpu.roll(x, 1, 1))

    total = plus_side(q, q_plus, across, across_plus, wet * wet_plus)
    total += minus_side(q, q_minus, across, across_minus, wet * wet_minus)
    total += plus_side(q, ahead(q, corner_q), along, ahead(along, corner_along), wet * ahead(wet, corner_wet))
    total += minus_side(q, behind(q, corner_q), along, behind(along, corner_along), wet * behind(wet, corner_wet))
    below = jnp.where(row < levels - 1, pltpu.roll(q, levels - 1, 0) - q, 0.0)
    above = jnp.where(row > 0, q - pltpu.roll(q, 1, 0), 0.0)
    return q + total + wet * (KV * (below - above) + forcing)


def strips(tracer, levels, inner, outer, flux):
    width = outer[0].shape[1]
    lane = iota((1, width), 1)
    base = 7 * levels + 8
    north, south, east, west = outer

    def part(x, at, count=levels):
        return x[at : at + count]

    def corners(at, count):
        e, w = part(east, base + at, count), part(west, base + at, count)
        n = jnp.where(lane == width - 1, e, pltpu.roll(w, 1, 1))
        s = jnp.where(lane == width - 1, pltpu.roll(e, width - 1, 1), w)
        return n, s, e, w

    corner_q = corners(tracer * levels, levels)
    corner_u = corners(2 * levels, levels)
    corner_v = corners(3 * levels, levels)
    corner_wet = corners(4 * levels, 1)
    top = (iota((levels, 1), 0) == 0).astype(F32)
    profile = level_profile(levels, width)
    results = []
    for side in range(4):
        near, far = inner[side], outer[side]
        beside, out = part(near, tracer * levels), part(far, (2 + tracer) * levels)
        mid = part(far, tracer * levels)
        speed = 5 if side < 2 else 4
        along = part(far, (9 - speed) * levels)
        corner_along = (corner_u if side < 2 else corner_v)[side]
        across, across_in, across_out = part(far, speed * levels), part(near, speed * levels), part(far, 6 * levels)
        wet, wet_in, wet_out = part(far, 7 * levels, 1), part(near, 7 * levels, 1), part(far, 7 * levels + 1, 1)
        shortwave, heat, salt = flux[side]
        forcing = 0.3 * profile * shortwave + top * heat if tracer == 0 else top * salt
        if side % 2 == 0:
            pairs = (out, beside, across, across_out, across_in)
            wets = (wet, wet_out, wet_in)
        else:
            pairs = (beside, out, across, across_in, across_out)
            wets = (wet, wet_in, wet_out)
        results.append(strip_step(mid, *pairs, along, corner_q[side], corner_along, *wets, corner_wet[side], forcing))
    return results


def shifts(plane, north, south, east, west):
    height, width = plane.shape
    lane, row = iota(plane.shape, 1), iota(plane.shape, 0)
    return (
        jnp.where(lane == width - 1, east, pltpu.roll(plane, width - 1, 1)),
        jnp.where(lane == 0, west, pltpu.roll(plane, 1, 1)),
        jnp.where(row == height - 1, north, pltpu.roll(plane, height - 1, 0)),
        jnp.where(row == 0, south, pltpu.roll(plane, 1, 0)),
    )


def wet_products(wet, north, south, east, west):
    return [wet * other for other in shifts(wet, north, south, east, west)]


def coefficients(u, v, u_east, u_west, v_north, v_south, passable):
    east, west, north, south = passable
    height, width = u.shape
    lane, row = iota(u.shape, 1), iota(u.shape, 0)
    e = jnp.where(lane == width - 1, u_east, pltpu.roll(u, width - 1, 1))
    w = jnp.where(lane == 0, u_west, pltpu.roll(u, 1, 1))
    n = jnp.where(row == height - 1, v_north, pltpu.roll(v, height - 1, 0))
    s = jnp.where(row == 0, v_south, pltpu.roll(v, 1, 0))
    flow_e, flow_w = 0.25 * (u + e) * east, 0.25 * (w + u) * west
    flow_n, flow_s = 0.25 * (v + n) * north, 0.25 * (s + v) * south
    own = 1.0 + (flow_w - flow_e) + (flow_s - flow_n) - KH * (east + west + north + south)
    return own, KH * east - flow_e, KH * west + flow_w, KH * north - flow_n, KH * south + flow_s


def column(turned, index, lane):
    return pltpu.roll(turned, lax.rem(lane - index + 2 * turned.shape[1], turned.shape[1]), 1)


def corrected(edge, x_rows):
    row = iota((edge.shape[0], 1), 0)
    for at, x in x_rows:
        edge = edge + jnp.where(row == at, 0.1 * x, 0.0)
    return edge


def owner_sums(height, width, parts):
    sums = parts[0][...]
    for part in parts[1:]:
        sums = sums + part[...].astype(F32)
    return [sums[:height, f * width : (f + 1) * width] for f in range(SENT)], sums[height : height + 8]


def corrected_edges(levels, ext, stress_u, stress_v, near, far):
    height, width = stress_u.shape
    last = width - 1
    lane = iota((1, width), 1)

    def block(r, b):
        return ext[r : r + 1, b * width : (b + 1) * width]

    u, v, second = 4 * levels, 5 * levels, 6 * levels
    base = 7 * levels + 8
    corners = []
    for b in (3, 4):
        ne, nw, se, sw = [block(r, b) for r in (4, 5, 6, 7)]
        corners.append((jnp.where(lane == last, pltpu.roll(ne, last, 1), se), jnp.where(lane == last, nw, pltpu.roll(sw, 1, 1))))
    turned = stress_u.T
    own = [[(v, stress_v[last:])], [(v, stress_v[0:1])], [(u, turned[last:])], [(u, turned[0:1])]]
    beside = [
        [(u, block(0, 3)), (v, block(0, 4)), (second, block(1, 4))],
        [(u, block(2, 3)), (v, block(2, 4)), (second, block(3, 4))],
        [(u, block(6, 0)), (v, block(7, 0)), (second, block(5, 2)), (base + 2 * levels, corners[0][0]), (base + 3 * levels, corners[1][0])],
        [(u, block(6, 1)), (v, block(7, 1)), (second, block(7, 2)), (base + 2 * levels, corners[0][1]), (base + 3 * levels, corners[1][1])],
    ]
    near = [corrected(edge[...].astype(F32), x) for edge, x in zip(near, own)]
    return near, [corrected(edge[...].astype(F32), x) for edge, x in zip(far, beside)]


def surface_kernel(grid, chunk, levels, *refs):
    group = grid[0] * grid[1] * grid[2] // 2
    parts, refs = refs[:2], refs[2:]
    tracers, currents, land, own_n, own_s, own_e, own_w, from_n, from_s, from_e, from_w, *refs = refs
    (back,) = refs
    height, width = land.shape
    last = width - 1
    lane = iota((1, width), 1)
    (shortwave, heat, salt, stress_u, stress_v), ext = owner_sums(height, width, parts)
    wet = land[...].astype(F32)
    u0 = currents[0, 0] + 0.1 * stress_u
    v0 = currents[1, 0] + 0.1 * stress_v
    near, far = corrected_edges(levels, ext, stress_u, stress_v, (own_n, own_s, own_e, own_w), (from_n, from_s, from_e, from_w))
    far_n, far_s, far_e, far_w = far
    e_turned, w_turned = far_e[:width].T, far_w[:width].T
    east = lambda index: column(e_turned, index, last)
    west = lambda index: column(w_turned, index, 0)
    passable = wet_products(
        wet, far_n[7 * levels : 7 * levels + 1], far_s[7 * levels : 7 * levels + 1], east(7 * levels), west(7 * levels)
    )
    lines = strips(0, levels, near, far, rim_flux(ext, width))
    profile = level_profile(levels, width)
    mix = KV * wet
    warm = 0.3 * wet * shortwave

    def weights(l, u, v):
        v_n, v_s = [x[5 * levels + l : 5 * levels + l + 1] for x in (far_n, far_s)]
        return coefficients(u, v, east(4 * levels + l), west(4 * levels + l), v_n, v_s, passable)

    def horizontal(c, q, halo):
        e, w, n, s = shifts(q, *halo)
        return c[0] * q + c[1] * e + c[2] * w + c[3] * n + c[4] * s

    def start(l):
        return far_n[l : l + 1], far_s[l : l + 1], east(l), west(l)

    q0, q1, q2 = tracers[0, 0], tracers[0, 1], tracers[0, 2]
    c0 = weights(0, u0, v0)
    c1 = weights(1, currents[0, 1], currents[1, 1])
    t0 = horizontal(c0, q0, start(0)) + mix * (q1 - q0) + warm * profile[0:1] + wet * heat
    t1 = horizontal(c1, q1, start(1)) + mix * ((q2 - q1) - (q1 - q0)) + warm * profile[1:2]
    sides = jnp.concatenate([lines[2][0:8], lines[3][0:8], jnp.zeros((width - 16, width), F32)], axis=0).T
    halo = lines[0][0:1], lines[1][0:1], column(sides, 0, last), column(sides, 8, 0)
    t0 = horizontal(c0, t0, halo) + mix * (t1 - t0) + warm * profile[0:1] + wet * heat
    sst = t0.astype(BF16)
    index, half = place_of(this_device(grid), grid)
    for z, part in enumerate(parts):
        rows = part[height + 8 :].astype(F32)
        where = [rows[r : r + 1] for r in range(up(group * chunk, rows.shape[1]) // rows.shape[1])]
        where = jnp.concatenate(where, axis=1)[:, : group * chunk]
        hot = (iota((height, group * chunk), 0).astype(F32) == where).astype(F32)
        picked = dot(hot.T.astype(BF16), sst, NN).reshape(group, chunk, width)
        for i, m in enumerate(swap_order(group)):
            back[device_at(index ^ m, half ^ z, grid)] = picked[i, : back.shape[1]].astype(BF16)


def rim_flux(ext, width):
    def block(r, b):
        return ext[r : r + 1, b * width : (b + 1) * width]

    return (
        (block(0, 0), block(0, 1), block(0, 2)),
        (block(2, 0), block(2, 1), block(2, 2)),
        (block(4, 0), block(5, 0), block(4, 2)),
        (block(4, 1), block(5, 1), block(6, 2)),
    )


def stencil_kernel(*refs):
    count = 13
    given, result, here, refs = refs[:count], refs[count], refs[count + 1 : 2 * count + 1], refs[2 * count + 1 :]
    out, held, weights, edge_n, edge_s, line_n, line_s, depth, forced, passing, sems = refs
    parts, edges, (land, tracers, currents) = here[:2], here[2:10], here[10:]
    copies = [pltpu.make_async_copy(x, y, sems.at[i]) for i, (x, y) in enumerate(zip(given, here))]
    for copy in copies:
        copy.start()
    for copy in copies[:-2]:
        copy.wait()
    levels = tracers.shape[1]

    def send(l):
        return pltpu.make_async_copy(out.at[:, l], result.at[:, l], sems.at[count + l])

    height, width = land.shape
    last = width - 1
    wet = land[...].astype(F32)
    (shortwave, heat, salt, stress_u, stress_v), ext = owner_sums(height, width, parts)
    near, far = corrected_edges(levels, ext, stress_u, stress_v, edges[:4], edges[4:])
    far_n, far_s, far_e, far_w = far
    edge_n[...], edge_s[...] = far_n, far_s
    e_turned, w_turned = far_e[:width].T, far_w[:width].T
    at = 7 * levels
    for i, x in enumerate(
        wet_products(wet, far_n[at : at + 1], far_s[at : at + 1], column(e_turned, at, last), column(w_turned, at, 0))
    ):
        passing[i] = x
    forced[0], forced[1], forced[2] = 0.3 * wet * shortwave, wet * heat, wet * salt
    depth[...] = level_profile(levels, width)
    columns = []
    for tracer in range(2):
        lines = strips(
            tracer, levels, near, far, rim_flux(ext, width)
        )
        line_n[tracer * levels : (tracer + 1) * levels] = lines[0]
        line_s[tracer * levels : (tracer + 1) * levels] = lines[1]
        columns.append(lines[2:])
    blank = jnp.zeros((width - 2 * levels, width), F32)
    e_later, w_later = [jnp.concatenate([columns[0][i], columns[1][i], blank], axis=0).T for i in range(2)]

    def update(c, q, halo, under, over, forcing):
        e, w, n, s = shifts(q, *halo)
        mixed = KV * land[...].astype(F32) * ((under - q) - (q - over))
        return c[0] * q + c[1] * e + c[2] * w + c[3] * n + c[4] * s + mixed + forcing

    def forcing(tracer, l):
        top = jnp.where(l == 0, 1.0, 0.0)
        if tracer == 0:
            return forced[0] * depth[pl.ds(l, 1), :] + top * forced[1]
        return top * forced[2]

    for copy in copies[-2:]:
        copy.wait()
    currents[0, 0] = currents[0, 0] + 0.1 * stress_u
    currents[1, 0] = currents[1, 0] + 0.1 * stress_v

    def first_step(l, _):
        u, v = currents[0, l], currents[1, l]
        row = 5 * levels + l
        c = coefficients(
            u, v, column(e_turned, 4 * levels + l, last), column(w_turned, 4 * levels + l, 0),
            edge_n[pl.ds(row, 1), :], edge_s[pl.ds(row, 1), :], [passing[i] for i in range(4)],
        )
        for i, x in enumerate(c):
            weights[i, l] = x
        for tracer in range(2):
            row = tracer * levels + l
            halo = edge_n[pl.ds(row, 1), :], edge_s[pl.ds(row, 1), :], column(e_turned, row, last), column(w_turned, row, 0)
            under, over = tracers[tracer, jnp.minimum(l + 1, levels - 1)], tracers[tracer, jnp.maximum(l - 1, 0)]
            held[tracer, l] = update(c, tracers[tracer, l], halo, under, over, forcing(tracer, l))
        return 0

    lax.fori_loop(0, levels, first_step, 0, unroll=8)

    def second_step(l, _):
        c = [weights[i, l] for i in range(5)]
        for tracer in range(2):
            row = tracer * levels + l
            halo = line_n[pl.ds(row, 1), :], line_s[pl.ds(row, 1), :], column(e_later, row, last), column(w_later, row, 0)
            under, over = held[tracer, jnp.minimum(l + 1, levels - 1)], held[tracer, jnp.maximum(l - 1, 0)]
            out[tracer, l] = update(c, held[tracer, l], halo, under, over, forcing(tracer, l))
        send(l).start()
        return 0

    lax.fori_loop(0, levels, second_step, 0, unroll=8)
    for l in range(levels):
        send(l).wait()


def backward_kernel(parts, slots_in, src_in, back, w, out, held, wide, picked, terms, slots, src, sems):
    total, width = terms.shape
    blocks = out.shape[0]
    batch = total // parts

    def copy(c):
        return pltpu.make_async_copy(w.at[pl.ds(c * batch, batch)], held.at[pl.ds(c * batch, batch)], sems.at[c])

    slots_copy = pltpu.make_async_copy(slots_in, slots, sems.at[parts])
    src_copy = pltpu.make_async_copy(src_in, src, sems.at[parts + 1])
    slots_copy.start()
    src_copy.start()
    for c in range(parts):
        copy(c).start()
    slots_copy.wait()
    wide[...] = back[...].astype(F32).reshape(wide.shape)

    def pick(i, _):
        for j in range(16):
            picked[pl.ds(i * 16 + j, 1), :] = wide[pl.ds(slots[i * 16 + j], 1), :]
        return 0

    lax.fori_loop(0, total // 16, pick, 0, unroll=2)
    row = iota((16, width), 0)

    def work(c, _):
        copy(c).wait()
        for g in range(batch // 16):
            at = pl.multiple_of(c * batch + g * 16, 16)
            rows = picked[pl.ds(at, 16), :]
            left = [jnp.where((row == r) | (row == 8 + r), rows, 0.0).astype(BF16) for r in range(8)]
            block = held[pl.ds(at, 16)].reshape(2, 8 * width, width)
            both = dot(jnp.concatenate(left, axis=1), jnp.concatenate([block[0], block[1]], axis=1), NN)
            terms[pl.ds(at, 8), :] = both[:8, :width]
            terms[pl.ds(at + 8, 8), :] = both[8:, width:]
        return 0

    lax.fori_loop(0, parts, work, 0)
    src_copy.wait()
    hot = (iota((blocks, total), 0) == src[...]).astype(F32).astype(BF16)
    value = terms[...]
    high = value.astype(BF16)
    low = (value - high.astype(F32)).astype(BF16)
    both = dot(hot, jnp.concatenate([high, low], axis=1), NN)
    out[...] = both[:, :width] + both[:, width:]


def backward(back, w, src, slots, blocks, parts=10):
    total, width, _ = w.shape
    devices, cap, _ = back.shape
    return pl.pallas_call(
        functools.partial(backward_kernel, parts),
        in_specs=[ANY, ANY, VMEM, ANY],
        out_specs=VMEM,
        scratch_shapes=[
            pltpu.VMEM(w.shape, BF16),
            pltpu.VMEM((devices * cap, width), F32),
            pltpu.VMEM((total, width), F32),
            pltpu.VMEM((total, width), F32),
            pltpu.SMEM((total,), jnp.int32),
            pltpu.VMEM((1, total), jnp.int32),
            pltpu.SemaphoreType.DMA((parts + 2,)),
        ],
        out_shape=jax.ShapeDtypeStruct((blocks, width), F32),
        compiler_params=kernel_params(46),
        cost_estimate=pl.CostEstimate(flops=2 * total * 8 * width * width, bytes_accessed=total * width * width * 2, transcendentals=0),
        name="backward_remap",
    )(slots, src.reshape(1, total), back, w)


def kernel(body, outs, name, mebibytes, bytes_accessed, scratch=(), **specs):
    return pl.pallas_call(
        body,
        out_shape=[jax.ShapeDtypeStruct(shape, dtype) for shape, dtype in outs],
        scratch_shapes=list(scratch),
        compiler_params=kernel_params(mebibytes),
        cost_estimate=pl.CostEstimate(flops=bytes_accessed, bytes_accessed=bytes_accessed, transcendentals=0),
        name=name,
        **specs,
    )


def neighbours(axis):
    count = lax.axis_size(axis)
    forward_pairs = [(i, i + 1) for i in range(count - 1)]
    return forward_pairs, [(b, a) for a, b in forward_pairs]


def on_device(atm_flux, remap_weights, remap_src, remap_dst, remap_owner, tracers, currents, land_sea):
    grid = n_sec, n_gx, n_gy = [lax.axis_size(axis) for axis in EVERY]
    devices = n_sec * n_gx * n_gy
    group = devices // 2
    total, width, _ = remap_weights.shape
    _, levels, height, _ = tracers.shape
    cap = up(2 * total // devices, 8)
    wide = SENT * width

    *sends, slots = forward(atm_flux, remap_weights, remap_src, remap_owner.reshape(1, total), remap_dst, grid, cap)
    chunk = sends[0].shape[1]
    order = swap_order(group)
    got = [sends[0]] + [swapped(sends[m], grid, m, 0) for m in order[1:]]
    early = order.index(1)

    side = (width, width)
    end = (7 * levels + 80, width)
    to_north, to_south = neighbours(NORTH)
    to_east, to_west = neighbours("gy")
    got[early], tracers_there, currents_there = lax.optimization_barrier((got[early], tracers, currents))
    own_s, own_n = kernel(rows_kernel, [(side, BF16)] * 2, "edge_rows", 16, 1 << 20)(
        tracers_there.reshape(-1, width), currents_there.reshape(-1, width), land_sea
    )
    from_n = lax.ppermute(own_s, NORTH, to_south)
    from_s = lax.ppermute(own_n, NORTH, to_north)
    got, from_n, from_s = lax.optimization_barrier((got, from_n, from_s))
    own_w, own_e = kernel(columns_kernel, [(end, BF16)] * 2, "edge_columns", 16, 1 << 22, [pltpu.VMEM(end, F32)] * 2)(
        tracers, currents, land_sea, from_n, from_s
    )
    from_e = lax.ppermute(own_w, "gy", to_west)
    from_w = lax.ppermute(own_e, "gy", to_east)
    part = (height + 16, wide)
    merged = kernel(functools.partial(merge_kernel, group), [(part, F32), (part, BF16)], "merge", 24, 1 << 22)(*got)
    parts = [merged[0], swapped(merged[1], grid, 0, 1)]

    edges = own_n, own_s, own_e, own_w, from_n, from_s, from_e, from_w
    (back,) = kernel(
        functools.partial(surface_kernel, grid, chunk, levels),
        [((devices, cap, width), BF16)],
        "surface",
        24,
        1 << 22,
    )(*parts, tracers[0:1, 0:3], currents[:, 0:2], land_sea, *edges)
    returned = lax.all_to_all(back, EVERY, split_axis=0, concat_axis=0, tiled=True)

    plane = (height, width)
    given = (*parts, *edges, land_sea, tracers, currents)
    (tracers_out,) = kernel(
        stencil_kernel,
        [(tracers.shape, F32)],
        "substeps",
        58,
        1 << 24,
        [pltpu.VMEM(x.shape, x.dtype) for x in given]
        + [
            pltpu.VMEM(tracers.shape, F32),
            pltpu.VMEM(tracers.shape, F32),
            pltpu.VMEM((5, levels) + plane, F32),
            pltpu.VMEM(side, F32),
            pltpu.VMEM(side, F32),
            pltpu.VMEM((2 * levels, width), F32),
            pltpu.VMEM((2 * levels, width), F32),
            pltpu.VMEM((levels, width), F32),
            pltpu.VMEM((3,) + plane, F32),
            pltpu.VMEM((4,) + plane, F32),
            pltpu.SemaphoreType.DMA((len(given) + levels,)),
        ],
        in_specs=[ANY] * len(given),
        out_specs=[ANY],
    )(*given)
    return tracers_out, backward(returned, remap_weights, remap_src, slots, atm_flux.shape[0])


def solution(mesh):
    return jax.shard_map(
        on_device,
        mesh=mesh,
        in_specs=(
            P(EVERY, None, None),
            P(EVERY, None, None),
            P(EVERY),
            P(EVERY),
            P(EVERY, None),
            P(None, None, NORTH, "gy"),
            P(None, None, NORTH, "gy"),
            P(NORTH, "gy"),
        ),
        out_specs=(P(None, None, NORTH, "gy"), P(EVERY, None)),
        check_vma=False,
    )
```

```python
import functools

import jax
import jax.numpy as jnp
from jax import lax
from jax.experimental import pallas as pl
from jax.experimental.pallas import tpu as pltpu
from jax.sharding import PartitionSpec as P

F32 = jnp.float32
BF16 = jnp.bfloat16
NT = (((1,), (1,)), ((), ()))
NN = (((1,), (0,)), ((), ()))
TN = (((0,), (0,)), ((), ()))
EVERY = ("sec", "gx", "gy")
NORTH = ("sec", "gx")
SENT = 5
KH = 0.1
KV = 0.1


def dot(left, right, dims):
    return lax.dot_general(left, right, dims, preferred_element_type=F32)


def iota(shape, dim):
    return lax.broadcasted_iota(jnp.int32, shape, dim)


def up(number, step):
    return -(-number // step) * step


def kernel_params(mebibytes):
    return pltpu.CompilerParams(vmem_limit_bytes=mebibytes << 20)


VMEM = pl.BlockSpec(memory_space=pltpu.VMEM)
SMEM = pl.BlockSpec(memory_space=pltpu.SMEM)
ANY = pl.BlockSpec(memory_space=pl.ANY)


def forward_kernel(parts, cap, grid, src_in, own_in, dst_in, flux_in, w, *refs):
    sends, (slots, held, mixed, acc, rows, xs, counts, renumbered, sems, src, own, dst, flux) = refs[:-13], refs[-13:]
    n_sec, n_gx, n_gy = grid
    devices, _, wide = xs.shape
    total, width, _ = held.shape
    batch = total // parts
    fields = flux.shape[1]
    main = sends[0].shape[1] - 16
    first = 8
    last = width - 1

    def copy(c):
        return pltpu.make_async_copy(w.at[pl.ds(c * batch, batch)], held.at[pl.ds(c * batch, batch)], sems.at[c])

    small = [(src_in, src), (own_in, own), (dst_in, dst), (flux_in, flux)]
    small = [pltpu.make_async_copy(there, here, sems.at[parts + i]) for i, (there, here) in enumerate(small)]
    for load in small:
        load.start()
    for c in range(parts):
        copy(c).start()

    plane = lax.axis_index("sec") * n_gy + lax.axis_index("gy")
    line = lax.axis_index("gx")

    def renumber(owner):
        x = lax.div(owner, n_gy)
        there = lax.div(x, n_gx) * n_gy + lax.rem(owner, n_gy)
        return (there ^ plane) * n_gx + (lax.rem(x, n_gx) ^ line)

    def clear(o, _):
        counts[o] = 0
        renumbered[o] = renumber(o)
        return 0

    lax.fori_loop(0, devices, clear, 0)
    rows[...] = jnp.full_like(rows, 255.0)
    acc[...] = jnp.zeros_like(acc)
    xs[...] = jnp.zeros_like(xs)
    for load in small:
        load.wait()
    full = flux[...].astype(F32)
    one = [full[:, f : f + 1] for f in range(fields)]
    heat = 0.2 * (one[1] + one[2] + one[3]) - 0.15 * one[5]
    salt = 0.2 * one[4] - 0.1 * one[5]
    heat_high = heat.astype(BF16).astype(F32)
    salt_high = salt.astype(BF16).astype(F32)
    mixed[...] = jnp.concatenate(
        [one[0], heat_high, salt_high, one[6], one[7], heat - heat_high, salt - salt_high, jnp.zeros_like(heat)], axis=1
    ).astype(BF16)

    low_rows = iota((fields, width), 0)
    low_rows = (low_rows == 1) | (low_rows == 2)

    def work(c, _):
        copy(c).wait()
        for b in range(0, batch, 2):
            k = c * batch + b
            left = jnp.concatenate([mixed[src[k]], mixed[src[k + 1]]], axis=0)
            both = dot(left, held[pl.ds(k, 2)].reshape(2 * width, width), NT)
            for z, part in enumerate((both[:fields, :width], both[fields:, width:])):
                part = part + jnp.where(low_rows, pltpu.roll(part, fields - 4, 0), 0.0)
                owner = own[0, k + z]
                at = counts[owner]
                counts[owner] = at + 1
                at = jnp.minimum(at, cap - 1)
                slots[k + z] = owner * cap + at
                slot = renumbered[owner] * cap + at
                acc[pl.ds(pl.multiple_of(slot * fields, fields), fields), :] = part
                rows[pl.ds(slot, 1), :] = jnp.full((1, width), dst[k + z].astype(F32), F32)
        return 0

    lax.fori_loop(0, parts, work, 0)

    lane = iota((cap, width), 1).astype(F32)
    sub = iota((cap, width), 0).astype(F32)
    row = iota((24, wide), 0)
    picks = {
        4: (0, 0), 5: (1, 0), 6: (3, 0), 7: (4, 0), 12: (0, last), 13: (1, last), 14: (3, last), 15: (4, last),
        20: (2, 0), 21: (3, 1), 22: (2, last), 23: (3, last - 1),
    }
    pick = jnp.full((24, wide), -1, jnp.int32)
    for at, (field, column) in picks.items():
        pick = jnp.where(row == at, field * width + column, pick)
    select = (iota((24, wide), 1) == pick).astype(F32).astype(BF16)
    row = iota((8, cap), 0)
    wanted = jnp.zeros((8, cap), F32)
    for at, x in enumerate((0, 1, last, last - 1, 0, 0, last, last)):
        wanted = jnp.where(row == at, float(x), wanted)
    group = 16

    def owners(g):
        ds = [g * group + j for j in range(group)]
        five = []
        for d in ds:
            x = [acc[pl.ds(d * cap * fields + f, cap, stride=fields), :] for f in range(SENT)]
            x = jnp.concatenate(x, axis=1)
            if cap > main:
                xs[d, 0 : cap - main, :] = x[main:]
            x = x.astype(BF16)
            sends[d // n_gx][d % n_gx, 0:main, :] = x[:main]
            five.append(x)
        where = [rows[pl.ds(pl.multiple_of(d * cap, 8), cap), :] for d in ds]
        hot = [(lane == r).astype(F32).astype(BF16) for r in where]
        flat = [jnp.sum(jnp.where(lane == sub, r, 0.0), axis=0, keepdims=True) for r in where]
        flat = [jnp.where(lane[:1] < cap, f, 255.0) for f in flat]
        edge = [dot(select, x, NT).astype(BF16) for x in five]
        sides = [dot(e, h, NN) for e, h in zip(edge, hot)]
        ends = [dot((f[:, :cap] == wanted).astype(F32).astype(BF16), x, NN) for f, x in zip(flat, five)]
        for d, f, side, end in zip(ds, flat, sides, ends):
            here = (d // n_gx) ^ plane
            here = (lax.div(here, n_gy) * n_gx + ((d % n_gx) ^ line)) * n_gy + lax.rem(here, n_gy)

            def at(offset):
                return renumbered[lax.rem(here + offset + 2 * devices, devices)]

            south_of, north_of, west_of, east_of = at(-n_gy), at(n_gy), at(-1), at(1)

            xs[south_of, first : first + 1, :] = end[0:1]
            xs[south_of, first + 1 : first + 2, 4 * width :] = end[1:2, 4 * width :]
            xs[north_of, first + 2 : first + 3, :] = end[2:3]
            xs[north_of, first + 3 : first + 4, 4 * width :] = end[3:4, 4 * width :]
            xs[at(-n_gy - 1), first + 4 : first + 5, 3 * width :] = end[4:5, 3 * width :]
            xs[at(-n_gy + 1), first + 5 : first + 6, 3 * width :] = end[5:6, 3 * width :]
            xs[at(n_gy - 1), first + 6 : first + 7, 3 * width :] = end[6:7, 3 * width :]
            xs[at(n_gy + 1), first + 7 : first + 8, 3 * width :] = end[7:8, 3 * width :]
            xs[west_of, first + 4 : first + 8, 0:width] = side[4:8]
            xs[east_of, first + 4 : first + 8, width : 2 * width] = side[12:16]
            xs[west_of, first + 4 : first + 6, 2 * width : 3 * width] = side[20:22]
            xs[east_of, first + 6 : first + 8, 2 * width : 3 * width] = side[22:24]
            xs[d, first + 1 : first + 2, 0:width] = f

    for g in range(devices // group):
        owners(g)

    for m, send in enumerate(sends):
        send[:, main:, :] = xs[m * n_gx : (m + 1) * n_gx].astype(BF16)


def forward(flux, w, src, own, dst, grid, cap, parts=8):
    n_sec, n_gx, n_gy = grid
    devices = n_sec * n_gx * n_gy
    total, width, _ = w.shape
    chunk = up(cap + 8, 16)
    fields = flux.shape[1]
    wide = SENT * width
    return pl.pallas_call(
        functools.partial(forward_kernel, parts, cap, grid),
        in_specs=[ANY] * 5,
        out_specs=[VMEM] * (n_sec * n_gy) + [SMEM],
        scratch_shapes=[
            pltpu.VMEM(w.shape, BF16),
            pltpu.VMEM(flux.shape, BF16),
            pltpu.VMEM((devices * cap * fields, width), F32),
            pltpu.VMEM((devices * cap, width), F32),
            pltpu.VMEM((devices, 16, wide), F32),
            pltpu.SMEM((devices,), jnp.int32),
            pltpu.SMEM((devices,), jnp.int32),
            pltpu.SemaphoreType.DMA((parts + 4,)),
            pltpu.SMEM(src.shape, jnp.int32),
            pltpu.SMEM(own.shape, jnp.int32),
            pltpu.SMEM(dst.shape, jnp.int32),
            pltpu.VMEM(flux.shape, BF16),
        ],
        out_shape=[jax.ShapeDtypeStruct((n_gx, chunk, wide), BF16)] * (n_sec * n_gy) + [jax.ShapeDtypeStruct((total,), jnp.int32)],
        compiler_params=kernel_params(58),
        cost_estimate=pl.CostEstimate(flops=2 * total * 8 * width * width, bytes_accessed=total * width * width * 2, transcendentals=0),
        name="forward_remap",
    )(src, own, dst, flux, w)


def merge_kernel(n_sources, *refs):
    sources, outs = refs[:n_sources], refs[n_sources:]
    outs, salts = outs[: len(outs) // 2], outs[len(outs) // 2 :]
    width = salts[0].shape[1]
    chunk = sources[0].shape[1]
    height = outs[0].shape[0] - 8
    first = chunk - 8
    count = n_sources * chunk
    for z, out in enumerate(outs):
        ext = None
        where = []
        for source in sources:
            piece = source[z, first:chunk, :].astype(F32)
            where.append(piece[1:2, :chunk])
            ext = piece if ext is None else ext + piece
        where = jnp.concatenate(where, axis=1)
        hot = (iota((height, count), 0).astype(F32) == where).astype(F32).astype(BF16)
        sums = dot(hot, jnp.concatenate([source[z] for source in sources], axis=0), NN)
        both = jnp.concatenate([sums, ext], axis=0)
        salts[z][...] = both[:, 2 * width : 3 * width].astype(salts[z].dtype)
        if count < 4 * width:
            where = jnp.concatenate([where, jnp.zeros((1, 4 * width - count), F32)], axis=1)
        salt = ext[:, 2 * width : 3 * width]
        row1 = jnp.concatenate([salt[5:6], salt[7:8], where[:, 3 * width :], ext[1:2, 4 * width :]], axis=1)
        row3 = jnp.concatenate([where[:, : 3 * width], ext[3:4, 4 * width :]], axis=1)
        both = jnp.concatenate([both[:, : 2 * width], both[:, 3 * width :]], axis=1)
        ext, row = both[height:], iota((8, 1), 0)
        ext = jnp.where(row == 1, row1, jnp.where(row == 3, row3, ext))
        out[...] = jnp.concatenate([both[:height], ext], axis=0).astype(out.dtype)


def rows_kernel(tracers, currents, land, south, north):
    height, width = land.shape
    levels = tracers.shape[0] // 2 // height
    for out, edge, second in ((south, 0, 1), (north, height - 1, height - 2)):
        out[...] = jnp.concatenate(
            [
                tracers[pl.ds(edge, 2 * levels, stride=height), :],
                tracers[pl.ds(second, 2 * levels, stride=height), :],
                currents[pl.ds(edge, 2 * levels, stride=height), :],
                currents[pl.ds(levels * height + second, levels, stride=height), :],
                *[land[x : x + 1, :].astype(F32) for x in (edge, second)],
                jnp.zeros((out.shape[0] - 7 * levels - 2, width), F32),
            ],
            axis=0,
        ).astype(BF16)


def columns_kernel(tracers, currents, land, from_n, from_s, west, east, west_wide, east_wide):
    levels = tracers.shape[1]
    width = tracers.shape[3]
    last = width - 1
    lane = iota((1, width), 1)
    west_wide[...] = jnp.zeros_like(west_wide)
    east_wide[...] = jnp.zeros_like(east_wide)

    def put(plane, near, far):
        turned = plane.T
        for out, edge, second in ((west_wide, 0, 1), (east_wide, last, last - 1)):
            out[pl.ds(near, 1), :] = turned[edge : edge + 1]
            if far is not None:
                out[pl.ds(far, 1), :] = turned[second : second + 1]

    def level(l, _):
        for t in range(2):
            put(tracers[t, l], t * levels + l, (2 + t) * levels + l)
        put(currents[0, l], 4 * levels + l, 6 * levels + l)
        put(currents[1, l], 5 * levels + l, None)
        return 0

    lax.fori_loop(0, levels, level, 0, unroll=2)
    put(land[...].astype(F32), 7 * levels, 7 * levels + 1)
    base = 7 * levels + 8
    n_all, s_all = from_n[...].astype(F32), from_s[...].astype(F32)
    for start, stop, at in ((0, 2 * levels, 0), (4 * levels, 6 * levels, 2 * levels), (7 * levels, 7 * levels + 8, 4 * levels)):
        n, s = n_all[start:stop], s_all[start:stop]
        west_wide[base + at : base + at + stop - start] = jnp.where(lane == last, pltpu.roll(n, last, 1), s)
        east_wide[base + at : base + at + stop - start] = jnp.where(lane == last, n, pltpu.roll(s, 1, 1))
    west[...] = west_wide[...].astype(BF16)
    east[...] = east_wide[...].astype(BF16)


def plus_side(q, other, speed, speed_other, passable):
    return KH * passable * (other - q) - 0.25 * (speed + speed_other) * passable * (q + other)


def minus_side(q, other, speed, speed_other, passable):
    return KH * passable * (other - q) + 0.25 * (speed_other + speed) * passable * (other + q)


def level_profile(levels, width):
    depth = iota((levels, width), 0).astype(F32)
    return jnp.exp(-depth / 4.0) * (1.0 - jnp.exp(jnp.full((levels, width), -0.25, F32)))


def strip_step(q, q_plus, q_minus, across, across_plus, across_minus, along, corner_q, corner_along, wet, wet_plus, wet_minus, corner_wet, forcing):
    levels, width = q.shape
    lane = iota((1, width), 1)
    row = iota((levels, 1), 0)

    def ahead(x, corner):
        return jnp.where(lane == width - 1, corner, pltpu.roll(x, width - 1, 1))

    def behind(x, corner):
        return jnp.where(lane == 0, corner, pltpu.roll(x, 1, 1))

    total = plus_side(q, q_plus, across, across_plus, wet * wet_plus)
    total += minus_side(q, q_minus, across, across_minus, wet * wet_minus)
    total += plus_side(q, ahead(q, corner_q), along, ahead(along, corner_along), wet * ahead(wet, corner_wet))
    total += minus_side(q, behind(q, corner_q), along, behind(along, corner_along), wet * behind(wet, corner_wet))
    below = jnp.where(row < levels - 1, pltpu.roll(q, levels - 1, 0) - q, 0.0)
    above = jnp.where(row > 0, q - pltpu.roll(q, 1, 0), 0.0)
    return q + total + wet * (KV * (below - above) + forcing)


def strips(tracer, levels, inner, outer, flux):
    width = outer[0].shape[1]
    lane = iota((1, width), 1)
    base = 7 * levels + 8
    north, south, east, west = outer

    def part(x, at, count=levels):
        return x[at : at + count]

    def corners(at, count):
        e, w = part(east, base + at, count), part(west, base + at, count)
        n = jnp.where(lane == width - 1, e, pltpu.roll(w, 1, 1))
        s = jnp.where(lane == width - 1, pltpu.roll(e, width - 1, 1), w)
        return n, s, e, w

    corner_q = corners(tracer * levels, levels)
    corner_u = corners(2 * levels, levels)
    corner_v = corners(3 * levels, levels)
    corner_wet = corners(4 * levels, 1)
    top = (iota((levels, 1), 0) == 0).astype(F32)
    profile = level_profile(levels, width)
    results = []
    for side in range(4):
        near, far = inner[side], outer[side]
        beside, out = part(near, tracer * levels), part(far, (2 + tracer) * levels)
        mid = part(far, tracer * levels)
        speed = 5 if side < 2 else 4
        along = part(far, (9 - speed) * levels)
        corner_along = (corner_u if side < 2 else corner_v)[side]
        across, across_in, across_out = part(far, speed * levels), part(near, speed * levels), part(far, 6 * levels)
        wet, wet_in, wet_out = part(far, 7 * levels, 1), part(near, 7 * levels, 1), part(far, 7 * levels + 1, 1)
        shortwave, heat, salt = flux[side]
        forcing = 0.3 * profile * shortwave + top * heat if tracer == 0 else top * salt
        if side % 2 == 0:
            pairs = (out, beside, across, across_out, across_in)
            wets = (wet, wet_out, wet_in)
        else:
            pairs = (beside, out, across, across_in, across_out)
            wets = (wet, wet_in, wet_out)
        results.append(strip_step(mid, *pairs, along, corner_q[side], corner_along, *wets, corner_wet[side], forcing))
    return results


def shifts(plane, north, south, east, west):
    height, width = plane.shape
    lane, row = iota(plane.shape, 1), iota(plane.shape, 0)
    return (
        jnp.where(lane == width - 1, east, pltpu.roll(plane, width - 1, 1)),
        jnp.where(lane == 0, west, pltpu.roll(plane, 1, 1)),
        jnp.where(row == height - 1, north, pltpu.roll(plane, height - 1, 0)),
        jnp.where(row == 0, south, pltpu.roll(plane, 1, 0)),
    )


def wet_products(wet, north, south, east, west):
    return [wet * other for other in shifts(wet, north, south, east, west)]


def coefficients(u, v, u_east, u_west, v_north, v_south, passable):
    east, west, north, south = passable
    height, width = u.shape
    lane, row = iota(u.shape, 1), iota(u.shape, 0)
    e = jnp.where(lane == width - 1, u_east, pltpu.roll(u, width - 1, 1))
    w = jnp.where(lane == 0, u_west, pltpu.roll(u, 1, 1))
    n = jnp.where(row == height - 1, v_north, pltpu.roll(v, height - 1, 0))
    s = jnp.where(row == 0, v_south, pltpu.roll(v, 1, 0))
    flow_e, flow_w = 0.25 * (u + e) * east, 0.25 * (w + u) * west
    flow_n, flow_s = 0.25 * (v + n) * north, 0.25 * (s + v) * south
    own = 1.0 + (flow_w - flow_e) + (flow_s - flow_n) - KH * (east + west + north + south)
    return own, KH * east - flow_e, KH * west + flow_w, KH * north - flow_n, KH * south + flow_s


def column(turned, index, lane):
    return pltpu.roll(turned, lax.rem(lane - index + 2 * turned.shape[1], turned.shape[1]), 1)


def corrected(edge, x_rows):
    row = iota((edge.shape[0], 1), 0)
    for at, x in x_rows:
        edge = edge + jnp.where(row == at, 0.1 * x, 0.0)
    return edge


def added(parts):
    total = parts[0][...]
    for part in parts[1:]:
        total = total + part[...].astype(F32)
    return total


def owner_sums(height, width, parts, salts=None):
    sums = added(parts)
    salt = jnp.zeros((height + 8, width), F32) if salts is None else added(salts)
    ext, row = sums[height:], iota((8, 1), 0)
    third = jnp.where(row == 5, ext[1:2, :width], jnp.where(row == 7, ext[1:2, width : 2 * width], salt[height:]))
    shortwave, heat, stress_u, stress_v = [sums[:height, f * width : (f + 1) * width] for f in range(4)]
    ext = jnp.concatenate([ext[:, : 2 * width], third, ext[:, 2 * width :]], axis=1)
    return (shortwave, heat, salt[:height], stress_u, stress_v), ext


def corrected_edges(levels, ext, stress_u, stress_v, near, far):
    height, width = stress_u.shape
    last = width - 1
    lane = iota((1, width), 1)

    def block(r, b):
        return ext[r : r + 1, b * width : (b + 1) * width]

    u, v, second = 4 * levels, 5 * levels, 6 * levels
    base = 7 * levels + 8
    corners = []
    for b in (3, 4):
        ne, nw, se, sw = [block(r, b) for r in (4, 5, 6, 7)]
        corners.append((jnp.where(lane == last, pltpu.roll(ne, last, 1), se), jnp.where(lane == last, nw, pltpu.roll(sw, 1, 1))))
    turned = stress_u.T
    own = [[(v, stress_v[last:])], [(v, stress_v[0:1])], [(u, turned[last:])], [(u, turned[0:1])]]
    beside = [
        [(u, block(0, 3)), (v, block(0, 4)), (second, block(1, 4))],
        [(u, block(2, 3)), (v, block(2, 4)), (second, block(3, 4))],
        [(u, block(6, 0)), (v, block(7, 0)), (second, block(5, 2)), (base + 2 * levels, corners[0][0]), (base + 3 * levels, corners[1][0])],
        [(u, block(6, 1)), (v, block(7, 1)), (second, block(7, 2)), (base + 2 * levels, corners[0][1]), (base + 3 * levels, corners[1][1])],
    ]
    near = [corrected(edge[...].astype(F32), x) for edge, x in zip(near, own)]
    return near, [corrected(edge[...].astype(F32), x) for edge, x in zip(far, beside)]


def surface_kernel(grid, chunk, levels, *refs):
    n_sec, n_gx, n_gy = grid
    planes = n_sec * n_gy
    parts, refs = refs[:n_gx], refs[n_gx:]
    tracers, currents, land, own_n, own_s, own_e, own_w, from_n, from_s, from_e, from_w, *refs = refs
    (back,) = refs
    height, width = land.shape
    last = width - 1
    lane = iota((1, width), 1)
    (shortwave, heat, salt, stress_u, stress_v), ext = owner_sums(height, width, parts)
    wet = land[...].astype(F32)
    u0 = currents[0, 0] + 0.1 * stress_u
    v0 = currents[1, 0] + 0.1 * stress_v
    near, far = corrected_edges(levels, ext, stress_u, stress_v, (own_n, own_s, own_e, own_w), (from_n, from_s, from_e, from_w))
    far_n, far_s, far_e, far_w = far
    e_turned, w_turned = far_e[:width].T, far_w[:width].T
    east = lambda index: column(e_turned, index, last)
    west = lambda index: column(w_turned, index, 0)
    passable = wet_products(
        wet, far_n[7 * levels : 7 * levels + 1], far_s[7 * levels : 7 * levels + 1], east(7 * levels), west(7 * levels)
    )
    lines = strips(0, levels, near, far, rim_flux(ext, width))
    profile = level_profile(levels, width)
    mix = KV * wet
    warm = 0.3 * wet * shortwave

    def weights(l, u, v):
        v_n, v_s = [x[5 * levels + l : 5 * levels + l + 1] for x in (far_n, far_s)]
        return coefficients(u, v, east(4 * levels + l), west(4 * levels + l), v_n, v_s, passable)

    def horizontal(c, q, halo):
        e, w, n, s = shifts(q, *halo)
        return c[0] * q + c[1] * e + c[2] * w + c[3] * n + c[4] * s

    def start(l):
        return far_n[l : l + 1], far_s[l : l + 1], east(l), west(l)

    q0, q1, q2 = tracers[0, 0], tracers[0, 1], tracers[0, 2]
    c0 = weights(0, u0, v0)
    c1 = weights(1, currents[0, 1], currents[1, 1])
    t0 = horizontal(c0, q0, start(0)) + mix * (q1 - q0) + warm * profile[0:1] + wet * heat
    t1 = horizontal(c1, q1, start(1)) + mix * ((q2 - q1) - (q1 - q0)) + warm * profile[1:2]
    sides = jnp.concatenate([lines[2][0:8], lines[3][0:8], jnp.zeros((width - 16, width), F32)], axis=0).T
    halo = lines[0][0:1], lines[1][0:1], column(sides, 0, last), column(sides, 8, 0)
    t0 = horizontal(c0, t0, halo) + mix * (t1 - t0) + warm * profile[0:1] + wet * heat
    sst = t0.astype(BF16)
    plane = lax.axis_index("sec") * n_gy + lax.axis_index("gy")
    line = lax.axis_index("gx")
    for z, part in enumerate(parts):
        rows = part[height:].astype(F32)
        where = jnp.concatenate([rows[3:4, : 3 * width], rows[1:2, 2 * width : 3 * width]], axis=1)[:, : planes * chunk]
        hot = (iota((height, planes * chunk), 0).astype(F32) == where).astype(F32)
        picked = dot(hot.T.astype(BF16), sst, NN).reshape(planes, chunk, width)
        for i, m in enumerate(swap_order(planes)):
            there = plane ^ m
            device = (lax.div(there, n_gy) * n_gx + (line ^ z)) * n_gy + lax.rem(there, n_gy)
            back[device] = picked[i, : back.shape[1]].astype(BF16)


def rim_flux(ext, width):
    def block(r, b):
        return ext[r : r + 1, b * width : (b + 1) * width]

    return (
        (block(0, 0), block(0, 1), block(0, 2)),
        (block(2, 0), block(2, 1), block(2, 2)),
        (block(4, 0), block(5, 0), block(4, 2)),
        (block(4, 1), block(5, 1), block(6, 2)),
    )


def stencil_kernel(n_gx, *refs):
    count = 2 * n_gx + 11
    given, result, here, refs = refs[:count], refs[count], refs[count + 1 : 2 * count + 1], refs[2 * count + 1 :]
    out, held, weights, edge_n, edge_s, line_n, line_s, depth, forced, passing, sems = refs
    parts, salts, edges = here[:n_gx], here[n_gx : 2 * n_gx], here[2 * n_gx : 2 * n_gx + 8]
    land, tracers, currents = here[2 * n_gx + 8 :]
    copies = [pltpu.make_async_copy(x, y, sems.at[i]) for i, (x, y) in enumerate(zip(given, here))]
    for copy in copies:
        copy.start()
    for copy in copies[:-2]:
        copy.wait()
    levels = tracers.shape[1]

    def send(l):
        return pltpu.make_async_copy(out.at[:, l], result.at[:, l], sems.at[count + l])

    height, width = land.shape
    last = width - 1
    wet = land[...].astype(F32)
    (shortwave, heat, salt, stress_u, stress_v), ext = owner_sums(height, width, parts, salts)
    near, far = corrected_edges(levels, ext, stress_u, stress_v, edges[:4], edges[4:])
    far_n, far_s, far_e, far_w = far
    edge_n[...], edge_s[...] = far_n, far_s
    e_turned, w_turned = far_e[:width].T, far_w[:width].T
    at = 7 * levels
    for i, x in enumerate(
        wet_products(wet, far_n[at : at + 1], far_s[at : at + 1], column(e_turned, at, last), column(w_turned, at, 0))
    ):
        passing[i] = x
    forced[0], forced[1], forced[2] = 0.3 * wet * shortwave, wet * heat, wet * salt
    depth[...] = level_profile(levels, width)
    columns = []
    for tracer in range(2):
        lines = strips(
            tracer, levels, near, far, rim_flux(ext, width)
        )
        line_n[tracer * levels : (tracer + 1) * levels] = lines[0]
        line_s[tracer * levels : (tracer + 1) * levels] = lines[1]
        columns.append(lines[2:])
    blank = jnp.zeros((width - 2 * levels, width), F32)
    e_later, w_later = [jnp.concatenate([columns[0][i], columns[1][i], blank], axis=0).T for i in range(2)]

    def update(c, q, halo, under, over, forcing):
        e, w, n, s = shifts(q, *halo)
        mixed = KV * land[...].astype(F32) * ((under - q) - (q - over))
        return c[0] * q + c[1] * e + c[2] * w + c[3] * n + c[4] * s + mixed + forcing

    def forcing(tracer, l):
        top = jnp.where(l == 0, 1.0, 0.0)
        if tracer == 0:
            return forced[0] * depth[pl.ds(l, 1), :] + top * forced[1]
        return top * forced[2]

    for copy in copies[-2:]:
        copy.wait()
    currents[0, 0] = currents[0, 0] + 0.1 * stress_u
    currents[1, 0] = currents[1, 0] + 0.1 * stress_v

    def first_step(l, _):
        u, v = currents[0, l], currents[1, l]
        row = 5 * levels + l
        c = coefficients(
            u, v, column(e_turned, 4 * levels + l, last), column(w_turned, 4 * levels + l, 0),
            edge_n[pl.ds(row, 1), :], edge_s[pl.ds(row, 1), :], [passing[i] for i in range(4)],
        )
        for i, x in enumerate(c):
            weights[i, l] = x
        for tracer in range(2):
            row = tracer * levels + l
            halo = edge_n[pl.ds(row, 1), :], edge_s[pl.ds(row, 1), :], column(e_turned, row, last), column(w_turned, row, 0)
            under, over = tracers[tracer, jnp.minimum(l + 1, levels - 1)], tracers[tracer, jnp.maximum(l - 1, 0)]
            held[tracer, l] = update(c, tracers[tracer, l], halo, under, over, forcing(tracer, l))
        return 0

    lax.fori_loop(0, levels, first_step, 0, unroll=8)

    def second_step(l, _):
        c = [weights[i, l] for i in range(5)]
        for tracer in range(2):
            row = tracer * levels + l
            halo = line_n[pl.ds(row, 1), :], line_s[pl.ds(row, 1), :], column(e_later, row, last), column(w_later, row, 0)
            under, over = held[tracer, jnp.minimum(l + 1, levels - 1)], held[tracer, jnp.maximum(l - 1, 0)]
            out[tracer, l] = update(c, held[tracer, l], halo, under, over, forcing(tracer, l))
        send(l).start()
        return 0

    lax.fori_loop(0, levels, second_step, 0, unroll=8)
    for l in range(levels):
        send(l).wait()


def backward_kernel(parts, slots_in, src_in, back, w, out, held, wide, picked, terms, slots, src, sems):
    total, width = terms.shape
    blocks = out.shape[0]
    batch = total // parts

    def copy(c):
        return pltpu.make_async_copy(w.at[pl.ds(c * batch, batch)], held.at[pl.ds(c * batch, batch)], sems.at[c])

    slots_copy = pltpu.make_async_copy(slots_in, slots, sems.at[parts])
    src_copy = pltpu.make_async_copy(src_in, src, sems.at[parts + 1])
    slots_copy.start()
    src_copy.start()
    for c in range(parts):
        copy(c).start()
    slots_copy.wait()
    wide[...] = back[...].astype(F32).reshape(wide.shape)

    def pick(i, _):
        for j in range(16):
            picked[pl.ds(i * 16 + j, 1), :] = wide[pl.ds(slots[i * 16 + j], 1), :]
        return 0

    lax.fori_loop(0, total // 16, pick, 0, unroll=2)
    row = iota((16, width), 0)

    def work(c, _):
        copy(c).wait()
        for g in range(batch // 16):
            at = pl.multiple_of(c * batch + g * 16, 16)
            rows = picked[pl.ds(at, 16), :]
            left = [jnp.where((row == r) | (row == 8 + r), rows, 0.0).astype(BF16) for r in range(8)]
            block = held[pl.ds(at, 16)].reshape(2, 8 * width, width)
            both = dot(jnp.concatenate(left, axis=1), jnp.concatenate([block[0], block[1]], axis=1), NN)
            terms[pl.ds(at, 8), :] = both[:8, :width]
            terms[pl.ds(at + 8, 8), :] = both[8:, width:]
        return 0

    lax.fori_loop(0, parts, work, 0)
    src_copy.wait()
    hot = (iota((blocks, total), 0) == src[...]).astype(F32).astype(BF16)
    value = terms[...]
    high = value.astype(BF16)
    low = (value - high.astype(F32)).astype(BF16)
    both = dot(hot, jnp.concatenate([high, low], axis=1), NN)
    out[...] = both[:, :width] + both[:, width:]


def backward(back, w, src, slots, blocks, parts=10):
    total, width, _ = w.shape
    devices, cap, _ = back.shape
    return pl.pallas_call(
        functools.partial(backward_kernel, parts),
        in_specs=[ANY, ANY, VMEM, ANY],
        out_specs=VMEM,
        scratch_shapes=[
            pltpu.VMEM(w.shape, BF16),
            pltpu.VMEM((devices * cap, width), F32),
            pltpu.VMEM((total, width), F32),
            pltpu.VMEM((total, width), F32),
            pltpu.SMEM((total,), jnp.int32),
            pltpu.VMEM((1, total), jnp.int32),
            pltpu.SemaphoreType.DMA((parts + 2,)),
        ],
        out_shape=jax.ShapeDtypeStruct((blocks, width), F32),
        compiler_params=kernel_params(46),
        cost_estimate=pl.CostEstimate(flops=2 * total * 8 * width * width, bytes_accessed=total * width * width * 2, transcendentals=0),
        name="backward_remap",
    )(slots, src.reshape(1, total), back, w)


def kernel(body, outs, name, mebibytes, bytes_accessed, scratch=(), **specs):
    return pl.pallas_call(
        body,
        out_shape=[jax.ShapeDtypeStruct(shape, dtype) for shape, dtype in outs],
        scratch_shapes=list(scratch),
        compiler_params=kernel_params(mebibytes),
        cost_estimate=pl.CostEstimate(flops=bytes_accessed, bytes_accessed=bytes_accessed, transcendentals=0),
        name=name,
        **specs,
    )


def neighbours(axis):
    count = lax.axis_size(axis)
    forward_pairs = [(i, i + 1) for i in range(count - 1)]
    return forward_pairs, [(b, a) for a, b in forward_pairs]


def swap_order(count):
    return [0, count - 1, count - 2, 1] + list(range(count - 3, 1, -1))


def swapped(array, axes, count, step):
    return lax.ppermute(array, axes, [(i, i ^ step) for i in range(count)])


def on_device(atm_flux, remap_weights, remap_src, remap_dst, remap_owner, tracers, currents, land_sea):
    grid = n_sec, n_gx, n_gy = [lax.axis_size(axis) for axis in EVERY]
    planes = n_sec * n_gy
    total, width, _ = remap_weights.shape
    _, levels, height, _ = tracers.shape
    cap = up(2 * total // (planes * n_gx), 8)
    wide = SENT * width

    *sends, slots = forward(atm_flux, remap_weights, remap_src, remap_owner.reshape(1, total), remap_dst, grid, cap)
    chunk = sends[0].shape[1]
    order = swap_order(planes)
    got = [sends[0]] + [swapped(sends[m], ("sec", "gy"), planes, m) for m in order[1:]]
    early = order.index(1)

    side = (width, width)
    end = (7 * levels + 80, width)
    to_north, to_south = neighbours(NORTH)
    to_east, to_west = neighbours("gy")
    got[early], tracers_there, currents_there = lax.optimization_barrier((got[early], tracers, currents))
    own_s, own_n = kernel(rows_kernel, [(side, BF16)] * 2, "edge_rows", 16, 1 << 20)(
        tracers_there.reshape(-1, width), currents_there.reshape(-1, width), land_sea
    )
    from_n = lax.ppermute(own_s, NORTH, to_south)
    from_s = lax.ppermute(own_n, NORTH, to_north)
    got, from_n, from_s = lax.optimization_barrier((got, from_n, from_s))
    own_w, own_e = kernel(columns_kernel, [(end, BF16)] * 2, "edge_columns", 16, 1 << 22, [pltpu.VMEM(end, F32)] * 2)(
        tracers, currents, land_sea, from_n, from_s
    )
    from_e = lax.ppermute(own_w, "gy", to_west)
    from_w = lax.ppermute(own_e, "gy", to_east)
    outs = [((height + 8, x), dtype) for x in (4 * width, width) for dtype in [F32] + [BF16] * (n_gx - 1)]
    merged = kernel(functools.partial(merge_kernel, planes), outs, "merge", 24, 1 << 22)(*got)
    parts, salts = merged[:n_gx], merged[n_gx:]
    parts = [parts[0]] + [swapped(parts[m], "gx", n_gx, m) for m in range(1, n_gx)]
    salts, from_e, from_w = lax.optimization_barrier((salts, from_e, from_w))
    salts = [salts[0]] + [swapped(salts[m], "gx", n_gx, m) for m in range(1, n_gx)]

    edges = own_n, own_s, own_e, own_w, from_n, from_s, from_e, from_w
    (back,) = kernel(
        functools.partial(surface_kernel, grid, chunk, levels),
        [((planes * n_gx, cap, width), BF16)],
        "surface",
        24,
        1 << 22,
    )(*parts, tracers[0:1, 0:3], currents[:, 0:2], land_sea, *edges)
    returned = lax.all_to_all(back, EVERY, split_axis=0, concat_axis=0, tiled=True)

    plane = (height, width)
    given = (*parts, *salts, *edges, land_sea, tracers, currents)
    (tracers_out,) = kernel(
        functools.partial(stencil_kernel, n_gx),
        [(tracers.shape, F32)],
        "substeps",
        58,
        1 << 24,
        [pltpu.VMEM(x.shape, x.dtype) for x in given]
        + [
            pltpu.VMEM(tracers.shape, F32),
            pltpu.VMEM(tracers.shape, F32),
            pltpu.VMEM((5, levels) + plane, F32),
            pltpu.VMEM(side, F32),
            pltpu.VMEM(side, F32),
            pltpu.VMEM((2 * levels, width), F32),
            pltpu.VMEM((2 * levels, width), F32),
            pltpu.VMEM((levels, width), F32),
            pltpu.VMEM((3,) + plane, F32),
            pltpu.VMEM((4,) + plane, F32),
            pltpu.SemaphoreType.DMA((len(given) + levels,)),
        ],
        in_specs=[ANY] * len(given),
        out_specs=[ANY],
    )(*given)
    return tracers_out, backward(returned, remap_weights, remap_src, slots, atm_flux.shape[0])


def solution(mesh):
    return jax.shard_map(
        on_device,
        mesh=mesh,
        in_specs=(
            P(EVERY, None, None),
            P(EVERY, None, None),
            P(EVERY),
            P(EVERY),
            P(EVERY, None),
            P(None, None, NORTH, "gy"),
            P(None, None, NORTH, "gy"),
            P(NORTH, "gy"),
        ),
        out_specs=(P(None, None, NORTH, "gy"), P(EVERY, None)),
        check_vma=False,
    )
```

```python
import functools

import jax
import jax.numpy as jnp
from jax import lax
from jax.experimental import pallas as pl
from jax.experimental.pallas import tpu as pltpu
from jax.sharding import PartitionSpec as P

F32 = jnp.float32
BF16 = jnp.bfloat16
NT = (((1,), (1,)), ((), ()))
NN = (((1,), (0,)), ((), ()))
TN = (((0,), (0,)), ((), ()))
EVERY = ("sec", "gx", "gy")
NORTH = ("sec", "gx")
SENT = 5
KH = 0.1
KV = 0.1


def dot(left, right, dims):
    return lax.dot_general(left, right, dims, preferred_element_type=F32)


def iota(shape, dim):
    return lax.broadcasted_iota(jnp.int32, shape, dim)


def up(number, step):
    return -(-number // step) * step


def kernel_params(mebibytes):
    return pltpu.CompilerParams(vmem_limit_bytes=mebibytes << 20)


VMEM = pl.BlockSpec(memory_space=pltpu.VMEM)
SMEM = pl.BlockSpec(memory_space=pltpu.SMEM)
ANY = pl.BlockSpec(memory_space=pl.ANY)


def forward_kernel(parts, cap, grid, src_in, own_in, dst_in, flux_in, w, *refs):
    sends, (slots, held, mixed, acc, rows, xs, counts, renumbered, sems, src, own, dst, flux) = refs[:-13], refs[-13:]
    n_sec, n_gx, n_gy = grid
    devices, _, wide = xs.shape
    total, width, _ = held.shape
    batch = total // parts
    fields = flux.shape[1]
    main = sends[0].shape[1] - 16
    first = 8
    last = width - 1

    def copy(c):
        return pltpu.make_async_copy(w.at[pl.ds(c * batch, batch)], held.at[pl.ds(c * batch, batch)], sems.at[c])

    small = [(src_in, src), (own_in, own), (dst_in, dst), (flux_in, flux)]
    small = [pltpu.make_async_copy(there, here, sems.at[parts + i]) for i, (there, here) in enumerate(small)]
    for load in small:
        load.start()
    for c in range(parts):
        copy(c).start()

    plane = lax.axis_index("sec") * n_gy + lax.axis_index("gy")
    line = lax.axis_index("gx")

    def renumber(owner):
        x = lax.div(owner, n_gy)
        there = lax.div(x, n_gx) * n_gy + lax.rem(owner, n_gy)
        return (there ^ plane) * n_gx + (lax.rem(x, n_gx) ^ line)

    def clear(o, _):
        counts[o] = 0
        renumbered[o] = renumber(o)
        return 0

    lax.fori_loop(0, devices, clear, 0)
    rows[...] = jnp.full_like(rows, 255.0)
    acc[...] = jnp.zeros_like(acc)
    xs[...] = jnp.zeros_like(xs)
    for load in small:
        load.wait()
    full = flux[...].astype(F32)
    one = [full[:, f : f + 1] for f in range(fields)]
    heat = 0.2 * (one[1] + one[2] + one[3]) - 0.15 * one[5]
    salt = 0.2 * one[4] - 0.1 * one[5]
    heat_high = heat.astype(BF16).astype(F32)
    salt_high = salt.astype(BF16).astype(F32)
    mixed[...] = jnp.concatenate(
        [one[0], heat_high, salt_high, one[6], one[7], heat - heat_high, salt - salt_high, jnp.zeros_like(heat)], axis=1
    ).astype(BF16)

    low_rows = iota((fields, width), 0)
    low_rows = (low_rows == 1) | (low_rows == 2)

    def work(c, _):
        copy(c).wait()
        for b in range(0, batch, 2):
            k = c * batch + b
            left = jnp.concatenate([mixed[src[k]], mixed[src[k + 1]]], axis=0)
            both = dot(left, held[pl.ds(k, 2)].reshape(2 * width, width), NT)
            for z, part in enumerate((both[:fields, :width], both[fields:, width:])):
                part = part + jnp.where(low_rows, pltpu.roll(part, fields - 4, 0), 0.0)
                owner = own[0, k + z]
                at = counts[owner]
                counts[owner] = at + 1
                at = jnp.minimum(at, cap - 1)
                slots[k + z] = owner * cap + at
                slot = renumbered[owner] * cap + at
                acc[pl.ds(pl.multiple_of(slot * fields, fields), fields), :] = part
                rows[pl.ds(slot, 1), :] = jnp.full((1, width), dst[k + z].astype(F32), F32)
        return 0

    lax.fori_loop(0, parts, work, 0)

    lane = iota((cap, width), 1).astype(F32)
    sub = iota((cap, width), 0).astype(F32)
    row = iota((24, wide), 0)
    picks = {
        4: (0, 0), 5: (1, 0), 6: (3, 0), 7: (4, 0), 12: (0, last), 13: (1, last), 14: (3, last), 15: (4, last),
        20: (2, 0), 21: (3, 1), 22: (2, last), 23: (3, last - 1),
    }
    pick = jnp.full((24, wide), -1, jnp.int32)
    for at, (field, column) in picks.items():
        pick = jnp.where(row == at, field * width + column, pick)
    select = (iota((24, wide), 1) == pick).astype(F32).astype(BF16)
    row = iota((8, cap), 0)
    wanted = jnp.zeros((8, cap), F32)
    for at, x in enumerate((0, 1, last, last - 1, 0, 0, last, last)):
        wanted = jnp.where(row == at, float(x), wanted)
    group = 16

    def owners(g):
        ds = [g * group + j for j in range(group)]
        five = []
        for d in ds:
            x = [acc[pl.ds(d * cap * fields + f, cap, stride=fields), :] for f in range(SENT)]
            x = jnp.concatenate(x, axis=1)
            if cap > main:
                xs[d, 0 : cap - main, :] = x[main:]
            x = x.astype(BF16)
            sends[d // n_gx][d % n_gx, 0:main, :] = x[:main]
            five.append(x)
        where = [rows[pl.ds(pl.multiple_of(d * cap, 8), cap), :] for d in ds]
        hot = [(lane == r).astype(F32).astype(BF16) for r in where]
        flat = [jnp.sum(jnp.where(lane == sub, r, 0.0), axis=0, keepdims=True) for r in where]
        flat = [jnp.where(lane[:1] < cap, f, 255.0) for f in flat]
        edge = [dot(select, x, NT).astype(BF16) for x in five]
        sides = [dot(e, h, NN) for e, h in zip(edge, hot)]
        ends = [dot((f[:, :cap] == wanted).astype(F32).astype(BF16), x, NN) for f, x in zip(flat, five)]
        for d, f, side, end in zip(ds, flat, sides, ends):
            here = (d // n_gx) ^ plane
            here = (lax.div(here, n_gy) * n_gx + ((d % n_gx) ^ line)) * n_gy + lax.rem(here, n_gy)

            def at(offset):
                return renumbered[lax.rem(here + offset + 2 * devices, devices)]

            south_of, north_of, west_of, east_of = at(-n_gy), at(n_gy), at(-1), at(1)

            xs[south_of, first : first + 1, :] = end[0:1]
            xs[south_of, first + 1 : first + 2, 4 * width :] = end[1:2, 4 * width :]
            xs[north_of, first + 2 : first + 3, :] = end[2:3]
            xs[north_of, first + 3 : first + 4, 4 * width :] = end[3:4, 4 * width :]
            xs[at(-n_gy - 1), first + 4 : first + 5, 3 * width :] = end[4:5, 3 * width :]
            xs[at(-n_gy + 1), first + 5 : first + 6, 3 * width :] = end[5:6, 3 * width :]
            xs[at(n_gy - 1), first + 6 : first + 7, 3 * width :] = end[6:7, 3 * width :]
            xs[at(n_gy + 1), first + 7 : first + 8, 3 * width :] = end[7:8, 3 * width :]
            xs[west_of, first + 4 : first + 8, 0:width] = side[4:8]
            xs[east_of, first + 4 : first + 8, width : 2 * width] = side[12:16]
            xs[west_of, first + 4 : first + 6, 2 * width : 3 * width] = side[20:22]
            xs[east_of, first + 6 : first + 8, 2 * width : 3 * width] = side[22:24]
            xs[d, first + 1 : first + 2, 0:width] = f

    for g in range(devices // group):
        owners(g)

    for m, send in enumerate(sends):
        send[:, main:, :] = xs[m * n_gx : (m + 1) * n_gx].astype(BF16)


def forward(flux, w, src, own, dst, grid, cap, parts=8):
    n_sec, n_gx, n_gy = grid
    devices = n_sec * n_gx * n_gy
    total, width, _ = w.shape
    chunk = up(cap + 8, 16)
    fields = flux.shape[1]
    wide = SENT * width
    return pl.pallas_call(
        functools.partial(forward_kernel, parts, cap, grid),
        in_specs=[ANY] * 5,
        out_specs=[VMEM] * (n_sec * n_gy) + [SMEM],
        scratch_shapes=[
            pltpu.VMEM(w.shape, BF16),
            pltpu.VMEM(flux.shape, BF16),
            pltpu.VMEM((devices * cap * fields, width), F32),
            pltpu.VMEM((devices * cap, width), F32),
            pltpu.VMEM((devices, 16, wide), F32),
            pltpu.SMEM((devices,), jnp.int32),
            pltpu.SMEM((devices,), jnp.int32),
            pltpu.SemaphoreType.DMA((parts + 4,)),
            pltpu.SMEM(src.shape, jnp.int32),
            pltpu.SMEM(own.shape, jnp.int32),
            pltpu.SMEM(dst.shape, jnp.int32),
            pltpu.VMEM(flux.shape, BF16),
        ],
        out_shape=[jax.ShapeDtypeStruct((n_gx, chunk, wide), BF16)] * (n_sec * n_gy) + [jax.ShapeDtypeStruct((total,), jnp.int32)],
        compiler_params=kernel_params(58),
        cost_estimate=pl.CostEstimate(flops=2 * total * 8 * width * width, bytes_accessed=total * width * width * 2, transcendentals=0),
        name="forward_remap",
    )(src, own, dst, flux, w)


def merge_kernel(n_sources, *refs):
    sources, outs = refs[:n_sources], refs[n_sources:]
    outs, salts = outs[: len(outs) // 2], outs[len(outs) // 2 :]
    width = salts[0].shape[1]
    chunk = sources[0].shape[1]
    height = outs[0].shape[0] - 8
    first = chunk - 8
    count = n_sources * chunk
    for z, out in enumerate(outs):
        ext = None
        where = []
        for source in sources:
            piece = source[z, first:chunk, :].astype(F32)
            where.append(piece[1:2, :chunk])
            ext = piece if ext is None else ext + piece
        where = jnp.concatenate(where, axis=1)
        hot = (iota((height, count), 0).astype(F32) == where).astype(F32).astype(BF16)
        sums = dot(hot, jnp.concatenate([source[z] for source in sources], axis=0), NN)
        both = jnp.concatenate([sums, ext], axis=0)
        salts[z][...] = both[:, 2 * width : 3 * width].astype(salts[z].dtype)
        if count < 4 * width:
            where = jnp.concatenate([where, jnp.zeros((1, 4 * width - count), F32)], axis=1)
        salt = ext[:, 2 * width : 3 * width]
        row1 = jnp.concatenate([salt[5:6], salt[7:8], where[:, 3 * width :], ext[1:2, 4 * width :]], axis=1)
        row3 = jnp.concatenate([where[:, : 3 * width], ext[3:4, 4 * width :]], axis=1)
        both = jnp.concatenate([both[:, : 2 * width], both[:, 3 * width :]], axis=1)
        ext, row = both[height:], iota((8, 1), 0)
        ext = jnp.where(row == 1, row1, jnp.where(row == 3, row3, ext))
        out[...] = jnp.concatenate([both[:height], ext], axis=0).astype(out.dtype)


def rows_kernel(tracers, currents, land, south, north):
    height, width = land.shape
    levels = tracers.shape[0] // 2 // height
    for out, edge, second in ((south, 0, 1), (north, height - 1, height - 2)):
        out[...] = jnp.concatenate(
            [
                tracers[pl.ds(edge, 2 * levels, stride=height), :],
                tracers[pl.ds(second, 2 * levels, stride=height), :],
                currents[pl.ds(edge, 2 * levels, stride=height), :],
                currents[pl.ds(levels * height + second, levels, stride=height), :],
                *[land[x : x + 1, :].astype(F32) for x in (edge, second)],
                jnp.zeros((out.shape[0] - 7 * levels - 2, width), F32),
            ],
            axis=0,
        ).astype(BF16)


def columns_kernel(tracers, currents, land, from_n, from_s, west, east, west_wide, east_wide):
    levels = tracers.shape[1]
    width = tracers.shape[3]
    last = width - 1
    lane = iota((1, width), 1)
    west_wide[...] = jnp.zeros_like(west_wide)
    east_wide[...] = jnp.zeros_like(east_wide)

    def put(plane, near, far):
        turned = plane.T
        for out, edge, second in ((west_wide, 0, 1), (east_wide, last, last - 1)):
            out[pl.ds(near, 1), :] = turned[edge : edge + 1]
            if far is not None:
                out[pl.ds(far, 1), :] = turned[second : second + 1]

    def level(l, _):
        for t in range(2):
            put(tracers[t, l], t * levels + l, (2 + t) * levels + l)
        put(currents[0, l], 4 * levels + l, 6 * levels + l)
        put(currents[1, l], 5 * levels + l, None)
        return 0

    lax.fori_loop(0, levels, level, 0, unroll=2)
    put(land[...].astype(F32), 7 * levels, 7 * levels + 1)
    base = 7 * levels + 8
    n_all, s_all = from_n[...].astype(F32), from_s[...].astype(F32)
    for start, stop, at in ((0, 2 * levels, 0), (4 * levels, 6 * levels, 2 * levels), (7 * levels, 7 * levels + 8, 4 * levels)):
        n, s = n_all[start:stop], s_all[start:stop]
        west_wide[base + at : base + at + stop - start] = jnp.where(lane == last, pltpu.roll(n, last, 1), s)
        east_wide[base + at : base + at + stop - start] = jnp.where(lane == last, n, pltpu.roll(s, 1, 1))
    west[...] = west_wide[...].astype(BF16)
    east[...] = east_wide[...].astype(BF16)


def plus_side(q, other, speed, speed_other, passable):
    return KH * passable * (other - q) - 0.25 * (speed + speed_other) * passable * (q + other)


def minus_side(q, other, speed, speed_other, passable):
    return KH * passable * (other - q) + 0.25 * (speed_other + speed) * passable * (other + q)


def level_profile(levels, width):
    depth = iota((levels, width), 0).astype(F32)
    return jnp.exp(-depth / 4.0) * (1.0 - jnp.exp(jnp.full((levels, width), -0.25, F32)))


def strip_step(q, q_plus, q_minus, across, across_plus, across_minus, along, corner_q, corner_along, wet, wet_plus, wet_minus, corner_wet, forcing):
    levels, width = q.shape
    lane = iota((1, width), 1)
    row = iota((levels, 1), 0)

    def ahead(x, corner):
        return jnp.where(lane == width - 1, corner, pltpu.roll(x, width - 1, 1))

    def behind(x, corner):
        return jnp.where(lane == 0, corner, pltpu.roll(x, 1, 1))

    total = plus_side(q, q_plus, across, across_plus, wet * wet_plus)
    total += minus_side(q, q_minus, across, across_minus, wet * wet_minus)
    total += plus_side(q, ahead(q, corner_q), along, ahead(along, corner_along), wet * ahead(wet, corner_wet))
    total += minus_side(q, behind(q, corner_q), along, behind(along, corner_along), wet * behind(wet, corner_wet))
    below = jnp.where(row < levels - 1, pltpu.roll(q, levels - 1, 0) - q, 0.0)
    above = jnp.where(row > 0, q - pltpu.roll(q, 1, 0), 0.0)
    return q + total + wet * (KV * (below - above) + forcing)


def strips(tracer, levels, inner, outer, flux):
    width = outer[0].shape[1]
    lane = iota((1, width), 1)
    base = 7 * levels + 8
    north, south, east, west = outer

    def part(x, at, count=levels):
        return x[at : at + count]

    def corners(at, count):
        e, w = part(east, base + at, count), part(west, base + at, count)
        n = jnp.where(lane == width - 1, e, pltpu.roll(w, 1, 1))
        s = jnp.where(lane == width - 1, pltpu.roll(e, width - 1, 1), w)
        return n, s, e, w

    corner_q = corners(tracer * levels, levels)
    corner_u = corners(2 * levels, levels)
    corner_v = corners(3 * levels, levels)
    corner_wet = corners(4 * levels, 1)
    top = (iota((levels, 1), 0) == 0).astype(F32)
    profile = level_profile(levels, width)
    results = []
    for side in range(4):
        near, far = inner[side], outer[side]
        beside, out = part(near, tracer * levels), part(far, (2 + tracer) * levels)
        mid = part(far, tracer * levels)
        speed = 5 if side < 2 else 4
        along = part(far, (9 - speed) * levels)
        corner_along = (corner_u if side < 2 else corner_v)[side]
        across, across_in, across_out = part(far, speed * levels), part(near, speed * levels), part(far, 6 * levels)
        wet, wet_in, wet_out = part(far, 7 * levels, 1), part(near, 7 * levels, 1), part(far, 7 * levels + 1, 1)
        shortwave, heat, salt = flux[side]
        forcing = 0.3 * profile * shortwave + top * heat if tracer == 0 else top * salt
        if side % 2 == 0:
            pairs = (out, beside, across, across_out, across_in)
            wets = (wet, wet_out, wet_in)
        else:
            pairs = (beside, out, across, across_in, across_out)
            wets = (wet, wet_in, wet_out)
        results.append(strip_step(mid, *pairs, along, corner_q[side], corner_along, *wets, corner_wet[side], forcing))
    return results


def shifts(plane, north, south, east, west):
    height, width = plane.shape
    lane, row = iota(plane.shape, 1), iota(plane.shape, 0)
    return (
        jnp.where(lane == width - 1, east, pltpu.roll(plane, width - 1, 1)),
        jnp.where(lane == 0, west, pltpu.roll(plane, 1, 1)),
        jnp.where(row == height - 1, north, pltpu.roll(plane, height - 1, 0)),
        jnp.where(row == 0, south, pltpu.roll(plane, 1, 0)),
    )


def wet_products(wet, north, south, east, west):
    return [wet * other for other in shifts(wet, north, south, east, west)]


def coefficients(u, v, u_east, u_west, v_north, v_south, passable):
    east, west, north, south = passable
    height, width = u.shape
    lane, row = iota(u.shape, 1), iota(u.shape, 0)
    e = jnp.where(lane == width - 1, u_east, pltpu.roll(u, width - 1, 1))
    w = jnp.where(lane == 0, u_west, pltpu.roll(u, 1, 1))
    n = jnp.where(row == height - 1, v_north, pltpu.roll(v, height - 1, 0))
    s = jnp.where(row == 0, v_south, pltpu.roll(v, 1, 0))
    flow_e, flow_w = 0.25 * (u + e) * east, 0.25 * (w + u) * west
    flow_n, flow_s = 0.25 * (v + n) * north, 0.25 * (s + v) * south
    own = 1.0 + (flow_w - flow_e) + (flow_s - flow_n) - KH * (east + west + north + south)
    return own, KH * east - flow_e, KH * west + flow_w, KH * north - flow_n, KH * south + flow_s


def column(turned, index, lane):
    return pltpu.roll(turned, lax.rem(lane - index + 2 * turned.shape[1], turned.shape[1]), 1)


def corrected(edge, x_rows):
    row = iota((edge.shape[0], 1), 0)
    for at, x in x_rows:
        edge = edge + jnp.where(row == at, 0.1 * x, 0.0)
    return edge


def added(parts):
    total = parts[0][...]
    for part in parts[1:]:
        total = total + part[...].astype(F32)
    return total


def owner_sums(height, width, parts, salts=None):
    sums = added(parts)
    salt = jnp.zeros((height + 8, width), F32) if salts is None else added(salts)
    ext, row = sums[height:], iota((8, 1), 0)
    third = jnp.where(row == 5, ext[1:2, :width], jnp.where(row == 7, ext[1:2, width : 2 * width], salt[height:]))
    shortwave, heat, stress_u, stress_v = [sums[:height, f * width : (f + 1) * width] for f in range(4)]
    ext = jnp.concatenate([ext[:, : 2 * width], third, ext[:, 2 * width :]], axis=1)
    return (shortwave, heat, salt[:height], stress_u, stress_v), ext


def corrected_edges(levels, ext, stress_u, stress_v, near, far):
    height, width = stress_u.shape
    last = width - 1
    lane = iota((1, width), 1)

    def block(r, b):
        return ext[r : r + 1, b * width : (b + 1) * width]

    u, v, second = 4 * levels, 5 * levels, 6 * levels
    base = 7 * levels + 8
    corners = []
    for b in (3, 4):
        ne, nw, se, sw = [block(r, b) for r in (4, 5, 6, 7)]
        corners.append((jnp.where(lane == last, pltpu.roll(ne, last, 1), se), jnp.where(lane == last, nw, pltpu.roll(sw, 1, 1))))
    turned = stress_u.T
    own = [[(v, stress_v[last:])], [(v, stress_v[0:1])], [(u, turned[last:])], [(u, turned[0:1])]]
    beside = [
        [(u, block(0, 3)), (v, block(0, 4)), (second, block(1, 4))],
        [(u, block(2, 3)), (v, block(2, 4)), (second, block(3, 4))],
        [(u, block(6, 0)), (v, block(7, 0)), (second, block(5, 2)), (base + 2 * levels, corners[0][0]), (base + 3 * levels, corners[1][0])],
        [(u, block(6, 1)), (v, block(7, 1)), (second, block(7, 2)), (base + 2 * levels, corners[0][1]), (base + 3 * levels, corners[1][1])],
    ]
    near = [corrected(edge[...].astype(F32), x) for edge, x in zip(near, own)]
    return near, [corrected(edge[...].astype(F32), x) for edge, x in zip(far, beside)]


def surface_kernel(grid, chunk, levels, *refs):
    n_sec, n_gx, n_gy = grid
    planes = n_sec * n_gy
    parts, refs = refs[:n_gx], refs[n_gx:]
    tracers, currents, land, own_n, own_s, own_e, own_w, from_n, from_s, from_e, from_w, *refs = refs
    (back,) = refs
    height, width = land.shape
    last = width - 1
    lane = iota((1, width), 1)
    (shortwave, heat, salt, stress_u, stress_v), ext = owner_sums(height, width, parts)
    wet = land[...].astype(F32)
    u0 = currents[0, 0] + 0.1 * stress_u
    v0 = currents[1, 0] + 0.1 * stress_v
    near, far = corrected_edges(levels, ext, stress_u, stress_v, (own_n, own_s, own_e, own_w), (from_n, from_s, from_e, from_w))
    far_n, far_s, far_e, far_w = far
    e_turned, w_turned = far_e[:width].T, far_w[:width].T
    east = lambda index: column(e_turned, index, last)
    west = lambda index: column(w_turned, index, 0)
    passable = wet_products(
        wet, far_n[7 * levels : 7 * levels + 1], far_s[7 * levels : 7 * levels + 1], east(7 * levels), west(7 * levels)
    )
    lines = strips(0, levels, near, far, rim_flux(ext, width))
    profile = level_profile(levels, width)
    mix = KV * wet
    warm = 0.3 * wet * shortwave

    def weights(l, u, v):
        v_n, v_s = [x[5 * levels + l : 5 * levels + l + 1] for x in (far_n, far_s)]
        return coefficients(u, v, east(4 * levels + l), west(4 * levels + l), v_n, v_s, passable)

    def horizontal(c, q, halo):
        e, w, n, s = shifts(q, *halo)
        return c[0] * q + c[1] * e + c[2] * w + c[3] * n + c[4] * s

    def start(l):
        return far_n[l : l + 1], far_s[l : l + 1], east(l), west(l)

    q0, q1, q2 = tracers[0, 0], tracers[0, 1], tracers[0, 2]
    c0 = weights(0, u0, v0)
    c1 = weights(1, currents[0, 1], currents[1, 1])
    t0 = horizontal(c0, q0, start(0)) + mix * (q1 - q0) + warm * profile[0:1] + wet * heat
    t1 = horizontal(c1, q1, start(1)) + mix * ((q2 - q1) - (q1 - q0)) + warm * profile[1:2]
    sides = jnp.concatenate([lines[2][0:8], lines[3][0:8], jnp.zeros((width - 16, width), F32)], axis=0).T
    halo = lines[0][0:1], lines[1][0:1], column(sides, 0, last), column(sides, 8, 0)
    t0 = horizontal(c0, t0, halo) + mix * (t1 - t0) + warm * profile[0:1] + wet * heat
    sst = t0.astype(BF16)
    plane = lax.axis_index("sec") * n_gy + lax.axis_index("gy")
    line = lax.axis_index("gx")
    for z, part in enumerate(parts):
        rows = part[height:].astype(F32)
        where = jnp.concatenate([rows[3:4, : 3 * width], rows[1:2, 2 * width : 3 * width]], axis=1)[:, : planes * chunk]
        hot = (iota((height, planes * chunk), 0).astype(F32) == where).astype(F32)
        picked = dot(hot.T.astype(BF16), sst, NN).reshape(planes, chunk, width)
        for i, m in enumerate(swap_order(planes)):
            there = plane ^ m
            device = (lax.div(there, n_gy) * n_gx + (line ^ z)) * n_gy + lax.rem(there, n_gy)
            back[device] = picked[i, : back.shape[1]].astype(BF16)


def rim_flux(ext, width):
    def block(r, b):
        return ext[r : r + 1, b * width : (b + 1) * width]

    return (
        (block(0, 0), block(0, 1), block(0, 2)),
        (block(2, 0), block(2, 1), block(2, 2)),
        (block(4, 0), block(5, 0), block(4, 2)),
        (block(4, 1), block(5, 1), block(6, 2)),
    )


def stencil_kernel(n_gx, *refs):
    count = 2 * n_gx + 11
    given, result, here, refs = refs[:count], refs[count], refs[count + 1 : 2 * count + 1], refs[2 * count + 1 :]
    out, held, weights, edge_n, edge_s, line_n, line_s, depth, forced, passing, sems = refs
    parts, salts, edges = here[:n_gx], here[n_gx : 2 * n_gx], here[2 * n_gx : 2 * n_gx + 8]
    land, tracers, currents = here[2 * n_gx + 8 :]
    copies = [pltpu.make_async_copy(x, y, sems.at[i]) for i, (x, y) in enumerate(zip(given, here))]
    for copy in copies:
        copy.start()
    for copy in copies[:-2]:
        copy.wait()
    levels = tracers.shape[1]

    def send(l):
        return pltpu.make_async_copy(out.at[:, l], result.at[:, l], sems.at[count + l])

    height, width = land.shape
    last = width - 1
    wet = land[...].astype(F32)
    (shortwave, heat, salt, stress_u, stress_v), ext = owner_sums(height, width, parts, salts)
    near, far = corrected_edges(levels, ext, stress_u, stress_v, edges[:4], edges[4:])
    far_n, far_s, far_e, far_w = far
    edge_n[...], edge_s[...] = far_n, far_s
    e_turned, w_turned = far_e[:width].T, far_w[:width].T
    at = 7 * levels
    for i, x in enumerate(
        wet_products(wet, far_n[at : at + 1], far_s[at : at + 1], column(e_turned, at, last), column(w_turned, at, 0))
    ):
        passing[i] = x
    forced[0], forced[1], forced[2] = 0.3 * wet * shortwave, wet * heat, wet * salt
    depth[...] = level_profile(levels, width)
    columns = []
    for tracer in range(2):
        lines = strips(
            tracer, levels, near, far, rim_flux(ext, width)
        )
        line_n[tracer * levels : (tracer + 1) * levels] = lines[0]
        line_s[tracer * levels : (tracer + 1) * levels] = lines[1]
        columns.append(lines[2:])
    blank = jnp.zeros((width - 2 * levels, width), F32)
    e_later, w_later = [jnp.concatenate([columns[0][i], columns[1][i], blank], axis=0).T for i in range(2)]

    def update(c, q, halo, under, over, forcing):
        e, w, n, s = shifts(q, *halo)
        mixed = KV * land[...].astype(F32) * ((under - q) - (q - over))
        return c[0] * q + c[1] * e + c[2] * w + c[3] * n + c[4] * s + mixed + forcing

    def forcing(tracer, l):
        top = jnp.where(l == 0, 1.0, 0.0)
        if tracer == 0:
            return forced[0] * depth[pl.ds(l, 1), :] + top * forced[1]
        return top * forced[2]

    for copy in copies[-2:]:
        copy.wait()
    currents[0, 0] = currents[0, 0] + 0.1 * stress_u
    currents[1, 0] = currents[1, 0] + 0.1 * stress_v

    def first_step(l, _):
        u, v = currents[0, l], currents[1, l]
        row = 5 * levels + l
        c = coefficients(
            u, v, column(e_turned, 4 * levels + l, last), column(w_turned, 4 * levels + l, 0),
            edge_n[pl.ds(row, 1), :], edge_s[pl.ds(row, 1), :], [passing[i] for i in range(4)],
        )
        for i, x in enumerate(c):
            weights[i, l] = x
        for tracer in range(2):
            row = tracer * levels + l
            halo = edge_n[pl.ds(row, 1), :], edge_s[pl.ds(row, 1), :], column(e_turned, row, last), column(w_turned, row, 0)
            under, over = tracers[tracer, jnp.minimum(l + 1, levels - 1)], tracers[tracer, jnp.maximum(l - 1, 0)]
            held[tracer, l] = update(c, tracers[tracer, l], halo, under, over, forcing(tracer, l))
        return 0

    lax.fori_loop(0, levels, first_step, 0, unroll=8)

    def second_step(l, _):
        c = [weights[i, l] for i in range(5)]
        for tracer in range(2):
            row = tracer * levels + l
            halo = line_n[pl.ds(row, 1), :], line_s[pl.ds(row, 1), :], column(e_later, row, last), column(w_later, row, 0)
            under, over = held[tracer, jnp.minimum(l + 1, levels - 1)], held[tracer, jnp.maximum(l - 1, 0)]
            out[tracer, l] = update(c, held[tracer, l], halo, under, over, forcing(tracer, l))
        send(l).start()
        return 0

    lax.fori_loop(0, levels, second_step, 0, unroll=8)
    for l in range(levels):
        send(l).wait()


def backward_kernel(parts, slots_in, src_in, back, w, out, held, wide, picked, terms, slots, src, sems):
    total, width = terms.shape
    blocks = out.shape[0]
    batch = total // parts

    def copy(c):
        return pltpu.make_async_copy(w.at[pl.ds(c * batch, batch)], held.at[pl.ds(c * batch, batch)], sems.at[c])

    slots_copy = pltpu.make_async_copy(slots_in, slots, sems.at[parts])
    src_copy = pltpu.make_async_copy(src_in, src, sems.at[parts + 1])
    slots_copy.start()
    src_copy.start()
    for c in range(parts):
        copy(c).start()
    slots_copy.wait()
    wide[...] = back[...].astype(F32).reshape(wide.shape)

    def pick(i, _):
        for j in range(16):
            picked[pl.ds(i * 16 + j, 1), :] = wide[pl.ds(slots[i * 16 + j], 1), :]
        return 0

    lax.fori_loop(0, total // 16, pick, 0, unroll=2)
    row = iota((16, width), 0)

    def work(c, _):
        copy(c).wait()
        for g in range(batch // 16):
            at = pl.multiple_of(c * batch + g * 16, 16)
            rows = picked[pl.ds(at, 16), :]
            left = [jnp.where((row == r) | (row == 8 + r), rows, 0.0).astype(BF16) for r in range(8)]
            block = held[pl.ds(at, 16)].reshape(2, 8 * width, width)
            both = dot(jnp.concatenate(left, axis=1), jnp.concatenate([block[0], block[1]], axis=1), NN)
            terms[pl.ds(at, 8), :] = both[:8, :width]
            terms[pl.ds(at + 8, 8), :] = both[8:, width:]
        return 0

    lax.fori_loop(0, parts, work, 0)
    src_copy.wait()
    hot = (iota((blocks, total), 0) == src[...]).astype(F32).astype(BF16)
    value = terms[...]
    high = value.astype(BF16)
    low = (value - high.astype(F32)).astype(BF16)
    both = dot(hot, jnp.concatenate([high, low], axis=1), NN)
    out[...] = both[:, :width] + both[:, width:]


def backward(back, w, src, slots, blocks, parts=20):
    total, width, _ = w.shape
    devices, cap, _ = back.shape
    return pl.pallas_call(
        functools.partial(backward_kernel, parts),
        in_specs=[ANY, ANY, VMEM, ANY],
        out_specs=VMEM,
        scratch_shapes=[
            pltpu.VMEM(w.shape, BF16),
            pltpu.VMEM((devices * cap, width), F32),
            pltpu.VMEM((total, width), F32),
            pltpu.VMEM((total, width), F32),
            pltpu.SMEM((total,), jnp.int32),
            pltpu.VMEM((1, total), jnp.int32),
            pltpu.SemaphoreType.DMA((parts + 2,)),
        ],
        out_shape=jax.ShapeDtypeStruct((blocks, width), F32),
        compiler_params=kernel_params(46),
        cost_estimate=pl.CostEstimate(flops=2 * total * 8 * width * width, bytes_accessed=total * width * width * 2, transcendentals=0),
        name="backward_remap",
    )(slots, src.reshape(1, total), back, w)


def kernel(body, outs, name, mebibytes, bytes_accessed, scratch=(), **specs):
    return pl.pallas_call(
        body,
        out_shape=[jax.ShapeDtypeStruct(shape, dtype) for shape, dtype in outs],
        scratch_shapes=list(scratch),
        compiler_params=kernel_params(mebibytes),
        cost_estimate=pl.CostEstimate(flops=bytes_accessed, bytes_accessed=bytes_accessed, transcendentals=0),
        name=name,
        **specs,
    )


def neighbours(axis):
    count = lax.axis_size(axis)
    forward_pairs = [(i, i + 1) for i in range(count - 1)]
    return forward_pairs, [(b, a) for a, b in forward_pairs]


def swap_order(count):
    return [0, count - 1, count - 2, 1] + list(range(count - 3, 1, -1))


def swapped(array, axes, count, step):
    return lax.ppermute(array, axes, [(i, i ^ step) for i in range(count)])


def on_device(atm_flux, remap_weights, remap_src, remap_dst, remap_owner, tracers, currents, land_sea):
    grid = n_sec, n_gx, n_gy = [lax.axis_size(axis) for axis in EVERY]
    planes = n_sec * n_gy
    total, width, _ = remap_weights.shape
    _, levels, height, _ = tracers.shape
    cap = up(2 * total // (planes * n_gx), 8)
    wide = SENT * width

    *sends, slots = forward(atm_flux, remap_weights, remap_src, remap_owner.reshape(1, total), remap_dst, grid, cap)
    chunk = sends[0].shape[1]
    order = swap_order(planes)
    got = [sends[0]] + [swapped(sends[m], ("sec", "gy"), planes, m) for m in order[1:]]
    early = order.index(1)

    side = (width, width)
    end = (7 * levels + 80, width)
    to_north, to_south = neighbours(NORTH)
    to_east, to_west = neighbours("gy")
    got[early], tracers_there, currents_there = lax.optimization_barrier((got[early], tracers, currents))
    own_s, own_n = kernel(rows_kernel, [(side, BF16)] * 2, "edge_rows", 16, 1 << 20)(
        tracers_there.reshape(-1, width), currents_there.reshape(-1, width), land_sea
    )
    from_n = lax.ppermute(own_s, NORTH, to_south)
    from_s = lax.ppermute(own_n, NORTH, to_north)
    got, from_n, from_s = lax.optimization_barrier((got, from_n, from_s))
    own_w, own_e = kernel(columns_kernel, [(end, BF16)] * 2, "edge_columns", 16, 1 << 22, [pltpu.VMEM(end, F32)] * 2)(
        tracers, currents, land_sea, from_n, from_s
    )
    from_e = lax.ppermute(own_w, "gy", to_west)
    from_w = lax.ppermute(own_e, "gy", to_east)
    outs = [((height + 8, x), dtype) for x in (4 * width, width) for dtype in [F32] + [BF16] * (n_gx - 1)]
    merged = kernel(functools.partial(merge_kernel, planes), outs, "merge", 24, 1 << 22)(*got)
    parts, salts = merged[:n_gx], merged[n_gx:]
    parts = [parts[0]] + [swapped(parts[m], "gx", n_gx, m) for m in range(1, n_gx)]
    salts, from_e, from_w = lax.optimization_barrier((salts, from_e, from_w))
    salts = [salts[0]] + [swapped(salts[m], "gx", n_gx, m) for m in range(1, n_gx)]

    edges = own_n, own_s, own_e, own_w, from_n, from_s, from_e, from_w
    (back,) = kernel(
        functools.partial(surface_kernel, grid, chunk, levels),
        [((planes * n_gx, cap, width), BF16)],
        "surface",
        24,
        1 << 22,
    )(*parts, tracers[0:1, 0:3], currents[:, 0:2], land_sea, *edges)
    back, salts = lax.optimization_barrier((back, salts))
    returned = lax.all_to_all(back, EVERY, split_axis=0, concat_axis=0, tiled=True)

    plane = (height, width)
    given = (*parts, *salts, *edges, land_sea, tracers, currents)
    (tracers_out,) = kernel(
        functools.partial(stencil_kernel, n_gx),
        [(tracers.shape, F32)],
        "substeps",
        58,
        1 << 24,
        [pltpu.VMEM(x.shape, x.dtype) for x in given]
        + [
            pltpu.VMEM(tracers.shape, F32),
            pltpu.VMEM(tracers.shape, F32),
            pltpu.VMEM((5, levels) + plane, F32),
            pltpu.VMEM(side, F32),
            pltpu.VMEM(side, F32),
            pltpu.VMEM((2 * levels, width), F32),
            pltpu.VMEM((2 * levels, width), F32),
            pltpu.VMEM((levels, width), F32),
            pltpu.VMEM((3,) + plane, F32),
            pltpu.VMEM((4,) + plane, F32),
            pltpu.SemaphoreType.DMA((len(given) + levels,)),
        ],
        in_specs=[ANY] * len(given),
        out_specs=[ANY],
    )(*given)
    return tracers_out, backward(returned, remap_weights, remap_src, slots, atm_flux.shape[0])


def solution(mesh):
    return jax.shard_map(
        on_device,
        mesh=mesh,
        in_specs=(
            P(EVERY, None, None),
            P(EVERY, None, None),
            P(EVERY),
            P(EVERY),
            P(EVERY, None),
            P(None, None, NORTH, "gy"),
            P(None, None, NORTH, "gy"),
            P(NORTH, "gy"),
        ),
        out_specs=(P(None, None, NORTH, "gy"), P(EVERY, None)),
        check_vma=False,
    )
```

```python
import functools

import jax
import jax.numpy as jnp
from jax import lax
from jax.experimental import pallas as pl
from jax.experimental.pallas import tpu as pltpu
from jax.sharding import PartitionSpec as P

F32 = jnp.float32
BF16 = jnp.bfloat16
NT = (((1,), (1,)), ((), ()))
NN = (((1,), (0,)), ((), ()))
TN = (((0,), (0,)), ((), ()))
EVERY = ("sec", "gx", "gy")
NORTH = ("sec", "gx")
SENT = 5
KH = 0.1
KV = 0.1


def dot(left, right, dims):
    return lax.dot_general(left, right, dims, preferred_element_type=F32)


def iota(shape, dim):
    return lax.broadcasted_iota(jnp.int32, shape, dim)


def up(number, step):
    return -(-number // step) * step


def kernel_params(mebibytes):
    return pltpu.CompilerParams(vmem_limit_bytes=mebibytes << 20)


VMEM = pl.BlockSpec(memory_space=pltpu.VMEM)
SMEM = pl.BlockSpec(memory_space=pltpu.SMEM)
ANY = pl.BlockSpec(memory_space=pl.ANY)


def forward_kernel(parts, cap, grid, src_in, own_in, dst_in, flux_in, w, *refs):
    sends, (slots, held, mixed, acc, rows, xs, counts, renumbered, sems, src, own, dst, flux) = refs[:-13], refs[-13:]
    n_sec, n_gx, n_gy = grid
    devices, _, wide = xs.shape
    total, width, _ = held.shape
    batch = total // parts
    fields = flux.shape[1]
    main = sends[0].shape[1] - 16
    first = 8
    last = width - 1

    def copy(c):
        return pltpu.make_async_copy(w.at[pl.ds(c * batch, batch)], held.at[pl.ds(c * batch, batch)], sems.at[c])

    small = [(src_in, src), (own_in, own), (dst_in, dst), (flux_in, flux)]
    small = [pltpu.make_async_copy(there, here, sems.at[parts + i]) for i, (there, here) in enumerate(small)]
    for load in small:
        load.start()
    for c in range(parts):
        copy(c).start()

    plane = lax.axis_index("sec") * n_gy + lax.axis_index("gy")
    line = lax.axis_index("gx")

    def renumber(owner):
        x = lax.div(owner, n_gy)
        there = lax.div(x, n_gx) * n_gy + lax.rem(owner, n_gy)
        return (there ^ plane) * n_gx + (lax.rem(x, n_gx) ^ line)

    def clear(o, _):
        counts[o] = 0
        renumbered[o] = renumber(o)
        return 0

    lax.fori_loop(0, devices, clear, 0)
    rows[...] = jnp.full_like(rows, 255.0)
    acc[...] = jnp.zeros_like(acc)
    xs[...] = jnp.zeros_like(xs)
    for load in small:
        load.wait()
    full = flux[...].astype(F32)
    one = [full[:, f : f + 1] for f in range(fields)]
    heat = 0.2 * (one[1] + one[2] + one[3]) - 0.15 * one[5]
    salt = 0.2 * one[4] - 0.1 * one[5]
    heat_high = heat.astype(BF16).astype(F32)
    salt_high = salt.astype(BF16).astype(F32)
    mixed[...] = jnp.concatenate(
        [one[0], heat_high, salt_high, one[6], one[7], heat - heat_high, salt - salt_high, jnp.zeros_like(heat)], axis=1
    ).astype(BF16)

    low_rows = iota((fields, width), 0)
    low_rows = (low_rows == 1) | (low_rows == 2)

    def work(c, _):
        copy(c).wait()
        for b in range(0, batch, 2):
            k = c * batch + b
            left = jnp.concatenate([mixed[src[k]], mixed[src[k + 1]]], axis=0)
            both = dot(left, held[pl.ds(k, 2)].reshape(2 * width, width), NT)
            for z, part in enumerate((both[:fields, :width], both[fields:, width:])):
                part = part + jnp.where(low_rows, pltpu.roll(part, fields - 4, 0), 0.0)
                owner = own[0, k + z]
                at = counts[owner]
                counts[owner] = at + 1
                at = jnp.minimum(at, cap - 1)
                slots[k + z] = owner * cap + at
                slot = renumbered[owner] * cap + at
                acc[pl.ds(pl.multiple_of(slot * fields, fields), fields), :] = part
                rows[pl.ds(slot, 1), :] = jnp.full((1, width), dst[k + z].astype(F32), F32)
        return 0

    lax.fori_loop(0, parts, work, 0)

    lane = iota((cap, width), 1).astype(F32)
    sub = iota((cap, width), 0).astype(F32)
    row = iota((24, wide), 0)
    picks = {
        4: (0, 0), 5: (1, 0), 6: (3, 0), 7: (4, 0), 12: (0, last), 13: (1, last), 14: (3, last), 15: (4, last),
        20: (2, 0), 21: (3, 1), 22: (2, last), 23: (3, last - 1),
    }
    pick = jnp.full((24, wide), -1, jnp.int32)
    for at, (field, column) in picks.items():
        pick = jnp.where(row == at, field * width + column, pick)
    select = (iota((24, wide), 1) == pick).astype(F32).astype(BF16)
    row = iota((8, cap), 0)
    wanted = jnp.zeros((8, cap), F32)
    for at, x in enumerate((0, 1, last, last - 1, 0, 0, last, last)):
        wanted = jnp.where(row == at, float(x), wanted)
    group = 16

    def owners(g):
        ds = [g * group + j for j in range(group)]
        five = []
        for d in ds:
            x = [acc[pl.ds(d * cap * fields + f, cap, stride=fields), :] for f in range(SENT)]
            x = jnp.concatenate(x, axis=1)
            if cap > main:
                xs[d, 0 : cap - main, :] = x[main:]
            x = x.astype(BF16)
            sends[d // n_gx][d % n_gx, 0:main, :] = x[:main]
            five.append(x)
        where = [rows[pl.ds(pl.multiple_of(d * cap, 8), cap), :] for d in ds]
        hot = [(lane == r).astype(F32).astype(BF16) for r in where]
        flat = [jnp.sum(jnp.where(lane == sub, r, 0.0), axis=0, keepdims=True) for r in where]
        flat = [jnp.where(lane[:1] < cap, f, 255.0) for f in flat]
        edge = [dot(select, x, NT).astype(BF16) for x in five]
        sides = [dot(e, h, NN) for e, h in zip(edge, hot)]
        ends = [dot((f[:, :cap] == wanted).astype(F32).astype(BF16), x, NN) for f, x in zip(flat, five)]
        for d, f, side, end in zip(ds, flat, sides, ends):
            here = (d // n_gx) ^ plane
            here = (lax.div(here, n_gy) * n_gx + ((d % n_gx) ^ line)) * n_gy + lax.rem(here, n_gy)

            def at(offset):
                return renumbered[lax.rem(here + offset + 2 * devices, devices)]

            south_of, north_of, west_of, east_of = at(-n_gy), at(n_gy), at(-1), at(1)

            xs[south_of, first : first + 1, :] = end[0:1]
            xs[south_of, first + 1 : first + 2, 4 * width :] = end[1:2, 4 * width :]
            xs[north_of, first + 2 : first + 3, :] = end[2:3]
            xs[north_of, first + 3 : first + 4, 4 * width :] = end[3:4, 4 * width :]
            xs[at(-n_gy - 1), first + 4 : first + 5, 3 * width :] = end[4:5, 3 * width :]
            xs[at(-n_gy + 1), first + 5 : first + 6, 3 * width :] = end[5:6, 3 * width :]
            xs[at(n_gy - 1), first + 6 : first + 7, 3 * width :] = end[6:7, 3 * width :]
            xs[at(n_gy + 1), first + 7 : first + 8, 3 * width :] = end[7:8, 3 * width :]
            xs[west_of, first + 4 : first + 8, 0:width] = side[4:8]
            xs[east_of, first + 4 : first + 8, width : 2 * width] = side[12:16]
            xs[west_of, first + 4 : first + 6, 2 * width : 3 * width] = side[20:22]
            xs[east_of, first + 6 : first + 8, 2 * width : 3 * width] = side[22:24]
            xs[d, first + 1 : first + 2, 0:width] = f

    for g in range(devices // group):
        owners(g)

    for m, send in enumerate(sends):
        send[:, main:, :] = xs[m * n_gx : (m + 1) * n_gx].astype(BF16)


def forward(flux, w, src, own, dst, grid, cap, parts=8):
    n_sec, n_gx, n_gy = grid
    devices = n_sec * n_gx * n_gy
    total, width, _ = w.shape
    chunk = up(cap + 8, 16)
    fields = flux.shape[1]
    wide = SENT * width
    return pl.pallas_call(
        functools.partial(forward_kernel, parts, cap, grid),
        in_specs=[ANY] * 5,
        out_specs=[VMEM] * (n_sec * n_gy) + [SMEM],
        scratch_shapes=[
            pltpu.VMEM(w.shape, BF16),
            pltpu.VMEM(flux.shape, BF16),
            pltpu.VMEM((devices * cap * fields, width), F32),
            pltpu.VMEM((devices * cap, width), F32),
            pltpu.VMEM((devices, 16, wide), F32),
            pltpu.SMEM((devices,), jnp.int32),
            pltpu.SMEM((devices,), jnp.int32),
            pltpu.SemaphoreType.DMA((parts + 4,)),
            pltpu.SMEM(src.shape, jnp.int32),
            pltpu.SMEM(own.shape, jnp.int32),
            pltpu.SMEM(dst.shape, jnp.int32),
            pltpu.VMEM(flux.shape, BF16),
        ],
        out_shape=[jax.ShapeDtypeStruct((n_gx, chunk, wide), BF16)] * (n_sec * n_gy) + [jax.ShapeDtypeStruct((total,), jnp.int32)],
        compiler_params=kernel_params(58),
        cost_estimate=pl.CostEstimate(flops=2 * total * 8 * width * width, bytes_accessed=total * width * width * 2, transcendentals=0),
        name="forward_remap",
    )(src, own, dst, flux, w)


def merge_kernel(n_sources, *refs):
    sources, outs = refs[:n_sources], refs[n_sources:]
    chunk = sources[0].shape[1]
    height = outs[0].shape[0] - 8
    count = n_sources * chunk
    for z, out in enumerate(outs):
        ext = None
        where = []
        for source in sources:
            piece = source[z, chunk - 16 : chunk, :].astype(F32)[8:]
            where.append(piece[1:2, :chunk])
            ext = piece if ext is None else ext + piece
        where = jnp.concatenate(where, axis=1)
        hot = (iota((height, count), 0).astype(F32) == where).astype(F32).astype(BF16)
        sums = dot(hot, jnp.concatenate([source[z] for source in sources], axis=0), NN)
        row3 = jnp.concatenate([where, ext[3:4, count:]], axis=1)
        ext = jnp.where(iota((8, 1), 0) == 3, row3, ext)
        out[...] = jnp.concatenate([sums, ext], axis=0).astype(out.dtype)


def rows_kernel(tracers, currents, land, south, north):
    height, width = land.shape
    levels = tracers.shape[0] // 2 // height
    for out, edge, second in ((south, 0, 1), (north, height - 1, height - 2)):
        out[...] = jnp.concatenate(
            [
                tracers[pl.ds(edge, 2 * levels, stride=height), :],
                tracers[pl.ds(second, 2 * levels, stride=height), :],
                currents[pl.ds(edge, 2 * levels, stride=height), :],
                currents[pl.ds(levels * height + second, levels, stride=height), :],
                *[land[x : x + 1, :].astype(F32) for x in (edge, second)],
                jnp.zeros((out.shape[0] - 7 * levels - 2, width), F32),
            ],
            axis=0,
        ).astype(BF16)


def columns_kernel(tracers, currents, land, from_n, from_s, west, east, west_wide, east_wide):
    levels = tracers.shape[1]
    width = tracers.shape[3]
    last = width - 1
    lane = iota((1, width), 1)
    west_wide[...] = jnp.zeros_like(west_wide)
    east_wide[...] = jnp.zeros_like(east_wide)

    def put(plane, near, far):
        turned = plane.T
        for out, edge, second in ((west_wide, 0, 1), (east_wide, last, last - 1)):
            out[pl.ds(near, 1), :] = turned[edge : edge + 1]
            if far is not None:
                out[pl.ds(far, 1), :] = turned[second : second + 1]

    def level(l, _):
        for t in range(2):
            put(tracers[t, l], t * levels + l, (2 + t) * levels + l)
        put(currents[0, l], 4 * levels + l, 6 * levels + l)
        put(currents[1, l], 5 * levels + l, None)
        return 0

    lax.fori_loop(0, levels, level, 0, unroll=2)
    put(land[...].astype(F32), 7 * levels, 7 * levels + 1)
    base = 7 * levels + 8
    n_all, s_all = from_n[...].astype(F32), from_s[...].astype(F32)
    for start, stop, at in ((0, 2 * levels, 0), (4 * levels, 6 * levels, 2 * levels), (7 * levels, 7 * levels + 8, 4 * levels)):
        n, s = n_all[start:stop], s_all[start:stop]
        west_wide[base + at : base + at + stop - start] = jnp.where(lane == last, pltpu.roll(n, last, 1), s)
        east_wide[base + at : base + at + stop - start] = jnp.where(lane == last, n, pltpu.roll(s, 1, 1))
    west[...] = west_wide[...].astype(BF16)
    east[...] = east_wide[...].astype(BF16)


def plus_side(q, other, speed, speed_other, passable):
    return KH * passable * (other - q) - 0.25 * (speed + speed_other) * passable * (q + other)


def minus_side(q, other, speed, speed_other, passable):
    return KH * passable * (other - q) + 0.25 * (speed_other + speed) * passable * (other + q)


def level_profile(levels, width):
    depth = iota((levels, width), 0).astype(F32)
    return jnp.exp(-depth / 4.0) * (1.0 - jnp.exp(jnp.full((levels, width), -0.25, F32)))


def strip_step(q, q_plus, q_minus, across, across_plus, across_minus, along, corner_q, corner_along, wet, wet_plus, wet_minus, corner_wet, forcing):
    levels, width = q.shape
    lane = iota((1, width), 1)
    row = iota((levels, 1), 0)

    def ahead(x, corner):
        return jnp.where(lane == width - 1, corner, pltpu.roll(x, width - 1, 1))

    def behind(x, corner):
        return jnp.where(lane == 0, corner, pltpu.roll(x, 1, 1))

    total = plus_side(q, q_plus, across, across_plus, wet * wet_plus)
    total += minus_side(q, q_minus, across, across_minus, wet * wet_minus)
    total += plus_side(q, ahead(q, corner_q), along, ahead(along, corner_along), wet * ahead(wet, corner_wet))
    total += minus_side(q, behind(q, corner_q), along, behind(along, corner_along), wet * behind(wet, corner_wet))
    below = jnp.where(row < levels - 1, pltpu.roll(q, levels - 1, 0) - q, 0.0)
    above = jnp.where(row > 0, q - pltpu.roll(q, 1, 0), 0.0)
    return q + total + wet * (KV * (below - above) + forcing)


def strips(tracer, levels, inner, outer, flux):
    width = outer[0].shape[1]
    lane = iota((1, width), 1)
    base = 7 * levels + 8
    north, south, east, west = outer

    def part(x, at, count=levels):
        return x[at : at + count]

    def corners(at, count):
        e, w = part(east, base + at, count), part(west, base + at, count)
        n = jnp.where(lane == width - 1, e, pltpu.roll(w, 1, 1))
        s = jnp.where(lane == width - 1, pltpu.roll(e, width - 1, 1), w)
        return n, s, e, w

    corner_q = corners(tracer * levels, levels)
    corner_u = corners(2 * levels, levels)
    corner_v = corners(3 * levels, levels)
    corner_wet = corners(4 * levels, 1)
    top = (iota((levels, 1), 0) == 0).astype(F32)
    profile = level_profile(levels, width)
    results = []
    for side in range(4):
        near, far = inner[side], outer[side]
        beside, out = part(near, tracer * levels), part(far, (2 + tracer) * levels)
        mid = part(far, tracer * levels)
        speed = 5 if side < 2 else 4
        along = part(far, (9 - speed) * levels)
        corner_along = (corner_u if side < 2 else corner_v)[side]
        across, across_in, across_out = part(far, speed * levels), part(near, speed * levels), part(far, 6 * levels)
        wet, wet_in, wet_out = part(far, 7 * levels, 1), part(near, 7 * levels, 1), part(far, 7 * levels + 1, 1)
        shortwave, heat, salt = flux[side]
        forcing = 0.3 * profile * shortwave + top * heat if tracer == 0 else top * salt
        if side % 2 == 0:
            pairs = (out, beside, across, across_out, across_in)
            wets = (wet, wet_out, wet_in)
        else:
            pairs = (beside, out, across, across_in, across_out)
            wets = (wet, wet_in, wet_out)
        results.append(strip_step(mid, *pairs, along, corner_q[side], corner_along, *wets, corner_wet[side], forcing))
    return results


def shifts(plane, north, south, east, west):
    height, width = plane.shape
    lane, row = iota(plane.shape, 1), iota(plane.shape, 0)
    return (
        jnp.where(lane == width - 1, east, pltpu.roll(plane, width - 1, 1)),
        jnp.where(lane == 0, west, pltpu.roll(plane, 1, 1)),
        jnp.where(row == height - 1, north, pltpu.roll(plane, height - 1, 0)),
        jnp.where(row == 0, south, pltpu.roll(plane, 1, 0)),
    )


def wet_products(wet, north, south, east, west):
    return [wet * other for other in shifts(wet, north, south, east, west)]


def coefficients(u, v, u_east, u_west, v_north, v_south, passable):
    east, west, north, south = passable
    height, width = u.shape
    lane, row = iota(u.shape, 1), iota(u.shape, 0)
    e = jnp.where(lane == width - 1, u_east, pltpu.roll(u, width - 1, 1))
    w = jnp.where(lane == 0, u_west, pltpu.roll(u, 1, 1))
    n = jnp.where(row == height - 1, v_north, pltpu.roll(v, height - 1, 0))
    s = jnp.where(row == 0, v_south, pltpu.roll(v, 1, 0))
    flow_e, flow_w = 0.25 * (u + e) * east, 0.25 * (w + u) * west
    flow_n, flow_s = 0.25 * (v + n) * north, 0.25 * (s + v) * south
    own = 1.0 + (flow_w - flow_e) + (flow_s - flow_n) - KH * (east + west + north + south)
    return own, KH * east - flow_e, KH * west + flow_w, KH * north - flow_n, KH * south + flow_s


def column(turned, index, lane):
    return pltpu.roll(turned, lax.rem(lane - index + 2 * turned.shape[1], turned.shape[1]), 1)


def corrected(edge, x_rows):
    row = iota((edge.shape[0], 1), 0)
    for at, x in x_rows:
        edge = edge + jnp.where(row == at, 0.1 * x, 0.0)
    return edge


def owner_sums(height, width, parts):
    sums = parts[0][...]
    for part in parts[1:]:
        sums = sums + part[...].astype(F32)
    return [sums[:height, f * width : (f + 1) * width] for f in range(SENT)], sums[height : height + 8]


def corrected_edges(levels, ext, stress_u, stress_v, near, far):
    height, width = stress_u.shape
    last = width - 1
    lane = iota((1, width), 1)

    def block(r, b):
        return ext[r : r + 1, b * width : (b + 1) * width]

    u, v, second = 4 * levels, 5 * levels, 6 * levels
    base = 7 * levels + 8
    corners = []
    for b in (3, 4):
        ne, nw, se, sw = [block(r, b) for r in (4, 5, 6, 7)]
        corners.append((jnp.where(lane == last, pltpu.roll(ne, last, 1), se), jnp.where(lane == last, nw, pltpu.roll(sw, 1, 1))))
    turned = stress_u.T
    own = [[(v, stress_v[last:])], [(v, stress_v[0:1])], [(u, turned[last:])], [(u, turned[0:1])]]
    beside = [
        [(u, block(0, 3)), (v, block(0, 4)), (second, block(1, 4))],
        [(u, block(2, 3)), (v, block(2, 4)), (second, block(3, 4))],
        [(u, block(6, 0)), (v, block(7, 0)), (second, block(5, 2)), (base + 2 * levels, corners[0][0]), (base + 3 * levels, corners[1][0])],
        [(u, block(6, 1)), (v, block(7, 1)), (second, block(7, 2)), (base + 2 * levels, corners[0][1]), (base + 3 * levels, corners[1][1])],
    ]
    near = [corrected(edge[...].astype(F32), x) for edge, x in zip(near, own)]
    return near, [corrected(edge[...].astype(F32), x) for edge, x in zip(far, beside)]


def surface_kernel(grid, chunk, levels, *refs):
    n_sec, n_gx, n_gy = grid
    planes = n_sec * n_gy
    parts, refs = refs[:n_gx], refs[n_gx:]
    tracers, currents, land, own_n, own_s, own_e, own_w, from_n, from_s, from_e, from_w, *refs = refs
    (back,) = refs
    height, width = land.shape
    last = width - 1
    lane = iota((1, width), 1)
    (shortwave, heat, salt, stress_u, stress_v), ext = owner_sums(height, width, parts)
    wet = land[...].astype(F32)
    u0 = currents[0, 0] + 0.1 * stress_u
    v0 = currents[1, 0] + 0.1 * stress_v
    near, far = corrected_edges(levels, ext, stress_u, stress_v, (own_n, own_s, own_e, own_w), (from_n, from_s, from_e, from_w))
    far_n, far_s, far_e, far_w = far
    e_turned, w_turned = far_e[:width].T, far_w[:width].T
    east = lambda index: column(e_turned, index, last)
    west = lambda index: column(w_turned, index, 0)
    passable = wet_products(
        wet, far_n[7 * levels : 7 * levels + 1], far_s[7 * levels : 7 * levels + 1], east(7 * levels), west(7 * levels)
    )
    lines = strips(0, levels, near, far, rim_flux(ext, width))
    profile = level_profile(levels, width)
    mix = KV * wet
    warm = 0.3 * wet * shortwave

    def weights(l, u, v):
        v_n, v_s = [x[5 * levels + l : 5 * levels + l + 1] for x in (far_n, far_s)]
        return coefficients(u, v, east(4 * levels + l), west(4 * levels + l), v_n, v_s, passable)

    def horizontal(c, q, halo):
        e, w, n, s = shifts(q, *halo)
        return c[0] * q + c[1] * e + c[2] * w + c[3] * n + c[4] * s

    def start(l):
        return far_n[l : l + 1], far_s[l : l + 1], east(l), west(l)

    q0, q1, q2 = tracers[0, 0], tracers[0, 1], tracers[0, 2]
    c0 = weights(0, u0, v0)
    c1 = weights(1, currents[0, 1], currents[1, 1])
    t0 = horizontal(c0, q0, start(0)) + mix * (q1 - q0) + warm * profile[0:1] + wet * heat
    t1 = horizontal(c1, q1, start(1)) + mix * ((q2 - q1) - (q1 - q0)) + warm * profile[1:2]
    sides = jnp.concatenate([lines[2][0:8], lines[3][0:8], jnp.zeros((width - 16, width), F32)], axis=0).T
    halo = lines[0][0:1], lines[1][0:1], column(sides, 0, last), column(sides, 8, 0)
    t0 = horizontal(c0, t0, halo) + mix * (t1 - t0) + warm * profile[0:1] + wet * heat
    sst = t0.astype(BF16)
    plane = lax.axis_index("sec") * n_gy + lax.axis_index("gy")
    line = lax.axis_index("gx")
    for z, part in enumerate(parts):
        where = part[...].astype(F32)[height + 3 : height + 4, : planes * chunk]
        hot = (iota((height, planes * chunk), 0).astype(F32) == where).astype(F32)
        picked = dot(hot.T.astype(BF16), sst, NN).reshape(planes, chunk, width)
        for i, m in enumerate(swap_order(planes)):
            there = plane ^ m
            device = (lax.div(there, n_gy) * n_gx + (line ^ z)) * n_gy + lax.rem(there, n_gy)
            back[device] = picked[i, : back.shape[1]].astype(BF16)


def rim_flux(ext, width):
    def block(r, b):
        return ext[r : r + 1, b * width : (b + 1) * width]

    return (
        (block(0, 0), block(0, 1), block(0, 2)),
        (block(2, 0), block(2, 1), block(2, 2)),
        (block(4, 0), block(5, 0), block(4, 2)),
        (block(4, 1), block(5, 1), block(6, 2)),
    )


def stencil_kernel(n_gx, *refs):
    count = n_gx + 11
    given, result, here, refs = refs[:count], refs[count], refs[count + 1 : 2 * count + 1], refs[2 * count + 1 :]
    out, held, weights, edge_n, edge_s, line_n, line_s, depth, forced, passing, sems = refs
    parts, edges, (land, tracers, currents) = here[:n_gx], here[n_gx : n_gx + 8], here[n_gx + 8 :]
    copies = [pltpu.make_async_copy(x, y, sems.at[i]) for i, (x, y) in enumerate(zip(given, here))]
    for copy in copies:
        copy.start()
    for copy in copies[:-2]:
        copy.wait()
    levels = tracers.shape[1]

    def send(l):
        return pltpu.make_async_copy(out.at[:, l], result.at[:, l], sems.at[count + l])

    height, width = land.shape
    last = width - 1
    wet = land[...].astype(F32)
    (shortwave, heat, salt, stress_u, stress_v), ext = owner_sums(height, width, parts)
    near, far = corrected_edges(levels, ext, stress_u, stress_v, edges[:4], edges[4:])
    far_n, far_s, far_e, far_w = far
    edge_n[...], edge_s[...] = far_n, far_s
    e_turned, w_turned = far_e[:width].T, far_w[:width].T
    at = 7 * levels
    for i, x in enumerate(
        wet_products(wet, far_n[at : at + 1], far_s[at : at + 1], column(e_turned, at, last), column(w_turned, at, 0))
    ):
        passing[i] = x
    forced[0], forced[1], forced[2] = 0.3 * wet * shortwave, wet * heat, wet * salt
    depth[...] = level_profile(levels, width)
    columns = []
    for tracer in range(2):
        lines = strips(
            tracer, levels, near, far, rim_flux(ext, width)
        )
        line_n[tracer * levels : (tracer + 1) * levels] = lines[0]
        line_s[tracer * levels : (tracer + 1) * levels] = lines[1]
        columns.append(lines[2:])
    blank = jnp.zeros((width - 2 * levels, width), F32)
    e_later, w_later = [jnp.concatenate([columns[0][i], columns[1][i], blank], axis=0).T for i in range(2)]

    def update(c, q, halo, under, over, forcing):
        e, w, n, s = shifts(q, *halo)
        mixed = KV * land[...].astype(F32) * ((under - q) - (q - over))
        return c[0] * q + c[1] * e + c[2] * w + c[3] * n + c[4] * s + mixed + forcing

    def forcing(tracer, l):
        top = jnp.where(l == 0, 1.0, 0.0)
        if tracer == 0:
            return forced[0] * depth[pl.ds(l, 1), :] + top * forced[1]
        return top * forced[2]

    for copy in copies[-2:]:
        copy.wait()
    currents[0, 0] = currents[0, 0] + 0.1 * stress_u
    currents[1, 0] = currents[1, 0] + 0.1 * stress_v

    def first_step(l, _):
        u, v = currents[0, l], currents[1, l]
        row = 5 * levels + l
        c = coefficients(
            u, v, column(e_turned, 4 * levels + l, last), column(w_turned, 4 * levels + l, 0),
            edge_n[pl.ds(row, 1), :], edge_s[pl.ds(row, 1), :], [passing[i] for i in range(4)],
        )
        for i, x in enumerate(c):
            weights[i, l] = x
        for tracer in range(2):
            row = tracer * levels + l
            halo = edge_n[pl.ds(row, 1), :], edge_s[pl.ds(row, 1), :], column(e_turned, row, last), column(w_turned, row, 0)
            under, over = tracers[tracer, jnp.minimum(l + 1, levels - 1)], tracers[tracer, jnp.maximum(l - 1, 0)]
            held[tracer, l] = update(c, tracers[tracer, l], halo, under, over, forcing(tracer, l))
        return 0

    lax.fori_loop(0, levels, first_step, 0, unroll=8)

    def second_step(l, _):
        c = [weights[i, l] for i in range(5)]
        for tracer in range(2):
            row = tracer * levels + l
            halo = line_n[pl.ds(row, 1), :], line_s[pl.ds(row, 1), :], column(e_later, row, last), column(w_later, row, 0)
            under, over = held[tracer, jnp.minimum(l + 1, levels - 1)], held[tracer, jnp.maximum(l - 1, 0)]
            out[tracer, l] = update(c, held[tracer, l], halo, under, over, forcing(tracer, l))
        send(l).start()
        return 0

    lax.fori_loop(0, levels, second_step, 0, unroll=8)
    for l in range(levels):
        send(l).wait()


def backward_kernel(parts, slots_in, src_in, back, w, out, held, wide, picked, terms, slots, src, sems):
    total, width = terms.shape
    blocks = out.shape[0]
    batch = total // parts

    def copy(c):
        return pltpu.make_async_copy(w.at[pl.ds(c * batch, batch)], held.at[pl.ds(c * batch, batch)], sems.at[c])

    slots_copy = pltpu.make_async_copy(slots_in, slots, sems.at[parts])
    src_copy = pltpu.make_async_copy(src_in, src, sems.at[parts + 1])
    slots_copy.start()
    src_copy.start()
    for c in range(parts):
        copy(c).start()
    slots_copy.wait()
    wide[...] = back[...].astype(F32).reshape(wide.shape)

    def pick(i, _):
        for j in range(16):
            picked[pl.ds(i * 16 + j, 1), :] = wide[pl.ds(slots[i * 16 + j], 1), :]
        return 0

    lax.fori_loop(0, total // 16, pick, 0, unroll=2)
    row = iota((16, width), 0)

    def work(c, _):
        copy(c).wait()
        for g in range(batch // 16):
            at = pl.multiple_of(c * batch + g * 16, 16)
            rows = picked[pl.ds(at, 16), :]
            left = [jnp.where((row == r) | (row == 8 + r), rows, 0.0).astype(BF16) for r in range(8)]
            block = held[pl.ds(at, 16)].reshape(2, 8 * width, width)
            both = dot(jnp.concatenate(left, axis=1), jnp.concatenate([block[0], block[1]], axis=1), NN)
            terms[pl.ds(at, 8), :] = both[:8, :width]
            terms[pl.ds(at + 8, 8), :] = both[8:, width:]
        return 0

    lax.fori_loop(0, parts, work, 0)
    src_copy.wait()
    hot = (iota((blocks, total), 0) == src[...]).astype(F32).astype(BF16)
    value = terms[...]
    high = value.astype(BF16)
    low = (value - high.astype(F32)).astype(BF16)
    both = dot(hot, jnp.concatenate([high, low], axis=1), NN)
    out[...] = both[:, :width] + both[:, width:]


def backward(back, w, src, slots, blocks, parts=20):
    total, width, _ = w.shape
    devices, cap, _ = back.shape
    return pl.pallas_call(
        functools.partial(backward_kernel, parts),
        in_specs=[ANY, ANY, VMEM, ANY],
        out_specs=VMEM,
        scratch_shapes=[
            pltpu.VMEM(w.shape, BF16),
            pltpu.VMEM((devices * cap, width), F32),
            pltpu.VMEM((total, width), F32),
            pltpu.VMEM((total, width), F32),
            pltpu.SMEM((total,), jnp.int32),
            pltpu.VMEM((1, total), jnp.int32),
            pltpu.SemaphoreType.DMA((parts + 2,)),
        ],
        out_shape=jax.ShapeDtypeStruct((blocks, width), F32),
        compiler_params=kernel_params(46),
        cost_estimate=pl.CostEstimate(flops=2 * total * 8 * width * width, bytes_accessed=total * width * width * 2, transcendentals=0),
        name="backward_remap",
    )(slots, src.reshape(1, total), back, w)


def kernel(body, outs, name, mebibytes, bytes_accessed, scratch=(), **specs):
    return pl.pallas_call(
        body,
        out_shape=[jax.ShapeDtypeStruct(shape, dtype) for shape, dtype in outs],
        scratch_shapes=list(scratch),
        compiler_params=kernel_params(mebibytes),
        cost_estimate=pl.CostEstimate(flops=bytes_accessed, bytes_accessed=bytes_accessed, transcendentals=0),
        name=name,
        **specs,
    )


def neighbours(axis):
    count = lax.axis_size(axis)
    forward_pairs = [(i, i + 1) for i in range(count - 1)]
    return forward_pairs, [(b, a) for a, b in forward_pairs]


def swap_order(count):
    return [0, count - 1, count - 2, 1] + list(range(count - 3, 1, -1))


def swapped(array, axes, count, step):
    return lax.ppermute(array, axes, [(i, i ^ step) for i in range(count)])


def on_device(atm_flux, remap_weights, remap_src, remap_dst, remap_owner, tracers, currents, land_sea):
    grid = n_sec, n_gx, n_gy = [lax.axis_size(axis) for axis in EVERY]
    planes = n_sec * n_gy
    total, width, _ = remap_weights.shape
    _, levels, height, _ = tracers.shape
    cap = up(2 * total // (planes * n_gx), 8)
    wide = SENT * width

    *sends, slots = forward(atm_flux, remap_weights, remap_src, remap_owner.reshape(1, total), remap_dst, grid, cap)
    chunk = sends[0].shape[1]
    order = swap_order(planes)
    got = [sends[0]] + [swapped(sends[m], ("sec", "gy"), planes, m) for m in order[1:]]
    early = order.index(1)

    side = (width, width)
    end = (7 * levels + 80, width)
    to_north, to_south = neighbours(NORTH)
    to_east, to_west = neighbours("gy")
    got[early], tracers_there, currents_there = lax.optimization_barrier((got[early], tracers, currents))
    own_s, own_n = kernel(rows_kernel, [(side, BF16)] * 2, "edge_rows", 16, 1 << 20)(
        tracers_there.reshape(-1, width), currents_there.reshape(-1, width), land_sea
    )
    from_n = lax.ppermute(own_s, NORTH, to_south)
    from_s = lax.ppermute(own_n, NORTH, to_north)
    got, from_n, from_s = lax.optimization_barrier((got, from_n, from_s))
    own_w, own_e = kernel(columns_kernel, [(end, BF16)] * 2, "edge_columns", 16, 1 << 22, [pltpu.VMEM(end, F32)] * 2)(
        tracers, currents, land_sea, from_n, from_s
    )
    from_e = lax.ppermute(own_w, "gy", to_west)
    from_w = lax.ppermute(own_e, "gy", to_east)
    part = (height + 8, wide)
    merged = kernel(functools.partial(merge_kernel, planes), [(part, F32)] + [(part, BF16)] * (n_gx - 1), "merge", 24, 1 << 22)(*got)
    parts = [merged[0]] + [swapped(merged[m], "gx", n_gx, m) for m in range(1, n_gx)]

    edges = own_n, own_s, own_e, own_w, from_n, from_s, from_e, from_w
    (back,) = kernel(
        functools.partial(surface_kernel, grid, chunk, levels),
        [((planes * n_gx, cap, width), BF16)],
        "surface",
        24,
        1 << 22,
    )(*parts, tracers[0:1, 0:3], currents[:, 0:2], land_sea, *edges)
    returned = lax.all_to_all(back, EVERY, split_axis=0, concat_axis=0, tiled=True)

    plane = (height, width)
    given = (*parts, *edges, land_sea, tracers, currents)
    (tracers_out,) = kernel(
        functools.partial(stencil_kernel, n_gx),
        [(tracers.shape, F32)],
        "substeps",
        58,
        1 << 24,
        [pltpu.VMEM(x.shape, x.dtype) for x in given]
        + [
            pltpu.VMEM(tracers.shape, F32),
            pltpu.VMEM(tracers.shape, F32),
            pltpu.VMEM((5, levels) + plane, F32),
            pltpu.VMEM(side, F32),
            pltpu.VMEM(side, F32),
            pltpu.VMEM((2 * levels, width), F32),
            pltpu.VMEM((2 * levels, width), F32),
            pltpu.VMEM((levels, width), F32),
            pltpu.VMEM((3,) + plane, F32),
            pltpu.VMEM((4,) + plane, F32),
            pltpu.SemaphoreType.DMA((len(given) + levels,)),
        ],
        in_specs=[ANY] * len(given),
        out_specs=[ANY],
    )(*given)
    return tracers_out, backward(returned, remap_weights, remap_src, slots, atm_flux.shape[0])


def solution(mesh):
    return jax.shard_map(
        on_device,
        mesh=mesh,
        in_specs=(
            P(EVERY, None, None),
            P(EVERY, None, None),
            P(EVERY),
            P(EVERY),
            P(EVERY, None),
            P(None, None, NORTH, "gy"),
            P(None, None, NORTH, "gy"),
            P(NORTH, "gy"),
        ),
        out_specs=(P(None, None, NORTH, "gy"), P(EVERY, None)),
        check_vma=False,
    )
```
